32 devices in a mesh: rep: 4 (over z), grp: 8 (over y, x, core).
Axes of the slice: x: 2, y: 2, z: 4, core: 2. Of those that a mesh axis runs over, the one named last changes fastest.
Arguments:
- hidden_in: bfloat16 [4, 1024, 1024], P('rep', 'grp'), may hold values from -6 to 6
- ln_gain: bfloat16 [2, 1024], P(None, 'grp'), may hold values from 0.5 to 1.5
- ln_bias: bfloat16 [2, 1024], P(None, 'grp'), may hold values from -2 to 2
- w_qkv: bfloat16 [2, 1024, 3072], P(None, 'grp'), may hold values from -0.1875 to 0.1875
- w_dense: bfloat16 [2, 1024, 1024], P(None, 'grp'), may hold values from -1.5 to 1.5
- w_fc1: bfloat16 [2, 1024, 4096], P(None, 'grp'), may hold values from -0.1875 to 0.1875
- b_fc1: bfloat16 [2, 4096], P(None, 'grp'), may hold values from -2 to 2
- w_fc2: bfloat16 [2, 4096, 1024], P(None, 'grp'), may hold values from -0.09375 to 0.09375
- b_fc2: bfloat16 [2, 1024], P(None, 'grp'), may hold values from -2 to 2
- output_grad: float32 [4, 1024, 1024], P('rep', 'grp'), may hold values from -6 to 6
Outputs:
- hidden_out: float32 [4, 1024, 1024], P('rep', 'grp')
- input_grad: float32 [4, 1024, 1024], P('rep', 'grp')
- grad_ln_gain: float32 [2, 1024], P(None, 'grp')
- grad_ln_bias: float32 [2, 1024], P(None, 'grp')
- grad_w_qkv: float32 [2, 1024, 3072], P(None, 'grp')
- grad_w_dense: float32 [2, 1024, 1024], P(None, 'grp')
- grad_w_fc1: float32 [2, 1024, 4096], P(None, 'grp')
- grad_b_fc1: float32 [2, 4096], P(None, 'grp')
- grad_w_fc2: float32 [2, 4096, 1024], P(None, 'grp')
- grad_b_fc2: float32 [2, 1024], P(None, 'grp')
The draws below stay inside these ranges and needn't reach their ends.
All inputs are finite; a program needn't handle non-finite values.
Results may differ from the reference program's by a relative error of at most 0.017.
Values may be sent and summed in bfloat16 or wider, within the bound.
No kernel may reach another device: no remote copies, remote signals or barrier semaphores. Data moves between devices by JAX's collectives and lax.ppermute only.
A program may use at most 384 MiB of HBM per device.

```python
import jax
import jax.numpy as jnp
from jax import lax

D = 1024
HEADS = 16
HEAD_DIM = 64
ROT = 32
FF = 4096
LAYERS = 2
SEQ = 1024
SEQS = 4


def steps_of(stream_key, shape, shards, least, high):
    level = 1.0
    for axis_at, shards_of in shards:
        heights = jax.random.uniform(jax.random.fold_in(jax.random.fold_in(stream_key, 6), axis_at), (shards_of,), jnp.float32, least / len(shards), high / len(shards))
        level = level * jnp.repeat(jnp.exp(heights), shape[axis_at] // shards_of).reshape((-1,) + (1,) * (len(shape) - 1 - axis_at))
    return level


def bell_draw(rng, shape, spread, bound, cuts=(), dtype=jnp.bfloat16):
    values = jax.random.normal(rng, shape, jnp.float32) * spread
    if len(cuts) > 0:
        values = steps_of(rng, shape, cuts, -0.22, 0.18) * values
    return jnp.clip(values, min=-bound, max=bound).astype(dtype)


def setup_inputs(seed: int = 0) -> dict:
    streams_of = jax.random.split(jax.random.key(seed), 11)
    return {
        "hidden_in": bell_draw(streams_of[0], (SEQS, SEQ, D), 1.0, 6.0, ((0, 4), (1, 8))),
        "ln_gain": jnp.clip(1.0 + 0.1 * jax.random.normal(streams_of[1], (LAYERS, D), jnp.float32), 0.5, 1.5).astype(jnp.bfloat16),
        "ln_bias": bell_draw(streams_of[2], (LAYERS, D), 0.3, 2.0, ((1, 8),)),
        "w_qkv": bell_draw(streams_of[3], (LAYERS, D, 3 * D), D ** -0.5, 0.1875, ((1, 8),)),
        "w_dense": bell_draw(streams_of[4], (LAYERS, D, D), (D // 64) ** -0.5, 1.5, ((1, 8),)),
        "w_fc1": bell_draw(streams_of[5], (LAYERS, D, FF), D ** -0.5, 0.1875, ((1, 8),)),
        "b_fc1": bell_draw(streams_of[6], (LAYERS, FF), 0.3, 2.0, ((1, 8),)),
        "w_fc2": bell_draw(streams_of[7], (LAYERS, FF, D), FF ** -0.5, 0.09375, ((1, 8),)),
        "b_fc2": bell_draw(streams_of[8], (LAYERS, D), 0.3, 2.0, ((1, 8),)),
        "output_grad": bell_draw(streams_of[9], (SEQS, SEQ, D), 1.0, 6.0, ((0, 4), (1, 8)), jnp.float32),
    }


EPSILON = 1e-05
SCORE_SCALE = 0.125
NEGATIVE = -1000000000.0
HIGHEST = lax.Precision.HIGHEST

@jax.custom_vjp
def low(v):
    return lax.optimization_barrier(v.astype(jnp.bfloat16)).astype(jnp.float32)

@jax.custom_vjp
def low_back(v):
    return v

def low_keep(v):
    return (low(v), None)

def low_pass(kept, grad):
    return (grad,)

def back_keep(v):
    return (v, None)

def back_low(kept, grad):
    return (low(grad),)
low.defvjp(low_keep, low_pass)
low_back.defvjp(back_keep, back_low)

def normalize(hidden, ln_gain, ln_shift):
    mean_row = lax.optimization_barrier(jnp.mean(hidden, axis=-1, keepdims=True))
    centered = hidden - mean_row
    variance = lax.optimization_barrier(jnp.mean(centered * centered, axis=-1, keepdims=True))
    return centered * lax.rsqrt(variance + EPSILON) * ln_gain + ln_shift

def rotary_tables(count):
    positions = jnp.arange(count).astype(jnp.float32)
    frequency = 1.0 / 10000.0 ** (jnp.arange(ROT // 2).astype(jnp.float32) * 2.0 / ROT)
    angles = positions[:, None] * frequency[None, :]
    return (jnp.cos(angles), jnp.sin(angles))

def rotate(tensor, cosine_table, sine_table):
    pairs = tensor[..., :ROT].reshape(tensor.shape[:-1] + (ROT // 2, 2))
    even_part = pairs[..., 0]
    odd_part = pairs[..., 1]
    cosine = cosine_table[:, None, :]
    sine_wave = sine_table[:, None, :]
    turned = jnp.stack([even_part * cosine - odd_part * sine_wave, odd_part * cosine + even_part * sine_wave], axis=-1)
    return jnp.concatenate([turned.reshape(tensor.shape[:-1] + (ROT,)), tensor[..., ROT:]], axis=-1)

def attention(queries, keys_all, values_all):
    seq_len = keys_all.shape[0]
    block_rows = min(512, seq_len)
    key_place = jnp.arange(seq_len).astype(jnp.int32)

    def one_block(block_index):
        block_start = (block_index * block_rows).astype(jnp.int32)
        query_block = lax.dynamic_slice_in_dim(queries, block_start, block_rows, 0)
        scores = low_back(jnp.einsum('qhd,khd->hqk', query_block, keys_all, precision=HIGHEST) * SCORE_SCALE)
        query_place = block_start + jnp.arange(block_rows).astype(jnp.int32)
        causal = query_place[:, None] >= key_place[None, :]
        scores = jnp.where(causal[None], scores, NEGATIVE)
        row_max = lax.optimization_barrier(jnp.max(scores, axis=-1, keepdims=True))
        exponent = jnp.exp(scores - row_max)
        probabilities = low(exponent / lax.optimization_barrier(jnp.sum(exponent, axis=-1, keepdims=True)))
        return jnp.einsum('hqk,khd->qhd', probabilities, values_all, precision=HIGHEST)
    blocks = lax.map(jax.checkpoint(one_block), jnp.arange(seq_len // block_rows).astype(jnp.int32))
    return blocks.reshape(seq_len, HEADS * HEAD_DIM)

def forward(hidden, params):
    ln_gain, ln_bias, w_qkv, w_dense, w_fc1, b_fc1, w_fc2, b_fc2 = params
    seq_len = hidden.shape[0]
    cosine_table, sine_table = rotary_tables(seq_len)
    for layer_index in range(ln_gain.shape[0]):
        normed = low(normalize(hidden, ln_gain[layer_index], ln_bias[layer_index]))
        mixed = low_back(jnp.dot(normed, w_qkv[layer_index], precision=HIGHEST))
        queries = low(rotate(mixed[:, :D].reshape(seq_len, HEADS, HEAD_DIM), cosine_table, sine_table))
        keys_all = low(rotate(mixed[:, D:2 * D].reshape(seq_len, HEADS, HEAD_DIM), cosine_table, sine_table))
        values_all = low(mixed[:, 2 * D:].reshape(seq_len, HEADS, HEAD_DIM))
        attended = low(low_back(attention(queries, keys_all, values_all)))
        branch_attn = low_back(jnp.dot(attended, w_dense[layer_index], precision=HIGHEST))
        pre_act = low_back(jnp.dot(normed, w_fc1[layer_index], precision=HIGHEST) + b_fc1[layer_index])
        activation = low(jax.nn.gelu(pre_act, approximate=True))
        branch_ffn = low_back(jnp.dot(activation, w_fc2[layer_index], precision=HIGHEST) + b_fc2[layer_index])
        hidden = hidden + branch_attn + branch_ffn
    return hidden

def reference(hidden_in, ln_gain, ln_bias, w_qkv, w_dense, w_fc1, b_fc1, w_fc2, b_fc2, output_grad):
    params = (ln_gain.astype(jnp.float32), ln_bias.astype(jnp.float32), w_qkv.astype(jnp.float32), w_dense.astype(jnp.float32), w_fc1.astype(jnp.float32), b_fc1.astype(jnp.float32), w_fc2.astype(jnp.float32), b_fc2.astype(jnp.float32))
    inputs = hidden_in.astype(jnp.float32)
    cotangents = output_grad.astype(jnp.float32)

    def one_sequence(totals, pair):
        sequence_in, sequence_cot = pair
        result, pullback = jax.vjp(forward, sequence_in, params)
        grad_input, grad_params = pullback(sequence_cot)
        return (jax.tree.map(jnp.add, totals, grad_params), (result, grad_input))
    zero_grads = jax.tree.map(jnp.zeros_like, params)
    totals, (results, grad_inputs) = lax.scan(one_sequence, zero_grads, (inputs, cotangents))
    return (results, grad_inputs, totals[0], totals[1], totals[2], totals[3], totals[4], totals[5], totals[6], totals[7])
```

```python
from functools import partial

import jax
import jax.numpy as jnp
from jax import lax
from jax.experimental import pallas as pl
from jax.experimental.pallas import tpu as pltpu
from jax.sharding import PartitionSpec as P

HEAD_DIM = 64
ROT = 32
LANES = 128

EPSILON = 1e-05
SCORE_SCALE = 0.125
NEGATIVE = -1000000000.0
BF = jnp.bfloat16
F32 = jnp.float32


def dot(left, right):
    return jnp.dot(left, right, preferred_element_type=F32)


def dot_general(left, right, contract):
    return lax.dot_general(left, right, ((contract[:1], contract[1:]), ((), ())), preferred_element_type=F32)


def outer_sum(left, right):
    return dot_general(left, right, (0, 0))


def times_transposed(left, right):
    return dot_general(left, right, (1, 1))


def head_mask(head):
    lane = lax.broadcasted_iota(jnp.int32, (1, LANES), 1)
    return (lane >= head * HEAD_DIM) & (lane < (head + 1) * HEAD_DIM)


def turn(part, cosine, sine, sign):
    even = lax.broadcasted_iota(jnp.int32, part.shape, 1) % 2 == 0
    partner = jnp.where(even, pltpu.roll(part, LANES - 1, 1), pltpu.roll(part, 1, 1))
    return part * cosine + partner * (sine * sign)


def mask_diagonal(scores, block):
    keys, queries = scores.shape
    key_place = lax.broadcasted_iota(jnp.int32, (block, queries), 0)
    query_place = lax.broadcasted_iota(jnp.int32, (block, queries), 1)
    last = jnp.where(key_place <= query_place, scores[keys - block :], NEGATIVE)
    if keys == block:
        return last
    return jnp.concatenate([scores[: keys - block], last], axis=0)


def attend_kernel(heads, block, mix_q, mix_k, mix_v, cosine, sine, q_out, k_out, v_out, att_out, log_out):
    seq = mix_q.shape[0]
    q_out[...] = turn(mix_q[...], cosine[...], sine[...], 1.0).astype(BF)
    k_out[...] = turn(mix_k[...], cosine[...], sine[...], 1.0).astype(BF)
    v_out[...] = mix_v[...].astype(BF)
    values_down = mix_v[...].T.astype(BF)
    for start in range(0, seq, block):
        stop = start + block
        queries = q_out[start:stop, :] * SCORE_SCALE
        keys = k_out[:stop, :]
        total = jnp.zeros((LANES, block), F32)
        for head in range(heads):
            chosen = jnp.where(head_mask(head), queries, 0.0).astype(BF)
            scores = mask_diagonal(dot_general(keys, chosen, (1, 1)), block)
            row_max = jnp.max(scores, axis=0, keepdims=True)
            exponent = jnp.exp(scores - row_max)
            row_total = jnp.sum(exponent, axis=0, keepdims=True)
            probabilities = (exponent * (1.0 / row_total)).astype(BF)
            log_out[head : head + 1, start:stop] = row_max + jnp.log(row_total)
            found = dot(values_down[:, :stop], probabilities)
            down = lax.broadcasted_iota(jnp.int32, (LANES, 1), 0)
            own = (down >= head * HEAD_DIM) & (down < (head + 1) * HEAD_DIM)
            total = total + jnp.where(own, found, 0.0)
        att_out[start:stop, :] = total.T.astype(BF)


def attend_back_kernel(heads, block, q_in, k_in, v_in, grad_att, log_in, cosine, sine, q_out, k_out, v_out, k_sum, v_sum):
    seq = q_in.shape[0]
    k_sum[...] = jnp.zeros_like(k_sum)
    v_sum[...] = jnp.zeros_like(v_sum)
    keys_down = (k_in[...].astype(F32) * SCORE_SCALE).T.astype(BF)
    for start in range(0, seq, block):
        stop = start + block
        queries = q_in[start:stop, :] * SCORE_SCALE
        grads = grad_att[start:stop, :]
        grad_queries = jnp.zeros((LANES, block), F32)
        for head in range(heads):
            chosen = jnp.where(head_mask(head), queries, 0.0).astype(BF)
            chosen_grads = jnp.where(head_mask(head), grads, 0.0).astype(BF)
            scores = mask_diagonal(dot_general(k_in[:stop, :], chosen, (1, 1)), block)
            probabilities = jnp.exp(scores - log_in[head : head + 1, start:stop])
            grad_probs = dot_general(v_in[:stop, :], chosen_grads, (1, 1))
            row_inner = jnp.sum(grad_probs * probabilities, axis=0, keepdims=True)
            grad_scores = (probabilities * (grad_probs - row_inner)).astype(BF)
            k_sum[:stop, :] += dot(grad_scores, chosen)
            v_sum[:stop, :] += dot(probabilities.astype(BF), chosen_grads)
            down = lax.broadcasted_iota(jnp.int32, (LANES, 1), 0)
            own = (down >= head * HEAD_DIM) & (down < (head + 1) * HEAD_DIM)
            grad_queries = grad_queries + jnp.where(own, dot(keys_down[:, :stop], grad_scores), 0.0)
        q_out[start:stop, :] = turn(
            grad_queries.T, cosine[start:stop, :], sine[start:stop, :], -1.0
        ).astype(BF)
    k_out[...] = turn(k_sum[...], cosine[...], sine[...], -1.0).astype(BF)
    v_out[...] = v_sum[...].astype(BF)


VMEM_LIMIT = 48 * 1024 * 1024


def attend(mix_q, mix_k, mix_v, heads, cosine, sine):
    seq = mix_q.shape[0]
    out = jax.ShapeDtypeStruct((seq, LANES), BF)
    return pl.pallas_call(
        partial(attend_kernel, heads, min(256, seq)),
        out_shape=(out, out, out, out, jax.ShapeDtypeStruct((heads, seq), F32)),
        compiler_params=pltpu.CompilerParams(vmem_limit_bytes=VMEM_LIMIT),
    )(mix_q, mix_k, mix_v, cosine, sine)


def attend_back(queries, keys, values, grad_att, log_total, heads, cosine, sine):
    seq = queries.shape[0]
    out = jax.ShapeDtypeStruct((seq, LANES), BF)
    return pl.pallas_call(
        partial(attend_back_kernel, heads, min(256, seq)),
        out_shape=(out, out, out),
        scratch_shapes=[pltpu.VMEM((seq, LANES), F32), pltpu.VMEM((seq, LANES), F32)],
        compiler_params=pltpu.CompilerParams(vmem_limit_bytes=VMEM_LIMIT),
    )(queries, keys, values, grad_att, log_total, cosine, sine)


def rotary_tables(seq):
    positions = jnp.arange(seq).astype(F32)
    frequency = 1.0 / 10000.0 ** (jnp.arange(ROT // 2).astype(F32) * 2.0 / ROT)
    angles = positions[:, None] * frequency[None, :]
    cosine = jnp.repeat(jnp.cos(angles), 2, axis=1)
    sine = jnp.repeat(jnp.sin(angles), 2, axis=1) * jnp.tile(jnp.array([-1.0, 1.0], F32), ROT // 2)
    rest = HEAD_DIM - ROT
    cosine = jnp.concatenate([cosine, jnp.ones((seq, rest), F32)], axis=1)
    sine = jnp.concatenate([sine, jnp.zeros((seq, rest), F32)], axis=1)
    return jnp.tile(cosine, (1, LANES // HEAD_DIM)), jnp.tile(sine, (1, LANES // HEAD_DIM))


def swap(value, bits):
    return lax.ppermute(value, "grp", [(i, i ^ bits) for i in range(8)])


def add_low(left, right):
    return (left.astype(F32) + right.astype(F32)).astype(BF)


def by_chip(parts, chip):
    x, y = chip % 2 == 1, chip // 2 == 1
    near = jnp.where(x, jnp.stack([parts[1], parts[0]]), jnp.stack([parts[0], parts[1]]))
    far = jnp.where(x, jnp.stack([parts[3], parts[2]]), jnp.stack([parts[2], parts[3]]))
    return jnp.where(y, jnp.concatenate([far, near]), jnp.concatenate([near, far]))


def gather_rows(part):
    size = lax.axis_size("grp")
    if size != 8:
        return lax.all_gather(part, "grp", axis=0, tiled=True)
    rows, width = part.shape
    half = rows // 2
    index = lax.axis_index("grp")
    along_x, along_y = swap(part, 2), swap(part, 4)
    corner = jnp.concatenate([swap(along_y[:half], 2), swap(along_x[half:], 4)])
    mine = by_chip([part, along_x, along_y, corner], index // 2)
    other = swap(mine, 1)
    odd = index % 2 == 1
    both = jnp.stack([jnp.where(odd, other, mine), jnp.where(odd, mine, other)], axis=1)
    return both.reshape(8 * rows, width)


def scatter_sum(whole):
    size = lax.axis_size("grp")
    if size != 8:
        return lax.psum_scatter(whole, "grp", scatter_dimension=0, tiled=True).astype(F32)
    rows, width = whole.shape[0] // 8, whole.shape[1]
    half = rows // 2
    index = lax.axis_index("grp")
    chip, core = index // 2, index % 2
    blocks = whole.reshape(4, 2, rows, width)
    keep = lax.dynamic_index_in_dim(blocks, core, 1, False)
    give = lax.dynamic_index_in_dim(blocks, 1 - core, 1, False)
    summed = add_low(keep, swap(give, 1))
    own, for_x, for_y, corner = [lax.dynamic_index_in_dim(summed, chip ^ s, 0, False) for s in range(4)]
    by_x, by_y = swap(corner[:half], 2), swap(corner[half:], 4)
    for_y = jnp.concatenate([add_low(for_y[:half], by_x), for_y[half:]])
    for_x = jnp.concatenate([for_x[:half], add_low(for_x[half:], by_y)])
    return own.astype(F32) + swap(for_y, 4).astype(F32) + swap(for_x, 2).astype(F32)


def exchange(blocks):
    size = lax.axis_size("grp")
    if size != 8:
        return lax.all_to_all(blocks, "grp", 0, 0)
    index = lax.axis_index("grp")
    chip, core = index // 2, index % 2
    pairs = blocks.reshape((4, 2) + blocks.shape[1:])
    keep = lax.dynamic_index_in_dim(pairs, core, 1, False)
    give = lax.dynamic_index_in_dim(pairs, 1 - core, 1, False)
    came = swap(give, 1)
    odd = core == 1
    both = jnp.stack([jnp.where(odd, came, keep), jnp.where(odd, keep, came)], axis=1)
    parts = [lax.dynamic_index_in_dim(both, chip ^ s, 0, False) for s in range(4)]
    parts = [parts[0]] + [swap(parts[s], 2 * s) for s in (1, 2, 3)]
    return by_chip(parts, chip).reshape(blocks.shape)


def rep_sum(part):
    if lax.axis_size("rep") != 4:
        return lax.psum(part, "rep").astype(F32)
    place = lax.axis_index("rep")
    inward = lax.ppermute(part, "rep", [(0, 1), (3, 2)])
    half_sum = add_low(part, inward)
    across = lax.ppermute(half_sum, "rep", [(1, 2), (2, 1)])
    total = add_low(half_sum, across)
    outward = lax.ppermute(total, "rep", [(1, 0), (2, 3)])
    return jnp.where((place == 1) | (place == 2), total, outward).astype(F32)


def columns_of(w_qkv, w_fc1, group):
    rows, qkv = w_qkv.shape
    heads = w_qkv.reshape(rows, 3, group, qkv // 3 // group).transpose(2, 0, 1, 3).reshape(group, rows, -1)
    units = w_fc1.reshape(rows, group, -1).transpose(1, 0, 2)
    found = exchange(jnp.concatenate([heads, units], axis=2))
    found = found.reshape(group * rows, -1)
    return found[:, : qkv // group], found[:, qkv // group :]


def rows_of(grad_qkv, grad_fc1, group):
    rows = grad_qkv.shape[0] // group
    both = jnp.concatenate([grad_qkv, grad_fc1], axis=1).reshape(group, rows, -1)
    found = exchange(both)
    qkv = grad_qkv.shape[1]
    heads = found[:, :, :qkv].reshape(group, rows, 3, qkv // 3).transpose(1, 2, 0, 3).reshape(rows, -1)
    units = found[:, :, qkv:].transpose(1, 0, 2).reshape(rows, -1)
    return heads, units


def standardize(hidden):
    centered = hidden - jnp.mean(hidden, axis=-1, keepdims=True)
    scale = lax.rsqrt(jnp.mean(centered * centered, axis=-1, keepdims=True) + EPSILON)
    return centered * scale, scale


def widen(part):
    return jnp.pad(part, ((0, 0), (0, LANES - part.shape[1])))


def forward_layer(normed, weights, heads, tables):
    qkv_cols, fc1_cols, b_fc1, w_dense, w_fc2 = weights
    mixed = dot(normed, qkv_cols)
    own = heads * HEAD_DIM
    queries, keys, values, attended, log_total = attend(
        *(widen(mixed[:, i * own : (i + 1) * own]) for i in range(3)), heads, *tables
    )
    pre_act = dot(normed, fc1_cols) + b_fc1.astype(F32)
    activation = jax.nn.gelu(pre_act, approximate=True).astype(BF)
    partial_sum = (dot(attended[:, :own], w_dense) + dot(activation, w_fc2)).astype(BF)
    stored = (normed, queries, keys, values, attended, log_total, pre_act, activation)
    return partial_sum, stored


def backward_layer(grad_branch, weights, stored, heads, tables):
    qkv_cols, fc1_cols, b_fc1, w_dense, w_fc2 = weights
    normed, queries, keys, values, attended, log_total, pre_act, activation = stored
    own = heads * HEAD_DIM
    grad_w_fc2 = outer_sum(activation, grad_branch).astype(BF)
    grad_w_dense = outer_sum(attended[:, :own], grad_branch).astype(BF)
    _, gelu_back = jax.vjp(partial(jax.nn.gelu, approximate=True), pre_act)
    grad_pre = gelu_back(times_transposed(grad_branch, w_fc2))[0].astype(BF)
    grad_attended = widen(times_transposed(grad_branch, w_dense).astype(BF))
    grad_mixed = attend_back(queries, keys, values, grad_attended, log_total, heads, *tables)
    grad_mixed = jnp.concatenate([part[:, :own] for part in grad_mixed], axis=1)
    grad_fc1 = outer_sum(normed, grad_pre).astype(BF)
    grad_b_fc1 = jnp.sum(grad_pre.astype(F32), axis=0)
    grad_qkv = outer_sum(normed, grad_mixed).astype(BF)
    grad_normed = (times_transposed(grad_pre, fc1_cols) + times_transposed(grad_mixed, qkv_cols)).astype(BF)
    return grad_normed, (grad_w_fc2, grad_w_dense, grad_fc1, grad_qkv, grad_b_fc1)


def local(hidden_in, ln_gain, ln_bias, w_qkv, w_dense, w_fc1, b_fc1, w_fc2, b_fc2, output_grad):
    group = lax.axis_size("grp")
    index = lax.axis_index("grp")
    layers = w_qkv.shape[0]
    span, width = hidden_in.shape[1:]
    seq = span * group
    heads = width // HEAD_DIM // group
    tables = rotary_tables(seq)
    small = jnp.concatenate([ln_gain, ln_bias, b_fc2])
    small = lax.all_gather(small, "grp", axis=1, tiled=True).astype(F32)
    gains, shifts, b_fc2_all = small[:layers], small[layers : 2 * layers], small[2 * layers :]
    hidden = hidden_in.reshape(span, width).astype(F32)
    hidden_all = gather_rows(hidden_in.reshape(span, width))
    weights = []
    for layer in range(layers):
        qkv_cols, fc1_cols = columns_of(w_qkv[layer], w_fc1[layer], group)
        weights.append((qkv_cols, fc1_cols, b_fc1[layer], w_dense[layer], w_fc2[layer]))

    inputs, stored_layers = [], []
    for layer in range(layers):
        inputs.append(hidden)
        if layer == 0:
            normed = (standardize(hidden_all.astype(F32))[0] * gains[0] + shifts[0]).astype(BF)
        else:
            normed = gather_rows((standardize(hidden)[0] * gains[layer] + shifts[layer]).astype(BF))
        partial_sum, stored = forward_layer(normed, weights[layer], heads, tables)
        stored_layers.append(stored)
        hidden = hidden + scatter_sum(partial_sum) + b_fc2_all[layer]

    grad_hidden = output_grad.reshape(span, width)
    small_grads, large_grads = [None] * layers, [None] * layers
    for layer in reversed(range(layers)):
        grad_low = grad_hidden.astype(BF)
        grad_branch = gather_rows(grad_low)
        grad_normed, found = backward_layer(grad_branch, weights[layer], stored_layers[layer], heads, tables)
        grad_w_fc2, grad_w_dense, grad_fc1, grad_qkv, grad_b_fc1 = found
        grad_qkv, grad_fc1 = rows_of(grad_qkv, grad_fc1, group)
        large_grads[layer] = tuple(rep_sum(part) for part in (grad_w_fc2, grad_w_dense, grad_fc1, grad_qkv))
        grad_normed = scatter_sum(grad_normed)
        xhat, scale = standardize(inputs[layer])
        inner = grad_normed * gains[layer]
        mean_inner = jnp.mean(inner, axis=-1, keepdims=True)
        mean_along = jnp.mean(inner * xhat, axis=-1, keepdims=True)
        small_grads[layer] = jnp.concatenate(
            [
                jnp.sum(grad_normed * xhat, axis=0),
                jnp.sum(grad_normed, axis=0),
                jnp.sum(grad_low.astype(F32), axis=0),
                lax.dynamic_update_slice(
                    jnp.zeros((group * grad_b_fc1.shape[0],), F32), grad_b_fc1, (index * grad_b_fc1.shape[0],)
                ),
            ]
        )
        grad_hidden = grad_hidden + (inner - mean_inner - xhat * mean_along) * scale

    summed = lax.psum(jnp.stack(small_grads), ("rep", "grp"))
    own = width // group
    units = b_fc1.shape[1]

    def pick(start, count):
        return lax.dynamic_slice_in_dim(summed, start + index * count, count, 1)

    stacked = [jnp.stack([large_grads[layer][member] for layer in range(layers)]) for member in range(4)]
    return (
        hidden[None],
        grad_hidden[None],
        pick(0, own),
        pick(width, own),
        stacked[3],
        stacked[1],
        stacked[2],
        pick(3 * width, units),
        stacked[0],
        pick(2 * width, own),
    )


def solution(mesh):
    in_specs = (
        P("rep", "grp", None),
        P(None, "grp"),
        P(None, "grp"),
        P(None, "grp", None),
        P(None, "grp", None),
        P(None, "grp", None),
        P(None, "grp"),
        P(None, "grp", None),
        P(None, "grp"),
        P("rep", "grp", None),
    )
    out_specs = (
        P("rep", "grp", None),
        P("rep", "grp", None),
        P(None, "grp"),
        P(None, "grp"),
        P(None, "grp", None),
        P(None, "grp", None),
        P(None, "grp", None),
        P(None, "grp"),
        P(None, "grp", None),
        P(None, "grp"),
    )
    return jax.shard_map(local, mesh=mesh, in_specs=in_specs, out_specs=out_specs, check_vma=False)
```

```python
from functools import partial

import jax
import jax.numpy as jnp
import numpy as np
from jax import lax
from jax.experimental import pallas as pl
from jax.experimental.pallas import tpu as pltpu
from jax.sharding import PartitionSpec as P

HEAD_DIM = 64
ROT = 32
LANES = 128

EPSILON = 1e-05
SCORE_SCALE = 0.125
NEGATIVE = -1000000000.0
BF = jnp.bfloat16
F32 = jnp.float32


def dot(left, right):
    return jnp.dot(left, right, preferred_element_type=F32)


def dot_general(left, right, contract):
    return lax.dot_general(left, right, ((contract[:1], contract[1:]), ((), ())), preferred_element_type=F32)


def outer_sum(left, right):
    return dot_general(left, right, (0, 0))


def times_transposed(left, right):
    return dot_general(left, right, (1, 1))


def head_mask(head):
    lane = lax.broadcasted_iota(jnp.int32, (1, LANES), 1)
    return (lane >= head * HEAD_DIM) & (lane < (head + 1) * HEAD_DIM)


def turn(part, cosine, sine, sign):
    even = lax.broadcasted_iota(jnp.int32, part.shape, 1) % 2 == 0
    partner = jnp.where(even, pltpu.roll(part, LANES - 1, 1), pltpu.roll(part, 1, 1))
    return part * cosine + partner * (sine * sign)


def mask_diagonal(scores, block):
    keys, queries = scores.shape
    key_place = lax.broadcasted_iota(jnp.int32, (block, queries), 0)
    query_place = lax.broadcasted_iota(jnp.int32, (block, queries), 1)
    last = jnp.where(key_place <= query_place, scores[keys - block :], NEGATIVE)
    if keys == block:
        return last
    return jnp.concatenate([scores[: keys - block], last], axis=0)


def attend_kernel(heads, block, mix_q, mix_k, mix_v, cosine, sine, q_out, k_out, v_out, att_out, log_out):
    seq = mix_q.shape[0]
    q_out[...] = turn(mix_q[...], cosine[...], sine[...], 1.0).astype(BF)
    k_out[...] = turn(mix_k[...], cosine[...], sine[...], 1.0).astype(BF)
    v_out[...] = mix_v[...].astype(BF)
    values_down = mix_v[...].T.astype(BF)
    for start in range(0, seq, block):
        stop = start + block
        queries = q_out[start:stop, :] * SCORE_SCALE
        keys = k_out[:stop, :]
        total = jnp.zeros((LANES, block), F32)
        for head in range(heads):
            chosen = jnp.where(head_mask(head), queries, 0.0).astype(BF)
            scores = mask_diagonal(dot_general(keys, chosen, (1, 1)), block)
            row_max = jnp.max(scores, axis=0, keepdims=True)
            exponent = jnp.exp(scores - row_max)
            row_total = jnp.sum(exponent, axis=0, keepdims=True)
            probabilities = (exponent * (1.0 / row_total)).astype(BF)
            log_out[head : head + 1, start:stop] = row_max + jnp.log(row_total)
            found = dot(values_down[:, :stop], probabilities)
            down = lax.broadcasted_iota(jnp.int32, (LANES, 1), 0)
            own = (down >= head * HEAD_DIM) & (down < (head + 1) * HEAD_DIM)
            total = total + jnp.where(own, found, 0.0)
        att_out[start:stop, :] = total.T.astype(BF)


def attend_back_kernel(heads, block, q_in, k_in, v_in, grad_att, log_in, cosine, sine, q_out, k_out, v_out, k_sum, v_sum):
    seq = q_in.shape[0]
    k_sum[...] = jnp.zeros_like(k_sum)
    v_sum[...] = jnp.zeros_like(v_sum)
    keys_down = (k_in[...].astype(F32) * SCORE_SCALE).T.astype(BF)
    for start in range(0, seq, block):
        stop = start + block
        queries = q_in[start:stop, :] * SCORE_SCALE
        grads = grad_att[start:stop, :]
        grad_queries = jnp.zeros((LANES, block), F32)
        for head in range(heads):
            chosen = jnp.where(head_mask(head), queries, 0.0).astype(BF)
            chosen_grads = jnp.where(head_mask(head), grads, 0.0).astype(BF)
            scores = mask_diagonal(dot_general(k_in[:stop, :], chosen, (1, 1)), block)
            probabilities = jnp.exp(scores - log_in[head : head + 1, start:stop])
            grad_probs = dot_general(v_in[:stop, :], chosen_grads, (1, 1))
            row_inner = jnp.sum(grad_probs * probabilities, axis=0, keepdims=True)
            grad_scores = (probabilities * (grad_probs - row_inner)).astype(BF)
            k_sum[:stop, :] += dot(grad_scores, chosen)
            v_sum[:stop, :] += dot(probabilities.astype(BF), chosen_grads)
            down = lax.broadcasted_iota(jnp.int32, (LANES, 1), 0)
            own = (down >= head * HEAD_DIM) & (down < (head + 1) * HEAD_DIM)
            grad_queries = grad_queries + jnp.where(own, dot(keys_down[:, :stop], grad_scores), 0.0)
        q_out[start:stop, :] = turn(
            grad_queries.T, cosine[start:stop, :], sine[start:stop, :], -1.0
        ).astype(BF)
    k_out[...] = turn(k_sum[...], cosine[...], sine[...], -1.0).astype(BF)
    v_out[...] = v_sum[...].astype(BF)


VMEM_LIMIT = 48 * 1024 * 1024


def attend(mix_q, mix_k, mix_v, heads, cosine, sine):
    seq = mix_q.shape[0]
    out = jax.ShapeDtypeStruct((seq, LANES), BF)
    return pl.pallas_call(
        partial(attend_kernel, heads, min(256, seq)),
        out_shape=(out, out, out, out, jax.ShapeDtypeStruct((heads, seq), F32)),
        compiler_params=pltpu.CompilerParams(vmem_limit_bytes=VMEM_LIMIT),
    )(mix_q, mix_k, mix_v, cosine, sine)


def attend_back(queries, keys, values, grad_att, log_total, heads, cosine, sine):
    seq = queries.shape[0]
    out = jax.ShapeDtypeStruct((seq, LANES), BF)
    return pl.pallas_call(
        partial(attend_back_kernel, heads, min(256, seq)),
        out_shape=(out, out, out),
        scratch_shapes=[pltpu.VMEM((seq, LANES), F32), pltpu.VMEM((seq, LANES), F32)],
        compiler_params=pltpu.CompilerParams(vmem_limit_bytes=VMEM_LIMIT),
    )(queries, keys, values, grad_att, log_total, cosine, sine)


def rotary_tables(seq):
    frequency = (1.0 / 10000.0 ** (np.arange(ROT // 2, dtype=np.float32) * 2.0 / ROT)).astype(np.float32)
    angles = np.arange(seq, dtype=np.float32)[:, None] * frequency[None, :]
    cosine, sine = np.cos(angles.astype(np.float64)), np.sin(angles.astype(np.float64))
    cosine = np.repeat(cosine, 2, axis=1)
    sine = np.repeat(sine, 2, axis=1) * np.tile([-1.0, 1.0], ROT // 2)
    rest = HEAD_DIM - ROT
    cosine = np.concatenate([cosine, np.ones((seq, rest))], axis=1)
    sine = np.concatenate([sine, np.zeros((seq, rest))], axis=1)
    repeats = (1, LANES // HEAD_DIM)
    return np.tile(cosine, repeats).astype(np.float32), np.tile(sine, repeats).astype(np.float32)


def swap(value, bits):
    return lax.ppermute(value, "grp", [(i, i ^ bits) for i in range(8)])


def add_low(left, right):
    return (left.astype(F32) + right.astype(F32)).astype(BF)


def by_chip(parts, chip):
    x, y = chip % 2 == 1, chip // 2 == 1
    near = jnp.where(x, jnp.stack([parts[1], parts[0]]), jnp.stack([parts[0], parts[1]]))
    far = jnp.where(x, jnp.stack([parts[3], parts[2]]), jnp.stack([parts[2], parts[3]]))
    return jnp.where(y, jnp.concatenate([far, near]), jnp.concatenate([near, far]))


def gather_rows(part):
    size = lax.axis_size("grp")
    if size != 8:
        return lax.all_gather(part, "grp", axis=0, tiled=True)
    rows, width = part.shape
    half = rows // 2
    index = lax.axis_index("grp")
    along_x, along_y = swap(part, 2), swap(part, 4)
    corner = jnp.concatenate([swap(along_y[:half], 2), swap(along_x[half:], 4)])
    mine = by_chip([part, along_x, along_y, corner], index // 2)
    other = swap(mine, 1)
    odd = index % 2 == 1
    both = jnp.stack([jnp.where(odd, other, mine), jnp.where(odd, mine, other)], axis=1)
    return both.reshape(8 * rows, width)


def scatter_sum(whole):
    size = lax.axis_size("grp")
    if size != 8:
        return lax.psum_scatter(whole, "grp", scatter_dimension=0, tiled=True).astype(F32)
    rows, width = whole.shape[0] // 8, whole.shape[1]
    half = rows // 2
    index = lax.axis_index("grp")
    chip, core = index // 2, index % 2
    blocks = whole.reshape(4, 2, rows, width)
    keep = lax.dynamic_index_in_dim(blocks, core, 1, False)
    give = lax.dynamic_index_in_dim(blocks, 1 - core, 1, False)
    summed = add_low(keep, swap(give, 1))
    own, for_x, for_y, corner = [lax.dynamic_index_in_dim(summed, chip ^ s, 0, False) for s in range(4)]
    by_x, by_y = swap(corner[:half], 2), swap(corner[half:], 4)
    for_y = jnp.concatenate([add_low(for_y[:half], by_x), for_y[half:]])
    for_x = jnp.concatenate([for_x[:half], add_low(for_x[half:], by_y)])
    return own.astype(F32) + swap(for_y, 4).astype(F32) + swap(for_x, 2).astype(F32)


def exchange(blocks):
    size = lax.axis_size("grp")
    if size != 8:
        return lax.all_to_all(blocks, "grp", 0, 0)
    index = lax.axis_index("grp")
    chip, core = index // 2, index % 2
    pairs = blocks.reshape((4, 2) + blocks.shape[1:])
    keep = lax.dynamic_index_in_dim(pairs, core, 1, False)
    give = lax.dynamic_index_in_dim(pairs, 1 - core, 1, False)
    came = swap(give, 1)
    odd = core == 1
    both = jnp.stack([jnp.where(odd, came, keep), jnp.where(odd, keep, came)], axis=1)
    parts = [lax.dynamic_index_in_dim(both, chip ^ s, 0, False) for s in range(4)]
    parts = [parts[0]] + [swap(parts[s], 2 * s) for s in (1, 2, 3)]
    return by_chip(parts, chip).reshape(blocks.shape)


def rep_sum(part):
    if lax.axis_size("rep") != 4:
        return lax.psum(part, "rep").astype(F32)
    place = lax.axis_index("rep")
    inward = lax.ppermute(part, "rep", [(0, 1), (3, 2)])
    half_sum = add_low(part, inward)
    across = lax.ppermute(half_sum, "rep", [(1, 2), (2, 1)])
    total = add_low(half_sum, across)
    outward = lax.ppermute(total, "rep", [(1, 0), (2, 3)])
    return jnp.where((place == 1) | (place == 2), total, outward).astype(F32)


def columns_of(w_qkv, w_fc1, group):
    rows, qkv = w_qkv.shape
    heads = w_qkv.reshape(rows, 3, group, qkv // 3 // group).transpose(2, 0, 1, 3).reshape(group, rows, -1)
    units = w_fc1.reshape(rows, group, -1).transpose(1, 0, 2)
    found = exchange(jnp.concatenate([heads, units], axis=2))
    found = found.reshape(group * rows, -1)
    return found[:, : qkv // group], found[:, qkv // group :]


def rows_of(grad_qkv, grad_fc1, group):
    rows = grad_qkv.shape[0] // group
    both = jnp.concatenate([grad_qkv, grad_fc1], axis=1).reshape(group, rows, -1)
    found = exchange(both)
    qkv = grad_qkv.shape[1]
    heads = found[:, :, :qkv].reshape(group, rows, 3, qkv // 3).transpose(1, 2, 0, 3).reshape(rows, -1)
    units = found[:, :, qkv:].transpose(1, 0, 2).reshape(rows, -1)
    return heads, units


def standardize(hidden):
    centered = hidden - jnp.mean(hidden, axis=-1, keepdims=True)
    scale = lax.rsqrt(jnp.mean(centered * centered, axis=-1, keepdims=True) + EPSILON)
    return centered * scale, scale


def widen(part):
    return jnp.pad(part, ((0, 0), (0, LANES - part.shape[1])))


def forward_layer(normed, weights, heads, tables):
    qkv_cols, fc1_cols, b_fc1, w_dense, w_fc2 = weights
    mixed = dot(normed, qkv_cols)
    own = heads * HEAD_DIM
    queries, keys, values, attended, log_total = attend(
        *(widen(mixed[:, i * own : (i + 1) * own]) for i in range(3)), heads, *tables
    )
    pre_act = dot(normed, fc1_cols) + b_fc1.astype(F32)
    activation = jax.nn.gelu(pre_act, approximate=True).astype(BF)
    partial_sum = (dot(attended[:, :own], w_dense) + dot(activation, w_fc2)).astype(BF)
    stored = (normed, queries, keys, values, attended, log_total, pre_act, activation)
    return partial_sum, stored


def backward_layer(grad_branch, weights, stored, heads, tables):
    qkv_cols, fc1_cols, b_fc1, w_dense, w_fc2 = weights
    normed, queries, keys, values, attended, log_total, pre_act, activation = stored
    own = heads * HEAD_DIM
    grad_w_fc2 = outer_sum(activation, grad_branch).astype(BF)
    grad_w_dense = outer_sum(attended[:, :own], grad_branch).astype(BF)
    _, gelu_back = jax.vjp(partial(jax.nn.gelu, approximate=True), pre_act)
    grad_pre = gelu_back(times_transposed(grad_branch, w_fc2))[0].astype(BF)
    grad_attended = widen(times_transposed(grad_branch, w_dense).astype(BF))
    grad_mixed = attend_back(queries, keys, values, grad_attended, log_total, heads, *tables)
    grad_mixed = jnp.concatenate([part[:, :own] for part in grad_mixed], axis=1)
    grad_fc1 = outer_sum(normed, grad_pre).astype(BF)
    grad_b_fc1 = jnp.sum(grad_pre.astype(F32), axis=0)
    grad_qkv = outer_sum(normed, grad_mixed).astype(BF)
    grad_normed = (times_transposed(grad_pre, fc1_cols) + times_transposed(grad_mixed, qkv_cols)).astype(BF)
    return grad_normed, (grad_w_fc2, grad_w_dense, grad_fc1, grad_qkv, grad_b_fc1)


def local_any(hidden_in, ln_gain, ln_bias, w_qkv, w_dense, w_fc1, b_fc1, w_fc2, b_fc2, output_grad):
    group = lax.axis_size("grp")
    index = lax.axis_index("grp")
    layers = w_qkv.shape[0]
    span, width = hidden_in.shape[1:]
    seq = span * group
    heads = width // HEAD_DIM // group
    tables = rotary_tables(seq)
    small = jnp.concatenate([ln_gain, ln_bias, b_fc2])
    small = lax.all_gather(small, "grp", axis=1, tiled=True).astype(F32)
    gains, shifts, b_fc2_all = small[:layers], small[layers : 2 * layers], small[2 * layers :]
    hidden = hidden_in.reshape(span, width).astype(F32)
    hidden_all = gather_rows(hidden_in.reshape(span, width))
    weights = []
    for layer in range(layers):
        qkv_cols, fc1_cols = columns_of(w_qkv[layer], w_fc1[layer], group)
        weights.append((qkv_cols, fc1_cols, b_fc1[layer], w_dense[layer], w_fc2[layer]))

    inputs, stored_layers = [], []
    for layer in range(layers):
        inputs.append(hidden)
        if layer == 0:
            normed = (standardize(hidden_all.astype(F32))[0] * gains[0] + shifts[0]).astype(BF)
        else:
            normed = gather_rows((standardize(hidden)[0] * gains[layer] + shifts[layer]).astype(BF))
        partial_sum, stored = forward_layer(normed, weights[layer], heads, tables)
        stored_layers.append(stored)
        hidden = hidden + scatter_sum(partial_sum) + b_fc2_all[layer]

    grad_hidden = output_grad.reshape(span, width)
    small_grads, large_grads = [None] * layers, [None] * layers
    for layer in reversed(range(layers)):
        grad_low = grad_hidden.astype(BF)
        grad_branch = gather_rows(grad_low)
        grad_normed, found = backward_layer(grad_branch, weights[layer], stored_layers[layer], heads, tables)
        grad_w_fc2, grad_w_dense, grad_fc1, grad_qkv, grad_b_fc1 = found
        grad_qkv, grad_fc1 = rows_of(grad_qkv, grad_fc1, group)
        large_grads[layer] = tuple(rep_sum(part) for part in (grad_w_fc2, grad_w_dense, grad_fc1, grad_qkv))
        grad_normed = scatter_sum(grad_normed)
        xhat, scale = standardize(inputs[layer])
        inner = grad_normed * gains[layer]
        mean_inner = jnp.mean(inner, axis=-1, keepdims=True)
        mean_along = jnp.mean(inner * xhat, axis=-1, keepdims=True)
        small_grads[layer] = jnp.concatenate(
            [
                jnp.sum(grad_normed * xhat, axis=0),
                jnp.sum(grad_normed, axis=0),
                jnp.sum(grad_low.astype(F32), axis=0),
                lax.dynamic_update_slice(
                    jnp.zeros((group * grad_b_fc1.shape[0],), F32), grad_b_fc1, (index * grad_b_fc1.shape[0],)
                ),
            ]
        )
        grad_hidden = grad_hidden + (inner - mean_inner - xhat * mean_along) * scale

    summed = lax.psum(jnp.stack(small_grads), ("rep", "grp"))
    own = width // group
    units = b_fc1.shape[1]

    def pick(start, count):
        return lax.dynamic_slice_in_dim(summed, start + index * count, count, 1)

    stacked = [jnp.stack([large_grads[layer][member] for layer in range(layers)]) for member in range(4)]
    return (
        hidden[None],
        grad_hidden[None],
        pick(0, own),
        pick(width, own),
        stacked[3],
        stacked[1],
        stacked[2],
        pick(3 * width, units),
        stacked[0],
        pick(2 * width, own),
    )


SLOTS = [(s, k) for s in range(4) for k in range(2)]
ROWS = 128
EXTRA = 16


def slot_start(place, s, k, size):
    return pl.multiple_of(((place[0] ^ s) * 2 + (place[1] ^ k)) * size, size)


def slot_rows(place, s, k, size=ROWS):
    return pl.ds(slot_start(place, s, k, size), size)


SMALL = pl.CostEstimate(flops=0, bytes_accessed=0, transcendentals=0)


def call(body, outs, place, ins, scratch=(), aliases=None, mib=16):
    specs = [pl.BlockSpec(memory_space=pltpu.SMEM)]
    arrays = [place]
    for entry in ins:
        array, spec = entry if isinstance(entry, tuple) else (entry, pl.BlockSpec(memory_space=pltpu.VMEM))
        arrays.append(array)
        specs.append(spec)
    return pl.pallas_call(
        body,
        out_shape=[jax.ShapeDtypeStruct(*out) for out in outs],
        in_specs=specs,
        out_specs=[pl.BlockSpec(memory_space=pltpu.VMEM)] * len(outs),
        scratch_shapes=list(scratch),
        input_output_aliases=aliases or {},
        compiler_params=pltpu.CompilerParams(vmem_limit_bytes=mib * 1024 * 1024),
        cost_estimate=SMALL,
    )(*arrays)


def gather_pieces(part):
    mine = [part, swap(part, 2), swap(part, 4), swap(part, 6)]
    other = [swap(piece, 1) for piece in mine]
    return [piece for pair in zip(mine, other) for piece in pair]


def pack_kernel(place, w_qkv, w_fc1, small, *outs):
    for layer in range(2):
        keep_q, give_q, keep_f, give_f = outs[4 * layer : 4 * layer + 4]
        for s in range(4):
            for k, out_q, out_f in ((0, keep_q, keep_f), (1, give_q, give_f)):
                for j in range(3):
                    start = slot_start(place, s, k, LANES)
                    lanes = pl.ds(pl.multiple_of(j * (w_qkv.shape[2] // 3) + start, LANES), LANES)
                    out_q[s, :ROWS, j * LANES : (j + 1) * LANES] = w_qkv[layer, :, lanes]
                if layer == 0:
                    out_q[s, ROWS:, :LANES] = small[...]
                    out_q[s, ROWS:, LANES:] = jnp.zeros((EXTRA, 2 * LANES), BF)
                units = out_f.shape[2]
                out_f[s] = w_fc1[layer, :, pl.ds(slot_start(place, s, k, units), units)]


def pair_kernel(place, keep, came, *outs):
    for s in range(1, 4):
        outs[s - 1][0] = keep[s]
        outs[s - 1][1] = came[s]


def send_pairs(place, keep, came):
    shape = (2,) + keep.shape[1:]
    pairs = call(pair_kernel, [(shape, BF)] * 3, place, [keep, came])
    return [swap(pairs[s - 1], 2 * s) for s in (1, 2, 3)]


def block_of(s, k, keep, came, arrived):
    if s == 0:
        return (keep, came)[k].at[0]
    return arrived[s - 1].at[k]


def turn_block(part, cosine, sine, sign):
    return turn(part, cosine, sine, sign)


def project_heads(normed, weight, cosine, sine, q_out, k_out, v_out, values_down):
    step = 256
    for start in range(0, normed.shape[0], step):
        rows = slice(start, start + step)
        mixed = dot(normed[rows, :], weight[...])
        q_out[rows, :] = turn(mixed[:, :LANES], cosine[rows, :], sine[rows, :], 1.0).astype(BF)
        k_out[rows, :] = turn(mixed[:, LANES : 2 * LANES], cosine[rows, :], sine[rows, :], 1.0).astype(BF)
        values = mixed[:, 2 * LANES :]
        v_out[rows, :] = values.astype(BF)
        values_down[:, rows] = values.T.astype(BF)


def own_head(head):
    down = lax.broadcasted_iota(jnp.int32, (LANES, 1), 0)
    return (down >= head * HEAD_DIM) & (down < (head + 1) * HEAD_DIM)


def softmax_block(keys, chosen, block):
    scores = mask_diagonal(dot_general(keys, chosen, (1, 1)), block)
    row_max = jnp.max(scores, axis=0, keepdims=True)
    exponent = jnp.exp(scores - row_max)
    row_total = jnp.sum(exponent, axis=0, keepdims=True)
    return exponent * (1.0 / row_total), row_max + jnp.log(row_total)


BLOCK = 256
HEADS_HERE = LANES // HEAD_DIM


def first_attend_kernel(place, *refs):
    hidden, refs = refs[:8], refs[8:]
    keep, came, arrived, refs = refs[0], refs[1], refs[2:5], refs[5:]
    cosine, sine, normed, xhat_out, weight, params, q_out, k_out, v_out, att_out, log_out, values_down = refs
    for s, k in SLOTS:
        piece = block_of(s, k, keep, came, arrived)
        weight[slot_rows(place, s, k), :] = piece[:ROWS, :]
        params[:, slot_rows(place, s, k)] = piece[ROWS:, :LANES].astype(F32)
    gain, shift = params[0:1, :], params[2:3, :]
    for (s, k), part in zip(SLOTS, hidden):
        xhat = standardize(part[...].astype(F32))[0]
        xhat_out[slot_rows(place, s, k), :] = xhat.astype(BF)
        normed[slot_rows(place, s, k), :] = (xhat * gain + shift).astype(BF)
    project_heads(normed, weight, cosine, sine, q_out, k_out, v_out, values_down)
    for start in range(0, normed.shape[0], BLOCK):
        stop = start + BLOCK
        queries = q_out[start:stop, :] * SCORE_SCALE
        total = jnp.zeros((LANES, BLOCK), F32)
        for head in range(HEADS_HERE):
            chosen = jnp.where(head_mask(head), queries, 0.0).astype(BF)
            probabilities, log_total = softmax_block(k_out[:stop, :], chosen, BLOCK)
            log_out[head : head + 1, start:stop] = log_total
            found = dot(values_down[:, :stop], probabilities.astype(BF))
            total = total + jnp.where(own_head(head), found, 0.0)
        att_out[start:stop, :] = total.T.astype(BF)


GELU_A = 0.7978845608028654
GELU_B = 0.044715


def gelu_pair(pre):
    square = pre * pre
    wave = jnp.tanh(GELU_A * pre * (1.0 + GELU_B * square))
    half = 0.5 * (1.0 + wave)
    slope = half + 0.5 * pre * (1.0 - wave * wave) * (GELU_A * (1.0 + 3.0 * GELU_B * square))
    return pre * half, slope


def loop_rows(count, step, body):
    def one(i, carry):
        body(pl.ds(pl.multiple_of(i * step, step), step))
        return carry

    lax.fori_loop(0, count // step, one, 0)


def put_slots(place, rows_of_block, keep, give):
    for s in range(4):
        keep[s] = rows_of_block(slot_rows(place, s, 0))
        give[s] = rows_of_block(slot_rows(place, s, 1))


def first_units_kernel(place, normed, keep, came, a1, a2, a3, bias, w_fc2, w_dense, attended, weight, act, slope, keep_out, give_out, whole):
    for s, k in SLOTS:
        weight[slot_rows(place, s, k), :] = block_of(s, k, keep, came, (a1, a2, a3))[...]
    shift = bias[0:1, :].astype(F32)

    def rows_done(rows):
        found, found_slope = gelu_pair(dot(normed[rows, :], weight[...]) + shift)
        slope[rows, :] = found_slope
        act[rows, :] = found.astype(BF)
        whole[rows, :] = (dot(act[rows, :], w_fc2[0]) + dot(attended[rows, :], w_dense[0])).astype(BF)

    loop_rows(normed.shape[0], 256, rows_done)
    put_slots(place, lambda rows: whole[rows, :], keep_out, give_out)


def split_sum_kernel(place, keep, came, for_x, for_y, corner):
    for s, out in ((1, for_x), (2, for_y), (3, corner)):
        out[...] = (keep[s].astype(F32) + came[s].astype(F32)).astype(BF)


def begin_scatter(place, keep, give):
    came = swap(give, 1)
    shape = (keep.shape[1:], BF)
    for_x, for_y, corner = call(split_sum_kernel, [shape] * 3, place, [keep, came])
    from_corner, from_x, from_y = swap(corner, 6), swap(for_x, 2), swap(for_y, 4)
    return [keep, came, from_x, from_y, from_corner]


def sum_terms(terms):
    total = terms[0][0].astype(F32) + terms[1][0].astype(F32)
    for term in terms[2:]:
        total = total + term[...].astype(F32)
    return total


def next_hidden_kernel(place, *refs):
    terms, (hidden, params, hidden_out, normed) = refs[:5], refs[5:]
    found = hidden[...].astype(F32) + sum_terms(terms) + params[4:5, :]
    hidden_out[...] = found
    normed[...] = (standardize(found)[0] * params[1:2, :] + params[3:4, :]).astype(BF)


def assemble_kernel(place, *refs):
    for (s, k), piece in zip(SLOTS, refs[:8]):
        refs[8][slot_rows(place, s, k), :] = piece[...]


def last_hidden_kernel(place, act, attended, w_fc2, w_dense, keep, give, whole):
    def rows_done(rows):
        whole[rows, :] = (dot(act[rows, :], w_fc2[1]) + dot(attended[rows, :], w_dense[1])).astype(BF)

    loop_rows(act.shape[0], 256, rows_done)
    put_slots(place, lambda rows: whole[rows, :], keep, give)


def last_sum_kernel(place, *refs):
    terms, (hidden, params, out) = refs[:5], refs[5:]
    out[...] = hidden[...] + sum_terms(terms) + params[5:6, :]


def second_units_kernel(place, *refs):
    pieces, refs = refs[:8], refs[8:]
    keep, came, arrived, refs = refs[0], refs[1], refs[2:5], refs[5:]
    bias, grads, normed, weight, act, slope, grad_w = refs
    for s, k in SLOTS:
        weight[slot_rows(place, s, k), :] = block_of(s, k, keep, came, arrived)[...]
    for (s, k), piece in zip(SLOTS, pieces):
        normed[slot_rows(place, s, k), :] = piece[...]
    shift = bias[1:2, :].astype(F32)

    def rows_done(rows):
        found, found_slope = gelu_pair(dot(normed[rows, :], weight[...]) + shift)
        slope[rows, :] = found_slope
        act[rows, :] = found.astype(BF)

    loop_rows(normed.shape[0], 256, rows_done)
    for start in range(0, act.shape[1], 256):
        rows = slice(start, start + 256)
        grad_w[rows, :] = outer_sum(act[:, rows], grads[...]).astype(BF)


def units_back_kernel(layer, place, grads, w_fc2, slope, normed, weight, keep_f, give_f, sums, part_normed, grad_pre, grad_w):
    sums[...] = jnp.zeros_like(sums)
    width = grads.shape[1]
    units = slope.shape[1]

    def rows_done(rows):
        found = (times_transposed(grads[rows, :], w_fc2[layer]) * slope[rows, :]).astype(BF)
        grad_pre[rows, :] = found
        sums[0:1, :width] += jnp.sum(grads[rows, :].astype(F32), axis=0, keepdims=True)
        sums[1:2, :units] += jnp.sum(found.astype(F32), axis=0, keepdims=True)
        part_normed[rows, :] = times_transposed(found, weight[...])

    loop_rows(grads.shape[0], 256, rows_done)
    for start in range(0, width, 256):
        rows = slice(start, start + 256)
        grad_w[rows, :] = outer_sum(normed[:, rows], grad_pre[...]).astype(BF)
    put_slots(place, lambda rows: grad_w[rows, :], keep_f, give_f)


def attend_back_block(start, q_ref, k_ref, v_ref, grad_att, keys_down, k_sum, v_sum, cosine, sine, mixed, found_p):
    stop = start + BLOCK
    queries = q_ref[start:stop, :] * SCORE_SCALE
    grad_queries = jnp.zeros((LANES, BLOCK), F32)
    for head in range(HEADS_HERE):
        chosen = jnp.where(head_mask(head), queries, 0.0).astype(BF)
        chosen_grads = jnp.where(head_mask(head), grad_att, 0.0).astype(BF)
        probabilities = found_p(head, chosen)
        grad_probs = dot_general(v_ref[:stop, :], chosen_grads, (1, 1))
        row_inner = jnp.sum(grad_probs * probabilities, axis=0, keepdims=True)
        grad_scores = (probabilities * (grad_probs - row_inner)).astype(BF)
        k_sum[:stop, :] += dot(grad_scores, chosen)
        v_sum[:stop, :] += dot(probabilities.astype(BF), chosen_grads)
        grad_queries = grad_queries + jnp.where(own_head(head), dot(keys_down[:, :stop], grad_scores), 0.0)
    rows = slice(start, stop)
    mixed[rows, :LANES] = turn(grad_queries.T, cosine[rows, :], sine[rows, :], -1.0).astype(BF)


def mixed_back(place, normed, weight, cosine, sine, mixed, k_sum, v_sum, grad_w, part_normed, whole):
    mixed[:, LANES : 2 * LANES] = turn(k_sum[...], cosine[...], sine[...], -1.0).astype(BF)
    mixed[:, 2 * LANES :] = v_sum[...].astype(BF)
    for start in range(0, normed.shape[1], 256):
        rows = slice(start, start + 256)
        grad_w[rows, :] = outer_sum(normed[:, rows], mixed[...]).astype(BF)

    def rows_done(rows):
        whole[rows, :] = (times_transposed(mixed[rows, :], weight[...]) + part_normed[rows, :]).astype(BF)

    loop_rows(normed.shape[0], 256, rows_done)


def second_attend_kernel(place, normed, keep, came, a1, a2, a3, cosine, sine, grads, w_dense, part_normed, att_out, grad_w_dense, keep_q, give_q, keep_n, give_n, weight, q_ref, k_ref, v_ref, values_down, keys_down, k_sum, v_sum, mixed, grad_w, whole):
    for s, k in SLOTS:
        weight[slot_rows(place, s, k), :] = block_of(s, k, keep, came, (a1, a2, a3))[...]
    project_heads(normed, weight, cosine, sine, q_ref, k_ref, v_ref, values_down)
    k_sum[...] = jnp.zeros_like(k_sum)
    v_sum[...] = jnp.zeros_like(v_sum)
    keys_down[...] = (k_ref[...].astype(F32) * SCORE_SCALE).T.astype(BF)
    for start in range(0, normed.shape[0], BLOCK):
        stop = start + BLOCK
        total = [jnp.zeros((LANES, BLOCK), F32)]

        def found_p(head, chosen):
            probabilities, _ = softmax_block(k_ref[:stop, :], chosen, BLOCK)
            found = dot(values_down[:, :stop], probabilities.astype(BF))
            total[0] = total[0] + jnp.where(own_head(head), found, 0.0)
            return probabilities

        grad_att = times_transposed(grads[start:stop, :], w_dense[1]).astype(BF)
        attend_back_block(start, q_ref, k_ref, v_ref, grad_att, keys_down, k_sum, v_sum, cosine, sine, mixed, found_p)
        att_out[start:stop, :] = total[0].T.astype(BF)
    grad_w_dense[...] = outer_sum(att_out[...], grads[...]).astype(BF)
    mixed_back(place, normed, weight, cosine, sine, mixed, k_sum, v_sum, grad_w, part_normed, whole)
    put_slots(place, lambda rows: grad_w[rows, :], keep_q, give_q)
    put_slots(place, lambda rows: whole[rows, :], keep_n, give_n)


def norm_back_kernel(gain_row, place, *refs):
    terms, (hidden, params, grads, grads_out, grads_low, sums) = refs[:5], refs[5:]
    grad_normed = sum_terms(terms)
    xhat, scale = standardize(hidden[...].astype(F32))
    inner = grad_normed * params[gain_row : gain_row + 1, :]
    mean_inner = jnp.mean(inner, axis=-1, keepdims=True)
    mean_along = jnp.mean(inner * xhat, axis=-1, keepdims=True)
    found = grads[...] + (inner - mean_inner - xhat * mean_along) * scale
    grads_out[...] = found
    grads_low[...] = found.astype(BF)
    sums[0:1, :] = jnp.sum(grad_normed * xhat, axis=0, keepdims=True)
    sums[1:2, :] = jnp.sum(grad_normed, axis=0, keepdims=True)


def first_outer_kernel(place, *refs):
    pieces, (act, attended, grads, grad_w) = refs[:8], refs[8:]
    for (s, k), piece in zip(SLOTS, pieces):
        grads[slot_rows(place, s, k), :] = piece[...]
    units = act.shape[1]
    for start in range(0, units, 256):
        rows = slice(start, start + 256)
        grad_w[rows, :] = outer_sum(act[:, rows], grads[...]).astype(BF)
    grad_w[units:, :] = outer_sum(attended[...], grads[...]).astype(BF)


def first_attend_back_kernel(place, grads, w_dense, q_ref, k_ref, v_ref, log_in, cosine, sine, normed, xhat, weight, part_normed, sums0, sums1, ln_sums1, keep_q, give_q, keep_n, give_n, keys_down, k_sum, v_sum, mixed, grad_w, whole, ln_sums):
    k_sum[...] = jnp.zeros_like(k_sum)
    v_sum[...] = jnp.zeros_like(v_sum)
    keys_down[...] = (k_ref[...].astype(F32) * SCORE_SCALE).T.astype(BF)
    for start in range(0, normed.shape[0], BLOCK):
        stop = start + BLOCK

        def found_p(head, chosen):
            scores = mask_diagonal(dot_general(k_ref[:stop, :], chosen, (1, 1)), BLOCK)
            return jnp.exp(scores - log_in[head : head + 1, start:stop])

        grad_att = times_transposed(grads[start:stop, :], w_dense[0]).astype(BF)
        attend_back_block(start, q_ref, k_ref, v_ref, grad_att, keys_down, k_sum, v_sum, cosine, sine, mixed, found_p)
    mixed_back(place, normed, weight, cosine, sine, mixed, k_sum, v_sum, grad_w, part_normed, whole)
    put_slots(place, lambda rows: whole[rows, :], keep_n, give_n)
    ln_sums[...] = jnp.zeros_like(ln_sums)

    def rows_done(rows):
        part = whole[rows, :].astype(F32)
        ln_sums[0:1, :] += jnp.sum(part * xhat[rows, :].astype(F32), axis=0, keepdims=True)
        ln_sums[2:3, :] += jnp.sum(part, axis=0, keepdims=True)

    loop_rows(normed.shape[0], 256, rows_done)
    ln_sums[1:2, :] = ln_sums1[0:1, :]
    ln_sums[3:4, :] = ln_sums1[1:2, :]
    for s in range(4):
        for k, out in ((0, keep_q), (1, give_q)):
            rows = slot_rows(place, s, k)
            out[s, :ROWS, :] = grad_w[rows, :]
            out[s, ROWS:, :] = jnp.zeros((EXTRA, out.shape[2]), BF)
            out[s, ROWS : ROWS + 8, :LANES] = ln_sums[:, rows].astype(BF)
    own = slot_rows(place, 0, 0)
    for layer, sums in ((0, sums0), (1, sums1)):
        units = sums[1:2, : 4 * LANES].astype(BF)
        row = ROWS + 8 + layer * 4
        keep_q[0, row : row + 1, :LANES] = sums[0:1, own].astype(BF)
        for j in range(2):
            keep_q[0, row + 1 + j : row + 2 + j, : 2 * LANES] = units[:, 2 * j * LANES : 2 * (j + 1) * LANES]


def join_kernel(place, keep, came, a1, a2, a3, out):
    for s, k in SLOTS:
        out[s, k] = block_of(s, k, keep, came, (a1, a2, a3))[...]


def exchange_blocks(place, keep, give):
    came = swap(give, 1)
    arrived = send_pairs(place, keep, came)
    shape = (4, 2) + keep.shape[1:]
    return call(join_kernel, [(shape, BF)], place, [keep, came, *arrived])[0]


def rep_chain(part):
    inward = lax.ppermute(part, "rep", [(0, 1), (3, 2)])
    half_sum = add_low(part, inward)
    across = lax.ppermute(half_sum, "rep", [(1, 2), (2, 1)])
    total = add_low(half_sum, across)
    outward = lax.ppermute(total, "rep", [(1, 0), (2, 3)])
    return total, outward


def chosen_sum(place, total, outward):
    middle = (place[2] == 1) | (place[2] == 2)
    return jnp.where(middle, total, outward).astype(F32)


def final_call(body, place, pair, shapes, layer, before):
    before = before or []
    n = len(before)
    return pl.pallas_call(
        body,
        grid=(1,),
        out_shape=[jax.ShapeDtypeStruct((2,) + shape, F32) for shape in shapes],
        in_specs=[pl.BlockSpec(memory_space=pltpu.SMEM)]
        + [pl.BlockSpec(memory_space=pltpu.VMEM)] * 2
        + [pl.BlockSpec(memory_space=pl.ANY)] * n,
        out_specs=[pl.BlockSpec((None,) + shape, lambda step, m=len(shape): (layer,) + (0,) * m) for shape in shapes],
        input_output_aliases={3 + i: i for i in range(n)},
        compiler_params=pltpu.CompilerParams(vmem_limit_bytes=16 * 1024 * 1024),
        cost_estimate=SMALL,
    )(place, *pair, *before)


def final_rows_kernel(splits, n_before, place, total, outward, *refs):
    outs = refs[n_before:]
    start = 0
    for rows, out in zip(splits, outs):
        out[...] = chosen_sum(place, total[start : start + rows, :], outward[start : start + rows, :])
        start += rows


def final_units_kernel(n_before, place, total, outward, *refs):
    out = refs[n_before]
    units = total.shape[3]
    for s, k in SLOTS:
        out[:, slot_rows(place, s, k, units)] = chosen_sum(place, total[s, k], outward[s, k])


def final_heads_kernel(n_before, place, total, outward, *refs):
    out = refs[n_before]
    third = out.shape[1] // 3
    for s, k in SLOTS:
        found = chosen_sum(place, total[s, k], outward[s, k])
        for j in range(3):
            lanes = pl.ds(pl.multiple_of(j * third + slot_start(place, s, k, LANES), LANES), LANES)
            out[:, lanes] = found[:ROWS, j * LANES : (j + 1) * LANES]


def final_small_kernel(place, total, outward, gain, shift, bias_fc1, bias_fc2):
    summed = jnp.zeros((EXTRA, LANES), F32)
    for s, k in SLOTS:
        summed = summed + chosen_sum(place, total[s, k, ROWS:, :LANES], outward[s, k, ROWS:, :LANES])
    gain[...] = summed[0:2, :]
    shift[...] = summed[2:4, :]
    mine = chosen_sum(place, total[0, 0, ROWS:, :], outward[0, 0, ROWS:, :])
    for layer in range(2):
        row = 8 + layer * 4
        bias_fc2[layer : layer + 1, :] = mine[row : row + 1, :LANES]
        for j in range(2):
            bias_fc1[layer : layer + 1, 2 * j * LANES : 2 * (j + 1) * LANES] = mine[row + 1 + j : row + 2 + j, : 2 * LANES]


def local_plane(hidden_in, ln_gain, ln_bias, w_qkv, w_dense, w_fc1, b_fc1, w_fc2, b_fc2, output_grad):
    index = lax.axis_index("grp")
    place = jnp.stack([index // 2, index % 2, lax.axis_index("rep")]).astype(jnp.int32)
    span, width = hidden_in.shape[1:]
    seq = span * 8
    units = b_fc1.shape[1]
    own = 3 * LANES
    cosine, sine = rotary_tables(seq)
    hidden0 = hidden_in.reshape(span, width)
    grads1 = output_grad.reshape(span, width)

    small = jnp.concatenate([ln_gain, ln_bias, b_fc2, jnp.zeros((EXTRA - 6, LANES), BF)])
    hidden_pieces = gather_pieces(hidden0)

    shapes = [((4, ROWS + extra, own), BF) for extra in (EXTRA, 0)], ((4, ROWS, units), BF)
    packed = call(
        pack_kernel,
        [shapes[0][0]] * 2 + [shapes[1]] * 2 + [shapes[0][1]] * 2 + [shapes[1]] * 2,
        place,
        [w_qkv, w_fc1, small],
    )
    weights = []
    for layer in range(2):
        keep_q, give_q, keep_f, give_f = packed[4 * layer : 4 * layer + 4]
        came_q = swap(give_q, 1)
        heads_blocks = [keep_q, came_q, *send_pairs(place, keep_q, came_q)]
        came_f = swap(give_f, 1)
        units_blocks = [keep_f, came_f, *send_pairs(place, keep_f, came_f)]
        weights.append((heads_blocks, units_blocks))

    grads1_low = call(lambda place, grads, dep, out: out.__setitem__(Ellipsis, grads[...].astype(BF)), [((span, width), BF)], place, [grads1, hidden_pieces[6]])[0]
    grad_branch1 = call(assemble_kernel, [((seq, width), BF)], place, gather_pieces(grads1_low))[0]
    wide, column = ((seq, width), BF), ((seq, LANES), BF)
    blocks_n = ((4, ROWS, width), BF)
    normed0, xhat0, weight_q0, params, q0, k0, v0, att0, log0 = call(
        first_attend_kernel,
        [wide, wide, ((width, own), BF), ((EXTRA, width), F32), column, column, column, column, ((8, seq), F32)],
        place,
        [*hidden_pieces, *weights[0][0], cosine, sine],
        [pltpu.VMEM((LANES, seq), BF)],
    )
    weight_f0, act0, slope0, keep, give = call(
        first_units_kernel,
        [((width, units), BF), ((seq, units), BF), ((seq, units), F32), blocks_n, blocks_n],
        place,
        [normed0, *weights[0][1], b_fc1, w_fc2, w_dense, att0],
        [pltpu.VMEM((seq, width), BF)],
    )
    terms = begin_scatter(place, keep, give)
    mine, mine_low = ((span, width), F32), ((span, width), BF)
    hidden1, normed1_own = call(next_hidden_kernel, [mine, mine_low], place, [*terms, hidden0, params])

    normed1, weight_f1, act1, slope1, grad_fc2 = call(
        second_units_kernel,
        [wide, ((width, units), BF), ((seq, units), BF), ((seq, units), F32), ((units, width), BF)],
        place,
        [*gather_pieces(normed1_own), *weights[1][1], b_fc1, grad_branch1],
    )
    chain_fc2 = rep_chain(grad_fc2)
    blocks_f = ((4, ROWS, units), BF)
    keep, give, sums1, part_normed = call(
        partial(units_back_kernel, 1),
        [blocks_f, blocks_f, ((8, width), F32), ((seq, width), F32)],
        place,
        [grad_branch1, w_fc2, slope1, normed1, weight_f1],
        [pltpu.VMEM((seq, units), BF), pltpu.VMEM((width, units), BF)],
    )
    chain_fc1 = rep_chain(exchange_blocks(place, keep, give))
    blocks_q = ((4, ROWS, own), BF)
    head_scratch = [pltpu.VMEM((LANES, seq), BF), pltpu.VMEM((seq, LANES), F32), pltpu.VMEM((seq, LANES), F32)]
    back_scratch = [pltpu.VMEM((seq, own), BF), pltpu.VMEM((width, own), BF), pltpu.VMEM((seq, width), BF)]
    column_scratch = [pltpu.VMEM((seq, LANES), BF)] * 3
    att1, grad_dense, keep, give, keep_n, give_n = call(
        second_attend_kernel,
        [column, ((LANES, width), BF), blocks_q, blocks_q, blocks_n, blocks_n],
        place,
        [normed1, *weights[1][0], cosine, sine, grad_branch1, w_dense, part_normed],
        [pltpu.VMEM((width, own), BF), *column_scratch, pltpu.VMEM((LANES, seq), BF), *head_scratch, *back_scratch],
    )
    terms = begin_scatter(place, keep_n, give_n)
    joined = exchange_blocks(place, keep, give)
    chain_heads = rep_chain(joined)
    chain_dense = rep_chain(grad_dense)
    grads0, grads0_low, ln_sums1 = call(
        partial(norm_back_kernel, 1), [mine, mine_low, ((8, width), F32)], place, [*terms, hidden1, params, grads1]
    )
    keep, give = call(
        last_hidden_kernel, [blocks_n, blocks_n], place, [act1, att1, w_fc2, w_dense], [pltpu.VMEM((seq, width), BF)]
    )
    (hidden_out,) = call(last_sum_kernel, [mine], place, [*begin_scatter(place, keep, give), hidden1, params])

    grad_branch0, grad_rows = call(
        first_outer_kernel,
        [wide, ((units + LANES, width), BF)],
        place,
        [*gather_pieces(grads0_low), act0, att0],
    )
    chain_rows0 = rep_chain(grad_rows)
    keep, give, sums0, part_normed = call(
        partial(units_back_kernel, 0),
        [blocks_f, blocks_f, ((8, width), F32), ((seq, width), F32)],
        place,
        [grad_branch0, w_fc2, slope0, normed0, weight_f0],
        [pltpu.VMEM((seq, units), BF), pltpu.VMEM((width, units), BF)],
    )
    chain_fc1_0 = rep_chain(exchange_blocks(place, keep, give))
    blocks_q0 = ((4, ROWS + EXTRA, own), BF)
    keep, give, keep_n, give_n = call(
        first_attend_back_kernel,
        [blocks_q0, blocks_q0, blocks_n, blocks_n],
        place,
        [grad_branch0, w_dense, q0, k0, v0, log0, cosine, sine, normed0, xhat0, weight_q0, part_normed, sums0, sums1, ln_sums1],
        [*head_scratch, *back_scratch, pltpu.VMEM((8, width), F32)],
    )
    chain_heads0 = rep_chain(exchange_blocks(place, keep, give))
    terms = begin_scatter(place, keep_n, give_n)
    input_grad, _, _ = call(
        partial(norm_back_kernel, 0), [mine, mine_low, ((8, width), F32)], place, [*terms, hidden0, params, grads0]
    )

    (out_fc2,) = final_call(partial(final_rows_kernel, (units,), 0), place, chain_fc2, [(units, width)], 1, None)
    (out_dense,) = final_call(partial(final_rows_kernel, (LANES,), 0), place, chain_dense, [(LANES, width)], 1, None)
    out_fc2, out_dense = final_call(
        partial(final_rows_kernel, (units, LANES), 2), place, chain_rows0, [(units, width), (LANES, width)], 0, [out_fc2, out_dense]
    )
    (out_fc1,) = final_call(partial(final_units_kernel, 0), place, chain_fc1, [(ROWS, w_fc1.shape[2])], 1, None)
    (out_fc1,) = final_call(partial(final_units_kernel, 1), place, chain_fc1_0, [(ROWS, w_fc1.shape[2])], 0, [out_fc1])
    (out_qkv,) = final_call(partial(final_heads_kernel, 0), place, chain_heads, [(ROWS, w_qkv.shape[2])], 1, None)
    (out_qkv,) = final_call(partial(final_heads_kernel, 1), place, chain_heads0, [(ROWS, w_qkv.shape[2])], 0, [out_qkv])
    vector = ((2, LANES), F32)
    out_gain, out_shift, out_b_fc1, out_b_fc2 = call(
        final_small_kernel, [vector, vector, ((2, units), F32), vector], place, list(chain_heads0)
    )
    return (
        hidden_out[None],
        input_grad[None],
        out_gain,
        out_shift,
        out_qkv,
        out_dense,
        out_fc1,
        out_b_fc1,
        out_fc2,
        out_b_fc2,
    )


def local(hidden_in, ln_gain, ln_bias, w_qkv, w_dense, w_fc1, b_fc1, w_fc2, b_fc2, output_grad):
    arguments = (hidden_in, ln_gain, ln_bias, w_qkv, w_dense, w_fc1, b_fc1, w_fc2, b_fc2, output_grad)
    plane = lax.axis_size("grp") == 8 and lax.axis_size("rep") == 4
    plane = plane and hidden_in.shape[:2] == (1, ROWS) and w_qkv.shape == (2, LANES, 3 * 8 * LANES)
    return (local_plane if plane else local_any)(*arguments)


def solution(mesh):
    in_specs = (
        P("rep", "grp", None),
        P(None, "grp"),
        P(None, "grp"),
        P(None, "grp", None),
        P(None, "grp", None),
        P(None, "grp", None),
        P(None, "grp"),
        P(None, "grp", None),
        P(None, "grp"),
        P("rep", "grp", None),
    )
    out_specs = (
        P("rep", "grp", None),
        P("rep", "grp", None),
        P(None, "grp"),
        P(None, "grp"),
        P(None, "grp", None),
        P(None, "grp", None),
        P(None, "grp", None),
        P(None, "grp"),
        P(None, "grp", None),
        P(None, "grp"),
    )
    return jax.shard_map(local, mesh=mesh, in_specs=in_specs, out_specs=out_specs, check_vma=False)
```

```python
from functools import partial

import jax
import jax.numpy as jnp
import numpy as np
from jax import lax
from jax.experimental import pallas as pl
from jax.experimental.pallas import tpu as pltpu
from jax.sharding import PartitionSpec as P

HEAD_DIM = 64
ROT = 32
LANES = 128

EPSILON = 1e-05
SCORE_SCALE = 0.125
NEGATIVE = -1000000000.0
BF = jnp.bfloat16
F32 = jnp.float32


def dot(left, right):
    return jnp.dot(left, right, preferred_element_type=F32)


def dot_general(left, right, contract):
    return lax.dot_general(left, right, ((contract[:1], contract[1:]), ((), ())), preferred_element_type=F32)


def outer_sum(left, right):
    return dot_general(left, right, (0, 0))


def times_transposed(left, right):
    return dot_general(left, right, (1, 1))


def head_mask(head):
    lane = lax.broadcasted_iota(jnp.int32, (1, LANES), 1)
    return (lane >= head * HEAD_DIM) & (lane < (head + 1) * HEAD_DIM)


def turn(part, cosine, sine, sign):
    even = lax.broadcasted_iota(jnp.int32, part.shape, 1) % 2 == 0
    partner = jnp.where(even, pltpu.roll(part, LANES - 1, 1), pltpu.roll(part, 1, 1))
    return part * cosine + partner * (sine * sign)


def mask_diagonal(scores, block):
    keys, queries = scores.shape
    key_place = lax.broadcasted_iota(jnp.int32, (block, queries), 0)
    query_place = lax.broadcasted_iota(jnp.int32, (block, queries), 1)
    last = jnp.where(key_place <= query_place, scores[keys - block :], NEGATIVE)
    if keys == block:
        return last
    return jnp.concatenate([scores[: keys - block], last], axis=0)


def attend_kernel(heads, block, mix_q, mix_k, mix_v, cosine, sine, q_out, k_out, v_out, att_out, log_out):
    seq = mix_q.shape[0]
    q_out[...] = turn(mix_q[...], cosine[...], sine[...], 1.0).astype(BF)
    k_out[...] = turn(mix_k[...], cosine[...], sine[...], 1.0).astype(BF)
    v_out[...] = mix_v[...].astype(BF)
    values_down = mix_v[...].T.astype(BF)
    for start in range(0, seq, block):
        stop = start + block
        queries = q_out[start:stop, :] * SCORE_SCALE
        keys = k_out[:stop, :]
        total = jnp.zeros((LANES, block), F32)
        for head in range(heads):
            chosen = jnp.where(head_mask(head), queries, 0.0).astype(BF)
            scores = mask_diagonal(dot_general(keys, chosen, (1, 1)), block)
            row_max = jnp.max(scores, axis=0, keepdims=True)
            exponent = jnp.exp(scores - row_max)
            row_total = jnp.sum(exponent, axis=0, keepdims=True)
            probabilities = (exponent * (1.0 / row_total)).astype(BF)
            log_out[head : head + 1, start:stop] = row_max + jnp.log(row_total)
            found = dot(values_down[:, :stop], probabilities)
            down = lax.broadcasted_iota(jnp.int32, (LANES, 1), 0)
            own = (down >= head * HEAD_DIM) & (down < (head + 1) * HEAD_DIM)
            total = total + jnp.where(own, found, 0.0)
        att_out[start:stop, :] = total.T.astype(BF)


def attend_back_kernel(heads, block, q_in, k_in, v_in, grad_att, log_in, cosine, sine, q_out, k_out, v_out, k_sum, v_sum):
    seq = q_in.shape[0]
    k_sum[...] = jnp.zeros_like(k_sum)
    v_sum[...] = jnp.zeros_like(v_sum)
    keys_down = (k_in[...].astype(F32) * SCORE_SCALE).T.astype(BF)
    for start in range(0, seq, block):
        stop = start + block
        queries = q_in[start:stop, :] * SCORE_SCALE
        grads = grad_att[start:stop, :]
        grad_queries = jnp.zeros((LANES, block), F32)
        for head in range(heads):
            chosen = jnp.where(head_mask(head), queries, 0.0).astype(BF)
            chosen_grads = jnp.where(head_mask(head), grads, 0.0).astype(BF)
            scores = mask_diagonal(dot_general(k_in[:stop, :], chosen, (1, 1)), block)
            probabilities = jnp.exp(scores - log_in[head : head + 1, start:stop])
            grad_probs = dot_general(v_in[:stop, :], chosen_grads, (1, 1))
            row_inner = jnp.sum(grad_probs * probabilities, axis=0, keepdims=True)
            grad_scores = (probabilities * (grad_probs - row_inner)).astype(BF)
            k_sum[:stop, :] += dot(grad_scores, chosen)
            v_sum[:stop, :] += dot(probabilities.astype(BF), chosen_grads)
            down = lax.broadcasted_iota(jnp.int32, (LANES, 1), 0)
            own = (down >= head * HEAD_DIM) & (down < (head + 1) * HEAD_DIM)
            grad_queries = grad_queries + jnp.where(own, dot(keys_down[:, :stop], grad_scores), 0.0)
        q_out[start:stop, :] = turn(
            grad_queries.T, cosine[start:stop, :], sine[start:stop, :], -1.0
        ).astype(BF)
    k_out[...] = turn(k_sum[...], cosine[...], sine[...], -1.0).astype(BF)
    v_out[...] = v_sum[...].astype(BF)


VMEM_LIMIT = 48 * 1024 * 1024


def attend(mix_q, mix_k, mix_v, heads, cosine, sine):
    seq = mix_q.shape[0]
    out = jax.ShapeDtypeStruct((seq, LANES), BF)
    return pl.pallas_call(
        partial(attend_kernel, heads, min(256, seq)),
        out_shape=(out, out, out, out, jax.ShapeDtypeStruct((heads, seq), F32)),
        compiler_params=pltpu.CompilerParams(vmem_limit_bytes=VMEM_LIMIT),
    )(mix_q, mix_k, mix_v, cosine, sine)


def attend_back(queries, keys, values, grad_att, log_total, heads, cosine, sine):
    seq = queries.shape[0]
    out = jax.ShapeDtypeStruct((seq, LANES), BF)
    return pl.pallas_call(
        partial(attend_back_kernel, heads, min(256, seq)),
        out_shape=(out, out, out),
        scratch_shapes=[pltpu.VMEM((seq, LANES), F32), pltpu.VMEM((seq, LANES), F32)],
        compiler_params=pltpu.CompilerParams(vmem_limit_bytes=VMEM_LIMIT),
    )(queries, keys, values, grad_att, log_total, cosine, sine)


def rotary_tables(seq):
    frequency = (1.0 / 10000.0 ** (np.arange(ROT // 2, dtype=np.float32) * 2.0 / ROT)).astype(np.float32)
    angles = np.arange(seq, dtype=np.float32)[:, None] * frequency[None, :]
    cosine, sine = np.cos(angles.astype(np.float64)), np.sin(angles.astype(np.float64))
    cosine = np.repeat(cosine, 2, axis=1)
    sine = np.repeat(sine, 2, axis=1) * np.tile([-1.0, 1.0], ROT // 2)
    rest = HEAD_DIM - ROT
    cosine = np.concatenate([cosine, np.ones((seq, rest))], axis=1)
    sine = np.concatenate([sine, np.zeros((seq, rest))], axis=1)
    repeats = (1, LANES // HEAD_DIM)
    return np.tile(cosine, repeats).astype(np.float32), np.tile(sine, repeats).astype(np.float32)


def swap(value, bits):
    return lax.ppermute(value, "grp", [(i, i ^ bits) for i in range(8)])


def add_low(left, right):
    return (left.astype(F32) + right.astype(F32)).astype(BF)


def by_chip(parts, chip):
    x, y = chip % 2 == 1, chip // 2 == 1
    near = jnp.where(x, jnp.stack([parts[1], parts[0]]), jnp.stack([parts[0], parts[1]]))
    far = jnp.where(x, jnp.stack([parts[3], parts[2]]), jnp.stack([parts[2], parts[3]]))
    return jnp.where(y, jnp.concatenate([far, near]), jnp.concatenate([near, far]))


def gather_rows(part):
    size = lax.axis_size("grp")
    if size != 8:
        return lax.all_gather(part, "grp", axis=0, tiled=True)
    rows, width = part.shape
    half = rows // 2
    index = lax.axis_index("grp")
    along_x, along_y = swap(part, 2), swap(part, 4)
    corner = jnp.concatenate([swap(along_y[:half], 2), swap(along_x[half:], 4)])
    mine = by_chip([part, along_x, along_y, corner], index // 2)
    other = swap(mine, 1)
    odd = index % 2 == 1
    both = jnp.stack([jnp.where(odd, other, mine), jnp.where(odd, mine, other)], axis=1)
    return both.reshape(8 * rows, width)


def scatter_sum(whole):
    size = lax.axis_size("grp")
    if size != 8:
        return lax.psum_scatter(whole, "grp", scatter_dimension=0, tiled=True).astype(F32)
    rows, width = whole.shape[0] // 8, whole.shape[1]
    half = rows // 2
    index = lax.axis_index("grp")
    chip, core = index // 2, index % 2
    blocks = whole.reshape(4, 2, rows, width)
    keep = lax.dynamic_index_in_dim(blocks, core, 1, False)
    give = lax.dynamic_index_in_dim(blocks, 1 - core, 1, False)
    summed = add_low(keep, swap(give, 1))
    own, for_x, for_y, corner = [lax.dynamic_index_in_dim(summed, chip ^ s, 0, False) for s in range(4)]
    by_x, by_y = swap(corner[:half], 2), swap(corner[half:], 4)
    for_y = jnp.concatenate([add_low(for_y[:half], by_x), for_y[half:]])
    for_x = jnp.concatenate([for_x[:half], add_low(for_x[half:], by_y)])
    return own.astype(F32) + swap(for_y, 4).astype(F32) + swap(for_x, 2).astype(F32)


def exchange(blocks):
    size = lax.axis_size("grp")
    if size != 8:
        return lax.all_to_all(blocks, "grp", 0, 0)
    index = lax.axis_index("grp")
    chip, core = index // 2, index % 2
    pairs = blocks.reshape((4, 2) + blocks.shape[1:])
    keep = lax.dynamic_index_in_dim(pairs, core, 1, False)
    give = lax.dynamic_index_in_dim(pairs, 1 - core, 1, False)
    came = swap(give, 1)
    odd = core == 1
    both = jnp.stack([jnp.where(odd, came, keep), jnp.where(odd, keep, came)], axis=1)
    parts = [lax.dynamic_index_in_dim(both, chip ^ s, 0, False) for s in range(4)]
    parts = [parts[0]] + [swap(parts[s], 2 * s) for s in (1, 2, 3)]
    return by_chip(parts, chip).reshape(blocks.shape)


def rep_sum(part):
    if lax.axis_size("rep") != 4:
        return lax.psum(part, "rep").astype(F32)
    place = lax.axis_index("rep")
    inward = lax.ppermute(part, "rep", [(0, 1), (3, 2)])
    half_sum = add_low(part, inward)
    across = lax.ppermute(half_sum, "rep", [(1, 2), (2, 1)])
    total = add_low(half_sum, across)
    outward = lax.ppermute(total, "rep", [(1, 0), (2, 3)])
    return jnp.where((place == 1) | (place == 2), total, outward).astype(F32)


def columns_of(w_qkv, w_fc1, group):
    rows, qkv = w_qkv.shape
    heads = w_qkv.reshape(rows, 3, group, qkv // 3 // group).transpose(2, 0, 1, 3).reshape(group, rows, -1)
    units = w_fc1.reshape(rows, group, -1).transpose(1, 0, 2)
    found = exchange(jnp.concatenate([heads, units], axis=2))
    found = found.reshape(group * rows, -1)
    return found[:, : qkv // group], found[:, qkv // group :]


def rows_of(grad_qkv, grad_fc1, group):
    rows = grad_qkv.shape[0] // group
    both = jnp.concatenate([grad_qkv, grad_fc1], axis=1).reshape(group, rows, -1)
    found = exchange(both)
    qkv = grad_qkv.shape[1]
    heads = found[:, :, :qkv].reshape(group, rows, 3, qkv // 3).transpose(1, 2, 0, 3).reshape(rows, -1)
    units = found[:, :, qkv:].transpose(1, 0, 2).reshape(rows, -1)
    return heads, units


def standardize(hidden):
    centered = hidden - jnp.mean(hidden, axis=-1, keepdims=True)
    scale = lax.rsqrt(jnp.mean(centered * centered, axis=-1, keepdims=True) + EPSILON)
    return centered * scale, scale


def widen(part):
    return jnp.pad(part, ((0, 0), (0, LANES - part.shape[1])))


def forward_layer(normed, weights, heads, tables):
    qkv_cols, fc1_cols, b_fc1, w_dense, w_fc2 = weights
    mixed = dot(normed, qkv_cols)
    own = heads * HEAD_DIM
    queries, keys, values, attended, log_total = attend(
        *(widen(mixed[:, i * own : (i + 1) * own]) for i in range(3)), heads, *tables
    )
    pre_act = dot(normed, fc1_cols) + b_fc1.astype(F32)
    activation = jax.nn.gelu(pre_act, approximate=True).astype(BF)
    partial_sum = (dot(attended[:, :own], w_dense) + dot(activation, w_fc2)).astype(BF)
    stored = (normed, queries, keys, values, attended, log_total, pre_act, activation)
    return partial_sum, stored


def backward_layer(grad_branch, weights, stored, heads, tables):
    qkv_cols, fc1_cols, b_fc1, w_dense, w_fc2 = weights
    normed, queries, keys, values, attended, log_total, pre_act, activation = stored
    own = heads * HEAD_DIM
    grad_w_fc2 = outer_sum(activation, grad_branch).astype(BF)
    grad_w_dense = outer_sum(attended[:, :own], grad_branch).astype(BF)
    _, gelu_back = jax.vjp(partial(jax.nn.gelu, approximate=True), pre_act)
    grad_pre = gelu_back(times_transposed(grad_branch, w_fc2))[0].astype(BF)
    grad_attended = widen(times_transposed(grad_branch, w_dense).astype(BF))
    grad_mixed = attend_back(queries, keys, values, grad_attended, log_total, heads, *tables)
    grad_mixed = jnp.concatenate([part[:, :own] for part in grad_mixed], axis=1)
    grad_fc1 = outer_sum(normed, grad_pre).astype(BF)
    grad_b_fc1 = jnp.sum(grad_pre.astype(F32), axis=0)
    grad_qkv = outer_sum(normed, grad_mixed).astype(BF)
    grad_normed = (times_transposed(grad_pre, fc1_cols) + times_transposed(grad_mixed, qkv_cols)).astype(BF)
    return grad_normed, (grad_w_fc2, grad_w_dense, grad_fc1, grad_qkv, grad_b_fc1)


def local_any(hidden_in, ln_gain, ln_bias, w_qkv, w_dense, w_fc1, b_fc1, w_fc2, b_fc2, output_grad):
    group = lax.axis_size("grp")
    index = lax.axis_index("grp")
    layers = w_qkv.shape[0]
    span, width = hidden_in.shape[1:]
    seq = span * group
    heads = width // HEAD_DIM // group
    tables = rotary_tables(seq)
    small = jnp.concatenate([ln_gain, ln_bias, b_fc2])
    small = lax.all_gather(small, "grp", axis=1, tiled=True).astype(F32)
    gains, shifts, b_fc2_all = small[:layers], small[layers : 2 * layers], small[2 * layers :]
    hidden = hidden_in.reshape(span, width).astype(F32)
    hidden_all = gather_rows(hidden_in.reshape(span, width))
    weights = []
    for layer in range(layers):
        qkv_cols, fc1_cols = columns_of(w_qkv[layer], w_fc1[layer], group)
        weights.append((qkv_cols, fc1_cols, b_fc1[layer], w_dense[layer], w_fc2[layer]))

    inputs, stored_layers = [], []
    for layer in range(layers):
        inputs.append(hidden)
        if layer == 0:
            normed = (standardize(hidden_all.astype(F32))[0] * gains[0] + shifts[0]).astype(BF)
        else:
            normed = gather_rows((standardize(hidden)[0] * gains[layer] + shifts[layer]).astype(BF))
        partial_sum, stored = forward_layer(normed, weights[layer], heads, tables)
        stored_layers.append(stored)
        hidden = hidden + scatter_sum(partial_sum) + b_fc2_all[layer]

    grad_hidden = output_grad.reshape(span, width)
    small_grads, large_grads = [None] * layers, [None] * layers
    for layer in reversed(range(layers)):
        grad_low = grad_hidden.astype(BF)
        grad_branch = gather_rows(grad_low)
        grad_normed, found = backward_layer(grad_branch, weights[layer], stored_layers[layer], heads, tables)
        grad_w_fc2, grad_w_dense, grad_fc1, grad_qkv, grad_b_fc1 = found
        grad_qkv, grad_fc1 = rows_of(grad_qkv, grad_fc1, group)
        large_grads[layer] = tuple(rep_sum(part) for part in (grad_w_fc2, grad_w_dense, grad_fc1, grad_qkv))
        grad_normed = scatter_sum(grad_normed)
        xhat, scale = standardize(inputs[layer])
        inner = grad_normed * gains[layer]
        mean_inner = jnp.mean(inner, axis=-1, keepdims=True)
        mean_along = jnp.mean(inner * xhat, axis=-1, keepdims=True)
        small_grads[layer] = jnp.concatenate(
            [
                jnp.sum(grad_normed * xhat, axis=0),
                jnp.sum(grad_normed, axis=0),
                jnp.sum(grad_low.astype(F32), axis=0),
                lax.dynamic_update_slice(
                    jnp.zeros((group * grad_b_fc1.shape[0],), F32), grad_b_fc1, (index * grad_b_fc1.shape[0],)
                ),
            ]
        )
        grad_hidden = grad_hidden + (inner - mean_inner - xhat * mean_along) * scale

    summed = lax.psum(jnp.stack(small_grads), ("rep", "grp"))
    own = width // group
    units = b_fc1.shape[1]

    def pick(start, count):
        return lax.dynamic_slice_in_dim(summed, start + index * count, count, 1)

    stacked = [jnp.stack([large_grads[layer][member] for layer in range(layers)]) for member in range(4)]
    return (
        hidden[None],
        grad_hidden[None],
        pick(0, own),
        pick(width, own),
        stacked[3],
        stacked[1],
        stacked[2],
        pick(3 * width, units),
        stacked[0],
        pick(2 * width, own),
    )


SLOTS = [(s, k) for s in range(4) for k in range(2)]
ROWS = 128
EXTRA = 16


def slot_start(place, s, k, size):
    return pl.multiple_of(((place[0] ^ s) * 2 + (place[1] ^ k)) * size, size)


def slot_rows(place, s, k, size=ROWS):
    return pl.ds(slot_start(place, s, k, size), size)


SMALL = pl.CostEstimate(flops=0, bytes_accessed=0, transcendentals=0)


def call(body, outs, place, ins, scratch=(), after=(), hbm=0, mib=16):
    def run(place, *refs):
        body(place, *refs[len(after) :])

    return pl.pallas_call(
        run,
        name=getattr(body, "func", body).__name__,
        out_shape=[jax.ShapeDtypeStruct(*out) for out in outs],
        in_specs=[pl.BlockSpec(memory_space=pltpu.SMEM)]
        + [pl.BlockSpec(memory_space=pl.ANY)] * len(after)
        + [pl.BlockSpec(memory_space=pltpu.HBM)] * hbm
        + [pl.BlockSpec(memory_space=pltpu.VMEM)] * (len(ins) - hbm),
        out_specs=[pl.BlockSpec(memory_space=pltpu.VMEM)] * len(outs),
        scratch_shapes=list(scratch),
        compiler_params=pltpu.CompilerParams(vmem_limit_bytes=mib * 1024 * 1024),
        cost_estimate=SMALL,
    )(place, *after, *ins)


def gather_pieces(part):
    mine = [part, swap(part, 2), swap(part, 4), swap(part, 6)]
    other = [swap(piece, 1) for piece in mine]
    return [piece for pair in zip(mine, other) for piece in pair]


def put_columns(out, start, value):
    for b in range(value.shape[1] // LANES):
        out[start + b * ROWS : start + (b + 1) * ROWS, :] = value[:, b * LANES : (b + 1) * LANES]


def heads_of(place, w_qkv, layer, s, k, j):
    start = j * (w_qkv.shape[2] // 3) + slot_start(place, s, k, LANES)
    return w_qkv[layer, :, pl.ds(pl.multiple_of(start, LANES), LANES)]


FIRST_MINE, FIRST_OTHERS, FIRST_SMALL = 8 * ROWS, 15 * ROWS, 22 * ROWS
FIRST_ROWS = FIRST_SMALL + EXTRA
OTHERS_MINE, OTHERS_SMALL = 8 * ROWS, 15 * ROWS
OTHERS_ROWS = OTHERS_SMALL + EXTRA


def pack_first_kernel(place, hidden_from, qkv_from, fc1_from, small, o0, o1, o2, o3, hidden, w_qkv, w_fc1, sems):
    outs = (o0, o1, o2, o3)
    moves = (
        pltpu.make_async_copy(hidden_from, hidden, sems.at[0]),
        pltpu.make_async_copy(qkv_from.at[0], w_qkv, sems.at[1]),
        pltpu.make_async_copy(fc1_from.at[0], w_fc1, sems.at[2]),
    )
    for move in moves:
        move.start()
    moves[0].wait()
    for out in outs:
        put_columns(out, 0, hidden[...])
        out[FIRST_SMALL:, :] = small[...]
    moves[1].wait()
    third = w_qkv.shape[1] // 3
    for s, k in SLOTS:
        row = (FIRST_MINE, FIRST_OTHERS)[k]
        for j in range(3):
            lanes = pl.ds(pl.multiple_of(j * third + slot_start(place, s, k, LANES), LANES), LANES)
            outs[s][row + j * ROWS : row + (j + 1) * ROWS, :] = w_qkv[:, lanes]
    moves[2].wait()
    for s, k in SLOTS:
        row = (FIRST_MINE, FIRST_OTHERS)[k]
        put_columns(outs[s], row + 3 * ROWS, w_fc1[:, pl.ds(slot_start(place, s, k, 4 * LANES), 4 * LANES)])


def others_first_kernel(place, b0, b1, b2, b3, out):
    for s, block in enumerate((b0, b1, b2, b3)):
        out[s, :OTHERS_MINE, :] = block[:FIRST_MINE, :]
        out[s, OTHERS_MINE:, :] = block[FIRST_OTHERS:, :]


def first_block(s, k, blocks):
    if k:
        return blocks[4].at[s], OTHERS_MINE, OTHERS_SMALL
    return blocks[s], FIRST_MINE, FIRST_SMALL


def pack_heads_kernel(layer, place, w_qkv, *outs):
    for s, k in SLOTS:
        for j in range(3):
            outs[s][k, :, j * LANES : (j + 1) * LANES] = heads_of(place, w_qkv, layer, s, k, j)


def pack_units_kernel(layer, place, w_fc1, *outs):
    units = outs[0].shape[2]
    for s, k in SLOTS:
        outs[s][k] = w_fc1[layer, :, pl.ds(slot_start(place, s, k, units), units)]


def pack_units_grads_kernel(layer, place, w_fc1, grads, *outs):
    units = outs[0].shape[2]
    low = grads[...].astype(BF)
    for s in range(4):
        for k in range(2):
            outs[s][k] = w_fc1[layer, :, pl.ds(slot_start(place, s, k, units), units)]
            outs[s][2 + k] = low[:, k * units : (k + 1) * units]


def others_units_grads_kernel(place, b0, b1, b2, b3, out):
    for s, block in enumerate((b0, b1, b2, b3)):
        out[s] = block[1:]


def send_blocks(place, packed):
    return [packed[0]] + [swap(packed[s], 2 * s) for s in (1, 2, 3)]


def others_kernel(place, b0, b1, b2, b3, out):
    for s, block in enumerate((b0, b1, b2, b3)):
        out[s] = block[1]


def swap_others(place, blocks, after=()):
    (other,) = call(others_kernel, [((4,) + blocks[0].shape[1:], BF)], place, blocks, after=after)
    return [*blocks, swap(other, 1)]


def block_of(s, k, blocks):
    return blocks[4].at[s] if k else blocks[s].at[0]


def project_heads(normed, weight, cosine, sine, q_out, k_out, v_out, values_down):
    step = 256
    for start in range(0, normed.shape[0], step):
        rows = slice(start, start + step)
        mixed = dot(normed[rows, :], weight[...])
        q_out[rows, :] = turn(mixed[:, :LANES], cosine[rows, :], sine[rows, :], 1.0).astype(BF)
        k_out[rows, :] = turn(mixed[:, LANES : 2 * LANES], cosine[rows, :], sine[rows, :], 1.0).astype(BF)
        values = mixed[:, 2 * LANES :]
        v_out[rows, :] = values.astype(BF)
        values_down[:, rows] = values.T.astype(BF)


def own_head(head):
    down = lax.broadcasted_iota(jnp.int32, (LANES, 1), 0)
    return (down >= head * HEAD_DIM) & (down < (head + 1) * HEAD_DIM)


def softmax_block(keys, chosen, block):
    scores = mask_diagonal(dot_general(keys, chosen, (1, 1)), block)
    row_max = jnp.max(scores, axis=0, keepdims=True)
    exponent = jnp.exp(scores - row_max)
    row_total = jnp.sum(exponent, axis=0, keepdims=True)
    return exponent * (1.0 / row_total), row_max + jnp.log(row_total)


BLOCK = 256
HEADS_HERE = LANES // HEAD_DIM


def first_attend_kernel(place, b0, b1, b2, b3, b4, cosine, sine, normed, xhat_out, weight, params, q_out, k_out, v_out, att_out, log_out, values_down):
    for s, k in SLOTS:
        rows = slot_rows(place, s, k)
        block, mine_at, small_at = first_block(s, k, (b0, b1, b2, b3, b4))
        for j in range(3):
            weight[rows, j * LANES : (j + 1) * LANES] = block[mine_at + j * ROWS : mine_at + (j + 1) * ROWS, :]
        params[:, rows] = block[small_at:, :].astype(F32)
        for b in range(8):
            normed[rows, b * LANES : (b + 1) * LANES] = block[b * ROWS : (b + 1) * ROWS, :]
    gain, shift = params[0:1, :], params[2:3, :]

    def norm_rows(rows):
        xhat = standardize(normed[rows, :].astype(F32))[0]
        xhat_out[rows, :] = xhat.astype(BF)
        normed[rows, :] = (xhat * gain + shift).astype(BF)

    loop_rows(normed.shape[0], 4 * ROWS, norm_rows)
    project_heads(normed, weight, cosine, sine, q_out, k_out, v_out, values_down)
    for start in range(0, normed.shape[0], BLOCK):
        stop = start + BLOCK
        queries = q_out[start:stop, :] * SCORE_SCALE
        total = jnp.zeros((LANES, BLOCK), F32)
        for head in range(HEADS_HERE):
            chosen = jnp.where(head_mask(head), queries, 0.0).astype(BF)
            probabilities, log_total = softmax_block(k_out[:stop, :], chosen, BLOCK)
            log_out[head : head + 1, start:stop] = log_total
            found = dot(values_down[:, :stop], probabilities.astype(BF))
            total = total + jnp.where(own_head(head), found, 0.0)
        att_out[start:stop, :] = total.T.astype(BF)


GELU_A = 0.7978845608028654
GELU_B = 0.044715


def gelu_pair(pre):
    square = pre * pre
    wave = jnp.tanh(GELU_A * pre * (1.0 + GELU_B * square))
    half = 0.5 * (1.0 + wave)
    slope = half + 0.5 * pre * (1.0 - wave * wave) * (GELU_A * (1.0 + 3.0 * GELU_B * square))
    return pre * half, slope


def loop_rows(count, step, body):
    def one(i, carry):
        body(pl.ds(pl.multiple_of(i * step, step), step))
        return carry

    lax.fori_loop(0, count // step, one, 0)


def put_slots(place, rows_of_block, keep, give):
    for s in range(4):
        keep[s] = rows_of_block(slot_rows(place, s, 0))
        give[s] = rows_of_block(slot_rows(place, s, 1))


def put_pairs(place, rows_of_block, outs):
    for s, k in SLOTS:
        outs[s][k] = rows_of_block(slot_rows(place, s, k))


def first_units_kernel(place, normed, b0, b1, b2, b3, b4, bias, w_fc2, w_dense, attended, weight, act, slope, whole):
    for s, k in SLOTS:
        block, mine_at, _ = first_block(s, k, (b0, b1, b2, b3, b4))
        for j in range(3, 7):
            part = block[mine_at + j * ROWS : mine_at + (j + 1) * ROWS, :]
            weight[slot_rows(place, s, k), (j - 3) * LANES : (j - 2) * LANES] = part
    shift = bias[0:1, :].astype(F32)

    def rows_done(rows):
        found, found_slope = gelu_pair(dot(normed[rows, :], weight[...]) + shift)
        slope[rows, :] = found_slope
        act[rows, :] = found.astype(BF)
        whole[rows, :] = (dot(act[rows, :], w_fc2[0]) + dot(attended[rows, :], w_dense[0])).astype(BF)

    loop_rows(normed.shape[0], 256, rows_done)


def split_kernel(place, whole, keep, give):
    put_slots(place, lambda rows: whole[rows, :], keep, give)


def split_sum_kernel(place, keep, came, for_x, for_y, corner):
    def rows_done(rows):
        for s, out in ((1, for_x), (2, for_y), (3, corner)):
            out[rows, :] = (keep[s, rows, :].astype(F32) + came[s, rows, :].astype(F32)).astype(BF)

    loop_rows(for_x.shape[0], 16, rows_done)


def begin_scatter(place, keep, give, after=()):
    came = swap(give, 1)
    shape = (keep.shape[1:], BF)
    for_x, for_y, corner = call(split_sum_kernel, [shape] * 3, place, [keep, came], after=after)
    from_corner, from_x, from_y = swap(corner, 6), swap(for_x, 2), swap(for_y, 4)
    return [keep, came, from_x, from_y, from_corner]


def sum_terms(terms):
    total = terms[0][0].astype(F32) + terms[1][0].astype(F32)
    for term in terms[2:]:
        total = total + term[...].astype(F32)
    return total


def next_hidden_kernel(place, *refs):
    terms, (hidden, params, hidden_out, normed) = refs[:5], refs[5:]
    found = hidden[...].astype(F32) + sum_terms(terms) + params[4:5, :]
    hidden_out[...] = found
    normed[...] = (standardize(found)[0] * params[1:2, :] + params[3:4, :]).astype(BF)


def low_kernel(place, wide, low):
    low[...] = wide[...].astype(BF)


def assemble_kernel(place, *refs):
    for (s, k), piece in zip(SLOTS, refs[:8]):
        refs[8][slot_rows(place, s, k), :] = piece[...]


def last_hidden_kernel(place, act, attended, w_fc2, w_dense, keep, give, whole):
    def rows_done(rows):
        whole[rows, :] = (dot(act[rows, :], w_fc2[1]) + dot(attended[rows, :], w_dense[1])).astype(BF)

    loop_rows(act.shape[0], 256, rows_done)
    put_slots(place, lambda rows: whole[rows, :], keep, give)


def last_sum_kernel(place, *refs):
    terms, (hidden, params, out, token) = refs[:5], refs[5:]
    token[...] = jnp.zeros_like(token)
    out[...] = hidden[...] + sum_terms(terms) + params[5:6, :]


def put_halves(out, value):
    half = out.shape[1]
    rows = value.shape[0]
    for j in range(2):
        out[j * rows : (j + 1) * rows, :] = value[:, j * half : (j + 1) * half]


def second_units_kernel(place, *refs):
    pieces, refs = refs[:8], refs[8:]
    blocks, other, refs = refs[:4], refs[4], refs[5:]
    bias, normed, weight, act, slope, grads, chunk, grad_w = refs
    units = weight.shape[1]
    for (s, k), piece in zip(SLOTS, pieces):
        rows = slot_rows(place, s, k)
        normed[rows, :] = piece[...]
        weight[rows, :] = other[s, 0] if k else blocks[s][0]
        for j in range(2):
            grads[rows, j * units : (j + 1) * units] = other[s, 1 + j] if k else blocks[s][2 + j]
    shift = bias[1:2, :].astype(F32)

    def rows_done(rows):
        found, found_slope = gelu_pair(dot(normed[rows, :], weight[...]) + shift)
        slope[rows, :] = found_slope
        act[rows, :] = found.astype(BF)

    loop_rows(normed.shape[0], 256, rows_done)
    for start in range(0, units, 256):
        rows = slice(start, start + 256)
        grad_w[rows, :] = outer_sum(act[:, rows], grads[...]).astype(BF)
    put_halves(chunk, grad_w[...])


def units_back(layer, place, grads, w_fc2, slope, normed, weight, chunk, sums, part_normed, grad_pre, grad_w):
    sums[...] = jnp.zeros_like(sums)
    width = grads.shape[1]
    units = slope.shape[1]

    def rows_done(rows):
        found = (times_transposed(grads[rows, :], w_fc2[layer]) * slope[rows, :]).astype(BF)
        grad_pre[rows, :] = found
        sums[0:1, :width] += jnp.sum(grads[rows, :].astype(F32), axis=0, keepdims=True)
        sums[1:2, :units] += jnp.sum(found.astype(F32), axis=0, keepdims=True)
        part_normed[rows, :] = times_transposed(found, weight[...])

    loop_rows(grads.shape[0], 256, rows_done)
    for start in range(0, width, 256):
        rows = slice(start, start + 256)
        grad_w[rows, :] = outer_sum(normed[:, rows], grad_pre[...]).astype(BF)
    for i, (s, k) in enumerate(SLOTS):
        chunk[i * ROWS : (i + 1) * ROWS, :] = grad_w[slot_rows(place, s, k), :]


def second_units_back_kernel(place, *refs):
    units_back(1, place, *refs)


def first_units_back_kernel(place, *refs):
    pieces, (act, w_fc2, slope, normed, weight, grads, chunk_rows, chunk, sums, part_normed, grad_pre, grad_w) = refs[:8], refs[8:]
    for (s, k), piece in zip(SLOTS, pieces):
        grads[slot_rows(place, s, k), :] = piece[...]
    units_back(0, place, grads, w_fc2, slope, normed, weight, chunk, sums, part_normed, grad_pre, grad_w)
    half, units = chunk_rows.shape[1], act.shape[1]
    for start in range(0, units, 256):
        found = outer_sum(act[:, start : start + 256], grads[...]).astype(BF)
        for j in range(2):
            chunk_rows[j * units + start : j * units + start + 256, :] = found[:, j * half : (j + 1) * half]


def attend_back_block(start, q_ref, k_ref, v_ref, grad_att, keys_down, k_sum, v_sum, cosine, sine, mixed, found_p):
    stop = start + BLOCK
    queries = q_ref[start:stop, :] * SCORE_SCALE
    grad_queries = jnp.zeros((LANES, BLOCK), F32)
    for head in range(HEADS_HERE):
        chosen = jnp.where(head_mask(head), queries, 0.0).astype(BF)
        chosen_grads = jnp.where(head_mask(head), grad_att, 0.0).astype(BF)
        probabilities = found_p(head, chosen)
        grad_probs = dot_general(v_ref[:stop, :], chosen_grads, (1, 1))
        row_inner = jnp.sum(grad_probs * probabilities, axis=0, keepdims=True)
        grad_scores = (probabilities * (grad_probs - row_inner)).astype(BF)
        k_sum[:stop, :] += dot(grad_scores, chosen)
        v_sum[:stop, :] += dot(probabilities.astype(BF), chosen_grads)
        grad_queries = grad_queries + jnp.where(own_head(head), dot(keys_down[:, :stop], grad_scores), 0.0)
    rows = slice(start, stop)
    mixed[rows, :LANES] = turn(grad_queries.T, cosine[rows, :], sine[rows, :], -1.0).astype(BF)


def mixed_back(place, normed, weight, cosine, sine, mixed, k_sum, v_sum, grad_w, part_normed, whole):
    mixed[:, LANES : 2 * LANES] = turn(k_sum[...], cosine[...], sine[...], -1.0).astype(BF)
    mixed[:, 2 * LANES :] = v_sum[...].astype(BF)
    for start in range(0, normed.shape[1], 256):
        rows = slice(start, start + 256)
        grad_w[rows, :] = outer_sum(normed[:, rows], mixed[...]).astype(BF)

    def rows_done(rows):
        whole[rows, :] = (times_transposed(mixed[rows, :], weight[...]) + part_normed[rows, :]).astype(BF)

    loop_rows(normed.shape[0], 256, rows_done)


def put_heads_chunk(place, chunk, grad_w, grad_dense):
    heads = grad_w.shape[1]
    for i, (s, k) in enumerate(SLOTS):
        rows = slice(i * ROWS, (i + 1) * ROWS)
        chunk[rows, :heads] = grad_w[slot_rows(place, s, k), :]
        chunk[rows, heads:] = grad_dense[:, rows]


def second_attend_kernel(place, normed, b0, b1, b2, b3, b4, cosine, sine, grads, w_dense, part_normed, att_out, chunk, keep_n, give_n, weight, q_ref, k_ref, v_ref, values_down, keys_down, k_sum, v_sum, mixed, grad_w, whole):
    for s, k in SLOTS:
        weight[slot_rows(place, s, k), :] = block_of(s, k, (b0, b1, b2, b3, b4))[...]
    project_heads(normed, weight, cosine, sine, q_ref, k_ref, v_ref, values_down)
    k_sum[...] = jnp.zeros_like(k_sum)
    v_sum[...] = jnp.zeros_like(v_sum)
    keys_down[...] = (k_ref[...].astype(F32) * SCORE_SCALE).T.astype(BF)
    for start in range(0, normed.shape[0], BLOCK):
        stop = start + BLOCK
        total = [jnp.zeros((LANES, BLOCK), F32)]

        def found_p(head, chosen):
            probabilities, _ = softmax_block(k_ref[:stop, :], chosen, BLOCK)
            found = dot(values_down[:, :stop], probabilities.astype(BF))
            total[0] = total[0] + jnp.where(own_head(head), found, 0.0)
            return probabilities

        grad_att = times_transposed(grads[start:stop, :], w_dense[1]).astype(BF)
        attend_back_block(start, q_ref, k_ref, v_ref, grad_att, keys_down, k_sum, v_sum, cosine, sine, mixed, found_p)
        att_out[start:stop, :] = total[0].T.astype(BF)
    mixed_back(place, normed, weight, cosine, sine, mixed, k_sum, v_sum, grad_w, part_normed, whole)
    put_heads_chunk(place, chunk, grad_w, outer_sum(att_out[...], grads[...]).astype(BF))
    put_slots(place, lambda rows: whole[rows, :], keep_n, give_n)


def norm_back(gain_row, grad_normed, hidden, params, grads):
    xhat, scale = standardize(hidden[...].astype(F32))
    inner = grad_normed * params[gain_row : gain_row + 1, :]
    mean_inner = jnp.mean(inner, axis=-1, keepdims=True)
    mean_along = jnp.mean(inner * xhat, axis=-1, keepdims=True)
    return grads[...] + (inner - mean_inner - xhat * mean_along) * scale, xhat


def second_norm_back_kernel(place, *refs):
    terms, (hidden, params, grads, grads_out, grads_low, sums) = refs[:5], refs[5:]
    grad_normed = sum_terms(terms)
    found, xhat = norm_back(1, grad_normed, hidden, params, grads)
    grads_out[...] = found
    grads_low[...] = found.astype(BF)
    sums[0:1, :] = jnp.sum(grad_normed * xhat, axis=0, keepdims=True)
    sums[1:2, :] = jnp.sum(grad_normed, axis=0, keepdims=True)


SMALL_ROWS = 16


def first_norm_back_kernel(place, *refs):
    terms, (hidden, params, grads, sums0, sums1, grads_out, small) = refs[:5], refs[5:]
    total = sum_terms(terms)
    grads_out[...] = norm_back(0, total[:ROWS, :], hidden, params, grads)[0]
    small[0:8, :] = total[ROWS : ROWS + 8, :LANES]
    for layer, sums in ((0, sums0), (1, sums1)):
        small[4 + layer : 5 + layer, :] = sums[0:1, slot_rows(place, 0, 0)]
        for j in range(4):
            small[8 + 4 * layer + j : 9 + 4 * layer + j, :] = sums[1:2, j * LANES : (j + 1) * LANES]


def first_attend_back_kernel(place, grads, w_dense, attended, q_ref, k_ref, v_ref, log_in, cosine, sine, normed, xhat, weight, part_normed, ln_sums1, chunk, keep_n, give_n, keys_down, k_sum, v_sum, mixed, grad_w, whole, ln_sums):
    k_sum[...] = jnp.zeros_like(k_sum)
    v_sum[...] = jnp.zeros_like(v_sum)
    keys_down[...] = (k_ref[...].astype(F32) * SCORE_SCALE).T.astype(BF)
    for start in range(0, normed.shape[0], BLOCK):
        stop = start + BLOCK

        def found_p(head, chosen):
            scores = mask_diagonal(dot_general(k_ref[:stop, :], chosen, (1, 1)), BLOCK)
            return jnp.exp(scores - log_in[head : head + 1, start:stop])

        grad_att = times_transposed(grads[start:stop, :], w_dense[0]).astype(BF)
        attend_back_block(start, q_ref, k_ref, v_ref, grad_att, keys_down, k_sum, v_sum, cosine, sine, mixed, found_p)
    mixed_back(place, normed, weight, cosine, sine, mixed, k_sum, v_sum, grad_w, part_normed, whole)
    put_heads_chunk(place, chunk, grad_w, outer_sum(attended[...], grads[...]).astype(BF))
    ln_sums[...] = jnp.zeros_like(ln_sums)

    def rows_done(rows):
        part = whole[rows, :].astype(F32)
        ln_sums[0:1, :] += jnp.sum(part * xhat[rows, :].astype(F32), axis=0, keepdims=True)
        ln_sums[2:3, :] += jnp.sum(part, axis=0, keepdims=True)

    loop_rows(normed.shape[0], 256, rows_done)
    ln_sums[1:2, :] = ln_sums1[0:1, :]
    ln_sums[3:4, :] = ln_sums1[1:2, :]
    for s in range(4):
        for k, out in ((0, keep_n), (1, give_n)):
            rows = slot_rows(place, s, k)
            out[s, :ROWS, :] = whole[rows, :]
            out[s, ROWS:, :] = jnp.zeros((EXTRA, out.shape[2]), BF)
            out[s, ROWS : ROWS + 8, :LANES] = ln_sums[:, rows].astype(BF)


INWARD, ACROSS, OUTWARD = [(0, 1), (3, 2)], [(1, 2), (2, 1)], [(1, 0), (2, 3)]


def along(value, pairs):
    return lax.ppermute(value, "rep", pairs)


def low_sum(left, right):
    return (left[...].astype(F32) + right[...].astype(F32)).astype(left.dtype)


def is_middle(place):
    return (place[2] == 1) | (place[2] == 2)


def tick_kernel(has, place, *refs):
    refs = list(refs)
    if has[0]:
        chunk, came = refs.pop(0), refs.pop(0)
    if has[1]:
        before, crossed = refs.pop(0), refs.pop(0)
    if has[2]:
        coming = refs.pop(0)
    half = refs.pop(0) if has[0] else None
    total = refs.pop(0) if has[1] else None
    going = refs.pop(0) if has[1] and has[2] else None

    def rows_done(rows):
        if has[0]:
            half[rows, :] = low_sum(chunk.at[rows, :], came.at[rows, :])
        if has[1]:
            found = low_sum(before.at[rows, :], crossed.at[rows, :])
            total[rows, :] = found
            if has[2]:
                going[rows, :] = jnp.where(is_middle(place), found, coming[rows, :])

    size = (half if has[0] else total).shape[0]
    loop_rows(size, min(size, ROWS), rows_done)


def tick(place, step, last, coming, after=()):
    ins, outs = [], []
    for pair in (step, last):
        if pair is not None:
            ins += pair
            outs.append((pair[0].shape, pair[0].dtype))
    if coming is not None:
        ins.append(coming)
        outs.append((coming.shape, coming.dtype))
    has = (step is not None, last is not None, coming is not None)
    return call(partial(tick_kernel, has), outs, place, ins, after=after)


def pick_kernel(place, total, came, o0, o1, o2, o3, *rest):
    heads = o0.shape[2]
    for i, (s, k) in enumerate(SLOTS):
        out = (o0, o1, o2, o3)[s]

        def rows_done(rows):
            here = pl.ds(pl.multiple_of(rows.start + i * ROWS, rows.size), rows.size)
            found = jnp.where(is_middle(place), total[here, :], came[here, :])
            out[k, rows, :] = found[:, :heads]
            if rest:
                rest[0][rows, i * ROWS : (i + 1) * ROWS] = found[:, heads:].astype(F32)

        loop_rows(ROWS, 32, rows_done)


def pick(place, total, came, heads, after=()):
    outs = [((2, ROWS, heads), BF)] * 4
    if heads < total.shape[1]:
        outs.append(((ROWS, 8 * LANES), F32))
    return call(pick_kernel, outs, place, [total, came], after=after)


def chosen_sum(place, total, outward):
    middle = (place[2] == 1) | (place[2] == 2)
    return jnp.where(middle, total, outward).astype(F32)


def final_call(body, place, ins, shape, layer, before=None, after=()):
    skip = len(after) + (before is not None)

    def run(place, *refs):
        *ins, out, token, found, sems = refs[skip:]
        body(place, ins, out.at[layer], found, sems)
        token[...] = jnp.zeros_like(token)

    return pl.pallas_call(
        run,
        name=body.__name__,
        out_shape=[jax.ShapeDtypeStruct((2,) + shape, F32), jax.ShapeDtypeStruct((8, LANES), F32)],
        in_specs=[pl.BlockSpec(memory_space=pltpu.SMEM)]
        + [pl.BlockSpec(memory_space=pltpu.HBM)] * (before is not None)
        + [pl.BlockSpec(memory_space=pl.ANY)] * len(after)
        + [pl.BlockSpec(memory_space=pltpu.VMEM)] * len(ins),
        out_specs=[pl.BlockSpec(memory_space=pltpu.HBM), pl.BlockSpec(memory_space=pltpu.VMEM)],
        scratch_shapes=[pltpu.VMEM(shape, F32), pltpu.SemaphoreType.DMA((8,))],
        input_output_aliases={} if before is None else {1: 0},
        compiler_params=pltpu.CompilerParams(vmem_limit_bytes=16 * 1024 * 1024),
        cost_estimate=SMALL,
    )(place, *([] if before is None else [before]), *after, *ins)


def final_rows_kernel(place, ins, out, found, sems):
    total, came = ins
    half, rows = total.shape[1], out.shape[0]
    step = rows // 4

    def move(i):
        put = pl.ds(pl.multiple_of(i * step, step), step)
        return pltpu.make_async_copy(found.at[put, :], out.at[put, :], sems.at[i])

    def one(i, carry):
        put = pl.ds(pl.multiple_of(i * step, step), step)
        for j in range(2):
            part = pl.ds(pl.multiple_of(i * step + j * rows, step), step)
            found[put, j * half : (j + 1) * half] = jnp.where(is_middle(place), total[part, :], came[part, :]).astype(F32)
        move(i).start()
        return carry

    lax.fori_loop(0, 4, one, 0)
    for i in range(4):
        move(i).wait()


def final_units_kernel(place, blocks, out, found, sems):
    units, moves = blocks[0].shape[2], []
    for i, (s, k) in enumerate(SLOTS):
        put = slice(i * units, (i + 1) * units)
        block = block_of(s, k, blocks)

        def rows_done(rows):
            found[rows, put] = block[rows, :].astype(F32)

        loop_rows(ROWS, 32, rows_done)
        moves.append(pltpu.make_async_copy(found.at[:, put], out.at[:, slot_rows(place, s, k, units)], sems.at[i]))
        moves[-1].start()
    for move in moves:
        move.wait()


def final_heads_kernel(place, blocks, out, found, sems):
    third = out.shape[1] // 3
    for s, k in SLOTS:
        block = block_of(s, k, blocks)

        def rows_done(rows):
            part = block[rows, :].astype(F32)
            for j in range(3):
                lanes = pl.ds(pl.multiple_of(j * third + slot_start(place, s, k, LANES), LANES), LANES)
                found[rows, lanes] = part[:, j * LANES : (j + 1) * LANES]

        loop_rows(ROWS, 32, rows_done)
    move = pltpu.make_async_copy(found, out, sems.at[0])
    move.start()
    move.wait()


def final_small_kernel(place, total, came, gain, shift, bias_fc1, bias_fc2):
    found = jnp.where(is_middle(place), total[...], came[...])
    gain[...] = found[0:2, :]
    shift[...] = found[2:4, :]
    bias_fc2[...] = found[4:6, :]
    for layer in range(2):
        for j in range(4):
            bias_fc1[layer : layer + 1, j * LANES : (j + 1) * LANES] = found[8 + 4 * layer + j : 9 + 4 * layer + j, :]


def local_plane(hidden_in, ln_gain, ln_bias, w_qkv, w_dense, w_fc1, b_fc1, w_fc2, b_fc2, output_grad):
    index = lax.axis_index("grp")
    place = jnp.stack([index // 2, index % 2, lax.axis_index("rep")]).astype(jnp.int32)
    span, width = hidden_in.shape[1:]
    seq = span * 8
    units = b_fc1.shape[1]
    own = 3 * LANES
    cosine, sine = rotary_tables(seq)
    hidden0 = hidden_in.reshape(span, width)
    grads1 = output_grad.reshape(span, width)

    wide, column, chunk_shape = ((seq, width), BF), ((seq, LANES), BF), ((seq, units), BF)
    blocks_n, blocks_n0 = ((4, ROWS, width), BF), ((4, ROWS + EXTRA, width), BF)
    blocks_f, blocks_q = ((2, ROWS, units), BF), ((2, ROWS, own), BF)
    mine, mine_low = ((span, width), F32), ((span, width), BF)
    sums_shape, part_shape = ((8, width), F32), ((seq, width), F32)
    head_scratch = [pltpu.VMEM((LANES, seq), BF), pltpu.VMEM((seq, LANES), F32), pltpu.VMEM((seq, LANES), F32)]
    back_scratch = [pltpu.VMEM((seq, own), BF), pltpu.VMEM((width, own), BF), pltpu.VMEM((seq, width), BF)]
    column_scratch = [pltpu.VMEM((seq, LANES), BF)] * 3
    units_scratch = [pltpu.VMEM((seq, units), BF), pltpu.VMEM((width, units), BF)]

    small = jnp.concatenate([ln_gain, ln_bias, b_fc2, jnp.zeros((EXTRA - 6, LANES), BF)])
    packed = call(
        pack_first_kernel,
        [((FIRST_ROWS, LANES), BF)] * 4,
        place,
        [hidden0, w_qkv, w_fc1, small],
        [pltpu.VMEM(a, BF) for a in (hidden0.shape, w_qkv.shape[1:], w_fc1.shape[1:])] + [pltpu.SemaphoreType.DMA((3,))],
        hbm=3,
        mib=60,
    )
    first = send_blocks(place, packed)
    packed = call(partial(pack_units_grads_kernel, 1), [((4, ROWS, units), BF)] * 4, place, [w_fc1, grads1])
    (others0,) = call(others_first_kernel, [((4, OTHERS_ROWS, LANES), BF)], place, first, after=[packed[0]])
    units1 = send_blocks(place, packed)
    first = [*first, swap(others0, 1)]

    normed0, xhat0, weight_q0, params, q0, k0, v0, att0, log0 = call(
        first_attend_kernel,
        [wide, wide, ((width, own), BF), ((EXTRA, width), F32), column, column, column, column, ((8, seq), F32)],
        place,
        [*first, cosine, sine],
        [pltpu.VMEM((LANES, seq), BF)],
    )
    weight_f0, act0, slope0, partial_sum = call(
        first_units_kernel,
        [((width, units), BF), ((seq, units), BF), ((seq, units), F32), wide],
        place,
        [normed0, *first, b_fc1, w_fc2, w_dense, att0],
    )
    keep, give = call(split_kernel, [blocks_n, blocks_n], place, [partial_sum], after=units1[1:])
    terms = begin_scatter(place, keep, give)
    (others1,) = call(others_units_grads_kernel, [((4, 3, ROWS, units), BF)], place, units1, after=[terms[1]])
    hidden1, normed1_own = call(next_hidden_kernel, [mine, mine_low], place, [*terms, hidden0, params])
    pieces = gather_pieces(normed1_own)

    packed = call(partial(pack_heads_kernel, 1), [blocks_q] * 4, place, [w_qkv], after=[normed1_own])
    heads1 = send_blocks(place, packed)
    normed1, weight_f1, act1, slope1, grad_branch1, chunk1 = call(
        second_units_kernel,
        [wide, ((width, units), BF), ((seq, units), BF), ((seq, units), F32), wide, chunk_shape],
        place,
        [*pieces, *units1, swap(others1, 1), b_fc1],
        [pltpu.VMEM((units, width), BF)],
        after=[packed[0]],
    )
    came1 = along(chunk1, INWARD)
    chunk2, sums1, part_normed = call(
        second_units_back_kernel,
        [chunk_shape, sums_shape, part_shape],
        place,
        [grad_branch1, w_fc2, slope1, normed1, weight_f1],
        units_scratch,
    )
    att1, chunk3, keep, give = call(
        second_attend_kernel,
        [column, chunk_shape, blocks_n, blocks_n],
        place,
        [normed1, *swap_others(place, heads1, after=[chunk2]), cosine, sine, grad_branch1, w_dense, part_normed],
        [pltpu.VMEM((width, own), BF), *column_scratch, pltpu.VMEM((LANES, seq), BF), *head_scratch, *back_scratch],
    )
    terms = begin_scatter(place, keep, give)
    (half1,) = tick(place, (chunk1, came1), None, None, after=[give])
    cross1, came2 = along(half1, ACROSS), along(chunk2, INWARD)
    grads0, grads0_low, ln_sums1 = call(
        second_norm_back_kernel, [mine, mine_low, sums_shape], place, [*terms, hidden1, params, grads1], after=[half1]
    )

    keep_h, give_h = call(
        last_hidden_kernel,
        [blocks_n, blocks_n],
        place,
        [act1, att1, w_fc2, w_dense],
        [pltpu.VMEM((seq, width), BF)],
        after=[half1],
    )
    pieces = gather_pieces(grads0_low)
    half2, total1, send3 = tick(place, (chunk2, came2), (half1, cross1), chunk3, after=[grads0_low, give_h])
    terms_h = begin_scatter(place, keep_h, give_h, after=[half2])
    cross2, came3 = along(half2, ACROSS), along(send3, INWARD + OUTWARD)
    grad_branch0, chunk6, chunk4, sums0, part_normed = call(
        first_units_back_kernel,
        [wide, chunk_shape, chunk_shape, sums_shape, part_shape],
        place,
        [*pieces, act0, w_fc2, slope0, normed0, weight_f0],
        units_scratch,
        after=[half2, terms_h[1]],
    )
    half3, total2, send4 = tick(place, (chunk3, came3), (half2, cross2), chunk4)
    cross3, came4 = along(half3, ACROSS), along(send4, INWARD + OUTWARD)
    chunk5, keep, give = call(
        first_attend_back_kernel,
        [chunk_shape, blocks_n0, blocks_n0],
        place,
        [grad_branch0, w_dense, att0, q0, k0, v0, log0, cosine, sine, normed0, xhat0, weight_q0, part_normed, ln_sums1],
        [*head_scratch, *back_scratch, pltpu.VMEM((8, width), F32)],
        after=[half3],
    )
    token = ((8, LANES), F32)
    out_fc2, done = final_call(final_rows_kernel, place, [total1, came3], (units, width), 1, after=[give])
    hidden_out, done_h = call(last_sum_kernel, [mine, token], place, [*terms_h, hidden1, params], after=[done])
    half4, total3, send5 = tick(place, (chunk4, came4), (half3, cross3), chunk5, after=[done_h])
    cross4, came5 = along(half4, ACROSS), along(send5, INWARD + OUTWARD)
    picked2 = pick(place, total2, came4, units, after=[half4])
    terms = begin_scatter(place, keep, give, after=[half4])
    input_grad, small_sums = call(
        first_norm_back_kernel,
        [mine, ((SMALL_ROWS, LANES), F32)],
        place,
        [*terms, hidden0, params, grads0, sums0, sums1],
    )
    half5, total4, send6 = tick(place, (chunk5, came5), (half4, cross4), chunk6, after=[small_sums, picked2[0]])
    cross5, came6 = along(half5, ACROSS), along(send6, INWARD + OUTWARD)
    *picked3, dense1 = pick(place, total3, came5, own, after=[half5])
    blocks2 = swap_others(place, send_blocks(place, picked2), after=[picked3[0]])
    out_fc1, done2 = final_call(final_units_kernel, place, blocks2, (ROWS, w_fc1.shape[2]), 1)
    (small_half,) = tick(place, (small_sums, along(small_sums, INWARD)), None, None, after=[picked3[0]])
    half6, total5 = tick(place, (chunk6, came6), (half5, cross5), None, after=[small_half, done2])
    cross6, came7 = along(half6, ACROSS), along(total5, OUTWARD)
    (small_total,) = tick(place, None, (small_half, along(small_half, ACROSS)), None, after=[half6])
    picked4 = pick(place, total4, came6, units, after=[half6])
    blocks3 = swap_others(place, send_blocks(place, picked3), after=[picked4[0]])
    out_qkv, done3 = final_call(final_heads_kernel, place, blocks3, (ROWS, w_qkv.shape[2]), 1)
    vector = ((2, LANES), F32)
    out_gain, out_shift, out_b_fc1, out_b_fc2 = call(
        final_small_kernel, [vector, vector, ((2, units), F32), vector], place, [small_total, along(small_total, OUTWARD)]
    )
    (total6,) = tick(place, None, (half6, cross6), None, after=[done3, out_gain])
    came8 = along(total6, OUTWARD)
    *picked5, dense0 = pick(place, total5, came7, own, after=[total6])
    blocks4 = swap_others(place, send_blocks(place, picked4), after=[picked5[0]])
    out_fc1, done4 = final_call(final_units_kernel, place, blocks4, (ROWS, w_fc1.shape[2]), 0, out_fc1)
    blocks5 = swap_others(place, send_blocks(place, picked5), after=[done4])
    out_qkv, done5 = final_call(final_heads_kernel, place, blocks5, (ROWS, w_qkv.shape[2]), 0, out_qkv)
    out_fc2, _ = final_call(final_rows_kernel, place, [total6, came8], (units, width), 0, out_fc2, after=[done5])
    out_dense = jnp.stack([dense0, dense1])
    return (
        hidden_out[None],
        input_grad[None],
        out_gain,
        out_shift,
        out_qkv,
        out_dense,
        out_fc1,
        out_b_fc1,
        out_fc2,
        out_b_fc2,
    )


def local(hidden_in, ln_gain, ln_bias, w_qkv, w_dense, w_fc1, b_fc1, w_fc2, b_fc2, output_grad):
    arguments = (hidden_in, ln_gain, ln_bias, w_qkv, w_dense, w_fc1, b_fc1, w_fc2, b_fc2, output_grad)
    plane = lax.axis_size("grp") == 8 and lax.axis_size("rep") == 4
    plane = plane and hidden_in.shape[:2] == (1, ROWS) and w_qkv.shape == (2, LANES, 3 * 8 * LANES)
    return (local_plane if plane else local_any)(*arguments)


def solution(mesh):
    in_specs = (
        P("rep", "grp", None),
        P(None, "grp"),
        P(None, "grp"),
        P(None, "grp", None),
        P(None, "grp", None),
        P(None, "grp", None),
        P(None, "grp"),
        P(None, "grp", None),
        P(None, "grp"),
        P("rep", "grp", None),
    )
    out_specs = (
        P("rep", "grp", None),
        P("rep", "grp", None),
        P(None, "grp"),
        P(None, "grp"),
        P(None, "grp", None),
        P(None, "grp", None),
        P(None, "grp", None),
        P(None, "grp"),
        P(None, "grp", None),
        P(None, "grp"),
    )
    return jax.shard_map(local, mesh=mesh, in_specs=in_specs, out_specs=out_specs, check_vma=False)
```

```python
from functools import partial

import jax
import jax.numpy as jnp
import numpy as np
from jax import lax
from jax.experimental import pallas as pl
from jax.experimental.pallas import tpu as pltpu
from jax.sharding import PartitionSpec as P

HEAD_DIM = 64
ROT = 32
LANES = 128

EPSILON = 1e-05
SCORE_SCALE = 0.125
NEGATIVE = -1000000000.0
BF = jnp.bfloat16
F32 = jnp.float32


def dot(left, right):
    return jnp.dot(left, right, preferred_element_type=F32)


def dot_general(left, right, contract):
    return lax.dot_general(left, right, ((contract[:1], contract[1:]), ((), ())), preferred_element_type=F32)


def outer_sum(left, right):
    return dot_general(left, right, (0, 0))


def times_transposed(left, right):
    return dot_general(left, right, (1, 1))


def head_mask(head):
    lane = lax.broadcasted_iota(jnp.int32, (1, LANES), 1)
    return (lane >= head * HEAD_DIM) & (lane < (head + 1) * HEAD_DIM)


def turn(part, cosine, sine, sign):
    even = lax.broadcasted_iota(jnp.int32, part.shape, 1) % 2 == 0
    partner = jnp.where(even, pltpu.roll(part, LANES - 1, 1), pltpu.roll(part, 1, 1))
    return part * cosine + partner * (sine * sign)


def mask_diagonal(scores, block):
    keys, queries = scores.shape
    key_place = lax.broadcasted_iota(jnp.int32, (block, queries), 0)
    query_place = lax.broadcasted_iota(jnp.int32, (block, queries), 1)
    last = jnp.where(key_place <= query_place, scores[keys - block :], NEGATIVE)
    if keys == block:
        return last
    return jnp.concatenate([scores[: keys - block], last], axis=0)


def attend_kernel(heads, block, mix_q, mix_k, mix_v, cosine, sine, q_out, k_out, v_out, att_out, log_out):
    seq = mix_q.shape[0]
    q_out[...] = turn(mix_q[...], cosine[...], sine[...], 1.0).astype(BF)
    k_out[...] = turn(mix_k[...], cosine[...], sine[...], 1.0).astype(BF)
    v_out[...] = mix_v[...].astype(BF)
    values_down = mix_v[...].T.astype(BF)
    for start in range(0, seq, block):
        stop = start + block
        queries = q_out[start:stop, :] * SCORE_SCALE
        keys = k_out[:stop, :]
        total = jnp.zeros((LANES, block), F32)
        for head in range(heads):
            chosen = jnp.where(head_mask(head), queries, 0.0).astype(BF)
            scores = mask_diagonal(dot_general(keys, chosen, (1, 1)), block)
            row_max = jnp.max(scores, axis=0, keepdims=True)
            exponent = jnp.exp(scores - row_max)
            row_total = jnp.sum(exponent, axis=0, keepdims=True)
            probabilities = (exponent * (1.0 / row_total)).astype(BF)
            log_out[head : head + 1, start:stop] = row_max + jnp.log(row_total)
            found = dot(values_down[:, :stop], probabilities)
            down = lax.broadcasted_iota(jnp.int32, (LANES, 1), 0)
            own = (down >= head * HEAD_DIM) & (down < (head + 1) * HEAD_DIM)
            total = total + jnp.where(own, found, 0.0)
        att_out[start:stop, :] = total.T.astype(BF)


def attend_back_kernel(heads, block, q_in, k_in, v_in, grad_att, log_in, cosine, sine, q_out, k_out, v_out, k_sum, v_sum):
    seq = q_in.shape[0]
    k_sum[...] = jnp.zeros_like(k_sum)
    v_sum[...] = jnp.zeros_like(v_sum)
    keys_down = (k_in[...].astype(F32) * SCORE_SCALE).T.astype(BF)
    for start in range(0, seq, block):
        stop = start + block
        queries = q_in[start:stop, :] * SCORE_SCALE
        grads = grad_att[start:stop, :]
        grad_queries = jnp.zeros((LANES, block), F32)
        for head in range(heads):
            chosen = jnp.where(head_mask(head), queries, 0.0).astype(BF)
            chosen_grads = jnp.where(head_mask(head), grads, 0.0).astype(BF)
            scores = mask_diagonal(dot_general(k_in[:stop, :], chosen, (1, 1)), block)
            probabilities = jnp.exp(scores - log_in[head : head + 1, start:stop])
            grad_probs = dot_general(v_in[:stop, :], chosen_grads, (1, 1))
            row_inner = jnp.sum(grad_probs * probabilities, axis=0, keepdims=True)
            grad_scores = (probabilities * (grad_probs - row_inner)).astype(BF)
            k_sum[:stop, :] += dot(grad_scores, chosen)
            v_sum[:stop, :] += dot(probabilities.astype(BF), chosen_grads)
            down = lax.broadcasted_iota(jnp.int32, (LANES, 1), 0)
            own = (down >= head * HEAD_DIM) & (down < (head + 1) * HEAD_DIM)
            grad_queries = grad_queries + jnp.where(own, dot(keys_down[:, :stop], grad_scores), 0.0)
        q_out[start:stop, :] = turn(
            grad_queries.T, cosine[start:stop, :], sine[start:stop, :], -1.0
        ).astype(BF)
    k_out[...] = turn(k_sum[...], cosine[...], sine[...], -1.0).astype(BF)
    v_out[...] = v_sum[...].astype(BF)


VMEM_LIMIT = 48 * 1024 * 1024


def attend(mix_q, mix_k, mix_v, heads, cosine, sine):
    seq = mix_q.shape[0]
    out = jax.ShapeDtypeStruct((seq, LANES), BF)
    return pl.pallas_call(
        partial(attend_kernel, heads, min(256, seq)),
        out_shape=(out, out, out, out, jax.ShapeDtypeStruct((heads, seq), F32)),
        compiler_params=pltpu.CompilerParams(vmem_limit_bytes=VMEM_LIMIT),
    )(mix_q, mix_k, mix_v, cosine, sine)


def attend_back(queries, keys, values, grad_att, log_total, heads, cosine, sine):
    seq = queries.shape[0]
    out = jax.ShapeDtypeStruct((seq, LANES), BF)
    return pl.pallas_call(
        partial(attend_back_kernel, heads, min(256, seq)),
        out_shape=(out, out, out),
        scratch_shapes=[pltpu.VMEM((seq, LANES), F32), pltpu.VMEM((seq, LANES), F32)],
        compiler_params=pltpu.CompilerParams(vmem_limit_bytes=VMEM_LIMIT),
    )(queries, keys, values, grad_att, log_total, cosine, sine)


def rotary_tables(seq):
    frequency = (1.0 / 10000.0 ** (np.arange(ROT // 2, dtype=np.float32) * 2.0 / ROT)).astype(np.float32)
    angles = np.arange(seq, dtype=np.float32)[:, None] * frequency[None, :]
    cosine, sine = np.cos(angles.astype(np.float64)), np.sin(angles.astype(np.float64))
    cosine = np.repeat(cosine, 2, axis=1)
    sine = np.repeat(sine, 2, axis=1) * np.tile([-1.0, 1.0], ROT // 2)
    rest = HEAD_DIM - ROT
    cosine = np.concatenate([cosine, np.ones((seq, rest))], axis=1)
    sine = np.concatenate([sine, np.zeros((seq, rest))], axis=1)
    repeats = (1, LANES // HEAD_DIM)
    return np.tile(cosine, repeats).astype(np.float32), np.tile(sine, repeats).astype(np.float32)


def swap(value, bits):
    return lax.ppermute(value, "grp", [(i, i ^ bits) for i in range(8)])


def add_low(left, right):
    return (left.astype(F32) + right.astype(F32)).astype(BF)


def by_chip(parts, chip):
    x, y = chip % 2 == 1, chip // 2 == 1
    near = jnp.where(x, jnp.stack([parts[1], parts[0]]), jnp.stack([parts[0], parts[1]]))
    far = jnp.where(x, jnp.stack([parts[3], parts[2]]), jnp.stack([parts[2], parts[3]]))
    return jnp.where(y, jnp.concatenate([far, near]), jnp.concatenate([near, far]))


def gather_rows(part):
    size = lax.axis_size("grp")
    if size != 8:
        return lax.all_gather(part, "grp", axis=0, tiled=True)
    rows, width = part.shape
    half = rows // 2
    index = lax.axis_index("grp")
    along_x, along_y = swap(part, 2), swap(part, 4)
    corner = jnp.concatenate([swap(along_y[:half], 2), swap(along_x[half:], 4)])
    mine = by_chip([part, along_x, along_y, corner], index // 2)
    other = swap(mine, 1)
    odd = index % 2 == 1
    both = jnp.stack([jnp.where(odd, other, mine), jnp.where(odd, mine, other)], axis=1)
    return both.reshape(8 * rows, width)


def scatter_sum(whole):
    size = lax.axis_size("grp")
    if size != 8:
        return lax.psum_scatter(whole, "grp", scatter_dimension=0, tiled=True).astype(F32)
    rows, width = whole.shape[0] // 8, whole.shape[1]
    half = rows // 2
    index = lax.axis_index("grp")
    chip, core = index // 2, index % 2
    blocks = whole.reshape(4, 2, rows, width)
    keep = lax.dynamic_index_in_dim(blocks, core, 1, False)
    give = lax.dynamic_index_in_dim(blocks, 1 - core, 1, False)
    summed = add_low(keep, swap(give, 1))
    own, for_x, for_y, corner = [lax.dynamic_index_in_dim(summed, chip ^ s, 0, False) for s in range(4)]
    by_x, by_y = swap(corner[:half], 2), swap(corner[half:], 4)
    for_y = jnp.concatenate([add_low(for_y[:half], by_x), for_y[half:]])
    for_x = jnp.concatenate([for_x[:half], add_low(for_x[half:], by_y)])
    return own.astype(F32) + swap(for_y, 4).astype(F32) + swap(for_x, 2).astype(F32)


def exchange(blocks):
    size = lax.axis_size("grp")
    if size != 8:
        return lax.all_to_all(blocks, "grp", 0, 0)
    index = lax.axis_index("grp")
    chip, core = index // 2, index % 2
    pairs = blocks.reshape((4, 2) + blocks.shape[1:])
    keep = lax.dynamic_index_in_dim(pairs, core, 1, False)
    give = lax.dynamic_index_in_dim(pairs, 1 - core, 1, False)
    came = swap(give, 1)
    odd = core == 1
    both = jnp.stack([jnp.where(odd, came, keep), jnp.where(odd, keep, came)], axis=1)
    parts = [lax.dynamic_index_in_dim(both, chip ^ s, 0, False) for s in range(4)]
    parts = [parts[0]] + [swap(parts[s], 2 * s) for s in (1, 2, 3)]
    return by_chip(parts, chip).reshape(blocks.shape)


def rep_sum(part):
    if lax.axis_size("rep") != 4:
        return lax.psum(part, "rep").astype(F32)
    place = lax.axis_index("rep")
    inward = lax.ppermute(part, "rep", [(0, 1), (3, 2)])
    half_sum = add_low(part, inward)
    across = lax.ppermute(half_sum, "rep", [(1, 2), (2, 1)])
    total = add_low(half_sum, across)
    outward = lax.ppermute(total, "rep", [(1, 0), (2, 3)])
    return jnp.where((place == 1) | (place == 2), total, outward).astype(F32)


def columns_of(w_qkv, w_fc1, group):
    rows, qkv = w_qkv.shape
    heads = w_qkv.reshape(rows, 3, group, qkv // 3 // group).transpose(2, 0, 1, 3).reshape(group, rows, -1)
    units = w_fc1.reshape(rows, group, -1).transpose(1, 0, 2)
    found = exchange(jnp.concatenate([heads, units], axis=2))
    found = found.reshape(group * rows, -1)
    return found[:, : qkv // group], found[:, qkv // group :]


def rows_of(grad_qkv, grad_fc1, group):
    rows = grad_qkv.shape[0] // group
    both = jnp.concatenate([grad_qkv, grad_fc1], axis=1).reshape(group, rows, -1)
    found = exchange(both)
    qkv = grad_qkv.shape[1]
    heads = found[:, :, :qkv].reshape(group, rows, 3, qkv // 3).transpose(1, 2, 0, 3).reshape(rows, -1)
    units = found[:, :, qkv:].transpose(1, 0, 2).reshape(rows, -1)
    return heads, units


def standardize(hidden):
    centered = hidden - jnp.mean(hidden, axis=-1, keepdims=True)
    scale = lax.rsqrt(jnp.mean(centered * centered, axis=-1, keepdims=True) + EPSILON)
    return centered * scale, scale


def widen(part):
    return jnp.pad(part, ((0, 0), (0, LANES - part.shape[1])))


def forward_layer(normed, weights, heads, tables):
    qkv_cols, fc1_cols, b_fc1, w_dense, w_fc2 = weights
    mixed = dot(normed, qkv_cols)
    own = heads * HEAD_DIM
    queries, keys, values, attended, log_total = attend(
        *(widen(mixed[:, i * own : (i + 1) * own]) for i in range(3)), heads, *tables
    )
    pre_act = dot(normed, fc1_cols) + b_fc1.astype(F32)
    activation = jax.nn.gelu(pre_act, approximate=True).astype(BF)
    partial_sum = (dot(attended[:, :own], w_dense) + dot(activation, w_fc2)).astype(BF)
    stored = (normed, queries, keys, values, attended, log_total, pre_act, activation)
    return partial_sum, stored


def backward_layer(grad_branch, weights, stored, heads, tables):
    qkv_cols, fc1_cols, b_fc1, w_dense, w_fc2 = weights
    normed, queries, keys, values, attended, log_total, pre_act, activation = stored
    own = heads * HEAD_DIM
    grad_w_fc2 = outer_sum(activation, grad_branch).astype(BF)
    grad_w_dense = outer_sum(attended[:, :own], grad_branch).astype(BF)
    _, gelu_back = jax.vjp(partial(jax.nn.gelu, approximate=True), pre_act)
    grad_pre = gelu_back(times_transposed(grad_branch, w_fc2))[0].astype(BF)
    grad_attended = widen(times_transposed(grad_branch, w_dense).astype(BF))
    grad_mixed = attend_back(queries, keys, values, grad_attended, log_total, heads, *tables)
    grad_mixed = jnp.concatenate([part[:, :own] for part in grad_mixed], axis=1)
    grad_fc1 = outer_sum(normed, grad_pre).astype(BF)
    grad_b_fc1 = jnp.sum(grad_pre.astype(F32), axis=0)
    grad_qkv = outer_sum(normed, grad_mixed).astype(BF)
    grad_normed = (times_transposed(grad_pre, fc1_cols) + times_transposed(grad_mixed, qkv_cols)).astype(BF)
    return grad_normed, (grad_w_fc2, grad_w_dense, grad_fc1, grad_qkv, grad_b_fc1)


def local_any(hidden_in, ln_gain, ln_bias, w_qkv, w_dense, w_fc1, b_fc1, w_fc2, b_fc2, output_grad):
    group = lax.axis_size("grp")
    index = lax.axis_index("grp")
    layers = w_qkv.shape[0]
    span, width = hidden_in.shape[1:]
    seq = span * group
    heads = width // HEAD_DIM // group
    tables = rotary_tables(seq)
    small = jnp.concatenate([ln_gain, ln_bias, b_fc2])
    small = lax.all_gather(small, "grp", axis=1, tiled=True).astype(F32)
    gains, shifts, b_fc2_all = small[:layers], small[layers : 2 * layers], small[2 * layers :]
    hidden = hidden_in.reshape(span, width).astype(F32)
    hidden_all = gather_rows(hidden_in.reshape(span, width))
    weights = []
    for layer in range(layers):
        qkv_cols, fc1_cols = columns_of(w_qkv[layer], w_fc1[layer], group)
        weights.append((qkv_cols, fc1_cols, b_fc1[layer], w_dense[layer], w_fc2[layer]))

    inputs, stored_layers = [], []
    for layer in range(layers):
        inputs.append(hidden)
        if layer == 0:
            normed = (standardize(hidden_all.astype(F32))[0] * gains[0] + shifts[0]).astype(BF)
        else:
            normed = gather_rows((standardize(hidden)[0] * gains[layer] + shifts[layer]).astype(BF))
        partial_sum, stored = forward_layer(normed, weights[layer], heads, tables)
        stored_layers.append(stored)
        hidden = hidden + scatter_sum(partial_sum) + b_fc2_all[layer]

    grad_hidden = output_grad.reshape(span, width)
    small_grads, large_grads = [None] * layers, [None] * layers
    for layer in reversed(range(layers)):
        grad_low = grad_hidden.astype(BF)
        grad_branch = gather_rows(grad_low)
        grad_normed, found = backward_layer(grad_branch, weights[layer], stored_layers[layer], heads, tables)
        grad_w_fc2, grad_w_dense, grad_fc1, grad_qkv, grad_b_fc1 = found
        grad_qkv, grad_fc1 = rows_of(grad_qkv, grad_fc1, group)
        large_grads[layer] = tuple(rep_sum(part) for part in (grad_w_fc2, grad_w_dense, grad_fc1, grad_qkv))
        grad_normed = scatter_sum(grad_normed)
        xhat, scale = standardize(inputs[layer])
        inner = grad_normed * gains[layer]
        mean_inner = jnp.mean(inner, axis=-1, keepdims=True)
        mean_along = jnp.mean(inner * xhat, axis=-1, keepdims=True)
        small_grads[layer] = jnp.concatenate(
            [
                jnp.sum(grad_normed * xhat, axis=0),
                jnp.sum(grad_normed, axis=0),
                jnp.sum(grad_low.astype(F32), axis=0),
                lax.dynamic_update_slice(
                    jnp.zeros((group * grad_b_fc1.shape[0],), F32), grad_b_fc1, (index * grad_b_fc1.shape[0],)
                ),
            ]
        )
        grad_hidden = grad_hidden + (inner - mean_inner - xhat * mean_along) * scale

    summed = lax.psum(jnp.stack(small_grads), ("rep", "grp"))
    own = width // group
    units = b_fc1.shape[1]

    def pick(start, count):
        return lax.dynamic_slice_in_dim(summed, start + index * count, count, 1)

    stacked = [jnp.stack([large_grads[layer][member] for layer in range(layers)]) for member in range(4)]
    return (
        hidden[None],
        grad_hidden[None],
        pick(0, own),
        pick(width, own),
        stacked[3],
        stacked[1],
        stacked[2],
        pick(3 * width, units),
        stacked[0],
        pick(2 * width, own),
    )


SLOTS = [(s, k) for s in range(4) for k in range(2)]
ROWS = 128
EXTRA = 16


def slot_start(place, s, k, size):
    return pl.multiple_of(((place[0] ^ s) * 2 + (place[1] ^ k)) * size, size)


def slot_rows(place, s, k, size=ROWS):
    return pl.ds(slot_start(place, s, k, size), size)


SMALL = pl.CostEstimate(flops=0, bytes_accessed=0, transcendentals=0)


def call(body, outs, place, ins, scratch=(), after=(), hbm=0, mib=16):
    def run(place, *refs):
        body(place, *refs[len(after) :])

    return pl.pallas_call(
        run,
        name=getattr(body, "func", body).__name__,
        out_shape=[jax.ShapeDtypeStruct(*out) for out in outs],
        in_specs=[pl.BlockSpec(memory_space=pltpu.SMEM)]
        + [pl.BlockSpec(memory_space=pl.ANY)] * len(after)
        + [pl.BlockSpec(memory_space=pltpu.HBM)] * hbm
        + [pl.BlockSpec(memory_space=pltpu.VMEM)] * (len(ins) - hbm),
        out_specs=[pl.BlockSpec(memory_space=pltpu.VMEM)] * len(outs),
        scratch_shapes=list(scratch),
        compiler_params=pltpu.CompilerParams(vmem_limit_bytes=mib * 1024 * 1024),
        cost_estimate=SMALL,
    )(place, *after, *ins)


def gather_pieces(part):
    mine = [part, swap(part, 2), swap(part, 4), swap(part, 6)]
    other = [swap(piece, 1) for piece in mine]
    return [piece for pair in zip(mine, other) for piece in pair]


def put_columns(out, start, value):
    for b in range(value.shape[1] // LANES):
        out[start + b * ROWS : start + (b + 1) * ROWS, :] = value[:, b * LANES : (b + 1) * LANES]


def heads_of(place, w_qkv, layer, s, k, j):
    start = j * (w_qkv.shape[2] // 3) + slot_start(place, s, k, LANES)
    return w_qkv[layer, :, pl.ds(pl.multiple_of(start, LANES), LANES)]


FIRST_MINE, FIRST_OTHERS, FIRST_SMALL = 8 * ROWS, 15 * ROWS, 22 * ROWS
FIRST_ROWS = FIRST_SMALL + EXTRA
OTHERS_MINE, OTHERS_SMALL = 8 * ROWS, 15 * ROWS
OTHERS_ROWS = OTHERS_SMALL + EXTRA


def pack_first_kernel(place, hidden_from, qkv_from, fc1_from, small, o0, o1, o2, o3, hidden, w_qkv, w_fc1, sems):
    outs = (o0, o1, o2, o3)
    moves = (
        pltpu.make_async_copy(hidden_from, hidden, sems.at[0]),
        pltpu.make_async_copy(qkv_from.at[0], w_qkv, sems.at[1]),
        pltpu.make_async_copy(fc1_from.at[0], w_fc1, sems.at[2]),
    )
    for move in moves:
        move.start()
    moves[0].wait()
    for out in outs:
        put_columns(out, 0, hidden[...])
        out[FIRST_SMALL:, :] = small[...]
    moves[1].wait()
    third = w_qkv.shape[1] // 3
    for s, k in SLOTS:
        row = (FIRST_MINE, FIRST_OTHERS)[k]
        for j in range(3):
            lanes = pl.ds(pl.multiple_of(j * third + slot_start(place, s, k, LANES), LANES), LANES)
            outs[s][row + j * ROWS : row + (j + 1) * ROWS, :] = w_qkv[:, lanes]
    moves[2].wait()
    for s, k in SLOTS:
        row = (FIRST_MINE, FIRST_OTHERS)[k]
        put_columns(outs[s], row + 3 * ROWS, w_fc1[:, pl.ds(slot_start(place, s, k, 4 * LANES), 4 * LANES)])


def others_first_kernel(place, b0, b1, b2, b3, out):
    for s, block in enumerate((b0, b1, b2, b3)):
        out[s, :OTHERS_MINE, :] = block[:FIRST_MINE, :]
        out[s, OTHERS_MINE:, :] = block[FIRST_OTHERS:, :]


def first_block(s, k, blocks):
    if k:
        return blocks[4].at[s], OTHERS_MINE, OTHERS_SMALL
    return blocks[s], FIRST_MINE, FIRST_SMALL


def pack_heads_kernel(layer, place, w_qkv, keep, give):
    for s, k in SLOTS:
        for j in range(3):
            (keep, give)[k][s, :, j * LANES : (j + 1) * LANES] = heads_of(place, w_qkv, layer, s, k, j)


def pair_kernel(place, keep, came, *outs):
    for s, out in enumerate(outs):
        out[0], out[1] = keep[s], came[s]


def pack_units_kernel(layer, place, w_fc1, *outs):
    units = outs[0].shape[2]
    for s, k in SLOTS:
        outs[s][k] = w_fc1[layer, :, pl.ds(slot_start(place, s, k, units), units)]


HALF = ROWS // 2


def half_start(place, other):
    parity = place[2] & 1
    return pl.multiple_of((1 - parity if other else parity) * HALF, HALF)


def pack_units_grads_kernel(layer, place, w_fc1, grads, *outs):
    units = outs[0].shape[1]
    low = grads[...].astype(BF)
    for s in range(4):
        for k in range(2):
            lanes = pl.ds(slot_start(place, s, k, units), units)
            outs[s][k * HALF : (k + 1) * HALF, :] = w_fc1[layer, pl.ds(half_start(place, False), HALF), lanes]
            outs[s][(1 + k) * ROWS : (2 + k) * ROWS, :] = low[:, k * units : (k + 1) * units]


def near_units_kernel(place, b0, b1, b2, b3, out):
    for s, block in enumerate((b0, b1, b2, b3)):
        out[s] = block[:ROWS, :]


def others_units_grads_kernel(place, b0, b1, b2, b3, far, out):
    for s, block in enumerate((b0, b1, b2, b3)):
        out[s, :HALF, :] = block[HALF:ROWS, :]
        out[s, HALF:ROWS, :] = far[s, HALF:, :]
        out[s, ROWS:, :] = block[ROWS:, :]


def send_blocks(place, packed):
    return [packed[0]] + [swap(packed[s], 2 * s) for s in (1, 2, 3)]


def others_kernel(place, b0, b1, b2, b3, out):
    for s, block in enumerate((b0, b1, b2, b3)):
        out[s] = block[1]


def swap_others(place, blocks, after=()):
    (other,) = call(others_kernel, [((4,) + blocks[0].shape[1:], BF)], place, blocks, after=after)
    return [*blocks, swap(other, 1)]


def block_of(s, k, blocks):
    return blocks[4].at[s] if k else blocks[s].at[0]


def project_heads(normed, weight, cosine, sine, q_out, k_out, v_out, values_down):
    step = 256
    for start in range(0, normed.shape[0], step):
        rows = slice(start, start + step)
        mixed = dot(normed[rows, :], weight[...])
        q_out[rows, :] = turn(mixed[:, :LANES], cosine[rows, :], sine[rows, :], 1.0).astype(BF)
        k_out[rows, :] = turn(mixed[:, LANES : 2 * LANES], cosine[rows, :], sine[rows, :], 1.0).astype(BF)
        values = mixed[:, 2 * LANES :]
        v_out[rows, :] = values.astype(BF)
        values_down[:, rows] = values.T.astype(BF)


def own_head(head):
    down = lax.broadcasted_iota(jnp.int32, (LANES, 1), 0)
    return (down >= head * HEAD_DIM) & (down < (head + 1) * HEAD_DIM)


def softmax_block(keys, chosen, block):
    scores = mask_diagonal(dot_general(keys, chosen, (1, 1)), block)
    row_max = jnp.max(scores, axis=0, keepdims=True)
    exponent = jnp.exp(scores - row_max)
    row_total = jnp.sum(exponent, axis=0, keepdims=True)
    return exponent * (1.0 / row_total), row_max + jnp.log(row_total)


BLOCK = 256
HEADS_HERE = LANES // HEAD_DIM


def first_attend_kernel(place, b0, b1, b2, b3, b4, cosine, sine, normed, xhat_out, weight, params, q_out, k_out, v_out, att_out, log_out, values_down):
    for s, k in SLOTS:
        rows = slot_rows(place, s, k)
        block, mine_at, small_at = first_block(s, k, (b0, b1, b2, b3, b4))
        for j in range(3):
            weight[rows, j * LANES : (j + 1) * LANES] = block[mine_at + j * ROWS : mine_at + (j + 1) * ROWS, :]
        params[:, rows] = block[small_at:, :].astype(F32)
        for b in range(8):
            normed[rows, b * LANES : (b + 1) * LANES] = block[b * ROWS : (b + 1) * ROWS, :]
    gain, shift = params[0:1, :], params[2:3, :]

    def norm_rows(rows):
        xhat = standardize(normed[rows, :].astype(F32))[0]
        xhat_out[rows, :] = xhat.astype(BF)
        normed[rows, :] = (xhat * gain + shift).astype(BF)

    loop_rows(normed.shape[0], 4 * ROWS, norm_rows)
    project_heads(normed, weight, cosine, sine, q_out, k_out, v_out, values_down)
    for start in range(0, normed.shape[0], BLOCK):
        stop = start + BLOCK
        queries = q_out[start:stop, :] * SCORE_SCALE
        total = jnp.zeros((LANES, BLOCK), F32)
        for head in range(HEADS_HERE):
            chosen = jnp.where(head_mask(head), queries, 0.0).astype(BF)
            probabilities, log_total = softmax_block(k_out[:stop, :], chosen, BLOCK)
            log_out[head : head + 1, start:stop] = log_total
            found = dot(values_down[:, :stop], probabilities.astype(BF))
            total = total + jnp.where(own_head(head), found, 0.0)
        att_out[start:stop, :] = total.T.astype(BF)


GELU_A = 0.7978845608028654
GELU_B = 0.044715


def gelu_pair(pre):
    square = pre * pre
    wave = jnp.tanh(GELU_A * pre * (1.0 + GELU_B * square))
    half = 0.5 * (1.0 + wave)
    slope = half + 0.5 * pre * (1.0 - wave * wave) * (GELU_A * (1.0 + 3.0 * GELU_B * square))
    return pre * half, slope


def loop_rows(count, step, body):
    def one(i, carry):
        body(pl.ds(pl.multiple_of(i * step, step), step))
        return carry

    lax.fori_loop(0, count // step, one, 0)


def put_slots(place, rows_of_block, keep, give):
    for s in range(4):
        keep[s] = rows_of_block(slot_rows(place, s, 0))
        give[s] = rows_of_block(slot_rows(place, s, 1))


def put_pairs(place, rows_of_block, outs):
    for s, k in SLOTS:
        outs[s][k] = rows_of_block(slot_rows(place, s, k))


def first_units_kernel(place, normed, b0, b1, b2, b3, b4, bias, w_fc2, w_dense, attended, weight, act, slope, whole):
    for s, k in SLOTS:
        block, mine_at, _ = first_block(s, k, (b0, b1, b2, b3, b4))
        for j in range(3, 7):
            part = block[mine_at + j * ROWS : mine_at + (j + 1) * ROWS, :]
            weight[slot_rows(place, s, k), (j - 3) * LANES : (j - 2) * LANES] = part
    shift = bias[0:1, :].astype(F32)

    def rows_done(rows):
        found, found_slope = gelu_pair(dot(normed[rows, :], weight[...]) + shift)
        slope[rows, :] = found_slope
        act[rows, :] = found.astype(BF)
        whole[rows, :] = (dot(act[rows, :], w_fc2[0]) + dot(attended[rows, :], w_dense[0])).astype(BF)

    loop_rows(normed.shape[0], 256, rows_done)


def split_kernel(place, whole, keep, give):
    put_slots(place, lambda rows: whole[rows, :], keep, give)


def split_sum_kernel(place, keep, came, for_x, for_y, corner):
    def rows_done(rows):
        for s, out in ((1, for_x), (2, for_y), (3, corner)):
            out[rows, :] = (keep[s, rows, :].astype(F32) + came[s, rows, :].astype(F32)).astype(BF)

    loop_rows(for_x.shape[0], 16, rows_done)


def begin_scatter(place, keep, give, after=()):
    came = swap(give, 1)
    shape = (keep.shape[1:], BF)
    for_x, for_y, corner = call(split_sum_kernel, [shape] * 3, place, [keep, came], after=after)
    from_corner, from_x, from_y = swap(corner, 6), swap(for_x, 2), swap(for_y, 4)
    return [keep, came, from_x, from_y, from_corner], for_x


def sum_terms(terms):
    total = terms[0][0].astype(F32) + terms[1][0].astype(F32)
    for term in terms[2:]:
        total = total + term[...].astype(F32)
    return total


def next_hidden_kernel(place, *refs):
    terms, (hidden, params, hidden_out, normed) = refs[:5], refs[5:]
    found = hidden[...].astype(F32) + sum_terms(terms) + params[4:5, :]
    hidden_out[...] = found
    normed[...] = (standardize(found)[0] * params[1:2, :] + params[3:4, :]).astype(BF)


def low_kernel(place, wide, low):
    low[...] = wide[...].astype(BF)


def assemble_kernel(place, *refs):
    for (s, k), piece in zip(SLOTS, refs[:8]):
        refs[8][slot_rows(place, s, k), :] = piece[...]


def last_hidden_kernel(place, act, attended, w_fc2, w_dense, keep, give, whole):
    def rows_done(rows):
        whole[rows, :] = (dot(act[rows, :], w_fc2[1]) + dot(attended[rows, :], w_dense[1])).astype(BF)

    loop_rows(act.shape[0], 256, rows_done)
    put_slots(place, lambda rows: whole[rows, :], keep, give)


def last_sum_kernel(place, *refs):
    terms, (hidden, params, out, token) = refs[:5], refs[5:]
    token[...] = jnp.zeros_like(token)
    out[...] = hidden[...] + sum_terms(terms) + params[5:6, :]


SMALL_ROWS = 16


def clear_rest(chunk):
    chunk[chunk.shape[0] - SMALL_ROWS :, :] = jnp.zeros((SMALL_ROWS, chunk.shape[1]), chunk.dtype)


def put_halves(out, value):
    half = out.shape[1]
    rows = value.shape[0]
    for j in range(2):
        out[j * rows : (j + 1) * rows, :] = value[:, j * half : (j + 1) * half]


def second_units_kernel(place, *refs):
    pieces, refs = refs[:8], refs[8:]
    blocks, other, far, refs = refs[:4], refs[4], refs[5], refs[6:]
    bias, normed, weight, act, slope, grads, chunk, grad_w = refs
    units = weight.shape[1]
    for (s, k), piece in zip(SLOTS, pieces):
        rows = slot_rows(place, s, k)
        normed[rows, :] = piece[...]
        block = other.at[s] if k else blocks[s]
        parts = (block[:HALF, :], block[HALF:ROWS, :] if k else far[s, :HALF, :])
        for part, other_plane in zip(parts, (False, True)):
            start = slot_start(place, s, k, ROWS) + half_start(place, other_plane)
            weight[pl.ds(pl.multiple_of(start, HALF), HALF), :] = part
        for j in range(2):
            grads[rows, j * units : (j + 1) * units] = block[(1 + j) * ROWS : (2 + j) * ROWS, :]
    shift = bias[1:2, :].astype(F32)

    def rows_done(rows):
        found, found_slope = gelu_pair(dot(normed[rows, :], weight[...]) + shift)
        slope[rows, :] = found_slope
        act[rows, :] = found.astype(BF)

    loop_rows(normed.shape[0], 256, rows_done)
    for start in range(0, units, 256):
        rows = slice(start, start + 256)
        grad_w[rows, :] = outer_sum(act[:, rows], grads[...]).astype(BF)
    put_halves(chunk, grad_w[...])
    clear_rest(chunk)


def units_back(layer, place, grads, w_fc2, slope, normed, weight, chunk, sums, part_normed, grad_pre, grad_w):
    sums[...] = jnp.zeros_like(sums)
    width = grads.shape[1]
    units = slope.shape[1]

    def rows_done(rows):
        found = (times_transposed(grads[rows, :], w_fc2[layer]) * slope[rows, :]).astype(BF)
        grad_pre[rows, :] = found
        sums[0:1, :width] += jnp.sum(grads[rows, :].astype(F32), axis=0, keepdims=True)
        sums[1:2, :units] += jnp.sum(found.astype(F32), axis=0, keepdims=True)
        part_normed[rows, :] = times_transposed(found, weight[...])

    loop_rows(grads.shape[0], 256, rows_done)
    for start in range(0, width, 256):
        rows = slice(start, start + 256)
        grad_w[rows, :] = outer_sum(normed[:, rows], grad_pre[...]).astype(BF)
    for i, (s, k) in enumerate(SLOTS):
        chunk[i * ROWS : (i + 1) * ROWS, :] = grad_w[slot_rows(place, s, k), :]
    clear_rest(chunk)


def second_units_back_kernel(place, *refs):
    units_back(1, place, *refs)


def first_units_back_kernel(place, *refs):
    pieces, (act, w_fc2, slope, normed, weight, grads, chunk_rows, chunk, sums, part_normed, grad_pre, grad_w) = refs[:8], refs[8:]
    for (s, k), piece in zip(SLOTS, pieces):
        grads[slot_rows(place, s, k), :] = piece[...]
    units_back(0, place, grads, w_fc2, slope, normed, weight, chunk, sums, part_normed, grad_pre, grad_w)
    half, units = chunk_rows.shape[1], act.shape[1]
    for start in range(0, units, 256):
        found = outer_sum(act[:, start : start + 256], grads[...]).astype(BF)
        for j in range(2):
            chunk_rows[j * units + start : j * units + start + 256, :] = found[:, j * half : (j + 1) * half]


def attend_back_block(start, q_ref, k_ref, v_ref, grad_att, keys_down, k_sum, v_sum, cosine, sine, mixed, found_p):
    stop = start + BLOCK
    queries = q_ref[start:stop, :] * SCORE_SCALE
    grad_queries = jnp.zeros((LANES, BLOCK), F32)
    for head in range(HEADS_HERE):
        chosen = jnp.where(head_mask(head), queries, 0.0).astype(BF)
        chosen_grads = jnp.where(head_mask(head), grad_att, 0.0).astype(BF)
        probabilities = found_p(head, chosen)
        grad_probs = dot_general(v_ref[:stop, :], chosen_grads, (1, 1))
        row_inner = jnp.sum(grad_probs * probabilities, axis=0, keepdims=True)
        grad_scores = (probabilities * (grad_probs - row_inner)).astype(BF)
        k_sum[:stop, :] += dot(grad_scores, chosen)
        v_sum[:stop, :] += dot(probabilities.astype(BF), chosen_grads)
        grad_queries = grad_queries + jnp.where(own_head(head), dot(keys_down[:, :stop], grad_scores), 0.0)
    rows = slice(start, stop)
    mixed[rows, :LANES] = turn(grad_queries.T, cosine[rows, :], sine[rows, :], -1.0).astype(BF)


def mixed_back(place, normed, weight, cosine, sine, mixed, k_sum, v_sum, grad_w, part_normed, whole):
    mixed[:, LANES : 2 * LANES] = turn(k_sum[...], cosine[...], sine[...], -1.0).astype(BF)
    mixed[:, 2 * LANES :] = v_sum[...].astype(BF)
    for start in range(0, normed.shape[1], 256):
        rows = slice(start, start + 256)
        grad_w[rows, :] = outer_sum(normed[:, rows], mixed[...]).astype(BF)

    def rows_done(rows):
        whole[rows, :] = (times_transposed(mixed[rows, :], weight[...]) + part_normed[rows, :]).astype(BF)

    loop_rows(normed.shape[0], 256, rows_done)


def put_heads_chunk(place, chunk, grad_w, grad_dense):
    heads = grad_w.shape[1]
    for i, (s, k) in enumerate(SLOTS):
        rows = slice(i * ROWS, (i + 1) * ROWS)
        chunk[rows, :heads] = grad_w[slot_rows(place, s, k), :]
        chunk[rows, heads:] = grad_dense[:, rows]
    clear_rest(chunk)


def second_attend_kernel(place, normed, b0, b1, b2, b3, cosine, sine, grads, w_dense, part_normed, att_out, chunk, keep_n, give_n, weight, q_ref, k_ref, v_ref, values_down, keys_down, k_sum, v_sum, mixed, grad_w, whole):
    for s, k in SLOTS:
        weight[slot_rows(place, s, k), :] = (b0, b1, b2, b3)[s][k]
    project_heads(normed, weight, cosine, sine, q_ref, k_ref, v_ref, values_down)
    k_sum[...] = jnp.zeros_like(k_sum)
    v_sum[...] = jnp.zeros_like(v_sum)
    keys_down[...] = (k_ref[...].astype(F32) * SCORE_SCALE).T.astype(BF)
    for start in range(0, normed.shape[0], BLOCK):
        stop = start + BLOCK
        total = [jnp.zeros((LANES, BLOCK), F32)]

        def found_p(head, chosen):
            probabilities, _ = softmax_block(k_ref[:stop, :], chosen, BLOCK)
            found = dot(values_down[:, :stop], probabilities.astype(BF))
            total[0] = total[0] + jnp.where(own_head(head), found, 0.0)
            return probabilities

        grad_att = times_transposed(grads[start:stop, :], w_dense[1]).astype(BF)
        attend_back_block(start, q_ref, k_ref, v_ref, grad_att, keys_down, k_sum, v_sum, cosine, sine, mixed, found_p)
        att_out[start:stop, :] = total[0].T.astype(BF)
    mixed_back(place, normed, weight, cosine, sine, mixed, k_sum, v_sum, grad_w, part_normed, whole)
    put_heads_chunk(place, chunk, grad_w, outer_sum(att_out[...], grads[...]).astype(BF))
    put_slots(place, lambda rows: whole[rows, :], keep_n, give_n)


def norm_back(gain_row, grad_normed, hidden, params, grads):
    xhat, scale = standardize(hidden[...].astype(F32))
    inner = grad_normed * params[gain_row : gain_row + 1, :]
    mean_inner = jnp.mean(inner, axis=-1, keepdims=True)
    mean_along = jnp.mean(inner * xhat, axis=-1, keepdims=True)
    return grads[...] + (inner - mean_inner - xhat * mean_along) * scale, xhat


def second_norm_back_kernel(place, *refs):
    terms, (hidden, params, grads, grads_out, grads_low, sums) = refs[:5], refs[5:]
    grad_normed = sum_terms(terms)
    found, xhat = norm_back(1, grad_normed, hidden, params, grads)
    grads_out[...] = found
    grads_low[...] = found.astype(BF)
    sums[0:1, :] = jnp.sum(grad_normed * xhat, axis=0, keepdims=True)
    sums[1:2, :] = jnp.sum(grad_normed, axis=0, keepdims=True)


def first_norm_back_kernel(place, *refs):
    terms, (hidden, params, grads, sums0, sums1, grads_out, small) = refs[:5], refs[5:]
    total = sum_terms(terms)
    grads_out[...] = norm_back(0, total[:ROWS, :], hidden, params, grads)[0]
    small[0:8, :] = total[ROWS : ROWS + 8, :LANES]
    for layer, sums in ((0, sums0), (1, sums1)):
        small[4 + layer : 5 + layer, :] = sums[0:1, slot_rows(place, 0, 0)]
        for j in range(4):
            small[8 + 4 * layer + j : 9 + 4 * layer + j, :] = sums[1:2, j * LANES : (j + 1) * LANES]


def first_attend_back_kernel(place, grads, w_dense, attended, q_ref, k_ref, v_ref, log_in, cosine, sine, normed, xhat, weight, part_normed, ln_sums1, chunk, keep_n, give_n, keys_down, k_sum, v_sum, mixed, grad_w, whole, ln_sums):
    k_sum[...] = jnp.zeros_like(k_sum)
    v_sum[...] = jnp.zeros_like(v_sum)
    keys_down[...] = (k_ref[...].astype(F32) * SCORE_SCALE).T.astype(BF)
    for start in range(0, normed.shape[0], BLOCK):
        stop = start + BLOCK

        def found_p(head, chosen):
            scores = mask_diagonal(dot_general(k_ref[:stop, :], chosen, (1, 1)), BLOCK)
            return jnp.exp(scores - log_in[head : head + 1, start:stop])

        grad_att = times_transposed(grads[start:stop, :], w_dense[0]).astype(BF)
        attend_back_block(start, q_ref, k_ref, v_ref, grad_att, keys_down, k_sum, v_sum, cosine, sine, mixed, found_p)
    mixed_back(place, normed, weight, cosine, sine, mixed, k_sum, v_sum, grad_w, part_normed, whole)
    put_heads_chunk(place, chunk, grad_w, outer_sum(attended[...], grads[...]).astype(BF))
    ln_sums[...] = jnp.zeros_like(ln_sums)

    def rows_done(rows):
        part = whole[rows, :].astype(F32)
        ln_sums[0:1, :] += jnp.sum(part * xhat[rows, :].astype(F32), axis=0, keepdims=True)
        ln_sums[2:3, :] += jnp.sum(part, axis=0, keepdims=True)

    loop_rows(normed.shape[0], 256, rows_done)
    ln_sums[1:2, :] = ln_sums1[0:1, :]
    ln_sums[3:4, :] = ln_sums1[1:2, :]
    for s in range(4):
        for k, out in ((0, keep_n), (1, give_n)):
            rows = slot_rows(place, s, k)
            out[s, :ROWS, :] = whole[rows, :]
            out[s, ROWS:, :] = jnp.zeros((EXTRA, out.shape[2]), BF)
            out[s, ROWS : ROWS + 8, :LANES] = ln_sums[:, rows].astype(BF)


INWARD, ACROSS, OUTWARD = [(0, 1), (3, 2)], [(1, 2), (2, 1)], [(1, 0), (2, 3)]


def along(value, pairs):
    return lax.ppermute(value, "rep", pairs)


def low_sum(left, right):
    return (left[...].astype(F32) + right[...].astype(F32)).astype(left.dtype)


def is_middle(place):
    return (place[2] == 1) | (place[2] == 2)


def tick_kernel(has, place, *refs):
    refs = list(refs)
    if has[0]:
        chunk, came = refs.pop(0), refs.pop(0)
    if has[1]:
        before, crossed = refs.pop(0), refs.pop(0)
    if has[2]:
        coming = refs.pop(0)
    half = refs.pop(0) if has[0] else None
    going = refs.pop(0) if has[1] else None

    def rows_done(rows):
        if has[0]:
            half[rows, :] = low_sum(chunk.at[rows, :], came.at[rows, :])
        if has[1]:
            found = low_sum(before.at[rows, :], crossed.at[rows, :])
            going[rows, :] = jnp.where(is_middle(place), found, coming[rows, :]) if has[2] else found

    loop_rows((half if has[0] else going).shape[0], 208, rows_done)


def tick(place, step, last, coming, after=()):
    ins, outs = [], []
    for pair in (step, last):
        if pair is not None:
            ins += pair
            outs.append((pair[0].shape, pair[0].dtype))
    if coming is not None:
        ins.append(coming)
    has = (step is not None, last is not None, coming is not None)
    return call(partial(tick_kernel, has), outs, place, ins, after=after)


def add_small_kernel(place, chunk, small, out):
    rows = chunk.shape[0] - SMALL_ROWS
    out[:rows, :] = chunk[:rows, :]
    out[rows:, :LANES] = small[...].astype(BF)
    out[rows:, LANES:] = jnp.zeros((SMALL_ROWS, chunk.shape[1] - LANES), BF)


def pick_kernel(place, total, came, o0, o1, o2, o3, *rest):
    heads = o0.shape[2]
    for i, (s, k) in enumerate(SLOTS):
        out = (o0, o1, o2, o3)[s]

        def rows_done(rows):
            here = pl.ds(pl.multiple_of(rows.start + i * ROWS, rows.size), rows.size)
            found = jnp.where(is_middle(place), total[here, :], came[here, :])
            out[k, rows, :] = found[:, :heads]
            if rest:
                rest[0][rows, i * ROWS : (i + 1) * ROWS] = found[:, heads:].astype(F32)

        loop_rows(ROWS, 32, rows_done)


def pick_both_kernel(place, total_f, came_f, total_q, came_q, o0, o1, o2, o3, dense):
    units = total_f.shape[1]
    heads = o0.shape[2] - units
    for i, (s, k) in enumerate(SLOTS):
        out = (o0, o1, o2, o3)[s]

        def rows_done(rows):
            here = pl.ds(pl.multiple_of(rows.start + i * ROWS, rows.size), rows.size)
            out[k, rows, :units] = jnp.where(is_middle(place), total_f[here, :], came_f[here, :])
            found = jnp.where(is_middle(place), total_q[here, :], came_q[here, :])
            out[k, rows, units:] = found[:, :heads]
            dense[rows, i * ROWS : (i + 1) * ROWS] = found[:, heads:].astype(F32)

        loop_rows(ROWS, 32, rows_done)


def pick_both(place, units_pair, heads_pair, heads, after=()):
    columns = units_pair[0].shape[1] + heads
    outs = [((2, ROWS, columns), BF)] * 4 + [((ROWS, 8 * LANES), F32)]
    return call(pick_both_kernel, outs, place, [*units_pair, *heads_pair], after=after)


def pick(place, total, came, heads, after=()):
    outs = [((2, ROWS, heads), BF)] * 4
    if heads < total.shape[1]:
        outs.append(((ROWS, 8 * LANES), F32))
    return call(pick_kernel, outs, place, [total, came], after=after)


def chosen_sum(place, total, outward):
    middle = (place[2] == 1) | (place[2] == 2)
    return jnp.where(middle, total, outward).astype(F32)


def final_call(body, place, ins, shape, layer, before=None, after=()):
    skip = len(after) + (before is not None)

    def run(place, *refs):
        *ins, out, token, found, sems = refs[skip:]
        body(place, ins, out.at[layer], found, sems)
        token[...] = jnp.zeros_like(token)

    return pl.pallas_call(
        run,
        name=body.__name__,
        out_shape=[jax.ShapeDtypeStruct((2,) + shape, F32), jax.ShapeDtypeStruct((8, LANES), F32)],
        in_specs=[pl.BlockSpec(memory_space=pltpu.SMEM)]
        + [pl.BlockSpec(memory_space=pltpu.HBM)] * (before is not None)
        + [pl.BlockSpec(memory_space=pl.ANY)] * len(after)
        + [pl.BlockSpec(memory_space=pltpu.VMEM)] * len(ins),
        out_specs=[pl.BlockSpec(memory_space=pltpu.HBM), pl.BlockSpec(memory_space=pltpu.VMEM)],
        scratch_shapes=[pltpu.VMEM(shape, F32), pltpu.SemaphoreType.DMA((8,))],
        input_output_aliases={} if before is None else {1: 0},
        compiler_params=pltpu.CompilerParams(vmem_limit_bytes=16 * 1024 * 1024),
        cost_estimate=SMALL,
    )(place, *([] if before is None else [before]), *after, *ins)


def final_rows_kernel(place, ins, out, found, sems):
    total, came = ins
    half, rows = total.shape[1], out.shape[0]
    step = rows // 4

    def move(i):
        put = pl.ds(pl.multiple_of(i * step, step), step)
        return pltpu.make_async_copy(found.at[put, :], out.at[put, :], sems.at[i])

    def one(i, carry):
        put = pl.ds(pl.multiple_of(i * step, step), step)
        for j in range(2):
            part = pl.ds(pl.multiple_of(i * step + j * rows, step), step)
            found[put, j * half : (j + 1) * half] = jnp.where(is_middle(place), total[part, :], came[part, :]).astype(F32)
        move(i).start()
        return carry

    lax.fori_loop(0, 4, one, 0)
    for i in range(4):
        move(i).wait()


def final_units_kernel(place, blocks, out, found, sems):
    units, moves = out.shape[1] // 8, []
    for i, (s, k) in enumerate(SLOTS):
        put = slice(i * units, (i + 1) * units)
        block = block_of(s, k, blocks)

        def rows_done(rows):
            found[rows, put] = block[rows, :units].astype(F32)

        loop_rows(ROWS, 32, rows_done)
        moves.append(pltpu.make_async_copy(found.at[:, put], out.at[:, slot_rows(place, s, k, units)], sems.at[i]))
        moves[-1].start()
    for move in moves:
        move.wait()


def final_heads_kernel(place, blocks, out, found, sems):
    third = out.shape[1] // 3
    for s, k in SLOTS:
        block = block_of(s, k, blocks)

        def rows_done(rows):
            part = block[rows, block.shape[1] - 3 * LANES :].astype(F32)
            for j in range(3):
                lanes = pl.ds(pl.multiple_of(j * third + slot_start(place, s, k, LANES), LANES), LANES)
                found[rows, lanes] = part[:, j * LANES : (j + 1) * LANES]

        loop_rows(ROWS, 32, rows_done)
    move = pltpu.make_async_copy(found, out, sems.at[0])
    move.start()
    move.wait()


def final_small_kernel(place, total, came, gain, shift, bias_fc1, bias_fc2):
    rows = slice(total.shape[0] - SMALL_ROWS, total.shape[0])
    found = jnp.where(is_middle(place), total[rows, :LANES], came[rows, :LANES]).astype(F32)
    gain[...] = found[0:2, :]
    shift[...] = found[2:4, :]
    bias_fc2[...] = found[4:6, :]
    for layer in range(2):
        for j in range(4):
            bias_fc1[layer : layer + 1, j * LANES : (j + 1) * LANES] = found[8 + 4 * layer + j : 9 + 4 * layer + j, :]


def local_plane(hidden_in, ln_gain, ln_bias, w_qkv, w_dense, w_fc1, b_fc1, w_fc2, b_fc2, output_grad):
    index = lax.axis_index("grp")
    place = jnp.stack([index // 2, index % 2, lax.axis_index("rep")]).astype(jnp.int32)
    span, width = hidden_in.shape[1:]
    seq = span * 8
    units = b_fc1.shape[1]
    own = 3 * LANES
    cosine, sine = rotary_tables(seq)
    hidden0 = hidden_in.reshape(span, width)
    grads1 = output_grad.reshape(span, width)

    wide, column, chunk_shape = ((seq, width), BF), ((seq, LANES), BF), ((seq + SMALL_ROWS, units), BF)
    blocks_n, blocks_n0 = ((4, ROWS, width), BF), ((4, ROWS + EXTRA, width), BF)
    blocks_f, blocks_q = ((2, ROWS, units), BF), ((2, ROWS, own), BF)
    mine, mine_low = ((span, width), F32), ((span, width), BF)
    sums_shape, part_shape = ((8, width), F32), ((seq, width), F32)
    head_scratch = [pltpu.VMEM((LANES, seq), BF), pltpu.VMEM((seq, LANES), F32), pltpu.VMEM((seq, LANES), F32)]
    back_scratch = [pltpu.VMEM((seq, own), BF), pltpu.VMEM((width, own), BF), pltpu.VMEM((seq, width), BF)]
    column_scratch = [pltpu.VMEM((seq, LANES), BF)] * 3
    units_scratch = [pltpu.VMEM((seq, units), BF), pltpu.VMEM((width, units), BF)]

    small = jnp.concatenate([ln_gain, ln_bias, b_fc2, jnp.zeros((EXTRA - 6, LANES), BF)])
    packed = call(
        pack_first_kernel,
        [((FIRST_ROWS, LANES), BF)] * 4,
        place,
        [hidden0, w_qkv, w_fc1, small],
        [pltpu.VMEM(a, BF) for a in (hidden0.shape, w_qkv.shape[1:], w_fc1.shape[1:])] + [pltpu.SemaphoreType.DMA((3,))],
        hbm=3,
        mib=60,
    )
    first = send_blocks(place, packed)
    packed = call(partial(pack_units_grads_kernel, 1), [((3 * ROWS, units), BF)] * 4, place, [w_fc1, grads1])
    keep, give = call(partial(pack_heads_kernel, 1), [((4, ROWS, own), BF)] * 2, place, [w_qkv], after=[packed[0]])
    pairs1 = call(pair_kernel, [blocks_q] * 4, place, [keep, swap(give, 1)])
    (others0,) = call(others_first_kernel, [((4, OTHERS_ROWS, LANES), BF)], place, first, after=[pairs1[0]])
    units1 = send_blocks(place, packed)
    first = [*first, swap(others0, 1)]

    normed0, xhat0, weight_q0, params, q0, k0, v0, att0, log0 = call(
        first_attend_kernel,
        [wide, wide, ((width, own), BF), ((EXTRA, width), F32), column, column, column, column, ((8, seq), F32)],
        place,
        [*first, cosine, sine],
        [pltpu.VMEM((LANES, seq), BF)],
    )
    weight_f0, act0, slope0, partial_sum = call(
        first_units_kernel,
        [((width, units), BF), ((seq, units), BF), ((seq, units), F32), wide],
        place,
        [normed0, *first, b_fc1, w_fc2, w_dense, att0],
    )
    (near1,) = call(near_units_kernel, [((4, ROWS, units), BF)], place, units1, after=[partial_sum])
    far1 = along(near1, INWARD + OUTWARD)
    keep, give = call(split_kernel, [blocks_n, blocks_n], place, [partial_sum], after=[near1])
    terms, sent = begin_scatter(place, keep, give)
    (others1,) = call(others_units_grads_kernel, [((4, 3 * ROWS, units), BF)], place, [*units1, far1], after=terms[2:])
    hidden1, normed1_own = call(next_hidden_kernel, [mine, mine_low], place, [*terms, hidden0, params], after=[others1])
    pieces = gather_pieces(normed1_own)

    normed1, weight_f1, act1, slope1, grad_branch1, chunk1 = call(
        second_units_kernel,
        [wide, ((width, units), BF), ((seq, units), BF), ((seq, units), F32), wide, chunk_shape],
        place,
        [*pieces, *units1, swap(others1, 1), far1, b_fc1],
        [pltpu.VMEM((units, width), BF)],
    )
    came1 = along(chunk1, INWARD)
    heads1 = send_blocks(place, pairs1)
    chunk2, sums1, part_normed = call(
        second_units_back_kernel,
        [chunk_shape, sums_shape, part_shape],
        place,
        [grad_branch1, w_fc2, slope1, normed1, weight_f1],
        units_scratch,
    )
    att1, chunk3, keep, give = call(
        second_attend_kernel,
        [column, chunk_shape, blocks_n, blocks_n],
        place,
        [normed1, *heads1, cosine, sine, grad_branch1, w_dense, part_normed],
        [pltpu.VMEM((width, own), BF), *column_scratch, pltpu.VMEM((LANES, seq), BF), *head_scratch, *back_scratch],
    )
    terms, _ = begin_scatter(place, keep, give)
    (half1,) = tick(place, (chunk1, came1), None, None, after=[give])
    cross1, came2 = along(half1, ACROSS), along(chunk2, INWARD)
    grads0, grads0_low, ln_sums1 = call(
        second_norm_back_kernel, [mine, mine_low, sums_shape], place, [*terms, hidden1, params, grads1], after=[half1]
    )

    keep_h, give_h = call(
        last_hidden_kernel,
        [blocks_n, blocks_n],
        place,
        [act1, att1, w_fc2, w_dense],
        [pltpu.VMEM((seq, width), BF)],
        after=[half1],
    )
    pieces = gather_pieces(grads0_low)
    half2, total1 = tick(place, (chunk2, came2), (half1, cross1), chunk3, after=[grads0_low, give_h])
    cross2, came3 = along(half2, ACROSS), along(total1, INWARD + OUTWARD)
    grad_branch0, chunk6, chunk4, sums0, part_normed = call(
        first_units_back_kernel,
        [wide, chunk_shape, chunk_shape, sums_shape, part_shape],
        place,
        [*pieces, act0, w_fc2, slope0, normed0, weight_f0],
        units_scratch,
        after=[half2],
    )
    half3, total2 = tick(place, (chunk3, came3), (half2, cross2), chunk4)
    cross3, came4 = along(half3, ACROSS), along(total2, INWARD + OUTWARD)
    chunk5, keep, give = call(
        first_attend_back_kernel,
        [chunk_shape, blocks_n0, blocks_n0],
        place,
        [grad_branch0, w_dense, att0, q0, k0, v0, log0, cosine, sine, normed0, xhat0, weight_q0, part_normed, ln_sums1],
        [*head_scratch, *back_scratch, pltpu.VMEM((8, width), F32)],
        after=[half3],
    )
    token = ((8, LANES), F32)
    out_fc2, done = final_call(final_rows_kernel, place, [total1, came3], (units, width), 1, after=[give])
    half4, total3 = tick(place, (chunk4, came4), (half3, cross3), chunk5, after=[done])
    cross4, came5 = along(half4, ACROSS), along(total3, INWARD + OUTWARD)
    terms, _ = begin_scatter(place, keep, give, after=[half4])
    input_grad, small_sums = call(
        first_norm_back_kernel,
        [mine, ((SMALL_ROWS, LANES), F32)],
        place,
        [*terms, hidden0, params, grads0, sums0, sums1],
    )
    (chunk6,) = call(add_small_kernel, [chunk_shape], place, [chunk6, small_sums])
    half5, total4 = tick(place, (chunk5, came5), (half4, cross4), chunk6)
    cross5, came6 = along(half5, ACROSS), along(total4, INWARD + OUTWARD)
    *picked1, dense1 = pick_both(place, (total2, came4), (total3, came5), own, after=[half5])
    blocks1 = swap_others(place, send_blocks(place, picked1))
    half6, total5 = tick(place, (chunk6, came6), (half5, cross5), None, after=[blocks1[1]])
    cross6, came7 = along(half6, ACROSS), along(total5, OUTWARD)
    picked4 = pick(place, total4, came6, units, after=[half6])
    out_fc1, done1 = final_call(final_units_kernel, place, blocks1, (ROWS, w_fc1.shape[2]), 1, after=[picked4[0]])
    out_qkv, done3 = final_call(final_heads_kernel, place, blocks1, (ROWS, w_qkv.shape[2]), 1, after=[done1])
    blocks4 = swap_others(place, send_blocks(place, picked4), after=[done3])
    (total6,) = tick(place, None, (half6, cross6), None, after=[blocks4[1]])
    came8 = along(total6, OUTWARD)
    terms, _ = begin_scatter(place, keep_h, give_h, after=[total6])
    out_fc1, done4 = final_call(final_units_kernel, place, blocks4, (ROWS, w_fc1.shape[2]), 0, out_fc1, after=[total6])
    *picked5, dense0 = pick(place, total5, came7, own, after=[done4])
    hidden_out, done_h = call(last_sum_kernel, [mine, token], place, [*terms, hidden1, params], after=[picked5[0]])
    blocks5 = swap_others(place, send_blocks(place, picked5), after=[done_h])
    out_qkv, done5 = final_call(final_heads_kernel, place, blocks5, (ROWS, w_qkv.shape[2]), 0, out_qkv)
    out_fc2, _ = final_call(final_rows_kernel, place, [total6, came8], (units, width), 0, out_fc2, after=[done5])
    vector = ((2, LANES), F32)
    out_gain, out_shift, out_b_fc1, out_b_fc2 = call(
        final_small_kernel, [vector, vector, ((2, units), F32), vector], place, [total6, came8]
    )
    out_dense = jnp.stack([dense0, dense1])
    return (
        hidden_out[None],
        input_grad[None],
        out_gain,
        out_shift,
        out_qkv,
        out_dense,
        out_fc1,
        out_b_fc1,
        out_fc2,
        out_b_fc2,
    )


def local(hidden_in, ln_gain, ln_bias, w_qkv, w_dense, w_fc1, b_fc1, w_fc2, b_fc2, output_grad):
    arguments = (hidden_in, ln_gain, ln_bias, w_qkv, w_dense, w_fc1, b_fc1, w_fc2, b_fc2, output_grad)
    plane = lax.axis_size("grp") == 8 and lax.axis_size("rep") == 4
    plane = plane and hidden_in.shape[:2] == (1, ROWS) and w_qkv.shape == (2, LANES, 3 * 8 * LANES)
    return (local_plane if plane else local_any)(*arguments)


def solution(mesh):
    in_specs = (
        P("rep", "grp", None),
        P(None, "grp"),
        P(None, "grp"),
        P(None, "grp", None),
        P(None, "grp", None),
        P(None, "grp", None),
        P(None, "grp"),
        P(None, "grp", None),
        P(None, "grp"),
        P("rep", "grp", None),
    )
    out_specs = (
        P("rep", "grp", None),
        P("rep", "grp", None),
        P(None, "grp"),
        P(None, "grp"),
        P(None, "grp", None),
        P(None, "grp", None),
        P(None, "grp", None),
        P(None, "grp"),
        P(None, "grp", None),
        P(None, "grp"),
    )
    return jax.shard_map(local, mesh=mesh, in_specs=in_specs, out_specs=out_specs, check_vma=False)
```

```python
from functools import partial

import jax
import jax.numpy as jnp
import numpy as np
from jax import lax
from jax.experimental import pallas as pl
from jax.experimental.pallas import tpu as pltpu
from jax.sharding import PartitionSpec as P

HEAD_DIM = 64
ROT = 32
LANES = 128

EPSILON = 1e-05
SCORE_SCALE = 0.125
NEGATIVE = -1000000000.0
BF = jnp.bfloat16
F32 = jnp.float32


def dot(left, right):
    return jnp.dot(left, right, preferred_element_type=F32)


def dot_general(left, right, contract):
    return lax.dot_general(left, right, ((contract[:1], contract[1:]), ((), ())), preferred_element_type=F32)


def outer_sum(left, right):
    return dot_general(left, right, (0, 0))


def times_transposed(left, right):
    return dot_general(left, right, (1, 1))


def head_mask(head):
    lane = lax.broadcasted_iota(jnp.int32, (1, LANES), 1)
    return (lane >= head * HEAD_DIM) & (lane < (head + 1) * HEAD_DIM)


def turn(part, cosine, sine, sign):
    even = lax.broadcasted_iota(jnp.int32, part.shape, 1) % 2 == 0
    partner = jnp.where(even, pltpu.roll(part, LANES - 1, 1), pltpu.roll(part, 1, 1))
    return part * cosine + partner * (sine * sign)


def mask_diagonal(scores, block):
    keys, queries = scores.shape
    key_place = lax.broadcasted_iota(jnp.int32, (block, queries), 0)
    query_place = lax.broadcasted_iota(jnp.int32, (block, queries), 1)
    last = jnp.where(key_place <= query_place, scores[keys - block :], NEGATIVE)
    if keys == block:
        return last
    return jnp.concatenate([scores[: keys - block], last], axis=0)


def attend_kernel(heads, block, mix_q, mix_k, mix_v, cosine, sine, q_out, k_out, v_out, att_out, log_out):
    seq = mix_q.shape[0]
    q_out[...] = turn(mix_q[...], cosine[...], sine[...], 1.0).astype(BF)
    k_out[...] = turn(mix_k[...], cosine[...], sine[...], 1.0).astype(BF)
    v_out[...] = mix_v[...].astype(BF)
    values_down = mix_v[...].T.astype(BF)
    for start in range(0, seq, block):
        stop = start + block
        queries = q_out[start:stop, :] * SCORE_SCALE
        keys = k_out[:stop, :]
        total = jnp.zeros((LANES, block), F32)
        for head in range(heads):
            chosen = jnp.where(head_mask(head), queries, 0.0).astype(BF)
            scores = mask_diagonal(dot_general(keys, chosen, (1, 1)), block)
            row_max = jnp.max(scores, axis=0, keepdims=True)
            exponent = jnp.exp(scores - row_max)
            row_total = jnp.sum(exponent, axis=0, keepdims=True)
            probabilities = (exponent * (1.0 / row_total)).astype(BF)
            log_out[head : head + 1, start:stop] = row_max + jnp.log(row_total)
            found = dot(values_down[:, :stop], probabilities)
            down = lax.broadcasted_iota(jnp.int32, (LANES, 1), 0)
            own = (down >= head * HEAD_DIM) & (down < (head + 1) * HEAD_DIM)
            total = total + jnp.where(own, found, 0.0)
        att_out[start:stop, :] = total.T.astype(BF)


def attend_back_kernel(heads, block, q_in, k_in, v_in, grad_att, log_in, cosine, sine, q_out, k_out, v_out, k_sum, v_sum):
    seq = q_in.shape[0]
    k_sum[...] = jnp.zeros_like(k_sum)
    v_sum[...] = jnp.zeros_like(v_sum)
    keys_down = (k_in[...].astype(F32) * SCORE_SCALE).T.astype(BF)
    for start in range(0, seq, block):
        stop = start + block
        queries = q_in[start:stop, :] * SCORE_SCALE
        grads = grad_att[start:stop, :]
        grad_queries = jnp.zeros((LANES, block), F32)
        for head in range(heads):
            chosen = jnp.where(head_mask(head), queries, 0.0).astype(BF)
            chosen_grads = jnp.where(head_mask(head), grads, 0.0).astype(BF)
            scores = mask_diagonal(dot_general(k_in[:stop, :], chosen, (1, 1)), block)
            probabilities = jnp.exp(scores - log_in[head : head + 1, start:stop])
            grad_probs = dot_general(v_in[:stop, :], chosen_grads, (1, 1))
            row_inner = jnp.sum(grad_probs * probabilities, axis=0, keepdims=True)
            grad_scores = (probabilities * (grad_probs - row_inner)).astype(BF)
            k_sum[:stop, :] += dot(grad_scores, chosen)
            v_sum[:stop, :] += dot(probabilities.astype(BF), chosen_grads)
            down = lax.broadcasted_iota(jnp.int32, (LANES, 1), 0)
            own = (down >= head * HEAD_DIM) & (down < (head + 1) * HEAD_DIM)
            grad_queries = grad_queries + jnp.where(own, dot(keys_down[:, :stop], grad_scores), 0.0)
        q_out[start:stop, :] = turn(
            grad_queries.T, cosine[start:stop, :], sine[start:stop, :], -1.0
        ).astype(BF)
    k_out[...] = turn(k_sum[...], cosine[...], sine[...], -1.0).astype(BF)
    v_out[...] = v_sum[...].astype(BF)


VMEM_LIMIT = 48 * 1024 * 1024


def attend(mix_q, mix_k, mix_v, heads, cosine, sine):
    seq = mix_q.shape[0]
    out = jax.ShapeDtypeStruct((seq, LANES), BF)
    return pl.pallas_call(
        partial(attend_kernel, heads, min(256, seq)),
        out_shape=(out, out, out, out, jax.ShapeDtypeStruct((heads, seq), F32)),
        compiler_params=pltpu.CompilerParams(vmem_limit_bytes=VMEM_LIMIT),
    )(mix_q, mix_k, mix_v, cosine, sine)


def attend_back(queries, keys, values, grad_att, log_total, heads, cosine, sine):
    seq = queries.shape[0]
    out = jax.ShapeDtypeStruct((seq, LANES), BF)
    return pl.pallas_call(
        partial(attend_back_kernel, heads, min(256, seq)),
        out_shape=(out, out, out),
        scratch_shapes=[pltpu.VMEM((seq, LANES), F32), pltpu.VMEM((seq, LANES), F32)],
        compiler_params=pltpu.CompilerParams(vmem_limit_bytes=VMEM_LIMIT),
    )(queries, keys, values, grad_att, log_total, cosine, sine)


def rotary_tables(seq):
    frequency = (1.0 / 10000.0 ** (np.arange(ROT // 2, dtype=np.float32) * 2.0 / ROT)).astype(np.float32)
    angles = np.arange(seq, dtype=np.float32)[:, None] * frequency[None, :]
    cosine, sine = np.cos(angles.astype(np.float64)), np.sin(angles.astype(np.float64))
    cosine = np.repeat(cosine, 2, axis=1)
    sine = np.repeat(sine, 2, axis=1) * np.tile([-1.0, 1.0], ROT // 2)
    rest = HEAD_DIM - ROT
    cosine = np.concatenate([cosine, np.ones((seq, rest))], axis=1)
    sine = np.concatenate([sine, np.zeros((seq, rest))], axis=1)
    repeats = (1, LANES // HEAD_DIM)
    return np.tile(cosine, repeats).astype(np.float32), np.tile(sine, repeats).astype(np.float32)


def swap(value, bits):
    return lax.ppermute(value, "grp", [(i, i ^ bits) for i in range(8)])


def add_low(left, right):
    return (left.astype(F32) + right.astype(F32)).astype(BF)


def by_chip(parts, chip):
    x, y = chip % 2 == 1, chip // 2 == 1
    near = jnp.where(x, jnp.stack([parts[1], parts[0]]), jnp.stack([parts[0], parts[1]]))
    far = jnp.where(x, jnp.stack([parts[3], parts[2]]), jnp.stack([parts[2], parts[3]]))
    return jnp.where(y, jnp.concatenate([far, near]), jnp.concatenate([near, far]))


def gather_rows(part):
    size = lax.axis_size("grp")
    if size != 8:
        return lax.all_gather(part, "grp", axis=0, tiled=True)
    rows, width = part.shape
    half = rows // 2
    index = lax.axis_index("grp")
    along_x, along_y = swap(part, 2), swap(part, 4)
    corner = jnp.concatenate([swap(along_y[:half], 2), swap(along_x[half:], 4)])
    mine = by_chip([part, along_x, along_y, corner], index // 2)
    other = swap(mine, 1)
    odd = index % 2 == 1
    both = jnp.stack([jnp.where(odd, other, mine), jnp.where(odd, mine, other)], axis=1)
    return both.reshape(8 * rows, width)


def scatter_sum(whole):
    size = lax.axis_size("grp")
    if size != 8:
        return lax.psum_scatter(whole, "grp", scatter_dimension=0, tiled=True).astype(F32)
    rows, width = whole.shape[0] // 8, whole.shape[1]
    half = rows // 2
    index = lax.axis_index("grp")
    chip, core = index // 2, index % 2
    blocks = whole.reshape(4, 2, rows, width)
    keep = lax.dynamic_index_in_dim(blocks, core, 1, False)
    give = lax.dynamic_index_in_dim(blocks, 1 - core, 1, False)
    summed = add_low(keep, swap(give, 1))
    own, for_x, for_y, corner = [lax.dynamic_index_in_dim(summed, chip ^ s, 0, False) for s in range(4)]
    by_x, by_y = swap(corner[:half], 2), swap(corner[half:], 4)
    for_y = jnp.concatenate([add_low(for_y[:half], by_x), for_y[half:]])
    for_x = jnp.concatenate([for_x[:half], add_low(for_x[half:], by_y)])
    return own.astype(F32) + swap(for_y, 4).astype(F32) + swap(for_x, 2).astype(F32)


def exchange(blocks):
    size = lax.axis_size("grp")
    if size != 8:
        return lax.all_to_all(blocks, "grp", 0, 0)
    index = lax.axis_index("grp")
    chip, core = index // 2, index % 2
    pairs = blocks.reshape((4, 2) + blocks.shape[1:])
    keep = lax.dynamic_index_in_dim(pairs, core, 1, False)
    give = lax.dynamic_index_in_dim(pairs, 1 - core, 1, False)
    came = swap(give, 1)
    odd = core == 1
    both = jnp.stack([jnp.where(odd, came, keep), jnp.where(odd, keep, came)], axis=1)
    parts = [lax.dynamic_index_in_dim(both, chip ^ s, 0, False) for s in range(4)]
    parts = [parts[0]] + [swap(parts[s], 2 * s) for s in (1, 2, 3)]
    return by_chip(parts, chip).reshape(blocks.shape)


def rep_sum(part):
    if lax.axis_size("rep") != 4:
        return lax.psum(part, "rep").astype(F32)
    place = lax.axis_index("rep")
    inward = lax.ppermute(part, "rep", [(0, 1), (3, 2)])
    half_sum = add_low(part, inward)
    across = lax.ppermute(half_sum, "rep", [(1, 2), (2, 1)])
    total = add_low(half_sum, across)
    outward = lax.ppermute(total, "rep", [(1, 0), (2, 3)])
    return jnp.where((place == 1) | (place == 2), total, outward).astype(F32)


def columns_of(w_qkv, w_fc1, group):
    rows, qkv = w_qkv.shape
    heads = w_qkv.reshape(rows, 3, group, qkv // 3 // group).transpose(2, 0, 1, 3).reshape(group, rows, -1)
    units = w_fc1.reshape(rows, group, -1).transpose(1, 0, 2)
    found = exchange(jnp.concatenate([heads, units], axis=2))
    found = found.reshape(group * rows, -1)
    return found[:, : qkv // group], found[:, qkv // group :]


def rows_of(grad_qkv, grad_fc1, group):
    rows = grad_qkv.shape[0] // group
    both = jnp.concatenate([grad_qkv, grad_fc1], axis=1).reshape(group, rows, -1)
    found = exchange(both)
    qkv = grad_qkv.shape[1]
    heads = found[:, :, :qkv].reshape(group, rows, 3, qkv // 3).transpose(1, 2, 0, 3).reshape(rows, -1)
    units = found[:, :, qkv:].transpose(1, 0, 2).reshape(rows, -1)
    return heads, units


def standardize(hidden):
    centered = hidden - jnp.mean(hidden, axis=-1, keepdims=True)
    scale = lax.rsqrt(jnp.mean(centered * centered, axis=-1, keepdims=True) + EPSILON)
    return centered * scale, scale


def widen(part):
    return jnp.pad(part, ((0, 0), (0, LANES - part.shape[1])))


def forward_layer(normed, weights, heads, tables):
    qkv_cols, fc1_cols, b_fc1, w_dense, w_fc2 = weights
    mixed = dot(normed, qkv_cols)
    own = heads * HEAD_DIM
    queries, keys, values, attended, log_total = attend(
        *(widen(mixed[:, i * own : (i + 1) * own]) for i in range(3)), heads, *tables
    )
    pre_act = dot(normed, fc1_cols) + b_fc1.astype(F32)
    activation = jax.nn.gelu(pre_act, approximate=True).astype(BF)
    partial_sum = (dot(attended[:, :own], w_dense) + dot(activation, w_fc2)).astype(BF)
    stored = (normed, queries, keys, values, attended, log_total, pre_act, activation)
    return partial_sum, stored


def backward_layer(grad_branch, weights, stored, heads, tables):
    qkv_cols, fc1_cols, b_fc1, w_dense, w_fc2 = weights
    normed, queries, keys, values, attended, log_total, pre_act, activation = stored
    own = heads * HEAD_DIM
    grad_w_fc2 = outer_sum(activation, grad_branch).astype(BF)
    grad_w_dense = outer_sum(attended[:, :own], grad_branch).astype(BF)
    _, gelu_back = jax.vjp(partial(jax.nn.gelu, approximate=True), pre_act)
    grad_pre = gelu_back(times_transposed(grad_branch, w_fc2))[0].astype(BF)
    grad_attended = widen(times_transposed(grad_branch, w_dense).astype(BF))
    grad_mixed = attend_back(queries, keys, values, grad_attended, log_total, heads, *tables)
    grad_mixed = jnp.concatenate([part[:, :own] for part in grad_mixed], axis=1)
    grad_fc1 = outer_sum(normed, grad_pre).astype(BF)
    grad_b_fc1 = jnp.sum(grad_pre.astype(F32), axis=0)
    grad_qkv = outer_sum(normed, grad_mixed).astype(BF)
    grad_normed = (times_transposed(grad_pre, fc1_cols) + times_transposed(grad_mixed, qkv_cols)).astype(BF)
    return grad_normed, (grad_w_fc2, grad_w_dense, grad_fc1, grad_qkv, grad_b_fc1)


def local_any(hidden_in, ln_gain, ln_bias, w_qkv, w_dense, w_fc1, b_fc1, w_fc2, b_fc2, output_grad):
    group = lax.axis_size("grp")
    index = lax.axis_index("grp")
    layers = w_qkv.shape[0]
    span, width = hidden_in.shape[1:]
    seq = span * group
    heads = width // HEAD_DIM // group
    tables = rotary_tables(seq)
    small = jnp.concatenate([ln_gain, ln_bias, b_fc2])
    small = lax.all_gather(small, "grp", axis=1, tiled=True).astype(F32)
    gains, shifts, b_fc2_all = small[:layers], small[layers : 2 * layers], small[2 * layers :]
    hidden = hidden_in.reshape(span, width).astype(F32)
    hidden_all = gather_rows(hidden_in.reshape(span, width))
    weights = []
    for layer in range(layers):
        qkv_cols, fc1_cols = columns_of(w_qkv[layer], w_fc1[layer], group)
        weights.append((qkv_cols, fc1_cols, b_fc1[layer], w_dense[layer], w_fc2[layer]))

    inputs, stored_layers = [], []
    for layer in range(layers):
        inputs.append(hidden)
        if layer == 0:
            normed = (standardize(hidden_all.astype(F32))[0] * gains[0] + shifts[0]).astype(BF)
        else:
            normed = gather_rows((standardize(hidden)[0] * gains[layer] + shifts[layer]).astype(BF))
        partial_sum, stored = forward_layer(normed, weights[layer], heads, tables)
        stored_layers.append(stored)
        hidden = hidden + scatter_sum(partial_sum) + b_fc2_all[layer]

    grad_hidden = output_grad.reshape(span, width)
    small_grads, large_grads = [None] * layers, [None] * layers
    for layer in reversed(range(layers)):
        grad_low = grad_hidden.astype(BF)
        grad_branch = gather_rows(grad_low)
        grad_normed, found = backward_layer(grad_branch, weights[layer], stored_layers[layer], heads, tables)
        grad_w_fc2, grad_w_dense, grad_fc1, grad_qkv, grad_b_fc1 = found
        grad_qkv, grad_fc1 = rows_of(grad_qkv, grad_fc1, group)
        large_grads[layer] = tuple(rep_sum(part) for part in (grad_w_fc2, grad_w_dense, grad_fc1, grad_qkv))
        grad_normed = scatter_sum(grad_normed)
        xhat, scale = standardize(inputs[layer])
        inner = grad_normed * gains[layer]
        mean_inner = jnp.mean(inner, axis=-1, keepdims=True)
        mean_along = jnp.mean(inner * xhat, axis=-1, keepdims=True)
        small_grads[layer] = jnp.concatenate(
            [
                jnp.sum(grad_normed * xhat, axis=0),
                jnp.sum(grad_normed, axis=0),
                jnp.sum(grad_low.astype(F32), axis=0),
                lax.dynamic_update_slice(
                    jnp.zeros((group * grad_b_fc1.shape[0],), F32), grad_b_fc1, (index * grad_b_fc1.shape[0],)
                ),
            ]
        )
        grad_hidden = grad_hidden + (inner - mean_inner - xhat * mean_along) * scale

    summed = lax.psum(jnp.stack(small_grads), ("rep", "grp"))
    own = width // group
    units = b_fc1.shape[1]

    def pick(start, count):
        return lax.dynamic_slice_in_dim(summed, start + index * count, count, 1)

    stacked = [jnp.stack([large_grads[layer][member] for layer in range(layers)]) for member in range(4)]
    return (
        hidden[None],
        grad_hidden[None],
        pick(0, own),
        pick(width, own),
        stacked[3],
        stacked[1],
        stacked[2],
        pick(3 * width, units),
        stacked[0],
        pick(2 * width, own),
    )


SLOTS = [(s, k) for s in range(4) for k in range(2)]
ROWS = 128
EXTRA = 16


def slot_start(place, s, k, size):
    return pl.multiple_of(((place[0] ^ s) * 2 + (place[1] ^ k)) * size, size)


def slot_rows(place, s, k, size=ROWS):
    return pl.ds(slot_start(place, s, k, size), size)


SMALL = pl.CostEstimate(flops=0, bytes_accessed=0, transcendentals=0)


def call(body, outs, place, ins, scratch=(), after=(), hbm=0, mib=16):
    def run(place, *refs):
        body(place, *refs[len(after) :])

    return pl.pallas_call(
        run,
        name=getattr(body, "func", body).__name__,
        out_shape=[jax.ShapeDtypeStruct(*out) for out in outs],
        in_specs=[pl.BlockSpec(memory_space=pltpu.SMEM)]
        + [pl.BlockSpec(memory_space=pl.ANY)] * len(after)
        + [pl.BlockSpec(memory_space=pltpu.HBM)] * hbm
        + [pl.BlockSpec(memory_space=pltpu.VMEM)] * (len(ins) - hbm),
        out_specs=[pl.BlockSpec(memory_space=pltpu.VMEM)] * len(outs),
        scratch_shapes=list(scratch),
        compiler_params=pltpu.CompilerParams(vmem_limit_bytes=mib * 1024 * 1024),
        cost_estimate=SMALL,
    )(place, *after, *ins)


def gather_pieces(part):
    mine = [part, swap(part, 2), swap(part, 4), swap(part, 6)]
    other = [swap(piece, 1) for piece in mine]
    return [piece for pair in zip(mine, other) for piece in pair]


def put_columns(out, start, value):
    rows = value.shape[0]
    for b in range(value.shape[1] // LANES):
        out[start + b * rows : start + (b + 1) * rows, :] = value[:, b * LANES : (b + 1) * LANES]


def heads_of(place, w_qkv, layer, s, k, j):
    start = j * (w_qkv.shape[2] // 3) + slot_start(place, s, k, LANES)
    return w_qkv[layer, :, pl.ds(pl.multiple_of(start, LANES), LANES)]


HALF = ROWS // 2
HEADS_ROWS, HALF_ROWS = 3 * ROWS, 4 * HALF
FIRST_MINE = 8 * ROWS
FIRST_OTHERS = FIRST_MINE + HEADS_ROWS + HALF_ROWS
FIRST_SMALL = FIRST_OTHERS + HEADS_ROWS + HALF_ROWS
FIRST_ROWS = FIRST_SMALL + EXTRA
OTHERS_MINE = 8 * ROWS
OTHERS_SMALL = OTHERS_MINE + HEADS_ROWS + HALF_ROWS
OTHERS_ROWS = OTHERS_SMALL + EXTRA


def half_start(place, other):
    parity = place[2] & 1
    return pl.multiple_of((1 - parity if other else parity) * HALF, HALF)


def pack_first_kernel(place, hidden_from, qkv_from, fc1_from, small, o0, o1, o2, o3, hidden, w_qkv, w_fc1, sems):
    outs = (o0, o1, o2, o3)
    moves = (
        pltpu.make_async_copy(hidden_from, hidden, sems.at[0]),
        pltpu.make_async_copy(qkv_from.at[0], w_qkv, sems.at[1]),
        pltpu.make_async_copy(fc1_from.at[0, pl.ds(half_start(place, False), HALF), :], w_fc1, sems.at[2]),
    )
    for move in moves:
        move.start()
    moves[0].wait()
    for out in outs:
        put_columns(out, 0, hidden[...])
        out[FIRST_SMALL:, :] = small[...]
    moves[1].wait()
    third = w_qkv.shape[1] // 3
    for s, k in SLOTS:
        row = (FIRST_MINE, FIRST_OTHERS)[k]
        for j in range(3):
            lanes = pl.ds(pl.multiple_of(j * third + slot_start(place, s, k, LANES), LANES), LANES)
            outs[s][row + j * ROWS : row + (j + 1) * ROWS, :] = w_qkv[:, lanes]
    moves[2].wait()
    for s, k in SLOTS:
        row = (FIRST_MINE, FIRST_OTHERS)[k] + HEADS_ROWS
        put_columns(outs[s], row, w_fc1[:, pl.ds(slot_start(place, s, k, 4 * LANES), 4 * LANES)])


def others_first_kernel(place, b0, b1, b2, b3, out):
    for s, block in enumerate((b0, b1, b2, b3)):
        out[s, :OTHERS_MINE, :] = block[:FIRST_MINE, :]
        out[s, OTHERS_MINE:OTHERS_SMALL, :] = block[FIRST_OTHERS:FIRST_SMALL, :]
        out[s, OTHERS_SMALL:, :] = block[FIRST_SMALL:, :]


def near_first_kernel(place, b0, b1, b2, b3, b4, out):
    for i, (s, k) in enumerate(SLOTS):
        block, mine_at, _ = first_block(s, k, (b0, b1, b2, b3, b4))
        out[i] = block[mine_at + HEADS_ROWS : mine_at + HEADS_ROWS + HALF_ROWS, :]


def first_block(s, k, blocks):
    if k:
        return blocks[4].at[s], OTHERS_MINE, OTHERS_SMALL
    return blocks[s], FIRST_MINE, FIRST_SMALL


def pack_heads_kernel(layer, place, w_qkv, keep, give):
    for s, k in SLOTS:
        for j in range(3):
            (keep, give)[k][s, :, j * LANES : (j + 1) * LANES] = heads_of(place, w_qkv, layer, s, k, j)


def pair_kernel(place, keep, came, *outs):
    for s, out in enumerate(outs):
        out[0], out[1] = keep[s], came[s]


def pack_units_kernel(layer, place, w_fc1, *outs):
    units = outs[0].shape[2]
    for s, k in SLOTS:
        outs[s][k] = w_fc1[layer, :, pl.ds(slot_start(place, s, k, units), units)]


def pack_units_grads_kernel(layer, place, w_fc1, grads, *outs):
    units = outs[0].shape[1]
    low = grads[...].astype(BF)
    for s in range(4):
        for k in range(2):
            lanes = pl.ds(slot_start(place, s, k, units), units)
            outs[s][k * HALF : (k + 1) * HALF, :] = w_fc1[layer, pl.ds(half_start(place, False), HALF), lanes]
            outs[s][(1 + k) * ROWS : (2 + k) * ROWS, :] = low[:, k * units : (k + 1) * units]


def near_units_kernel(place, b0, b1, b2, b3, out):
    for s, block in enumerate((b0, b1, b2, b3)):
        out[s] = block[:ROWS, :]


def others_units_grads_kernel(place, b0, b1, b2, b3, far, out):
    for s, block in enumerate((b0, b1, b2, b3)):
        out[s, :HALF, :] = block[HALF:ROWS, :]
        out[s, HALF:ROWS, :] = far[s, HALF:, :]
        out[s, ROWS:, :] = block[ROWS:, :]


def send_blocks(place, packed):
    return [packed[0]] + [swap(packed[s], 2 * s) for s in (1, 2, 3)]


def others_kernel(place, b0, b1, b2, b3, out):
    for s, block in enumerate((b0, b1, b2, b3)):
        out[s] = block[1]


def swap_others(place, blocks, after=()):
    (other,) = call(others_kernel, [((4,) + blocks[0].shape[1:], BF)], place, blocks, after=after)
    return [*blocks, swap(other, 1)]


def block_of(s, k, blocks):
    return blocks[4].at[s] if k else blocks[s].at[0]


def project_heads(normed, weight, cosine, sine, q_out, k_out, v_out, values_down):
    step = 256
    for start in range(0, normed.shape[0], step):
        rows = slice(start, start + step)
        mixed = dot(normed[rows, :], weight[...])
        q_out[rows, :] = turn(mixed[:, :LANES], cosine[rows, :], sine[rows, :], 1.0).astype(BF)
        k_out[rows, :] = turn(mixed[:, LANES : 2 * LANES], cosine[rows, :], sine[rows, :], 1.0).astype(BF)
        values = mixed[:, 2 * LANES :]
        v_out[rows, :] = values.astype(BF)
        values_down[:, rows] = values.T.astype(BF)


def own_head(head):
    down = lax.broadcasted_iota(jnp.int32, (LANES, 1), 0)
    return (down >= head * HEAD_DIM) & (down < (head + 1) * HEAD_DIM)


def softmax_block(keys, chosen, block):
    scores = mask_diagonal(dot_general(keys, chosen, (1, 1)), block)
    row_max = jnp.max(scores, axis=0, keepdims=True)
    exponent = jnp.exp(scores - row_max)
    row_total = jnp.sum(exponent, axis=0, keepdims=True)
    return exponent * (1.0 / row_total), row_max + jnp.log(row_total)


BLOCK = 256
HEADS_HERE = LANES // HEAD_DIM


def first_attend_kernel(place, b0, b1, b2, b3, b4, cosine, sine, normed, xhat_out, weight, params, q_out, k_out, v_out, att_out, log_out, values_down):
    for s, k in SLOTS:
        rows = slot_rows(place, s, k)
        block, mine_at, small_at = first_block(s, k, (b0, b1, b2, b3, b4))
        for j in range(3):
            weight[rows, j * LANES : (j + 1) * LANES] = block[mine_at + j * ROWS : mine_at + (j + 1) * ROWS, :]
        params[:, rows] = block[small_at:, :].astype(F32)
        for b in range(8):
            normed[rows, b * LANES : (b + 1) * LANES] = block[b * ROWS : (b + 1) * ROWS, :]
    gain, shift = params[0:1, :], params[2:3, :]

    def norm_rows(rows):
        xhat = standardize(normed[rows, :].astype(F32))[0]
        xhat_out[rows, :] = xhat.astype(BF)
        normed[rows, :] = (xhat * gain + shift).astype(BF)

    loop_rows(normed.shape[0], 4 * ROWS, norm_rows)
    project_heads(normed, weight, cosine, sine, q_out, k_out, v_out, values_down)
    for start in range(0, normed.shape[0], BLOCK):
        stop = start + BLOCK
        queries = q_out[start:stop, :] * SCORE_SCALE
        total = jnp.zeros((LANES, BLOCK), F32)
        for head in range(HEADS_HERE):
            chosen = jnp.where(head_mask(head), queries, 0.0).astype(BF)
            probabilities, log_total = softmax_block(k_out[:stop, :], chosen, BLOCK)
            log_out[head : head + 1, start:stop] = log_total
            found = dot(values_down[:, :stop], probabilities.astype(BF))
            total = total + jnp.where(own_head(head), found, 0.0)
        att_out[start:stop, :] = total.T.astype(BF)


GELU_A = 0.7978845608028654
GELU_B = 0.044715


def gelu(pre):
    return pre * (0.5 + 0.5 * jnp.tanh(GELU_A * pre * (1.0 + GELU_B * pre * pre)))


def gelu_slope(pre):
    square = pre * pre
    wave = jnp.tanh(GELU_A * pre * (1.0 + GELU_B * square))
    return 0.5 * (1.0 + wave) + 0.5 * pre * (1.0 - wave * wave) * (GELU_A * (1.0 + 3.0 * GELU_B * square))


def loop_rows(count, step, body):
    def one(i, carry):
        body(pl.ds(pl.multiple_of(i * step, step), step))
        return carry

    lax.fori_loop(0, count // step, one, 0)


def put_slots(place, rows_of_block, keep, give):
    for s in range(4):
        keep[s] = rows_of_block(slot_rows(place, s, 0))
        give[s] = rows_of_block(slot_rows(place, s, 1))


def put_pairs(place, rows_of_block, outs):
    for s, k in SLOTS:
        outs[s][k] = rows_of_block(slot_rows(place, s, k))


def first_units_kernel(place, normed, near, far, bias, w_fc2, w_dense, attended, weight, act, slope, whole):
    for s, k in SLOTS:
        for part, other_plane in ((near.at[SLOTS.index((s, k))], False), (far.at[SLOTS.index((s, k))], True)):
            start = slot_start(place, s, k, ROWS) + half_start(place, other_plane)
            for b in range(4):
                rows = pl.ds(pl.multiple_of(start, HALF), HALF)
                weight[rows, b * LANES : (b + 1) * LANES] = part[b * HALF : (b + 1) * HALF, :]
    shift = bias[0:1, :].astype(F32)

    def rows_done(rows):
        found = dot(normed[rows, :], weight[...]) + shift
        slope[rows, :] = gelu_slope(found)
        act[rows, :] = gelu(found).astype(BF)
        whole[rows, :] = (dot(act[rows, :], w_fc2[0]) + dot(attended[rows, :], w_dense[0])).astype(BF)

    loop_rows(normed.shape[0], 256, rows_done)


def split_kernel(place, whole, keep, give):
    put_slots(place, lambda rows: whole[rows, :], keep, give)


def split_sum_kernel(place, keep, came, for_x, for_y, corner):
    def rows_done(rows):
        for s, out in ((1, for_x), (2, for_y), (3, corner)):
            out[rows, :] = keep[s, rows, :] + came[s, rows, :]

    loop_rows(for_x.shape[0], 16, rows_done)


def begin_scatter(place, keep, give, after=()):
    came = swap(give, 1)
    shape = (keep.shape[1:], BF)
    for_x, for_y, corner = call(split_sum_kernel, [shape] * 3, place, [keep, came], after=after)
    from_corner, from_x, from_y = swap(corner, 6), swap(for_x, 2), swap(for_y, 4)
    return [keep, came, from_x, from_y, from_corner], for_x


def sum_terms(terms):
    total = terms[0][0].astype(F32) + terms[1][0].astype(F32)
    for term in terms[2:]:
        total = total + term[...].astype(F32)
    return total


def next_hidden_kernel(place, *refs):
    terms, (hidden, params, hidden_out, normed) = refs[:5], refs[5:]
    found = hidden[...].astype(F32) + sum_terms(terms) + params[4:5, :]
    hidden_out[...] = found
    normed[...] = (standardize(found)[0] * params[1:2, :] + params[3:4, :]).astype(BF)


def low_kernel(place, wide, low):
    low[...] = wide[...].astype(BF)


def assemble_kernel(place, *refs):
    for (s, k), piece in zip(SLOTS, refs[:8]):
        refs[8][slot_rows(place, s, k), :] = piece[...]


def last_hidden_kernel(place, act, attended, w_fc2, w_dense, keep, give, whole):
    def rows_done(rows):
        whole[rows, :] = (dot(act[rows, :], w_fc2[1]) + dot(attended[rows, :], w_dense[1])).astype(BF)

    loop_rows(act.shape[0], 256, rows_done)
    put_slots(place, lambda rows: whole[rows, :], keep, give)


def last_sum_kernel(place, *refs):
    terms, (hidden, params, out, token) = refs[:5], refs[5:]
    token[...] = jnp.zeros_like(token)
    out[...] = hidden[...] + sum_terms(terms) + params[5:6, :]


SMALL_ROWS = 16


def clear_rest(chunk):
    chunk[chunk.shape[0] - SMALL_ROWS :, :] = jnp.zeros((SMALL_ROWS, chunk.shape[1]), chunk.dtype)


def put_halves(out, value, start, rows):
    half = out.shape[1]
    for j in range(2):
        out[j * rows + start : j * rows + start + value.shape[0], :] = value[:, j * half : (j + 1) * half]


def second_ready_kernel(place, b0, b1, b2, b3, other, far, weight, grads):
    units = weight.shape[1]
    for s, k in SLOTS:
        block = other.at[s] if k else (b0, b1, b2, b3)[s]
        parts = (block[:HALF, :], block[HALF:ROWS, :] if k else far[s, :HALF, :])
        for part, other_plane in zip(parts, (False, True)):
            start = slot_start(place, s, k, ROWS) + half_start(place, other_plane)
            weight[pl.ds(pl.multiple_of(start, HALF), HALF), :] = part
        for j in range(2):
            grads[slot_rows(place, s, k), j * units : (j + 1) * units] = block[(1 + j) * ROWS : (2 + j) * ROWS, :]


def second_units_kernel(place, *refs):
    pieces, refs = refs[:8], refs[8:]
    bias, weight, grads, normed, act, pre, chunk = refs
    units = weight.shape[1]
    for (s, k), piece in zip(SLOTS, pieces):
        normed[slot_rows(place, s, k), :] = piece[...]
    shift = bias[1:2, :].astype(F32)

    def rows_done(rows):
        found = dot(normed[rows, :], weight[...]) + shift
        pre[rows, :] = found
        act[rows, :] = gelu(found).astype(BF)

    loop_rows(normed.shape[0], 256, rows_done)
    for start in range(0, units, 256):
        put_halves(chunk, outer_sum(act[:, start : start + 256], grads[...]).astype(BF), start, units)
    clear_rest(chunk)


def units_back(layer, place, grads, w_fc2, slope_of, normed, weight, chunk, sums, part_normed, grad_pre, grad_w):
    sums[...] = jnp.zeros_like(sums)
    width = grads.shape[1]
    units = weight.shape[1]

    def rows_done(rows):
        found = (times_transposed(grads[rows, :], w_fc2[layer]) * slope_of(rows)).astype(BF)
        grad_pre[rows, :] = found
        sums[0:1, :width] += jnp.sum(grads[rows, :].astype(F32), axis=0, keepdims=True)
        sums[1:2, :units] += jnp.sum(found.astype(F32), axis=0, keepdims=True)
        part_normed[rows, :] = times_transposed(found, weight[...])

    loop_rows(grads.shape[0], 256, rows_done)
    for start in range(0, width, 256):
        rows = slice(start, start + 256)
        grad_w[rows, :] = outer_sum(normed[:, rows], grad_pre[...]).astype(BF)
    for i, (s, k) in enumerate(SLOTS):
        chunk[i * ROWS : (i + 1) * ROWS, :] = grad_w[slot_rows(place, s, k), :]
    clear_rest(chunk)


def second_units_back_kernel(place, grads, w_fc2, w_dense, pre, normed, weight, chunk, sums, part_normed, grad_att, grad_pre, grad_w):
    def slope_of(rows):
        grad_att[rows, :] = times_transposed(grads[rows, :], w_dense[1]).astype(BF)
        return gelu_slope(pre[rows, :])

    units_back(1, place, grads, w_fc2, slope_of, normed, weight, chunk, sums, part_normed, grad_pre, grad_w)


def first_units_back_kernel(place, *refs):
    pieces, refs = refs[:8], refs[8:]
    act, w_fc2, slope, normed, weight, grads, chunk_rows, chunk, sums, part_normed, grad_pre, grad_w = refs
    for (s, k), piece in zip(SLOTS, pieces):
        grads[slot_rows(place, s, k), :] = piece[...]
    units_back(
        0, place, grads, w_fc2, lambda rows: slope[rows, :], normed, weight, chunk, sums, part_normed, grad_pre, grad_w
    )
    units = act.shape[1]
    for start in range(0, units, 256):
        put_halves(chunk_rows, outer_sum(act[:, start : start + 256], grads[...]).astype(BF), start, units)


def attend_back_block(start, q_ref, k_ref, v_ref, grad_att, keys_down, k_sum, v_sum, cosine, sine, mixed, found_p):
    stop = start + BLOCK
    queries = q_ref[start:stop, :] * SCORE_SCALE
    grad_queries = jnp.zeros((LANES, BLOCK), F32)
    for head in range(HEADS_HERE):
        chosen = jnp.where(head_mask(head), queries, 0.0).astype(BF)
        chosen_grads = jnp.where(head_mask(head), grad_att, 0.0).astype(BF)
        probabilities = found_p(head, chosen)
        grad_probs = dot_general(v_ref[:stop, :], chosen_grads, (1, 1))
        row_inner = jnp.sum(grad_probs * probabilities, axis=0, keepdims=True)
        grad_scores = (probabilities * (grad_probs - row_inner)).astype(BF)
        k_sum[:stop, :] += dot(grad_scores, chosen)
        v_sum[:stop, :] += dot(probabilities.astype(BF), chosen_grads)
        grad_queries = grad_queries + jnp.where(own_head(head), dot(keys_down[:, :stop], grad_scores), 0.0)
    rows = slice(start, stop)
    mixed[rows, :LANES] = turn(grad_queries.T, cosine[rows, :], sine[rows, :], -1.0).astype(BF)


def mixed_rest(cosine, sine, mixed, k_sum, v_sum):
    mixed[:, LANES : 2 * LANES] = turn(k_sum[...], cosine[...], sine[...], -1.0).astype(BF)
    mixed[:, 2 * LANES :] = v_sum[...].astype(BF)


def mixed_outer(normed, mixed, grad_w):
    for start in range(0, normed.shape[1], 256):
        rows = slice(start, start + 256)
        grad_w[rows, :] = outer_sum(normed[:, rows], mixed[...]).astype(BF)


def mixed_inner(normed, weight, mixed, part_normed, whole):
    def rows_done(rows):
        whole[rows, :] = (times_transposed(mixed[rows, :], weight[...]) + part_normed[rows, :]).astype(BF)

    loop_rows(normed.shape[0], 256, rows_done)


def mixed_back(place, normed, weight, cosine, sine, mixed, k_sum, v_sum, grad_w, part_normed, whole):
    mixed_rest(cosine, sine, mixed, k_sum, v_sum)
    mixed_outer(normed, mixed, grad_w)
    mixed_inner(normed, weight, mixed, part_normed, whole)


def put_heads_chunk(place, chunk, grad_w, grad_dense):
    heads = grad_w.shape[1]
    for i, (s, k) in enumerate(SLOTS):
        rows = slice(i * ROWS, (i + 1) * ROWS)
        chunk[rows, :heads] = grad_w[slot_rows(place, s, k), :]
        chunk[rows, heads:] = grad_dense[:, rows]
    clear_rest(chunk)


def second_attend_kernel(place, normed, b0, b1, b2, b3, cosine, sine, grad_att, part_normed, att_out, mixed, keep_n, give_n, weight, q_ref, k_ref, v_ref, values_down, keys_down, k_sum, v_sum):
    for s, k in SLOTS:
        weight[slot_rows(place, s, k), :] = (b0, b1, b2, b3)[s][k]
    project_heads(normed, weight, cosine, sine, q_ref, k_ref, v_ref, values_down)
    k_sum[...] = jnp.zeros_like(k_sum)
    v_sum[...] = jnp.zeros_like(v_sum)
    keys_down[...] = (k_ref[...].astype(F32) * SCORE_SCALE).T.astype(BF)
    for start in range(0, normed.shape[0], BLOCK):
        stop = start + BLOCK
        total = [jnp.zeros((LANES, BLOCK), F32)]

        def found_p(head, chosen):
            probabilities, _ = softmax_block(k_ref[:stop, :], chosen, BLOCK)
            found = dot(values_down[:, :stop], probabilities.astype(BF))
            total[0] = total[0] + jnp.where(own_head(head), found, 0.0)
            return probabilities

        attend_back_block(start, q_ref, k_ref, v_ref, grad_att[start:stop, :], keys_down, k_sum, v_sum, cosine, sine, mixed, found_p)
        att_out[start:stop, :] = total[0].T.astype(BF)
    mixed_rest(cosine, sine, mixed, k_sum, v_sum)
    for s in range(4):
        rows = pl.ds(pl.multiple_of((place[0] ^ s) * 2 * ROWS, 2 * ROWS), 2 * ROWS)
        found = (times_transposed(mixed[rows, :], weight[...]) + part_normed[rows, :]).astype(BF)
        odd = place[1] == 1
        keep_n[s] = jnp.where(odd, found[ROWS:, :], found[:ROWS, :])
        give_n[s] = jnp.where(odd, found[:ROWS, :], found[ROWS:, :])


def second_heads_kernel(place, normed, mixed, attended, grads, chunk, grad_w):
    mixed_outer(normed, mixed, grad_w)
    put_heads_chunk(place, chunk, grad_w, outer_sum(attended[...], grads[...]).astype(BF))


def norm_back(gain_row, grad_normed, hidden, params, grads):
    xhat, scale = standardize(hidden[...].astype(F32))
    inner = grad_normed * params[gain_row : gain_row + 1, :]
    mean_inner = jnp.mean(inner, axis=-1, keepdims=True)
    mean_along = jnp.mean(inner * xhat, axis=-1, keepdims=True)
    return grads[...] + (inner - mean_inner - xhat * mean_along) * scale, xhat


def second_norm_back_kernel(place, *refs):
    terms, (hidden, params, grads, grads_out, grads_low, sums) = refs[:5], refs[5:]
    grad_normed = sum_terms(terms)
    found, xhat = norm_back(1, grad_normed, hidden, params, grads)
    grads_out[...] = found
    grads_low[...] = found.astype(BF)
    sums[0:1, :] = jnp.sum(grad_normed * xhat, axis=0, keepdims=True)
    sums[1:2, :] = jnp.sum(grad_normed, axis=0, keepdims=True)


def first_norm_back_kernel(place, *refs):
    terms, (hidden, params, grads, sums0, sums1, grads_out, small) = refs[:5], refs[5:]
    total = sum_terms(terms)
    grads_out[...] = norm_back(0, total[:ROWS, :], hidden, params, grads)[0]
    small[0:8, :] = total[ROWS : ROWS + 8, :LANES]
    for layer, sums in ((0, sums0), (1, sums1)):
        small[4 + layer : 5 + layer, :] = sums[0:1, slot_rows(place, 0, 0)]
        for j in range(4):
            small[8 + 4 * layer + j : 9 + 4 * layer + j, :] = sums[1:2, j * LANES : (j + 1) * LANES]


def first_attend_back_kernel(place, grads, w_dense, attended, q_ref, k_ref, v_ref, log_in, cosine, sine, normed, xhat, weight, part_normed, ln_sums1, chunk, keep_n, give_n, keys_down, k_sum, v_sum, mixed, grad_w, whole, ln_sums):
    k_sum[...] = jnp.zeros_like(k_sum)
    v_sum[...] = jnp.zeros_like(v_sum)
    keys_down[...] = (k_ref[...].astype(F32) * SCORE_SCALE).T.astype(BF)
    for start in range(0, normed.shape[0], BLOCK):
        stop = start + BLOCK

        def found_p(head, chosen):
            scores = mask_diagonal(dot_general(k_ref[:stop, :], chosen, (1, 1)), BLOCK)
            return jnp.exp(scores - log_in[head : head + 1, start:stop])

        grad_att = times_transposed(grads[start:stop, :], w_dense[0]).astype(BF)
        attend_back_block(start, q_ref, k_ref, v_ref, grad_att, keys_down, k_sum, v_sum, cosine, sine, mixed, found_p)
    mixed_back(place, normed, weight, cosine, sine, mixed, k_sum, v_sum, grad_w, part_normed, whole)
    put_heads_chunk(place, chunk, grad_w, outer_sum(attended[...], grads[...]).astype(BF))
    ln_sums[...] = jnp.zeros_like(ln_sums)

    def rows_done(rows):
        part = whole[rows, :].astype(F32)
        ln_sums[0:1, :] += jnp.sum(part * xhat[rows, :].astype(F32), axis=0, keepdims=True)
        ln_sums[2:3, :] += jnp.sum(part, axis=0, keepdims=True)

    loop_rows(normed.shape[0], 256, rows_done)
    ln_sums[1:2, :] = ln_sums1[0:1, :]
    ln_sums[3:4, :] = ln_sums1[1:2, :]
    for s in range(4):
        for k, out in ((0, keep_n), (1, give_n)):
            rows = slot_rows(place, s, k)
            out[s, :ROWS, :] = whole[rows, :]
            out[s, ROWS:, :] = jnp.zeros((EXTRA, out.shape[2]), BF)
            out[s, ROWS : ROWS + 8, :LANES] = ln_sums[:, rows].astype(BF)


INWARD, ACROSS, OUTWARD = [(0, 1), (3, 2)], [(1, 2), (2, 1)], [(1, 0), (2, 3)]


def along(value, pairs):
    return lax.ppermute(value, "rep", pairs)


def low_sum(left, right):
    return left[...] + right[...]


def is_middle(place):
    return (place[2] == 1) | (place[2] == 2)


def tick_kernel(has, place, *refs):
    refs = list(refs)
    if has[0]:
        chunk, came = refs.pop(0), refs.pop(0)
    if has[1]:
        before, crossed = refs.pop(0), refs.pop(0)
    if has[2]:
        coming = refs.pop(0)
    half = refs.pop(0) if has[0] else None
    going = refs.pop(0) if has[1] else None

    def rows_done(rows):
        if has[0]:
            half[rows, :] = low_sum(chunk.at[rows, :], came.at[rows, :])
        if has[1]:
            found = low_sum(before.at[rows, :], crossed.at[rows, :])
            going[rows, :] = jnp.where(is_middle(place), found, coming[rows, :]) if has[2] else found

    loop_rows((half if has[0] else going).shape[0], 208, rows_done)


def tick(place, step, last, coming, after=()):
    if step is not None and last is not None:
        (half,) = tick(place, step, None, None, after)
        (going,) = tick(place, None, last, coming, (half,))
        return half, going
    ins, outs = [], []
    for pair in (step, last):
        if pair is not None:
            ins += pair
            outs.append((pair[0].shape, pair[0].dtype))
    if coming is not None:
        ins.append(coming)
    has = (step is not None, last is not None, coming is not None)
    return call(partial(tick_kernel, has), outs, place, ins, after=after)


def add_small_kernel(place, chunk, small, out):
    rows = chunk.shape[0] - SMALL_ROWS
    out[:rows, :] = chunk[:rows, :]
    out[rows:, :LANES] = small[...].astype(BF)
    out[rows:, LANES:] = jnp.zeros((SMALL_ROWS, chunk.shape[1] - LANES), BF)


def pick_kernel(place, total, came, o0, o1, o2, o3, *rest):
    heads = o0.shape[2]
    for i, (s, k) in enumerate(SLOTS):
        out = (o0, o1, o2, o3)[s]

        def rows_done(rows):
            here = pl.ds(pl.multiple_of(rows.start + i * ROWS, rows.size), rows.size)
            found = jnp.where(is_middle(place), total[here, :], came[here, :])
            out[k, rows, :] = found[:, :heads]
            if rest:
                rest[0][rows, i * ROWS : (i + 1) * ROWS] = found[:, heads:].astype(F32)

        loop_rows(ROWS, 32, rows_done)


def pick_both_kernel(place, total_f, came_f, total_q, came_q, o0, o1, o2, o3, dense):
    units = total_f.shape[1]
    heads = o0.shape[2] - units
    for i, (s, k) in enumerate(SLOTS):
        out = (o0, o1, o2, o3)[s]

        def rows_done(rows):
            here = pl.ds(pl.multiple_of(rows.start + i * ROWS, rows.size), rows.size)
            out[k, rows, :units] = jnp.where(is_middle(place), total_f[here, :], came_f[here, :])
            found = jnp.where(is_middle(place), total_q[here, :], came_q[here, :])
            out[k, rows, units:] = found[:, :heads]
            dense[rows, i * ROWS : (i + 1) * ROWS] = found[:, heads:].astype(F32)

        loop_rows(ROWS, 32, rows_done)


def pick_both(place, units_pair, heads_pair, heads, after=()):
    columns = units_pair[0].shape[1] + heads
    outs = [((2, ROWS, columns), BF)] * 4 + [((ROWS, 8 * LANES), F32)]
    return call(pick_both_kernel, outs, place, [*units_pair, *heads_pair], after=after)


def pick(place, total, came, heads, after=()):
    outs = [((2, ROWS, heads), BF)] * 4
    if heads < total.shape[1]:
        outs.append(((ROWS, 8 * LANES), F32))
    return call(pick_kernel, outs, place, [total, came], after=after)


def chosen_sum(place, total, outward):
    middle = (place[2] == 1) | (place[2] == 2)
    return jnp.where(middle, total, outward).astype(F32)


def final_call(body, place, ins, shape, layer, before=None, after=()):
    skip = len(after) + (before is not None)

    def run(place, *refs):
        *ins, out, token, found, sems = refs[skip:]
        body(place, ins, out.at[layer], found, sems)
        token[...] = jnp.zeros_like(token)

    return pl.pallas_call(
        run,
        name=body.__name__,
        out_shape=[jax.ShapeDtypeStruct((2,) + shape, F32), jax.ShapeDtypeStruct((8, LANES), F32)],
        in_specs=[pl.BlockSpec(memory_space=pltpu.SMEM)]
        + [pl.BlockSpec(memory_space=pltpu.HBM)] * (before is not None)
        + [pl.BlockSpec(memory_space=pl.ANY)] * len(after)
        + [pl.BlockSpec(memory_space=pltpu.VMEM)] * len(ins),
        out_specs=[pl.BlockSpec(memory_space=pltpu.HBM), pl.BlockSpec(memory_space=pltpu.VMEM)],
        scratch_shapes=[pltpu.VMEM(shape, F32), pltpu.SemaphoreType.DMA((8,))],
        input_output_aliases={} if before is None else {1: 0},
        compiler_params=pltpu.CompilerParams(vmem_limit_bytes=16 * 1024 * 1024),
        cost_estimate=SMALL,
    )(place, *([] if before is None else [before]), *after, *ins)


def final_rows_start(place, total, came, out, found, sems):
    half, rows = total.shape[1], out.shape[0]
    step = rows // 4

    def move(i):
        put = pl.ds(pl.multiple_of(i * step, step), step)
        return pltpu.make_async_copy(found.at[put, :], out.at[put, :], sems.at[i])

    def one(i, carry):
        put = pl.ds(pl.multiple_of(i * step, step), step)
        for j in range(2):
            part = pl.ds(pl.multiple_of(i * step + j * rows, step), step)
            found[put, j * half : (j + 1) * half] = jnp.where(is_middle(place), total[part, :], came[part, :]).astype(F32)
        move(i).start()
        return carry

    lax.fori_loop(0, 4, one, 0)
    return [move(i) for i in range(4)]


def final_rows_kernel(place, ins, out, found, sems):
    for move in final_rows_start(place, *ins, out, found, sems):
        move.wait()


def final_units_kernel(place, blocks, out, found, sems):
    units, moves = out.shape[1] // 8, []
    for i, (s, k) in enumerate(SLOTS):
        put = slice(i * units, (i + 1) * units)
        block = block_of(s, k, blocks)

        def rows_done(rows):
            found[rows, put] = block[rows, :units].astype(F32)

        loop_rows(ROWS, 32, rows_done)
        moves.append(pltpu.make_async_copy(found.at[:, put], out.at[:, slot_rows(place, s, k, units)], sems.at[i]))
        moves[-1].start()
    for move in moves:
        move.wait()


def final_heads_kernel(place, blocks, out, found, sems):
    third = out.shape[1] // 3
    for s, k in SLOTS:
        block = block_of(s, k, blocks)

        def rows_done(rows):
            part = block[rows, block.shape[1] - 3 * LANES :].astype(F32)
            for j in range(3):
                lanes = pl.ds(pl.multiple_of(j * third + slot_start(place, s, k, LANES), LANES), LANES)
                found[rows, lanes] = part[:, j * LANES : (j + 1) * LANES]

        loop_rows(ROWS, 32, rows_done)
    move = pltpu.make_async_copy(found, out, sems.at[0])
    move.start()
    move.wait()


def last_rows_kernel(place, before, total, came, out, gain, shift, bias_fc1, bias_fc2, found, sems):
    rows = slice(total.shape[0] - SMALL_ROWS, total.shape[0])
    small = jnp.where(is_middle(place), total[rows, :LANES], came[rows, :LANES]).astype(F32)
    moves = final_rows_start(place, total, came, out.at[0], found, sems)
    gain[...] = small[0:2, :]
    shift[...] = small[2:4, :]
    bias_fc2[...] = small[4:6, :]
    for layer in range(2):
        for j in range(4):
            bias_fc1[layer : layer + 1, j * LANES : (j + 1) * LANES] = small[8 + 4 * layer + j : 9 + 4 * layer + j, :]
    for move in moves:
        move.wait()


def local_plane(hidden_in, ln_gain, ln_bias, w_qkv, w_dense, w_fc1, b_fc1, w_fc2, b_fc2, output_grad):
    index = lax.axis_index("grp")
    place = jnp.stack([index // 2, index % 2, lax.axis_index("rep")]).astype(jnp.int32)
    span, width = hidden_in.shape[1:]
    seq = span * 8
    units = b_fc1.shape[1]
    own = 3 * LANES
    cosine, sine = rotary_tables(seq)
    hidden0 = hidden_in.reshape(span, width)
    grads1 = output_grad.reshape(span, width)

    wide, column, chunk_shape = ((seq, width), BF), ((seq, LANES), BF), ((seq + SMALL_ROWS, units), BF)
    blocks_n, blocks_n0 = ((4, ROWS, width), BF), ((4, ROWS + EXTRA, width), BF)
    blocks_f, blocks_q = ((2, ROWS, units), BF), ((2, ROWS, own), BF)
    mine, mine_low = ((span, width), F32), ((span, width), BF)
    sums_shape, part_shape = ((8, width), F32), ((seq, width), F32)
    head_scratch = [pltpu.VMEM((LANES, seq), BF), pltpu.VMEM((seq, LANES), F32), pltpu.VMEM((seq, LANES), F32)]
    back_scratch = [pltpu.VMEM((seq, own), BF), pltpu.VMEM((width, own), BF), pltpu.VMEM((seq, width), BF)]
    column_scratch = [pltpu.VMEM((seq, LANES), BF)] * 3
    units_scratch = [pltpu.VMEM((seq, units), BF), pltpu.VMEM((width, units), BF)]

    small = jnp.concatenate([ln_gain, ln_bias, b_fc2, jnp.zeros((EXTRA - 6, LANES), BF)])
    packed = call(
        pack_first_kernel,
        [((FIRST_ROWS, LANES), BF)] * 4,
        place,
        [hidden0, w_qkv, w_fc1, small],
        [pltpu.VMEM(a, BF) for a in (hidden0.shape, w_qkv.shape[1:], (HALF, w_fc1.shape[2]))] + [pltpu.SemaphoreType.DMA((3,))],
        hbm=3,
        mib=60,
    )
    first = send_blocks(place, packed)
    packed = call(partial(pack_units_grads_kernel, 1), [((3 * ROWS, units), BF)] * 4, place, [w_fc1, grads1])
    keep, give = call(partial(pack_heads_kernel, 1), [((4, ROWS, own), BF)] * 2, place, [w_qkv], after=[packed[0]])
    pairs1 = call(pair_kernel, [blocks_q] * 4, place, [keep, swap(give, 1)])
    (others0,) = call(others_first_kernel, [((4, OTHERS_ROWS, LANES), BF)], place, first, after=[pairs1[0]])
    units1 = send_blocks(place, packed)
    first = [*first, swap(others0, 1)]
    (near0,) = call(near_first_kernel, [((8, HALF_ROWS, LANES), BF)], place, first)
    far0 = along(near0, INWARD + OUTWARD)

    normed0, xhat0, weight_q0, params, q0, k0, v0, att0, log0 = call(
        first_attend_kernel,
        [wide, wide, ((width, own), BF), ((EXTRA, width), F32), column, column, column, column, ((8, seq), F32)],
        place,
        [*first, cosine, sine],
        [pltpu.VMEM((LANES, seq), BF)],
        after=[near0],
    )
    weight_f0, act0, slope0, partial_sum = call(
        first_units_kernel,
        [((width, units), BF), ((seq, units), BF), ((seq, units), F32), wide],
        place,
        [normed0, near0, far0, b_fc1, w_fc2, w_dense, att0],
    )
    (near1,) = call(near_units_kernel, [((4, ROWS, units), BF)], place, units1, after=[partial_sum])
    far1 = along(near1, INWARD + OUTWARD)
    keep, give = call(split_kernel, [blocks_n, blocks_n], place, [partial_sum], after=[near1])
    terms, sent = begin_scatter(place, keep, give)
    (others1,) = call(others_units_grads_kernel, [((4, 3 * ROWS, units), BF)], place, [*units1, far1], after=terms[2:])
    hidden1, normed1_own = call(next_hidden_kernel, [mine, mine_low], place, [*terms, hidden0, params], after=[others1])
    pieces = gather_pieces(normed1_own)

    weight_f1, grad_branch1 = call(
        second_ready_kernel, [((width, units), BF), wide], place, [*units1, swap(others1, 1), far1]
    )
    normed1, act1, pre1, chunk1 = call(
        second_units_kernel,
        [wide, ((seq, units), BF), ((seq, units), F32), chunk_shape],
        place,
        [*pieces, b_fc1, weight_f1, grad_branch1],
    )
    came1 = along(chunk1, INWARD)
    heads1 = send_blocks(place, pairs1)
    chunk2, sums1, part_normed, grad_att1 = call(
        second_units_back_kernel,
        [chunk_shape, sums_shape, part_shape, column],
        place,
        [grad_branch1, w_fc2, w_dense, pre1, normed1, weight_f1],
        units_scratch,
    )
    att1, mixed1, keep, give = call(
        second_attend_kernel,
        [column, ((seq, own), BF), blocks_n, blocks_n],
        place,
        [normed1, *heads1, cosine, sine, grad_att1, part_normed],
        [
            pltpu.VMEM((width, own), BF),
            *column_scratch,
            pltpu.VMEM((LANES, seq), BF),
            *head_scratch,
        ],
    )
    terms, sent = begin_scatter(place, keep, give)
    (half1,) = tick(place, (chunk1, came1), None, None, after=[give])
    (chunk3,) = call(
        second_heads_kernel,
        [chunk_shape],
        place,
        [normed1, mixed1, att1, grad_branch1],
        [pltpu.VMEM((width, own), BF)],
        after=[half1, sent],
    )
    cross1, came2 = along(half1, ACROSS), along(chunk2, INWARD)
    grads0, grads0_low, ln_sums1 = call(
        second_norm_back_kernel, [mine, mine_low, sums_shape], place, [*terms, hidden1, params, grads1], after=[half1]
    )

    keep_h, give_h = call(
        last_hidden_kernel,
        [blocks_n, blocks_n],
        place,
        [act1, att1, w_fc2, w_dense],
        [pltpu.VMEM((seq, width), BF)],
        after=[chunk3],
    )
    pieces = gather_pieces(grads0_low)
    half2, total1 = tick(place, (chunk2, came2), (half1, cross1), chunk3, after=[grads0_low, give_h])
    cross2, came3 = along(half2, ACROSS), along(total1, INWARD + OUTWARD)
    grad_branch0, chunk6, chunk4, sums0, part_normed = call(
        first_units_back_kernel,
        [wide, chunk_shape, chunk_shape, sums_shape, part_shape],
        place,
        [*pieces, act0, w_fc2, slope0, normed0, weight_f0],
        units_scratch,
        after=[half2],
    )
    half3, total2 = tick(place, (chunk3, came3), (half2, cross2), chunk4)
    cross3, came4 = along(half3, ACROSS), along(total2, INWARD + OUTWARD)
    chunk5, keep, give = call(
        first_attend_back_kernel,
        [chunk_shape, blocks_n0, blocks_n0],
        place,
        [grad_branch0, w_dense, att0, q0, k0, v0, log0, cosine, sine, normed0, xhat0, weight_q0, part_normed, ln_sums1],
        [*head_scratch, *back_scratch, pltpu.VMEM((8, width), F32)],
        after=[half3],
    )
    token = ((8, LANES), F32)
    out_fc2, done = final_call(final_rows_kernel, place, [total1, came3], (units, width), 1, after=[give])
    half4, total3 = tick(place, (chunk4, came4), (half3, cross3), chunk5, after=[done])
    cross4, came5 = along(half4, ACROSS), along(total3, INWARD + OUTWARD)
    terms, _ = begin_scatter(place, keep, give, after=[half4])
    input_grad, small_sums = call(
        first_norm_back_kernel,
        [mine, ((SMALL_ROWS, LANES), F32)],
        place,
        [*terms, hidden0, params, grads0, sums0, sums1],
    )
    (chunk6,) = call(add_small_kernel, [chunk_shape], place, [chunk6, small_sums])
    half5, total4 = tick(place, (chunk5, came5), (half4, cross4), chunk6)
    cross5, came6 = along(half5, ACROSS), along(total4, INWARD + OUTWARD)
    *picked1, dense1 = pick_both(place, (total2, came4), (total3, came5), own, after=[half5])
    blocks1 = swap_others(place, send_blocks(place, picked1))
    half6, total5 = tick(place, (chunk6, came6), (half5, cross5), None, after=[blocks1[1]])
    cross6, came7 = along(half6, ACROSS), along(total5, OUTWARD)
    picked4 = pick(place, total4, came6, units, after=[half6])
    out_fc1, done1 = final_call(final_units_kernel, place, blocks1, (ROWS, w_fc1.shape[2]), 1, after=[picked4[0]])
    out_qkv, done3 = final_call(final_heads_kernel, place, blocks1, (ROWS, w_qkv.shape[2]), 1, after=[done1])
    blocks4 = swap_others(place, send_blocks(place, picked4), after=[done3])
    (total6,) = tick(place, None, (half6, cross6), None, after=[blocks4[1]])
    came8 = along(total6, OUTWARD)
    terms, _ = begin_scatter(place, keep_h, give_h, after=[total6])
    out_fc1, done4 = final_call(final_units_kernel, place, blocks4, (ROWS, w_fc1.shape[2]), 0, out_fc1, after=[total6])
    *picked5, dense0 = pick(place, total5, came7, own, after=[done4])
    hidden_out, done_h = call(last_sum_kernel, [mine, token], place, [*terms, hidden1, params], after=[picked5[0]])
    blocks5 = swap_others(place, send_blocks(place, picked5), after=[done_h])
    out_qkv, done5 = final_call(final_heads_kernel, place, blocks5, (ROWS, w_qkv.shape[2]), 0, out_qkv)
    vector = jax.ShapeDtypeStruct((2, LANES), F32)
    out_fc2, out_gain, out_shift, out_b_fc1, out_b_fc2 = pl.pallas_call(
        lambda place, before, token, *refs: last_rows_kernel(place, before, *refs),
        name="last_rows_kernel",
        out_shape=[jax.ShapeDtypeStruct((2, units, width), F32), vector, vector, jax.ShapeDtypeStruct((2, units), F32), vector],
        in_specs=[pl.BlockSpec(memory_space=pltpu.SMEM), pl.BlockSpec(memory_space=pltpu.HBM)]
        + [pl.BlockSpec(memory_space=pl.ANY)]
        + [pl.BlockSpec(memory_space=pltpu.VMEM)] * 2,
        out_specs=[pl.BlockSpec(memory_space=pltpu.HBM)] + [pl.BlockSpec(memory_space=pltpu.VMEM)] * 4,
        scratch_shapes=[pltpu.VMEM((units, width), F32), pltpu.SemaphoreType.DMA((4,))],
        input_output_aliases={1: 0},
        compiler_params=pltpu.CompilerParams(vmem_limit_bytes=16 * 1024 * 1024),
        cost_estimate=SMALL,
    )(place, out_fc2, done5, total6, came8)
    out_dense = jnp.stack([dense0, dense1])
    return (
        hidden_out[None],
        input_grad[None],
        out_gain,
        out_shift,
        out_qkv,
        out_dense,
        out_fc1,
        out_b_fc1,
        out_fc2,
        out_b_fc2,
    )


def local(hidden_in, ln_gain, ln_bias, w_qkv, w_dense, w_fc1, b_fc1, w_fc2, b_fc2, output_grad):
    arguments = (hidden_in, ln_gain, ln_bias, w_qkv, w_dense, w_fc1, b_fc1, w_fc2, b_fc2, output_grad)
    plane = lax.axis_size("grp") == 8 and lax.axis_size("rep") == 4
    plane = plane and hidden_in.shape[:2] == (1, ROWS) and w_qkv.shape == (2, LANES, 3 * 8 * LANES)
    return (local_plane if plane else local_any)(*arguments)


def solution(mesh):
    in_specs = (
        P("rep", "grp", None),
        P(None, "grp"),
        P(None, "grp"),
        P(None, "grp", None),
        P(None, "grp", None),
        P(None, "grp", None),
        P(None, "grp"),
        P(None, "grp", None),
        P(None, "grp"),
        P("rep", "grp", None),
    )
    out_specs = (
        P("rep", "grp", None),
        P("rep", "grp", None),
        P(None, "grp"),
        P(None, "grp"),
        P(None, "grp", None),
        P(None, "grp", None),
        P(None, "grp", None),
        P(None, "grp"),
        P(None, "grp", None),
        P(None, "grp"),
    )
    return jax.shard_map(local, mesh=mesh, in_specs=in_specs, out_specs=out_specs, check_vma=False)
```

```python
from functools import partial

import jax
import jax.numpy as jnp
import numpy as np
from jax import lax
from jax.experimental import pallas as pl
from jax.experimental.pallas import tpu as pltpu
from jax.sharding import PartitionSpec as P

HEAD_DIM = 64
ROT = 32
LANES = 128

EPSILON = 1e-05
SCORE_SCALE = 0.125
NEGATIVE = -1000000000.0
BF = jnp.bfloat16
F32 = jnp.float32


def dot(left, right):
    return jnp.dot(left, right, preferred_element_type=F32)


def dot_general(left, right, contract):
    return lax.dot_general(left, right, ((contract[:1], contract[1:]), ((), ())), preferred_element_type=F32)


def outer_sum(left, right):
    return dot_general(left, right, (0, 0))


def times_transposed(left, right):
    return dot_general(left, right, (1, 1))


def head_mask(head):
    lane = lax.broadcasted_iota(jnp.int32, (1, LANES), 1)
    return (lane >= head * HEAD_DIM) & (lane < (head + 1) * HEAD_DIM)


def turn(part, cosine, sine, sign):
    even = lax.broadcasted_iota(jnp.int32, part.shape, 1) % 2 == 0
    partner = jnp.where(even, pltpu.roll(part, LANES - 1, 1), pltpu.roll(part, 1, 1))
    return part * cosine + partner * (sine * sign)


def mask_diagonal(scores, block):
    keys, queries = scores.shape
    key_place = lax.broadcasted_iota(jnp.int32, (block, queries), 0)
    query_place = lax.broadcasted_iota(jnp.int32, (block, queries), 1)
    last = jnp.where(key_place <= query_place, scores[keys - block :], NEGATIVE)
    if keys == block:
        return last
    return jnp.concatenate([scores[: keys - block], last], axis=0)


def attend_kernel(heads, block, mix_q, mix_k, mix_v, cosine, sine, q_out, k_out, v_out, att_out, log_out):
    seq = mix_q.shape[0]
    q_out[...] = turn(mix_q[...], cosine[...], sine[...], 1.0).astype(BF)
    k_out[...] = turn(mix_k[...], cosine[...], sine[...], 1.0).astype(BF)
    v_out[...] = mix_v[...].astype(BF)
    values_down = mix_v[...].T.astype(BF)
    for start in range(0, seq, block):
        stop = start + block
        queries = q_out[start:stop, :] * SCORE_SCALE
        keys = k_out[:stop, :]
        total = jnp.zeros((LANES, block), F32)
        for head in range(heads):
            chosen = jnp.where(head_mask(head), queries, 0.0).astype(BF)
            scores = mask_diagonal(dot_general(keys, chosen, (1, 1)), block)
            row_max = jnp.max(scores, axis=0, keepdims=True)
            exponent = jnp.exp(scores - row_max)
            row_total = jnp.sum(exponent, axis=0, keepdims=True)
            probabilities = (exponent * (1.0 / row_total)).astype(BF)
            log_out[head : head + 1, start:stop] = row_max + jnp.log(row_total)
            found = dot(values_down[:, :stop], probabilities)
            down = lax.broadcasted_iota(jnp.int32, (LANES, 1), 0)
            own = (down >= head * HEAD_DIM) & (down < (head + 1) * HEAD_DIM)
            total = total + jnp.where(own, found, 0.0)
        att_out[start:stop, :] = total.T.astype(BF)


def attend_back_kernel(heads, block, q_in, k_in, v_in, grad_att, log_in, cosine, sine, q_out, k_out, v_out, k_sum, v_sum):
    seq = q_in.shape[0]
    k_sum[...] = jnp.zeros_like(k_sum)
    v_sum[...] = jnp.zeros_like(v_sum)
    keys_down = (k_in[...].astype(F32) * SCORE_SCALE).T.astype(BF)
    for start in range(0, seq, block):
        stop = start + block
        queries = q_in[start:stop, :] * SCORE_SCALE
        grads = grad_att[start:stop, :]
        grad_queries = jnp.zeros((LANES, block), F32)
        for head in range(heads):
            chosen = jnp.where(head_mask(head), queries, 0.0).astype(BF)
            chosen_grads = jnp.where(head_mask(head), grads, 0.0).astype(BF)
            scores = mask_diagonal(dot_general(k_in[:stop, :], chosen, (1, 1)), block)
            probabilities = jnp.exp(scores - log_in[head : head + 1, start:stop])
            grad_probs = dot_general(v_in[:stop, :], chosen_grads, (1, 1))
            row_inner = jnp.sum(grad_probs * probabilities, axis=0, keepdims=True)
            grad_scores = (probabilities * (grad_probs - row_inner)).astype(BF)
            k_sum[:stop, :] += dot(grad_scores, chosen)
            v_sum[:stop, :] += dot(probabilities.astype(BF), chosen_grads)
            down = lax.broadcasted_iota(jnp.int32, (LANES, 1), 0)
            own = (down >= head * HEAD_DIM) & (down < (head + 1) * HEAD_DIM)
            grad_queries = grad_queries + jnp.where(own, dot(keys_down[:, :stop], grad_scores), 0.0)
        q_out[start:stop, :] = turn(
            grad_queries.T, cosine[start:stop, :], sine[start:stop, :], -1.0
        ).astype(BF)
    k_out[...] = turn(k_sum[...], cosine[...], sine[...], -1.0).astype(BF)
    v_out[...] = v_sum[...].astype(BF)


VMEM_LIMIT = 48 * 1024 * 1024


def attend(mix_q, mix_k, mix_v, heads, cosine, sine):
    seq = mix_q.shape[0]
    out = jax.ShapeDtypeStruct((seq, LANES), BF)
    return pl.pallas_call(
        partial(attend_kernel, heads, min(256, seq)),
        out_shape=(out, out, out, out, jax.ShapeDtypeStruct((heads, seq), F32)),
        compiler_params=pltpu.CompilerParams(vmem_limit_bytes=VMEM_LIMIT),
    )(mix_q, mix_k, mix_v, cosine, sine)


def attend_back(queries, keys, values, grad_att, log_total, heads, cosine, sine):
    seq = queries.shape[0]
    out = jax.ShapeDtypeStruct((seq, LANES), BF)
    return pl.pallas_call(
        partial(attend_back_kernel, heads, min(256, seq)),
        out_shape=(out, out, out),
        scratch_shapes=[pltpu.VMEM((seq, LANES), F32), pltpu.VMEM((seq, LANES), F32)],
        compiler_params=pltpu.CompilerParams(vmem_limit_bytes=VMEM_LIMIT),
    )(queries, keys, values, grad_att, log_total, cosine, sine)


def rotary_tables(seq):
    frequency = (1.0 / 10000.0 ** (np.arange(ROT // 2, dtype=np.float32) * 2.0 / ROT)).astype(np.float32)
    angles = np.arange(seq, dtype=np.float32)[:, None] * frequency[None, :]
    cosine, sine = np.cos(angles.astype(np.float64)), np.sin(angles.astype(np.float64))
    cosine = np.repeat(cosine, 2, axis=1)
    sine = np.repeat(sine, 2, axis=1) * np.tile([-1.0, 1.0], ROT // 2)
    rest = HEAD_DIM - ROT
    cosine = np.concatenate([cosine, np.ones((seq, rest))], axis=1)
    sine = np.concatenate([sine, np.zeros((seq, rest))], axis=1)
    repeats = (1, LANES // HEAD_DIM)
    return np.tile(cosine, repeats).astype(np.float32), np.tile(sine, repeats).astype(np.float32)


def swap(value, bits):
    return lax.ppermute(value, "grp", [(i, i ^ bits) for i in range(8)])


def add_low(left, right):
    return (left.astype(F32) + right.astype(F32)).astype(BF)


def by_chip(parts, chip):
    x, y = chip % 2 == 1, chip // 2 == 1
    near = jnp.where(x, jnp.stack([parts[1], parts[0]]), jnp.stack([parts[0], parts[1]]))
    far = jnp.where(x, jnp.stack([parts[3], parts[2]]), jnp.stack([parts[2], parts[3]]))
    return jnp.where(y, jnp.concatenate([far, near]), jnp.concatenate([near, far]))


def gather_rows(part):
    size = lax.axis_size("grp")
    if size != 8:
        return lax.all_gather(part, "grp", axis=0, tiled=True)
    rows, width = part.shape
    half = rows // 2
    index = lax.axis_index("grp")
    along_x, along_y = swap(part, 2), swap(part, 4)
    corner = jnp.concatenate([swap(along_y[:half], 2), swap(along_x[half:], 4)])
    mine = by_chip([part, along_x, along_y, corner], index // 2)
    other = swap(mine, 1)
    odd = index % 2 == 1
    both = jnp.stack([jnp.where(odd, other, mine), jnp.where(odd, mine, other)], axis=1)
    return both.reshape(8 * rows, width)


def scatter_sum(whole):
    size = lax.axis_size("grp")
    if size != 8:
        return lax.psum_scatter(whole, "grp", scatter_dimension=0, tiled=True).astype(F32)
    rows, width = whole.shape[0] // 8, whole.shape[1]
    half = rows // 2
    index = lax.axis_index("grp")
    chip, core = index // 2, index % 2
    blocks = whole.reshape(4, 2, rows, width)
    keep = lax.dynamic_index_in_dim(blocks, core, 1, False)
    give = lax.dynamic_index_in_dim(blocks, 1 - core, 1, False)
    summed = add_low(keep, swap(give, 1))
    own, for_x, for_y, corner = [lax.dynamic_index_in_dim(summed, chip ^ s, 0, False) for s in range(4)]
    by_x, by_y = swap(corner[:half], 2), swap(corner[half:], 4)
    for_y = jnp.concatenate([add_low(for_y[:half], by_x), for_y[half:]])
    for_x = jnp.concatenate([for_x[:half], add_low(for_x[half:], by_y)])
    return own.astype(F32) + swap(for_y, 4).astype(F32) + swap(for_x, 2).astype(F32)


def exchange(blocks):
    size = lax.axis_size("grp")
    if size != 8:
        return lax.all_to_all(blocks, "grp", 0, 0)
    index = lax.axis_index("grp")
    chip, core = index // 2, index % 2
    pairs = blocks.reshape((4, 2) + blocks.shape[1:])
    keep = lax.dynamic_index_in_dim(pairs, core, 1, False)
    give = lax.dynamic_index_in_dim(pairs, 1 - core, 1, False)
    came = swap(give, 1)
    odd = core == 1
    both = jnp.stack([jnp.where(odd, came, keep), jnp.where(odd, keep, came)], axis=1)
    parts = [lax.dynamic_index_in_dim(both, chip ^ s, 0, False) for s in range(4)]
    parts = [parts[0]] + [swap(parts[s], 2 * s) for s in (1, 2, 3)]
    return by_chip(parts, chip).reshape(blocks.shape)


def rep_sum(part):
    if lax.axis_size("rep") != 4:
        return lax.psum(part, "rep").astype(F32)
    place = lax.axis_index("rep")
    inward = lax.ppermute(part, "rep", [(0, 1), (3, 2)])
    half_sum = add_low(part, inward)
    across = lax.ppermute(half_sum, "rep", [(1, 2), (2, 1)])
    total = add_low(half_sum, across)
    outward = lax.ppermute(total, "rep", [(1, 0), (2, 3)])
    return jnp.where((place == 1) | (place == 2), total, outward).astype(F32)


def columns_of(w_qkv, w_fc1, group):
    rows, qkv = w_qkv.shape
    heads = w_qkv.reshape(rows, 3, group, qkv // 3 // group).transpose(2, 0, 1, 3).reshape(group, rows, -1)
    units = w_fc1.reshape(rows, group, -1).transpose(1, 0, 2)
    found = exchange(jnp.concatenate([heads, units], axis=2))
    found = found.reshape(group * rows, -1)
    return found[:, : qkv // group], found[:, qkv // group :]


def rows_of(grad_qkv, grad_fc1, group):
    rows = grad_qkv.shape[0] // group
    both = jnp.concatenate([grad_qkv, grad_fc1], axis=1).reshape(group, rows, -1)
    found = exchange(both)
    qkv = grad_qkv.shape[1]
    heads = found[:, :, :qkv].reshape(group, rows, 3, qkv // 3).transpose(1, 2, 0, 3).reshape(rows, -1)
    units = found[:, :, qkv:].transpose(1, 0, 2).reshape(rows, -1)
    return heads, units


def standardize(hidden):
    centered = hidden - jnp.mean(hidden, axis=-1, keepdims=True)
    scale = lax.rsqrt(jnp.mean(centered * centered, axis=-1, keepdims=True) + EPSILON)
    return centered * scale, scale


def widen(part):
    return jnp.pad(part, ((0, 0), (0, LANES - part.shape[1])))


def forward_layer(normed, weights, heads, tables):
    qkv_cols, fc1_cols, b_fc1, w_dense, w_fc2 = weights
    mixed = dot(normed, qkv_cols)
    own = heads * HEAD_DIM
    queries, keys, values, attended, log_total = attend(
        *(widen(mixed[:, i * own : (i + 1) * own]) for i in range(3)), heads, *tables
    )
    pre_act = dot(normed, fc1_cols) + b_fc1.astype(F32)
    activation = jax.nn.gelu(pre_act, approximate=True).astype(BF)
    partial_sum = (dot(attended[:, :own], w_dense) + dot(activation, w_fc2)).astype(BF)
    stored = (normed, queries, keys, values, attended, log_total, pre_act, activation)
    return partial_sum, stored


def backward_layer(grad_branch, weights, stored, heads, tables):
    qkv_cols, fc1_cols, b_fc1, w_dense, w_fc2 = weights
    normed, queries, keys, values, attended, log_total, pre_act, activation = stored
    own = heads * HEAD_DIM
    grad_w_fc2 = outer_sum(activation, grad_branch).astype(BF)
    grad_w_dense = outer_sum(attended[:, :own], grad_branch).astype(BF)
    _, gelu_back = jax.vjp(partial(jax.nn.gelu, approximate=True), pre_act)
    grad_pre = gelu_back(times_transposed(grad_branch, w_fc2))[0].astype(BF)
    grad_attended = widen(times_transposed(grad_branch, w_dense).astype(BF))
    grad_mixed = attend_back(queries, keys, values, grad_attended, log_total, heads, *tables)
    grad_mixed = jnp.concatenate([part[:, :own] for part in grad_mixed], axis=1)
    grad_fc1 = outer_sum(normed, grad_pre).astype(BF)
    grad_b_fc1 = jnp.sum(grad_pre.astype(F32), axis=0)
    grad_qkv = outer_sum(normed, grad_mixed).astype(BF)
    grad_normed = (times_transposed(grad_pre, fc1_cols) + times_transposed(grad_mixed, qkv_cols)).astype(BF)
    return grad_normed, (grad_w_fc2, grad_w_dense, grad_fc1, grad_qkv, grad_b_fc1)


def local_any(hidden_in, ln_gain, ln_bias, w_qkv, w_dense, w_fc1, b_fc1, w_fc2, b_fc2, output_grad):
    group = lax.axis_size("grp")
    index = lax.axis_index("grp")
    layers = w_qkv.shape[0]
    span, width = hidden_in.shape[1:]
    seq = span * group
    heads = width // HEAD_DIM // group
    tables = rotary_tables(seq)
    small = jnp.concatenate([ln_gain, ln_bias, b_fc2])
    small = lax.all_gather(small, "grp", axis=1, tiled=True).astype(F32)
    gains, shifts, b_fc2_all = small[:layers], small[layers : 2 * layers], small[2 * layers :]
    hidden = hidden_in.reshape(span, width).astype(F32)
    hidden_all = gather_rows(hidden_in.reshape(span, width))
    weights = []
    for layer in range(layers):
        qkv_cols, fc1_cols = columns_of(w_qkv[layer], w_fc1[layer], group)
        weights.append((qkv_cols, fc1_cols, b_fc1[layer], w_dense[layer], w_fc2[layer]))

    inputs, stored_layers = [], []
    for layer in range(layers):
        inputs.append(hidden)
        if layer == 0:
            normed = (standardize(hidden_all.astype(F32))[0] * gains[0] + shifts[0]).astype(BF)
        else:
            normed = gather_rows((standardize(hidden)[0] * gains[layer] + shifts[layer]).astype(BF))
        partial_sum, stored = forward_layer(normed, weights[layer], heads, tables)
        stored_layers.append(stored)
        hidden = hidden + scatter_sum(partial_sum) + b_fc2_all[layer]

    grad_hidden = output_grad.reshape(span, width)
    small_grads, large_grads = [None] * layers, [None] * layers
    for layer in reversed(range(layers)):
        grad_low = grad_hidden.astype(BF)
        grad_branch = gather_rows(grad_low)
        grad_normed, found = backward_layer(grad_branch, weights[layer], stored_layers[layer], heads, tables)
        grad_w_fc2, grad_w_dense, grad_fc1, grad_qkv, grad_b_fc1 = found
        grad_qkv, grad_fc1 = rows_of(grad_qkv, grad_fc1, group)
        large_grads[layer] = tuple(rep_sum(part) for part in (grad_w_fc2, grad_w_dense, grad_fc1, grad_qkv))
        grad_normed = scatter_sum(grad_normed)
        xhat, scale = standardize(inputs[layer])
        inner = grad_normed * gains[layer]
        mean_inner = jnp.mean(inner, axis=-1, keepdims=True)
        mean_along = jnp.mean(inner * xhat, axis=-1, keepdims=True)
        small_grads[layer] = jnp.concatenate(
            [
                jnp.sum(grad_normed * xhat, axis=0),
                jnp.sum(grad_normed, axis=0),
                jnp.sum(grad_low.astype(F32), axis=0),
                lax.dynamic_update_slice(
                    jnp.zeros((group * grad_b_fc1.shape[0],), F32), grad_b_fc1, (index * grad_b_fc1.shape[0],)
                ),
            ]
        )
        grad_hidden = grad_hidden + (inner - mean_inner - xhat * mean_along) * scale

    summed = lax.psum(jnp.stack(small_grads), ("rep", "grp"))
    own = width // group
    units = b_fc1.shape[1]

    def pick(start, count):
        return lax.dynamic_slice_in_dim(summed, start + index * count, count, 1)

    stacked = [jnp.stack([large_grads[layer][member] for layer in range(layers)]) for member in range(4)]
    return (
        hidden[None],
        grad_hidden[None],
        pick(0, own),
        pick(width, own),
        stacked[3],
        stacked[1],
        stacked[2],
        pick(3 * width, units),
        stacked[0],
        pick(2 * width, own),
    )


SLOTS = [(s, k) for s in range(4) for k in range(2)]
ROWS = 128
EXTRA = 16


def slot_start(place, s, k, size):
    return pl.multiple_of(((place[0] ^ s) * 2 + (place[1] ^ k)) * size, size)


def slot_rows(place, s, k, size=ROWS):
    return pl.ds(slot_start(place, s, k, size), size)


SMALL = pl.CostEstimate(flops=0, bytes_accessed=0, transcendentals=0)


def call(body, outs, place, ins, scratch=(), after=(), hbm=0, mib=16):
    def run(place, *refs):
        body(place, *refs[len(after) :])

    return pl.pallas_call(
        run,
        name=getattr(body, "func", body).__name__,
        out_shape=[jax.ShapeDtypeStruct(*out) for out in outs],
        in_specs=[pl.BlockSpec(memory_space=pltpu.SMEM)]
        + [pl.BlockSpec(memory_space=pl.ANY)] * len(after)
        + [pl.BlockSpec(memory_space=pltpu.HBM)] * hbm
        + [pl.BlockSpec(memory_space=pltpu.VMEM)] * (len(ins) - hbm),
        out_specs=[pl.BlockSpec(memory_space=pltpu.VMEM)] * len(outs),
        scratch_shapes=list(scratch),
        compiler_params=pltpu.CompilerParams(vmem_limit_bytes=mib * 1024 * 1024),
        cost_estimate=SMALL,
    )(place, *after, *ins)


def gather_pieces(part):
    mine = [part, swap(part, 2), swap(part, 4), swap(part, 6)]
    other = [swap(piece, 1) for piece in mine]
    return [piece for pair in zip(mine, other) for piece in pair]


def put_columns(out, start, value):
    rows = value.shape[0]
    for b in range(value.shape[1] // LANES):
        out[start + b * rows : start + (b + 1) * rows, :] = value[:, b * LANES : (b + 1) * LANES]


def heads_of(place, w_qkv, layer, s, k, j):
    start = j * (w_qkv.shape[2] // 3) + slot_start(place, s, k, LANES)
    return w_qkv[layer, :, pl.ds(pl.multiple_of(start, LANES), LANES)]


HALF = ROWS // 2
HEADS_ROWS, HALF_ROWS = 3 * ROWS, 4 * HALF
FIRST_MINE = 8 * ROWS
FIRST_OTHERS = FIRST_MINE + HEADS_ROWS + HALF_ROWS
FIRST_SMALL = FIRST_OTHERS + HEADS_ROWS + HALF_ROWS
FIRST_ROWS = FIRST_SMALL + EXTRA
OTHERS_MINE = 8 * ROWS
OTHERS_SMALL = OTHERS_MINE + HEADS_ROWS + HALF_ROWS
OTHERS_ROWS = OTHERS_SMALL + EXTRA


def half_start(place, other):
    parity = place[2] & 1
    return pl.multiple_of((1 - parity if other else parity) * HALF, HALF)


def pack_first_kernel(hidden_from, qkv_from, fc1_from, gain_from, shift_from, bias_from, o0, o1, o2, o3, hidden, w_qkv, w_fc1, gain, shift, bias, sems):
    index = lax.axis_index("grp")
    place = (index // 2, index % 2, lax.axis_index("rep"))
    outs = (o0, o1, o2, o3)
    pairs = (
        (hidden_from, hidden),
        (gain_from, gain),
        (shift_from, shift),
        (bias_from, bias),
        (qkv_from.at[0], w_qkv),
        (fc1_from.at[0, pl.ds(half_start(place, False), HALF), :], w_fc1),
    )
    moves = [pltpu.make_async_copy(*pair, sems.at[i]) for i, pair in enumerate(pairs)]
    for move in moves:
        move.start()
    for move in moves[:4]:
        move.wait()
    for out in outs:
        put_columns(out, 0, hidden[...])
        out[FIRST_SMALL:, :] = jnp.zeros((EXTRA, LANES), BF)
        for i, part in enumerate((gain, shift, bias)):
            out[FIRST_SMALL + 2 * i : FIRST_SMALL + 2 * i + 2, :] = part[...]
    moves[4].wait()
    third = w_qkv.shape[1] // 3
    for s, k in SLOTS:
        row = (FIRST_MINE, FIRST_OTHERS)[k]
        for j in range(3):
            lanes = pl.ds(pl.multiple_of(j * third + slot_start(place, s, k, LANES), LANES), LANES)
            outs[s][row + j * ROWS : row + (j + 1) * ROWS, :] = w_qkv[:, lanes]
    moves[5].wait()
    for s, k in SLOTS:
        row = (FIRST_MINE, FIRST_OTHERS)[k] + HEADS_ROWS
        put_columns(outs[s], row, w_fc1[:, pl.ds(slot_start(place, s, k, 4 * LANES), 4 * LANES)])


def others_first_kernel(place, b0, b1, b2, b3, out):
    for s, block in enumerate((b0, b1, b2, b3)):
        out[s, :OTHERS_MINE, :] = block[:FIRST_MINE, :]
        out[s, OTHERS_MINE:OTHERS_SMALL, :] = block[FIRST_OTHERS:FIRST_SMALL, :]
        out[s, OTHERS_SMALL:, :] = block[FIRST_SMALL:, :]


def near_first_kernel(place, b0, b1, b2, b3, b4, out):
    for i, (s, k) in enumerate(SLOTS):
        block, mine_at, _ = first_block(s, k, (b0, b1, b2, b3, b4))
        out[i] = block[mine_at + HEADS_ROWS : mine_at + HEADS_ROWS + HALF_ROWS, :]


def first_block(s, k, blocks):
    if k:
        return blocks[4].at[s], OTHERS_MINE, OTHERS_SMALL
    return blocks[s], FIRST_MINE, FIRST_SMALL


def pack_heads_kernel(layer, place, w_qkv, keep, give):
    for s, k in SLOTS:
        for j in range(3):
            (keep, give)[k][s, :, j * LANES : (j + 1) * LANES] = heads_of(place, w_qkv, layer, s, k, j)


def pair_kernel(place, keep, came, *outs):
    for s, out in enumerate(outs):
        out[0], out[1] = keep[s], came[s]


def pack_units_kernel(layer, place, w_fc1, *outs):
    units = outs[0].shape[2]
    for s, k in SLOTS:
        outs[s][k] = w_fc1[layer, :, pl.ds(slot_start(place, s, k, units), units)]


def pack_units_grads_kernel(layer, place, w_fc1, grads, *outs):
    units = outs[0].shape[1]
    low = grads[...].astype(BF)
    for s in range(4):
        for k in range(2):
            lanes = pl.ds(slot_start(place, s, k, units), units)
            outs[s][k * HALF : (k + 1) * HALF, :] = w_fc1[layer, pl.ds(half_start(place, False), HALF), lanes]
            outs[s][(1 + k) * ROWS : (2 + k) * ROWS, :] = low[:, k * units : (k + 1) * units]


def near_units_kernel(place, b0, b1, b2, b3, out):
    for s, block in enumerate((b0, b1, b2, b3)):
        out[s] = block[:ROWS, :]


def others_units_grads_kernel(place, b0, b1, b2, b3, far, out):
    for s, block in enumerate((b0, b1, b2, b3)):
        out[s, :HALF, :] = block[HALF:ROWS, :]
        out[s, HALF:ROWS, :] = far[s, HALF:, :]
        out[s, ROWS:, :] = block[ROWS:, :]


def send_blocks(place, packed):
    return [packed[0]] + [swap(packed[s], 2 * s) for s in (1, 2, 3)]


def others_kernel(place, b0, b1, b2, b3, out):
    for s, block in enumerate((b0, b1, b2, b3)):
        out[s] = block[1]


def swap_others(place, blocks, after=()):
    (other,) = call(others_kernel, [((4,) + blocks[0].shape[1:], BF)], place, blocks, after=after)
    return [*blocks, swap(other, 1)]


def block_of(s, k, blocks):
    return blocks[4].at[s] if k else blocks[s].at[0]


def project_heads(normed, weight, cosine, sine, q_out, k_out, v_out, values_down):
    step = 256
    for start in range(0, normed.shape[0], step):
        rows = slice(start, start + step)
        mixed = dot(normed[rows, :], weight[...])
        q_out[rows, :] = turn(mixed[:, :LANES], cosine[rows, :], sine[rows, :], 1.0).astype(BF)
        k_out[rows, :] = turn(mixed[:, LANES : 2 * LANES], cosine[rows, :], sine[rows, :], 1.0).astype(BF)
        values = mixed[:, 2 * LANES :]
        v_out[rows, :] = values.astype(BF)
        values_down[:, rows] = values.T.astype(BF)


def own_head(head):
    down = lax.broadcasted_iota(jnp.int32, (LANES, 1), 0)
    return (down >= head * HEAD_DIM) & (down < (head + 1) * HEAD_DIM)


def softmax_block(keys, chosen, block):
    scores = mask_diagonal(dot_general(keys, chosen, (1, 1)), block)
    row_max = jnp.max(scores, axis=0, keepdims=True)
    exponent = jnp.exp(scores - row_max)
    row_total = jnp.sum(exponent, axis=0, keepdims=True)
    return exponent * (1.0 / row_total), row_max + jnp.log(row_total)


BLOCK = 256
HEADS_HERE = LANES // HEAD_DIM


def first_attend_kernel(place, b0, b1, b2, b3, b4, cosine, sine, normed, xhat_out, weight, params, q_out, k_out, v_out, att_out, log_out, values_down):
    for s, k in SLOTS:
        rows = slot_rows(place, s, k)
        block, mine_at, small_at = first_block(s, k, (b0, b1, b2, b3, b4))
        for j in range(3):
            weight[rows, j * LANES : (j + 1) * LANES] = block[mine_at + j * ROWS : mine_at + (j + 1) * ROWS, :]
        params[:, rows] = block[small_at:, :].astype(F32)
        for b in range(8):
            normed[rows, b * LANES : (b + 1) * LANES] = block[b * ROWS : (b + 1) * ROWS, :]
    gain, shift = params[0:1, :], params[2:3, :]

    def norm_rows(rows):
        xhat = standardize(normed[rows, :].astype(F32))[0]
        xhat_out[rows, :] = xhat.astype(BF)
        normed[rows, :] = (xhat * gain + shift).astype(BF)

    loop_rows(normed.shape[0], 4 * ROWS, norm_rows)
    project_heads(normed, weight, cosine, sine, q_out, k_out, v_out, values_down)
    for start in range(0, normed.shape[0], BLOCK):
        stop = start + BLOCK
        queries = q_out[start:stop, :] * SCORE_SCALE
        total = jnp.zeros((LANES, BLOCK), F32)
        for head in range(HEADS_HERE):
            chosen = jnp.where(head_mask(head), queries, 0.0).astype(BF)
            probabilities, log_total = softmax_block(k_out[:stop, :], chosen, BLOCK)
            log_out[head : head + 1, start:stop] = log_total
            found = dot(values_down[:, :stop], probabilities.astype(BF))
            total = total + jnp.where(own_head(head), found, 0.0)
        att_out[start:stop, :] = total.T.astype(BF)


GELU_A = 0.7978845608028654
GELU_B = 0.044715


def gelu(pre):
    return pre * (0.5 + 0.5 * jnp.tanh(GELU_A * pre * (1.0 + GELU_B * pre * pre)))


def gelu_slope(pre):
    square = pre * pre
    wave = jnp.tanh(GELU_A * pre * (1.0 + GELU_B * square))
    return 0.5 * (1.0 + wave) + 0.5 * pre * (1.0 - wave * wave) * (GELU_A * (1.0 + 3.0 * GELU_B * square))


def loop_rows(count, step, body):
    def one(i, carry):
        body(pl.ds(pl.multiple_of(i * step, step), step))
        return carry

    lax.fori_loop(0, count // step, one, 0)


def put_slots(place, rows_of_block, keep, give):
    for s in range(4):
        keep[s] = rows_of_block(slot_rows(place, s, 0))
        give[s] = rows_of_block(slot_rows(place, s, 1))


def put_pairs(place, rows_of_block, outs):
    for s, k in SLOTS:
        outs[s][k] = rows_of_block(slot_rows(place, s, k))


def first_units_kernel(place, normed, near, far, bias, w_fc2, w_dense, attended, weight, act, slope, whole):
    for s, k in SLOTS:
        for part, other_plane in ((near.at[SLOTS.index((s, k))], False), (far.at[SLOTS.index((s, k))], True)):
            start = slot_start(place, s, k, ROWS) + half_start(place, other_plane)
            for b in range(4):
                rows = pl.ds(pl.multiple_of(start, HALF), HALF)
                weight[rows, b * LANES : (b + 1) * LANES] = part[b * HALF : (b + 1) * HALF, :]
    shift = bias[0:1, :].astype(F32)

    def rows_done(rows):
        found = dot(normed[rows, :], weight[...]) + shift
        slope[rows, :] = gelu_slope(found)
        act[rows, :] = gelu(found).astype(BF)
        whole[rows, :] = (dot(act[rows, :], w_fc2[0]) + dot(attended[rows, :], w_dense[0])).astype(BF)

    loop_rows(normed.shape[0], 256, rows_done)


def split_kernel(place, whole, keep, give):
    put_slots(place, lambda rows: whole[rows, :], keep, give)


def split_sum_kernel(place, keep, came, for_x, for_y, corner):
    def rows_done(rows):
        for s, out in ((1, for_x), (2, for_y), (3, corner)):
            out[rows, :] = keep[s, rows, :] + came[s, rows, :]

    loop_rows(for_x.shape[0], 16, rows_done)


def begin_scatter(place, keep, give, after=()):
    came = swap(give, 1)
    shape = (keep.shape[1:], BF)
    for_x, for_y, corner = call(split_sum_kernel, [shape] * 3, place, [keep, came], after=after)
    from_corner, from_x, from_y = swap(corner, 6), swap(for_x, 2), swap(for_y, 4)
    return [keep, came, from_x, from_y, from_corner], for_x


def sum_terms(terms):
    total = terms[0][0].astype(F32) + terms[1][0].astype(F32)
    for term in terms[2:]:
        total = total + term[...].astype(F32)
    return total


def next_hidden_kernel(place, *refs):
    terms, (hidden, params, hidden_out, normed) = refs[:5], refs[5:]
    found = hidden[...].astype(F32) + sum_terms(terms) + params[4:5, :]
    hidden_out[...] = found
    normed[...] = (standardize(found)[0] * params[1:2, :] + params[3:4, :]).astype(BF)


def low_kernel(place, wide, low):
    low[...] = wide[...].astype(BF)


def assemble_kernel(place, *refs):
    for (s, k), piece in zip(SLOTS, refs[:8]):
        refs[8][slot_rows(place, s, k), :] = piece[...]


def last_hidden_kernel(place, act, attended, w_fc2, w_dense, keep_a, give_a, keep_b, give_b, whole):
    half = keep_a.shape[2]

    def rows_done(rows):
        whole[rows, :] = (dot(act[rows, :], w_fc2[1]) + dot(attended[rows, :], w_dense[1])).astype(BF)

    loop_rows(act.shape[0], 256, rows_done)
    put_slots(place, lambda rows: whole[rows, :half], keep_a, give_a)
    put_slots(place, lambda rows: whole[rows, half:], keep_b, give_b)


def last_sum_kernel(place, *refs):
    terms, (hidden, params, out, token) = refs[:5], refs[5:]
    half = out.shape[1]
    token[...] = jnp.zeros_like(token)
    out[...] = hidden[:, :half] + sum_terms(terms) + params[5:6, :half]


def last_join_kernel(place, *refs):
    terms, (hidden, params, first, out, token) = refs[:5], refs[5:]
    half = first.shape[1]
    token[...] = jnp.zeros_like(token)
    out[:, :half] = first[...]
    out[:, half:] = hidden[:, half:] + sum_terms(terms) + params[5:6, half:]


SMALL_ROWS = 16


def put_halves(out, value, start, rows):
    half = out.shape[1]
    for j in range(2):
        out[j * rows + start : j * rows + start + value.shape[0], :] = value[:, j * half : (j + 1) * half]


def second_ready_kernel(place, b0, b1, b2, b3, other, far, weight, grads):
    units = weight.shape[1]
    for s, k in SLOTS:
        block = other.at[s] if k else (b0, b1, b2, b3)[s]
        parts = (block[:HALF, :], block[HALF:ROWS, :] if k else far[s, :HALF, :])
        for part, other_plane in zip(parts, (False, True)):
            start = slot_start(place, s, k, ROWS) + half_start(place, other_plane)
            weight[pl.ds(pl.multiple_of(start, HALF), HALF), :] = part
        for j in range(2):
            grads[slot_rows(place, s, k), j * units : (j + 1) * units] = block[(1 + j) * ROWS : (2 + j) * ROWS, :]


def second_units_kernel(place, *refs):
    pieces, refs = refs[:8], refs[8:]
    bias, weight, grads, normed, act, pre, chunk = refs
    units = weight.shape[1]
    for (s, k), piece in zip(SLOTS, pieces):
        normed[slot_rows(place, s, k), :] = piece[...]
    shift = bias[1:2, :].astype(F32)

    def rows_done(rows):
        found = dot(normed[rows, :], weight[...]) + shift
        pre[rows, :] = found
        act[rows, :] = gelu(found).astype(BF)

    loop_rows(normed.shape[0], 256, rows_done)
    for start in range(0, units, 256):
        put_halves(chunk, outer_sum(act[:, start : start + 256], grads[...]).astype(BF), start, units)


def units_back(layer, place, grads, w_fc2, slope_of, normed, weight, chunk, sums, part_normed, grad_pre, grad_w):
    sums[...] = jnp.zeros_like(sums)
    width = grads.shape[1]
    units = weight.shape[1]

    def rows_done(rows):
        found = (times_transposed(grads[rows, :], w_fc2[layer]) * slope_of(rows)).astype(BF)
        grad_pre[rows, :] = found
        sums[0:1, :width] += jnp.sum(grads[rows, :].astype(F32), axis=0, keepdims=True)
        sums[1:2, :units] += jnp.sum(found.astype(F32), axis=0, keepdims=True)
        part_normed[rows, :] = times_transposed(found, weight[...])

    loop_rows(grads.shape[0], 256, rows_done)
    for start in range(0, width, 256):
        rows = slice(start, start + 256)
        grad_w[rows, :] = outer_sum(normed[:, rows], grad_pre[...]).astype(BF)
    for i, (s, k) in enumerate(SLOTS):
        chunk[i * ROWS : (i + 1) * ROWS, :] = grad_w[slot_rows(place, s, k), :]


def second_units_back_kernel(place, grads, w_fc2, w_dense, pre, normed, weight, chunk, sums, part_normed, grad_att, grad_pre, grad_w):
    def slope_of(rows):
        grad_att[rows, :] = times_transposed(grads[rows, :], w_dense[1]).astype(BF)
        return gelu_slope(pre[rows, :])

    units_back(1, place, grads, w_fc2, slope_of, normed, weight, chunk, sums, part_normed, grad_pre, grad_w)


def first_units_back_kernel(place, *refs):
    pieces, refs = refs[:8], refs[8:]
    act, w_fc2, slope, normed, weight, grads, chunk_rows, chunk, sums, part_normed, grad_pre, grad_w = refs
    for (s, k), piece in zip(SLOTS, pieces):
        grads[slot_rows(place, s, k), :] = piece[...]
    units_back(
        0, place, grads, w_fc2, lambda rows: slope[rows, :], normed, weight, chunk, sums, part_normed, grad_pre, grad_w
    )
    units = act.shape[1]
    for start in range(0, units, 256):
        put_halves(chunk_rows, outer_sum(act[:, start : start + 256], grads[...]).astype(BF), start, units)


def attend_back_block(start, q_ref, k_ref, v_ref, grad_att, keys_down, k_sum, v_sum, cosine, sine, mixed, found_p):
    stop = start + BLOCK
    queries = q_ref[start:stop, :] * SCORE_SCALE
    grad_queries = jnp.zeros((LANES, BLOCK), F32)
    for head in range(HEADS_HERE):
        chosen = jnp.where(head_mask(head), queries, 0.0).astype(BF)
        chosen_grads = jnp.where(head_mask(head), grad_att, 0.0).astype(BF)
        probabilities = found_p(head, chosen)
        grad_probs = dot_general(v_ref[:stop, :], chosen_grads, (1, 1))
        row_inner = jnp.sum(grad_probs * probabilities, axis=0, keepdims=True)
        grad_scores = (probabilities * (grad_probs - row_inner)).astype(BF)
        k_sum[:stop, :] += dot(grad_scores, chosen)
        v_sum[:stop, :] += dot(probabilities.astype(BF), chosen_grads)
        grad_queries = grad_queries + jnp.where(own_head(head), dot(keys_down[:, :stop], grad_scores), 0.0)
    rows = slice(start, stop)
    mixed[rows, :LANES] = turn(grad_queries.T, cosine[rows, :], sine[rows, :], -1.0).astype(BF)


def mixed_rest(cosine, sine, mixed, k_sum, v_sum):
    mixed[:, LANES : 2 * LANES] = turn(k_sum[...], cosine[...], sine[...], -1.0).astype(BF)
    mixed[:, 2 * LANES :] = v_sum[...].astype(BF)


def mixed_outer(normed, mixed, grad_w):
    for start in range(0, normed.shape[1], 256):
        rows = slice(start, start + 256)
        grad_w[rows, :] = outer_sum(normed[:, rows], mixed[...]).astype(BF)


def mixed_inner(normed, weight, mixed, part_normed, whole):
    def rows_done(rows):
        whole[rows, :] = (times_transposed(mixed[rows, :], weight[...]) + part_normed[rows, :]).astype(BF)

    loop_rows(normed.shape[0], 256, rows_done)


def mixed_back(place, normed, weight, cosine, sine, mixed, k_sum, v_sum, grad_w, part_normed, whole):
    mixed_rest(cosine, sine, mixed, k_sum, v_sum)
    mixed_outer(normed, mixed, grad_w)
    mixed_inner(normed, weight, mixed, part_normed, whole)


def put_heads_chunk(place, chunk, grad_w, grad_dense):
    heads = grad_w.shape[1]
    for i, (s, k) in enumerate(SLOTS):
        rows = slice(i * ROWS, (i + 1) * ROWS)
        chunk[rows, :heads] = grad_w[slot_rows(place, s, k), :]
        chunk[rows, heads:] = grad_dense[:, rows]


def second_attend_kernel(place, normed, b0, b1, b2, b3, cosine, sine, grad_att, part_normed, att_out, mixed, keep_n, give_n, weight, q_ref, k_ref, v_ref, values_down, keys_down, k_sum, v_sum):
    for s, k in SLOTS:
        weight[slot_rows(place, s, k), :] = (b0, b1, b2, b3)[s][k]
    project_heads(normed, weight, cosine, sine, q_ref, k_ref, v_ref, values_down)
    k_sum[...] = jnp.zeros_like(k_sum)
    v_sum[...] = jnp.zeros_like(v_sum)
    keys_down[...] = (k_ref[...].astype(F32) * SCORE_SCALE).T.astype(BF)
    for start in range(0, normed.shape[0], BLOCK):
        stop = start + BLOCK
        total = [jnp.zeros((LANES, BLOCK), F32)]

        def found_p(head, chosen):
            probabilities, _ = softmax_block(k_ref[:stop, :], chosen, BLOCK)
            found = dot(values_down[:, :stop], probabilities.astype(BF))
            total[0] = total[0] + jnp.where(own_head(head), found, 0.0)
            return probabilities

        attend_back_block(start, q_ref, k_ref, v_ref, grad_att[start:stop, :], keys_down, k_sum, v_sum, cosine, sine, mixed, found_p)
        att_out[start:stop, :] = total[0].T.astype(BF)
    mixed_rest(cosine, sine, mixed, k_sum, v_sum)
    for s in range(4):
        rows = pl.ds(pl.multiple_of((place[0] ^ s) * 2 * ROWS, 2 * ROWS), 2 * ROWS)
        found = (times_transposed(mixed[rows, :], weight[...]) + part_normed[rows, :]).astype(BF)
        odd = place[1] == 1
        keep_n[s] = jnp.where(odd, found[ROWS:, :], found[:ROWS, :])
        give_n[s] = jnp.where(odd, found[:ROWS, :], found[ROWS:, :])


def second_heads_kernel(place, normed, mixed, attended, grads, chunk, grad_w):
    mixed_outer(normed, mixed, grad_w)
    put_heads_chunk(place, chunk, grad_w, outer_sum(attended[...], grads[...]).astype(BF))


def norm_back(gain_row, grad_normed, hidden, params, grads):
    xhat, scale = standardize(hidden[...].astype(F32))
    inner = grad_normed * params[gain_row : gain_row + 1, :]
    mean_inner = jnp.mean(inner, axis=-1, keepdims=True)
    mean_along = jnp.mean(inner * xhat, axis=-1, keepdims=True)
    return grads[...] + (inner - mean_inner - xhat * mean_along) * scale, xhat


def second_norm_back_kernel(place, *refs):
    terms, (hidden, params, grads, grads_out, grads_low, sums) = refs[:5], refs[5:]
    grad_normed = sum_terms(terms)
    found, xhat = norm_back(1, grad_normed, hidden, params, grads)
    grads_out[...] = found
    grads_low[...] = found.astype(BF)
    sums[0:1, :] = jnp.sum(grad_normed * xhat, axis=0, keepdims=True)
    sums[1:2, :] = jnp.sum(grad_normed, axis=0, keepdims=True)


def first_norm_back_kernel(place, *refs):
    terms, (hidden, params, grads, sums0, sums1, grads_out, small) = refs[:5], refs[5:]
    total = sum_terms(terms)
    grads_out[...] = norm_back(0, total[:ROWS, :], hidden, params, grads)[0]
    small[0:8, :] = total[ROWS : ROWS + 8, :LANES]
    for layer, sums in ((0, sums0), (1, sums1)):
        small[4 + layer : 5 + layer, :] = sums[0:1, slot_rows(place, 0, 0)]
        for j in range(4):
            small[8 + 4 * layer + j : 9 + 4 * layer + j, :] = sums[1:2, j * LANES : (j + 1) * LANES]


def first_attend_back_kernel(place, grads, w_dense, attended, q_ref, k_ref, v_ref, log_in, cosine, sine, normed, xhat, weight, part_normed, ln_sums1, chunk, keep_n, give_n, keys_down, k_sum, v_sum, mixed, grad_w, whole, ln_sums):
    k_sum[...] = jnp.zeros_like(k_sum)
    v_sum[...] = jnp.zeros_like(v_sum)
    keys_down[...] = (k_ref[...].astype(F32) * SCORE_SCALE).T.astype(BF)
    for start in range(0, normed.shape[0], BLOCK):
        stop = start + BLOCK

        def found_p(head, chosen):
            scores = mask_diagonal(dot_general(k_ref[:stop, :], chosen, (1, 1)), BLOCK)
            return jnp.exp(scores - log_in[head : head + 1, start:stop])

        grad_att = times_transposed(grads[start:stop, :], w_dense[0]).astype(BF)
        attend_back_block(start, q_ref, k_ref, v_ref, grad_att, keys_down, k_sum, v_sum, cosine, sine, mixed, found_p)
    mixed_back(place, normed, weight, cosine, sine, mixed, k_sum, v_sum, grad_w, part_normed, whole)
    put_heads_chunk(place, chunk, grad_w, outer_sum(attended[...], grads[...]).astype(BF))
    ln_sums[...] = jnp.zeros_like(ln_sums)

    def rows_done(rows):
        part = whole[rows, :].astype(F32)
        ln_sums[0:1, :] += jnp.sum(part * xhat[rows, :].astype(F32), axis=0, keepdims=True)
        ln_sums[2:3, :] += jnp.sum(part, axis=0, keepdims=True)

    loop_rows(normed.shape[0], 256, rows_done)
    ln_sums[1:2, :] = ln_sums1[0:1, :]
    ln_sums[3:4, :] = ln_sums1[1:2, :]
    for s in range(4):
        for k, out in ((0, keep_n), (1, give_n)):
            rows = slot_rows(place, s, k)
            out[s, :ROWS, :] = whole[rows, :]
            out[s, ROWS:, :] = jnp.zeros((EXTRA, out.shape[2]), BF)
            out[s, ROWS : ROWS + 8, :LANES] = ln_sums[:, rows].astype(BF)


INWARD, ACROSS, OUTWARD = [(0, 1), (3, 2)], [(1, 2), (2, 1)], [(1, 0), (2, 3)]


def along(value, pairs):
    return lax.ppermute(value, "rep", pairs)


def low_sum(left, right):
    return left[...] + right[...]


def is_middle(place):
    return (place[2] == 1) | (place[2] == 2)


def tick_kernel(has, place, *refs):
    refs = list(refs)
    if has[0]:
        chunk, came = refs.pop(0), refs.pop(0)
    if has[1]:
        before, crossed = refs.pop(0), refs.pop(0)
    if has[2]:
        coming = refs.pop(0)
    half = refs.pop(0) if has[0] else None
    going = refs.pop(0) if has[1] else None

    def half_rows(rows):
        half[rows, :] = low_sum(chunk.at[rows, :], came.at[rows, :])

    def going_rows(rows):
        found = low_sum(before.at[rows, :], crossed.at[rows, :])
        going[rows, :] = jnp.where(is_middle(place), found, coming[rows, :]) if has[2] else found

    for body, out, rows in ((half_rows, half, has[0] and chunk.shape[0]), (going_rows, going, has[1] and before.shape[0])):
        if out is not None:
            loop_rows(rows, 208 if rows % 208 == 0 else 256, body)
            if out.shape[0] > rows:
                out[rows:, :] = coming[rows:, :]


def tick(place, step, last, coming, after=(), joint=False):
    if step is not None and last is not None and not joint:
        (half,) = tick(place, step, None, None, after)
        (going,) = tick(place, None, last, coming, (half,))
        return half, going
    ins, outs = [], []
    for pair in (step, last):
        if pair is not None:
            ins += pair
            outs.append((pair[0].shape if coming is None or pair is step else coming.shape, pair[0].dtype))
    if coming is not None:
        ins.append(coming)
    has = (step is not None, last is not None, coming is not None)
    return call(partial(tick_kernel, has), outs, place, ins, after=after)


def add_small_kernel(place, chunk, small, out):
    rows = chunk.shape[0]
    out[:rows, :] = chunk[...]
    out[rows:, :LANES] = small[...].astype(BF)
    out[rows:, LANES:] = jnp.zeros((SMALL_ROWS, chunk.shape[1] - LANES), BF)


def pick_kernel(place, total, came, o0, o1, o2, o3, *rest):
    heads = o0.shape[2]
    for i, (s, k) in enumerate(SLOTS):
        out = (o0, o1, o2, o3)[s]

        def rows_done(rows):
            here = pl.ds(pl.multiple_of(rows.start + i * ROWS, rows.size), rows.size)
            found = jnp.where(is_middle(place), total[here, :], came[here, :])
            out[k, rows, :] = found[:, :heads]
            if rest:
                rest[0][rows, i * ROWS : (i + 1) * ROWS] = found[:, heads:].astype(F32)

        loop_rows(ROWS, 32, rows_done)


def pick_both_kernel(place, total_f, came_f, total_q, came_q, o0, o1, o2, o3, dense):
    units = total_f.shape[1]
    heads = o0.shape[2] - units
    for i, (s, k) in enumerate(SLOTS):
        out = (o0, o1, o2, o3)[s]

        def rows_done(rows):
            here = pl.ds(pl.multiple_of(rows.start + i * ROWS, rows.size), rows.size)
            out[k, rows, :units] = jnp.where(is_middle(place), total_f[here, :], came_f[here, :])
            found = jnp.where(is_middle(place), total_q[here, :], came_q[here, :])
            out[k, rows, units:] = found[:, :heads]
            dense[rows, i * ROWS : (i + 1) * ROWS] = found[:, heads:].astype(F32)

        loop_rows(ROWS, 32, rows_done)


def pick_both(place, units_pair, heads_pair, heads, after=()):
    columns = units_pair[0].shape[1] + heads
    outs = [((2, ROWS, columns), BF)] * 4 + [((ROWS, 8 * LANES), F32)]
    return call(pick_both_kernel, outs, place, [*units_pair, *heads_pair], after=after)


def pick(place, total, came, heads, after=()):
    outs = [((2, ROWS, heads), BF)] * 4
    if heads < total.shape[1]:
        outs.append(((ROWS, 8 * LANES), F32))
    return call(pick_kernel, outs, place, [total, came], after=after)


def chosen_sum(place, total, outward):
    middle = (place[2] == 1) | (place[2] == 2)
    return jnp.where(middle, total, outward).astype(F32)


def final_call(body, place, ins, shape, layer, before=None, after=()):
    skip = len(after) + (before is not None)

    def run(place, *refs):
        *ins, out, token, found, sems = refs[skip:]
        body(place, ins, out.at[layer], found, sems)
        token[...] = jnp.zeros_like(token)

    return pl.pallas_call(
        run,
        name=body.__name__,
        out_shape=[jax.ShapeDtypeStruct((2,) + shape, F32), jax.ShapeDtypeStruct((8, LANES), F32)],
        in_specs=[pl.BlockSpec(memory_space=pltpu.SMEM)]
        + [pl.BlockSpec(memory_space=pltpu.HBM)] * (before is not None)
        + [pl.BlockSpec(memory_space=pl.ANY)] * len(after)
        + [pl.BlockSpec(memory_space=pltpu.VMEM)] * len(ins),
        out_specs=[pl.BlockSpec(memory_space=pltpu.HBM), pl.BlockSpec(memory_space=pltpu.VMEM)],
        scratch_shapes=[pltpu.VMEM(shape, F32), pltpu.SemaphoreType.DMA((8,))],
        input_output_aliases={} if before is None else {1: 0},
        compiler_params=pltpu.CompilerParams(vmem_limit_bytes=16 * 1024 * 1024),
        cost_estimate=SMALL,
    )(place, *([] if before is None else [before]), *after, *ins)


def final_rows_start(place, total, came, out, found, sems):
    half, rows = total.shape[1], out.shape[0]
    step = rows // 4

    def move(i):
        put = pl.ds(pl.multiple_of(i * step, step), step)
        return pltpu.make_async_copy(found.at[put, :], out.at[put, :], sems.at[i])

    def one(i, carry):
        put = pl.ds(pl.multiple_of(i * step, step), step)
        for j in range(2):
            part = pl.ds(pl.multiple_of(i * step + j * rows, step), step)
            found[put, j * half : (j + 1) * half] = jnp.where(is_middle(place), total[part, :], came[part, :]).astype(F32)
        move(i).start()
        return carry

    lax.fori_loop(0, 4, one, 0)
    return [move(i) for i in range(4)]


def final_rows_kernel(place, ins, out, found, sems):
    for move in final_rows_start(place, *ins, out, found, sems):
        move.wait()


def final_units_kernel(place, blocks, out, found, sems):
    units, moves = out.shape[1] // 8, []
    for i, (s, k) in enumerate(SLOTS):
        put = slice(i * units, (i + 1) * units)
        block = block_of(s, k, blocks)

        def rows_done(rows):
            found[rows, put] = block[rows, :units].astype(F32)

        loop_rows(ROWS, 32, rows_done)
        moves.append(pltpu.make_async_copy(found.at[:, put], out.at[:, slot_rows(place, s, k, units)], sems.at[i]))
        moves[-1].start()
    for move in moves:
        move.wait()


def final_heads_kernel(place, blocks, out, found, sems):
    third = out.shape[1] // 3
    for s, k in SLOTS:
        block = block_of(s, k, blocks)

        def rows_done(rows):
            part = block[rows, block.shape[1] - 3 * LANES :].astype(F32)
            for j in range(3):
                lanes = pl.ds(pl.multiple_of(j * third + slot_start(place, s, k, LANES), LANES), LANES)
                found[rows, lanes] = part[:, j * LANES : (j + 1) * LANES]

        loop_rows(ROWS, 32, rows_done)
    move = pltpu.make_async_copy(found, out, sems.at[0])
    move.start()
    move.wait()


def last_rows_kernel(place, before, total, came, out, gain, shift, bias_fc1, bias_fc2, found, sems):
    rows = slice(total.shape[0] - SMALL_ROWS, total.shape[0])
    small = jnp.where(is_middle(place), total[rows, :LANES], came[rows, :LANES]).astype(F32)
    moves = final_rows_start(place, total, came, out.at[0], found, sems)
    gain[...] = small[0:2, :]
    shift[...] = small[2:4, :]
    bias_fc2[...] = small[4:6, :]
    for layer in range(2):
        for j in range(4):
            bias_fc1[layer : layer + 1, j * LANES : (j + 1) * LANES] = small[8 + 4 * layer + j : 9 + 4 * layer + j, :]
    for move in moves:
        move.wait()


def local_plane(hidden_in, ln_gain, ln_bias, w_qkv, w_dense, w_fc1, b_fc1, w_fc2, b_fc2, output_grad):
    index = lax.axis_index("grp")
    place = jnp.stack([index // 2, index % 2, lax.axis_index("rep")]).astype(jnp.int32)
    span, width = hidden_in.shape[1:]
    seq = span * 8
    units = b_fc1.shape[1]
    own = 3 * LANES
    cosine, sine = rotary_tables(seq)
    hidden0 = hidden_in.reshape(span, width)
    grads1 = output_grad.reshape(span, width)

    wide, column, chunk_shape = ((seq, width), BF), ((seq, LANES), BF), ((seq, units), BF)
    blocks_n, blocks_n0 = ((4, ROWS, width), BF), ((4, ROWS + EXTRA, width), BF)
    blocks_f, blocks_q = ((2, ROWS, units), BF), ((2, ROWS, own), BF)
    mine, mine_low = ((span, width), F32), ((span, width), BF)
    sums_shape, part_shape = ((8, width), F32), ((seq, width), F32)
    head_scratch = [pltpu.VMEM((LANES, seq), BF), pltpu.VMEM((seq, LANES), F32), pltpu.VMEM((seq, LANES), F32)]
    back_scratch = [pltpu.VMEM((seq, own), BF), pltpu.VMEM((width, own), BF), pltpu.VMEM((seq, width), BF)]
    column_scratch = [pltpu.VMEM((seq, LANES), BF)] * 3
    units_scratch = [pltpu.VMEM((seq, units), BF), pltpu.VMEM((width, units), BF)]

    rows = [hidden0.shape, ln_gain.shape, ln_bias.shape, b_fc2.shape, w_qkv.shape[1:], (HALF, w_fc1.shape[2])]
    rows = [rows[0], *rows[4:], *rows[1:4]]
    packed = pl.pallas_call(
        pack_first_kernel,
        name="pack_first_kernel",
        out_shape=[jax.ShapeDtypeStruct((FIRST_ROWS, LANES), BF)] * 4,
        in_specs=[pl.BlockSpec(memory_space=pltpu.HBM)] * 6,
        out_specs=[pl.BlockSpec(memory_space=pltpu.VMEM)] * 4,
        scratch_shapes=[pltpu.VMEM(shape, BF) for shape in rows] + [pltpu.SemaphoreType.DMA((6,))],
        compiler_params=pltpu.CompilerParams(vmem_limit_bytes=60 * 1024 * 1024),
        cost_estimate=SMALL,
    )(hidden0, w_qkv, w_fc1, ln_gain, ln_bias, b_fc2)
    first = send_blocks(place, packed)
    packed = call(partial(pack_units_grads_kernel, 1), [((3 * ROWS, units), BF)] * 4, place, [w_fc1, grads1])
    keep, give = call(partial(pack_heads_kernel, 1), [((4, ROWS, own), BF)] * 2, place, [w_qkv], after=[packed[0]])
    pairs1 = call(pair_kernel, [blocks_q] * 4, place, [keep, swap(give, 1)])
    (others0,) = call(others_first_kernel, [((4, OTHERS_ROWS, LANES), BF)], place, first, after=[pairs1[0]])
    units1 = send_blocks(place, packed)
    first = [*first, swap(others0, 1)]
    (near0,) = call(near_first_kernel, [((8, HALF_ROWS, LANES), BF)], place, first)
    far0 = along(near0, INWARD + OUTWARD)

    normed0, xhat0, weight_q0, params, q0, k0, v0, att0, log0 = call(
        first_attend_kernel,
        [wide, wide, ((width, own), BF), ((EXTRA, width), F32), column, column, column, column, ((8, seq), F32)],
        place,
        [*first, cosine, sine],
        [pltpu.VMEM((LANES, seq), BF)],
        after=[near0],
    )
    weight_f0, act0, slope0, partial_sum = call(
        first_units_kernel,
        [((width, units), BF), ((seq, units), BF), ((seq, units), F32), wide],
        place,
        [normed0, near0, far0, b_fc1, w_fc2, w_dense, att0],
    )
    (near1,) = call(near_units_kernel, [((4, ROWS, units), BF)], place, units1, after=[partial_sum])
    far1 = along(near1, INWARD + OUTWARD)
    keep, give = call(split_kernel, [blocks_n, blocks_n], place, [partial_sum], after=[near1])
    terms, sent = begin_scatter(place, keep, give)
    (others1,) = call(others_units_grads_kernel, [((4, 3 * ROWS, units), BF)], place, [*units1, far1], after=terms[2:])
    hidden1, normed1_own = call(next_hidden_kernel, [mine, mine_low], place, [*terms, hidden0, params], after=[others1])
    pieces = gather_pieces(normed1_own)

    weight_f1, grad_branch1 = call(
        second_ready_kernel, [((width, units), BF), wide], place, [*units1, swap(others1, 1), far1]
    )
    normed1, act1, pre1, chunk1 = call(
        second_units_kernel,
        [wide, ((seq, units), BF), ((seq, units), F32), chunk_shape],
        place,
        [*pieces, b_fc1, weight_f1, grad_branch1],
    )
    came1 = along(chunk1, INWARD)
    heads1 = send_blocks(place, pairs1)
    chunk2, sums1, part_normed, grad_att1 = call(
        second_units_back_kernel,
        [chunk_shape, sums_shape, part_shape, column],
        place,
        [grad_branch1, w_fc2, w_dense, pre1, normed1, weight_f1],
        units_scratch,
    )
    att1, mixed1, keep, give = call(
        second_attend_kernel,
        [column, ((seq, own), BF), blocks_n, blocks_n],
        place,
        [normed1, *heads1, cosine, sine, grad_att1, part_normed],
        [
            pltpu.VMEM((width, own), BF),
            *column_scratch,
            pltpu.VMEM((LANES, seq), BF),
            *head_scratch,
        ],
    )
    terms, sent = begin_scatter(place, keep, give)
    (half1,) = tick(place, (chunk1, came1), None, None, after=[give])
    (chunk3,) = call(
        second_heads_kernel,
        [chunk_shape],
        place,
        [normed1, mixed1, att1, grad_branch1],
        [pltpu.VMEM((width, own), BF)],
        after=[half1, sent],
    )
    cross1, came2 = along(half1, ACROSS), along(chunk2, INWARD)
    grads0, grads0_low, ln_sums1 = call(
        second_norm_back_kernel, [mine, mine_low, sums_shape], place, [*terms, hidden1, params, grads1], after=[half1]
    )

    keep_h, give_h, keep_e, give_e = call(
        last_hidden_kernel,
        [((4, ROWS, width // 2), BF)] * 4,
        place,
        [act1, att1, w_fc2, w_dense],
        [pltpu.VMEM((seq, width), BF)],
        after=[chunk3],
    )
    pieces = gather_pieces(grads0_low)
    half2, total1 = tick(place, (chunk2, came2), (half1, cross1), chunk3, after=[grads0_low, give_h])
    cross2, came3 = along(half2, ACROSS), along(total1, INWARD + OUTWARD)
    grad_branch0, chunk6, chunk4, sums0, part_normed = call(
        first_units_back_kernel,
        [wide, chunk_shape, chunk_shape, sums_shape, part_shape],
        place,
        [*pieces, act0, w_fc2, slope0, normed0, weight_f0],
        units_scratch,
        after=[half2],
    )
    half3, total2 = tick(place, (chunk3, came3), (half2, cross2), chunk4)
    cross3, came4 = along(half3, ACROSS), along(total2, INWARD + OUTWARD)
    chunk5, keep, give = call(
        first_attend_back_kernel,
        [chunk_shape, blocks_n0, blocks_n0],
        place,
        [grad_branch0, w_dense, att0, q0, k0, v0, log0, cosine, sine, normed0, xhat0, weight_q0, part_normed, ln_sums1],
        [*head_scratch, *back_scratch, pltpu.VMEM((8, width), F32)],
        after=[half3],
    )
    token = ((8, LANES), F32)
    terms_h, _ = begin_scatter(place, keep_h, give_h, after=[chunk5])
    out_fc2, done = final_call(final_rows_kernel, place, [total1, came3], (units, width), 1, after=[give])
    hidden_half, done_h = call(
        last_sum_kernel, [((span, width // 2), F32), ((8, LANES), F32)], place, [*terms_h, hidden1, params], after=[done]
    )
    half4, total3 = tick(place, (chunk4, came4), (half3, cross3), chunk5, after=[done_h])
    cross4, came5 = along(half4, ACROSS), along(total3, INWARD + OUTWARD)
    terms, _ = begin_scatter(place, keep, give, after=[half4])
    input_grad, small_sums = call(
        first_norm_back_kernel,
        [mine, ((SMALL_ROWS, LANES), F32)],
        place,
        [*terms, hidden0, params, grads0, sums0, sums1],
    )
    (chunk6,) = call(add_small_kernel, [((seq + SMALL_ROWS, units), BF)], place, [chunk6, small_sums])
    half5, total4 = tick(place, (chunk5, came5), (half4, cross4), chunk6, joint=True)
    cross5, came6 = along(half5, ACROSS), along(total4, INWARD + OUTWARD)
    *picked1, dense1 = pick_both(place, (total2, came4), (total3, came5), own, after=[half5])
    blocks1 = swap_others(place, send_blocks(place, picked1))
    half6, total5 = tick(place, (chunk6, came6), (half5, cross5), None, after=[blocks1[1]], joint=True)
    cross6, came7 = along(half6, ACROSS), along(total5, OUTWARD)
    picked4 = pick(place, total4, came6, units, after=[half6])
    out_fc1, done1 = final_call(final_units_kernel, place, blocks1, (ROWS, w_fc1.shape[2]), 1, after=[picked4[0]])
    out_qkv, done3 = final_call(final_heads_kernel, place, blocks1, (ROWS, w_qkv.shape[2]), 1, after=[done1])
    blocks4 = swap_others(place, send_blocks(place, picked4), after=[done3])
    (total6,) = tick(place, None, (half6, cross6), None, after=[blocks4[1]])
    came8 = along(total6, OUTWARD)
    *picked5, dense0 = pick(place, total5, came7, own, after=[total6])
    out_fc1, done4 = final_call(final_units_kernel, place, blocks4, (ROWS, w_fc1.shape[2]), 0, out_fc1, after=[picked5[0]])
    terms, _ = begin_scatter(place, keep_e, give_e, after=[total6])
    hidden_out, done_h = call(
        last_join_kernel, [mine, token], place, [*terms, hidden1, params, hidden_half], after=[picked5[0]]
    )
    blocks5 = swap_others(place, send_blocks(place, picked5), after=[done4, done_h])
    out_qkv, done5 = final_call(final_heads_kernel, place, blocks5, (ROWS, w_qkv.shape[2]), 0, out_qkv)
    vector = jax.ShapeDtypeStruct((2, LANES), F32)
    out_fc2, out_gain, out_shift, out_b_fc1, out_b_fc2 = pl.pallas_call(
        lambda place, before, token, *refs: last_rows_kernel(place, before, *refs),
        name="last_rows_kernel",
        out_shape=[jax.ShapeDtypeStruct((2, units, width), F32), vector, vector, jax.ShapeDtypeStruct((2, units), F32), vector],
        in_specs=[pl.BlockSpec(memory_space=pltpu.SMEM), pl.BlockSpec(memory_space=pltpu.HBM)]
        + [pl.BlockSpec(memory_space=pl.ANY)]
        + [pl.BlockSpec(memory_space=pltpu.VMEM)] * 2,
        out_specs=[pl.BlockSpec(memory_space=pltpu.HBM)] + [pl.BlockSpec(memory_space=pltpu.VMEM)] * 4,
        scratch_shapes=[pltpu.VMEM((units, width), F32), pltpu.SemaphoreType.DMA((4,))],
        input_output_aliases={1: 0},
        compiler_params=pltpu.CompilerParams(vmem_limit_bytes=16 * 1024 * 1024),
        cost_estimate=SMALL,
    )(place, out_fc2, done5, total6, came8)
    out_dense = jnp.stack([dense0, dense1])
    return (
        hidden_out[None],
        input_grad[None],
        out_gain,
        out_shift,
        out_qkv,
        out_dense,
        out_fc1,
        out_b_fc1,
        out_fc2,
        out_b_fc2,
    )


def local(hidden_in, ln_gain, ln_bias, w_qkv, w_dense, w_fc1, b_fc1, w_fc2, b_fc2, output_grad):
    arguments = (hidden_in, ln_gain, ln_bias, w_qkv, w_dense, w_fc1, b_fc1, w_fc2, b_fc2, output_grad)
    plane = lax.axis_size("grp") == 8 and lax.axis_size("rep") == 4
    plane = plane and hidden_in.shape[:2] == (1, ROWS) and w_qkv.shape == (2, LANES, 3 * 8 * LANES)
    return (local_plane if plane else local_any)(*arguments)


def solution(mesh):
    in_specs = (
        P("rep", "grp", None),
        P(None, "grp"),
        P(None, "grp"),
        P(None, "grp", None),
        P(None, "grp", None),
        P(None, "grp", None),
        P(None, "grp"),
        P(None, "grp", None),
        P(None, "grp"),
        P("rep", "grp", None),
    )
    out_specs = (
        P("rep", "grp", None),
        P("rep", "grp", None),
        P(None, "grp"),
        P(None, "grp"),
        P(None, "grp", None),
        P(None, "grp", None),
        P(None, "grp", None),
        P(None, "grp"),
        P(None, "grp", None),
        P(None, "grp"),
    )
    return jax.shard_map(local, mesh=mesh, in_specs=in_specs, out_specs=out_specs, check_vma=False)
```

```python
from functools import partial

import jax
import jax.numpy as jnp
import numpy as np
from jax import lax
from jax.experimental import pallas as pl
from jax.experimental.pallas import tpu as pltpu
from jax.sharding import PartitionSpec as P

HEAD_DIM = 64
ROT = 32
LANES = 128

EPSILON = 1e-05
SCORE_SCALE = 0.125
NEGATIVE = -1000000000.0
BF = jnp.bfloat16
F32 = jnp.float32


def dot(left, right):
    return jnp.dot(left, right, preferred_element_type=F32)


def dot_general(left, right, contract):
    return lax.dot_general(left, right, ((contract[:1], contract[1:]), ((), ())), preferred_element_type=F32)


def outer_sum(left, right):
    return dot_general(left, right, (0, 0))


def times_transposed(left, right):
    return dot_general(left, right, (1, 1))


def head_mask(head):
    lane = lax.broadcasted_iota(jnp.int32, (1, LANES), 1)
    return (lane >= head * HEAD_DIM) & (lane < (head + 1) * HEAD_DIM)


def turn(part, cosine, sine, sign):
    even = lax.broadcasted_iota(jnp.int32, part.shape, 1) % 2 == 0
    partner = jnp.where(even, pltpu.roll(part, LANES - 1, 1), pltpu.roll(part, 1, 1))
    return part * cosine + partner * (sine * sign)


def mask_diagonal(scores, block):
    keys, queries = scores.shape
    key_place = lax.broadcasted_iota(jnp.int32, (block, queries), 0)
    query_place = lax.broadcasted_iota(jnp.int32, (block, queries), 1)
    last = jnp.where(key_place <= query_place, scores[keys - block :], NEGATIVE)
    if keys == block:
        return last
    return jnp.concatenate([scores[: keys - block], last], axis=0)


def attend_kernel(heads, block, mix_q, mix_k, mix_v, cosine, sine, q_out, k_out, v_out, att_out, log_out):
    seq = mix_q.shape[0]
    q_out[...] = turn(mix_q[...], cosine[...], sine[...], 1.0).astype(BF)
    k_out[...] = turn(mix_k[...], cosine[...], sine[...], 1.0).astype(BF)
    v_out[...] = mix_v[...].astype(BF)
    values_down = mix_v[...].T.astype(BF)
    for start in range(0, seq, block):
        stop = start + block
        queries = q_out[start:stop, :] * SCORE_SCALE
        keys = k_out[:stop, :]
        total = jnp.zeros((LANES, block), F32)
        for head in range(heads):
            chosen = jnp.where(head_mask(head), queries, 0.0).astype(BF)
            scores = mask_diagonal(dot_general(keys, chosen, (1, 1)), block)
            row_max = jnp.max(scores, axis=0, keepdims=True)
            exponent = jnp.exp(scores - row_max)
            row_total = jnp.sum(exponent, axis=0, keepdims=True)
            probabilities = (exponent * (1.0 / row_total)).astype(BF)
            log_out[head : head + 1, start:stop] = row_max + jnp.log(row_total)
            found = dot(values_down[:, :stop], probabilities)
            down = lax.broadcasted_iota(jnp.int32, (LANES, 1), 0)
            own = (down >= head * HEAD_DIM) & (down < (head + 1) * HEAD_DIM)
            total = total + jnp.where(own, found, 0.0)
        att_out[start:stop, :] = total.T.astype(BF)


def attend_back_kernel(heads, block, q_in, k_in, v_in, grad_att, log_in, cosine, sine, q_out, k_out, v_out, k_sum, v_sum):
    seq = q_in.shape[0]
    k_sum[...] = jnp.zeros_like(k_sum)
    v_sum[...] = jnp.zeros_like(v_sum)
    keys_down = (k_in[...].astype(F32) * SCORE_SCALE).T.astype(BF)
    for start in range(0, seq, block):
        stop = start + block
        queries = q_in[start:stop, :] * SCORE_SCALE
        grads = grad_att[start:stop, :]
        grad_queries = jnp.zeros((LANES, block), F32)
        for head in range(heads):
            chosen = jnp.where(head_mask(head), queries, 0.0).astype(BF)
            chosen_grads = jnp.where(head_mask(head), grads, 0.0).astype(BF)
            scores = mask_diagonal(dot_general(k_in[:stop, :], chosen, (1, 1)), block)
            probabilities = jnp.exp(scores - log_in[head : head + 1, start:stop])
            grad_probs = dot_general(v_in[:stop, :], chosen_grads, (1, 1))
            row_inner = jnp.sum(grad_probs * probabilities, axis=0, keepdims=True)
            grad_scores = (probabilities * (grad_probs - row_inner)).astype(BF)
            k_sum[:stop, :] += dot(grad_scores, chosen)
            v_sum[:stop, :] += dot(probabilities.astype(BF), chosen_grads)
            down = lax.broadcasted_iota(jnp.int32, (LANES, 1), 0)
            own = (down >= head * HEAD_DIM) & (down < (head + 1) * HEAD_DIM)
            grad_queries = grad_queries + jnp.where(own, dot(keys_down[:, :stop], grad_scores), 0.0)
        q_out[start:stop, :] = turn(
            grad_queries.T, cosine[start:stop, :], sine[start:stop, :], -1.0
        ).astype(BF)
    k_out[...] = turn(k_sum[...], cosine[...], sine[...], -1.0).astype(BF)
    v_out[...] = v_sum[...].astype(BF)


VMEM_LIMIT = 48 * 1024 * 1024


def attend(mix_q, mix_k, mix_v, heads, cosine, sine):
    seq = mix_q.shape[0]
    out = jax.ShapeDtypeStruct((seq, LANES), BF)
    return pl.pallas_call(
        partial(attend_kernel, heads, min(256, seq)),
        out_shape=(out, out, out, out, jax.ShapeDtypeStruct((heads, seq), F32)),
        compiler_params=pltpu.CompilerParams(vmem_limit_bytes=VMEM_LIMIT),
    )(mix_q, mix_k, mix_v, cosine, sine)


def attend_back(queries, keys, values, grad_att, log_total, heads, cosine, sine):
    seq = queries.shape[0]
    out = jax.ShapeDtypeStruct((seq, LANES), BF)
    return pl.pallas_call(
        partial(attend_back_kernel, heads, min(256, seq)),
        out_shape=(out, out, out),
        scratch_shapes=[pltpu.VMEM((seq, LANES), F32), pltpu.VMEM((seq, LANES), F32)],
        compiler_params=pltpu.CompilerParams(vmem_limit_bytes=VMEM_LIMIT),
    )(queries, keys, values, grad_att, log_total, cosine, sine)


def rotary_tables(seq):
    frequency = (1.0 / 10000.0 ** (np.arange(ROT // 2, dtype=np.float32) * 2.0 / ROT)).astype(np.float32)
    angles = np.arange(seq, dtype=np.float32)[:, None] * frequency[None, :]
    cosine, sine = np.cos(angles.astype(np.float64)), np.sin(angles.astype(np.float64))
    cosine = np.repeat(cosine, 2, axis=1)
    sine = np.repeat(sine, 2, axis=1) * np.tile([-1.0, 1.0], ROT // 2)
    rest = HEAD_DIM - ROT
    cosine = np.concatenate([cosine, np.ones((seq, rest))], axis=1)
    sine = np.concatenate([sine, np.zeros((seq, rest))], axis=1)
    repeats = (1, LANES // HEAD_DIM)
    return np.tile(cosine, repeats).astype(np.float32), np.tile(sine, repeats).astype(np.float32)


def swap(value, bits):
    return lax.ppermute(value, "grp", [(i, i ^ bits) for i in range(8)])


def add_low(left, right):
    return (left.astype(F32) + right.astype(F32)).astype(BF)


def by_chip(parts, chip):
    x, y = chip % 2 == 1, chip // 2 == 1
    near = jnp.where(x, jnp.stack([parts[1], parts[0]]), jnp.stack([parts[0], parts[1]]))
    far = jnp.where(x, jnp.stack([parts[3], parts[2]]), jnp.stack([parts[2], parts[3]]))
    return jnp.where(y, jnp.concatenate([far, near]), jnp.concatenate([near, far]))


def gather_rows(part):
    size = lax.axis_size("grp")
    if size != 8:
        return lax.all_gather(part, "grp", axis=0, tiled=True)
    rows, width = part.shape
    half = rows // 2
    index = lax.axis_index("grp")
    along_x, along_y = swap(part, 2), swap(part, 4)
    corner = jnp.concatenate([swap(along_y[:half], 2), swap(along_x[half:], 4)])
    mine = by_chip([part, along_x, along_y, corner], index // 2)
    other = swap(mine, 1)
    odd = index % 2 == 1
    both = jnp.stack([jnp.where(odd, other, mine), jnp.where(odd, mine, other)], axis=1)
    return both.reshape(8 * rows, width)


def scatter_sum(whole):
    size = lax.axis_size("grp")
    if size != 8:
        return lax.psum_scatter(whole, "grp", scatter_dimension=0, tiled=True).astype(F32)
    rows, width = whole.shape[0] // 8, whole.shape[1]
    half = rows // 2
    index = lax.axis_index("grp")
    chip, core = index // 2, index % 2
    blocks = whole.reshape(4, 2, rows, width)
    keep = lax.dynamic_index_in_dim(blocks, core, 1, False)
    give = lax.dynamic_index_in_dim(blocks, 1 - core, 1, False)
    summed = add_low(keep, swap(give, 1))
    own, for_x, for_y, corner = [lax.dynamic_index_in_dim(summed, chip ^ s, 0, False) for s in range(4)]
    by_x, by_y = swap(corner[:half], 2), swap(corner[half:], 4)
    for_y = jnp.concatenate([add_low(for_y[:half], by_x), for_y[half:]])
    for_x = jnp.concatenate([for_x[:half], add_low(for_x[half:], by_y)])
    return own.astype(F32) + swap(for_y, 4).astype(F32) + swap(for_x, 2).astype(F32)


def exchange(blocks):
    size = lax.axis_size("grp")
    if size != 8:
        return lax.all_to_all(blocks, "grp", 0, 0)
    index = lax.axis_index("grp")
    chip, core = index // 2, index % 2
    pairs = blocks.reshape((4, 2) + blocks.shape[1:])
    keep = lax.dynamic_index_in_dim(pairs, core, 1, False)
    give = lax.dynamic_index_in_dim(pairs, 1 - core, 1, False)
    came = swap(give, 1)
    odd = core == 1
    both = jnp.stack([jnp.where(odd, came, keep), jnp.where(odd, keep, came)], axis=1)
    parts = [lax.dynamic_index_in_dim(both, chip ^ s, 0, False) for s in range(4)]
    parts = [parts[0]] + [swap(parts[s], 2 * s) for s in (1, 2, 3)]
    return by_chip(parts, chip).reshape(blocks.shape)


def rep_sum(part):
    if lax.axis_size("rep") != 4:
        return lax.psum(part, "rep").astype(F32)
    place = lax.axis_index("rep")
    inward = lax.ppermute(part, "rep", [(0, 1), (3, 2)])
    half_sum = add_low(part, inward)
    across = lax.ppermute(half_sum, "rep", [(1, 2), (2, 1)])
    total = add_low(half_sum, across)
    outward = lax.ppermute(total, "rep", [(1, 0), (2, 3)])
    return jnp.where((place == 1) | (place == 2), total, outward).astype(F32)


def columns_of(w_qkv, w_fc1, group):
    rows, qkv = w_qkv.shape
    heads = w_qkv.reshape(rows, 3, group, qkv // 3 // group).transpose(2, 0, 1, 3).reshape(group, rows, -1)
    units = w_fc1.reshape(rows, group, -1).transpose(1, 0, 2)
    found = exchange(jnp.concatenate([heads, units], axis=2))
    found = found.reshape(group * rows, -1)
    return found[:, : qkv // group], found[:, qkv // group :]


def rows_of(grad_qkv, grad_fc1, group):
    rows = grad_qkv.shape[0] // group
    both = jnp.concatenate([grad_qkv, grad_fc1], axis=1).reshape(group, rows, -1)
    found = exchange(both)
    qkv = grad_qkv.shape[1]
    heads = found[:, :, :qkv].reshape(group, rows, 3, qkv // 3).transpose(1, 2, 0, 3).reshape(rows, -1)
    units = found[:, :, qkv:].transpose(1, 0, 2).reshape(rows, -1)
    return heads, units


def standardize(hidden):
    centered = hidden - jnp.mean(hidden, axis=-1, keepdims=True)
    scale = lax.rsqrt(jnp.mean(centered * centered, axis=-1, keepdims=True) + EPSILON)
    return centered * scale, scale


def widen(part):
    return jnp.pad(part, ((0, 0), (0, LANES - part.shape[1])))


def forward_layer(normed, weights, heads, tables):
    qkv_cols, fc1_cols, b_fc1, w_dense, w_fc2 = weights
    mixed = dot(normed, qkv_cols)
    own = heads * HEAD_DIM
    queries, keys, values, attended, log_total = attend(
        *(widen(mixed[:, i * own : (i + 1) * own]) for i in range(3)), heads, *tables
    )
    pre_act = dot(normed, fc1_cols) + b_fc1.astype(F32)
    activation = jax.nn.gelu(pre_act, approximate=True).astype(BF)
    partial_sum = (dot(attended[:, :own], w_dense) + dot(activation, w_fc2)).astype(BF)
    stored = (normed, queries, keys, values, attended, log_total, pre_act, activation)
    return partial_sum, stored


def backward_layer(grad_branch, weights, stored, heads, tables):
    qkv_cols, fc1_cols, b_fc1, w_dense, w_fc2 = weights
    normed, queries, keys, values, attended, log_total, pre_act, activation = stored
    own = heads * HEAD_DIM
    grad_w_fc2 = outer_sum(activation, grad_branch).astype(BF)
    grad_w_dense = outer_sum(attended[:, :own], grad_branch).astype(BF)
    _, gelu_back = jax.vjp(partial(jax.nn.gelu, approximate=True), pre_act)
    grad_pre = gelu_back(times_transposed(grad_branch, w_fc2))[0].astype(BF)
    grad_attended = widen(times_transposed(grad_branch, w_dense).astype(BF))
    grad_mixed = attend_back(queries, keys, values, grad_attended, log_total, heads, *tables)
    grad_mixed = jnp.concatenate([part[:, :own] for part in grad_mixed], axis=1)
    grad_fc1 = outer_sum(normed, grad_pre).astype(BF)
    grad_b_fc1 = jnp.sum(grad_pre.astype(F32), axis=0)
    grad_qkv = outer_sum(normed, grad_mixed).astype(BF)
    grad_normed = (times_transposed(grad_pre, fc1_cols) + times_transposed(grad_mixed, qkv_cols)).astype(BF)
    return grad_normed, (grad_w_fc2, grad_w_dense, grad_fc1, grad_qkv, grad_b_fc1)


def local_any(hidden_in, ln_gain, ln_bias, w_qkv, w_dense, w_fc1, b_fc1, w_fc2, b_fc2, output_grad):
    group = lax.axis_size("grp")
    index = lax.axis_index("grp")
    layers = w_qkv.shape[0]
    span, width = hidden_in.shape[1:]
    seq = span * group
    heads = width // HEAD_DIM // group
    tables = rotary_tables(seq)
    small = jnp.concatenate([ln_gain, ln_bias, b_fc2])
    small = lax.all_gather(small, "grp", axis=1, tiled=True).astype(F32)
    gains, shifts, b_fc2_all = small[:layers], small[layers : 2 * layers], small[2 * layers :]
    hidden = hidden_in.reshape(span, width).astype(F32)
    hidden_all = gather_rows(hidden_in.reshape(span, width))
    weights = []
    for layer in range(layers):
        qkv_cols, fc1_cols = columns_of(w_qkv[layer], w_fc1[layer], group)
        weights.append((qkv_cols, fc1_cols, b_fc1[layer], w_dense[layer], w_fc2[layer]))

    inputs, stored_layers = [], []
    for layer in range(layers):
        inputs.append(hidden)
        if layer == 0:
            normed = (standardize(hidden_all.astype(F32))[0] * gains[0] + shifts[0]).astype(BF)
        else:
            normed = gather_rows((standardize(hidden)[0] * gains[layer] + shifts[layer]).astype(BF))
        partial_sum, stored = forward_layer(normed, weights[layer], heads, tables)
        stored_layers.append(stored)
        hidden = hidden + scatter_sum(partial_sum) + b_fc2_all[layer]

    grad_hidden = output_grad.reshape(span, width)
    small_grads, large_grads = [None] * layers, [None] * layers
    for layer in reversed(range(layers)):
        grad_low = grad_hidden.astype(BF)
        grad_branch = gather_rows(grad_low)
        grad_normed, found = backward_layer(grad_branch, weights[layer], stored_layers[layer], heads, tables)
        grad_w_fc2, grad_w_dense, grad_fc1, grad_qkv, grad_b_fc1 = found
        grad_qkv, grad_fc1 = rows_of(grad_qkv, grad_fc1, group)
        large_grads[layer] = tuple(rep_sum(part) for part in (grad_w_fc2, grad_w_dense, grad_fc1, grad_qkv))
        grad_normed = scatter_sum(grad_normed)
        xhat, scale = standardize(inputs[layer])
        inner = grad_normed * gains[layer]
        mean_inner = jnp.mean(inner, axis=-1, keepdims=True)
        mean_along = jnp.mean(inner * xhat, axis=-1, keepdims=True)
        small_grads[layer] = jnp.concatenate(
            [
                jnp.sum(grad_normed * xhat, axis=0),
                jnp.sum(grad_normed, axis=0),
                jnp.sum(grad_low.astype(F32), axis=0),
                lax.dynamic_update_slice(
                    jnp.zeros((group * grad_b_fc1.shape[0],), F32), grad_b_fc1, (index * grad_b_fc1.shape[0],)
                ),
            ]
        )
        grad_hidden = grad_hidden + (inner - mean_inner - xhat * mean_along) * scale

    summed = lax.psum(jnp.stack(small_grads), ("rep", "grp"))
    own = width // group
    units = b_fc1.shape[1]

    def pick(start, count):
        return lax.dynamic_slice_in_dim(summed, start + index * count, count, 1)

    stacked = [jnp.stack([large_grads[layer][member] for layer in range(layers)]) for member in range(4)]
    return (
        hidden[None],
        grad_hidden[None],
        pick(0, own),
        pick(width, own),
        stacked[3],
        stacked[1],
        stacked[2],
        pick(3 * width, units),
        stacked[0],
        pick(2 * width, own),
    )


SLOTS = [(s, k) for s in range(4) for k in range(2)]
ROWS = 128
EXTRA = 16


def slot_start(place, s, k, size):
    return pl.multiple_of(((place[0] ^ s) * 2 + (place[1] ^ k)) * size, size)


def slot_rows(place, s, k, size=ROWS):
    return pl.ds(slot_start(place, s, k, size), size)


SMALL = pl.CostEstimate(flops=0, bytes_accessed=0, transcendentals=0)


def call(body, outs, place, ins, scratch=(), after=(), hbm=0, mib=16):
    def run(place, *refs):
        body(place, *refs[len(after) :])

    return pl.pallas_call(
        run,
        name=getattr(body, "func", body).__name__,
        out_shape=[jax.ShapeDtypeStruct(*out) for out in outs],
        in_specs=[pl.BlockSpec(memory_space=pltpu.SMEM)]
        + [pl.BlockSpec(memory_space=pl.ANY)] * len(after)
        + [pl.BlockSpec(memory_space=pltpu.HBM)] * hbm
        + [pl.BlockSpec(memory_space=pltpu.VMEM)] * (len(ins) - hbm),
        out_specs=[pl.BlockSpec(memory_space=pltpu.VMEM)] * len(outs),
        scratch_shapes=list(scratch),
        compiler_params=pltpu.CompilerParams(vmem_limit_bytes=mib * 1024 * 1024),
        cost_estimate=SMALL,
    )(place, *after, *ins)


def gather_pieces(part):
    mine = [part, swap(part, 2), swap(part, 4), swap(part, 6)]
    other = [swap(piece, 1) for piece in mine]
    return [piece for pair in zip(mine, other) for piece in pair]


def put_columns(out, start, value):
    rows = value.shape[0]
    for b in range(value.shape[1] // LANES):
        out[start + b * rows : start + (b + 1) * rows, :] = value[:, b * LANES : (b + 1) * LANES]


def heads_of(place, w_qkv, layer, s, k, j):
    start = j * (w_qkv.shape[2] // 3) + slot_start(place, s, k, LANES)
    return w_qkv[layer, :, pl.ds(pl.multiple_of(start, LANES), LANES)]


HALF = ROWS // 2
HEADS_ROWS, HALF_ROWS = 3 * ROWS, 4 * HALF
FIRST_MINE = 8 * ROWS
FIRST_OTHERS = FIRST_MINE + HEADS_ROWS + HALF_ROWS
FIRST_SMALL = FIRST_OTHERS + HEADS_ROWS + HALF_ROWS
FIRST_ROWS = FIRST_SMALL + EXTRA
OTHERS_MINE = 8 * ROWS
OTHERS_SMALL = OTHERS_MINE + HEADS_ROWS + HALF_ROWS
OTHERS_ROWS = OTHERS_SMALL + EXTRA


def half_start(place, other):
    parity = place[2] & 1
    return pl.multiple_of((1 - parity if other else parity) * HALF, HALF)


def pack_first_kernel(hidden_from, qkv_from, fc1_from, gain_from, shift_from, bias_from, o0, o1, o2, o3, hidden, w_qkv, w_fc1, gain, shift, bias, sems):
    index = lax.axis_index("grp")
    place = (index // 2, index % 2, lax.axis_index("rep"))
    outs = (o0, o1, o2, o3)
    pairs = (
        (hidden_from, hidden),
        (gain_from, gain),
        (shift_from, shift),
        (bias_from, bias),
        (qkv_from.at[0], w_qkv),
        (fc1_from.at[0, pl.ds(half_start(place, False), HALF), :], w_fc1),
    )
    moves = [pltpu.make_async_copy(*pair, sems.at[i]) for i, pair in enumerate(pairs)]
    for move in moves:
        move.start()
    for move in moves[:4]:
        move.wait()
    for out in outs:
        put_columns(out, 0, hidden[...])
        out[FIRST_SMALL:, :] = jnp.zeros((EXTRA, LANES), BF)
        for i, part in enumerate((gain, shift, bias)):
            out[FIRST_SMALL + 2 * i : FIRST_SMALL + 2 * i + 2, :] = part[...]
    moves[4].wait()
    third = w_qkv.shape[1] // 3
    for s, k in SLOTS:
        row = (FIRST_MINE, FIRST_OTHERS)[k]
        for j in range(3):
            lanes = pl.ds(pl.multiple_of(j * third + slot_start(place, s, k, LANES), LANES), LANES)
            outs[s][row + j * ROWS : row + (j + 1) * ROWS, :] = w_qkv[:, lanes]
    moves[5].wait()
    for s, k in SLOTS:
        row = (FIRST_MINE, FIRST_OTHERS)[k] + HEADS_ROWS
        put_columns(outs[s], row, w_fc1[:, pl.ds(slot_start(place, s, k, 4 * LANES), 4 * LANES)])


def others_first_kernel(place, b0, b1, b2, b3, out):
    for s, block in enumerate((b0, b1, b2, b3)):
        out[s, :OTHERS_MINE, :] = block[:FIRST_MINE, :]
        out[s, OTHERS_MINE:OTHERS_SMALL, :] = block[FIRST_OTHERS:FIRST_SMALL, :]
        out[s, OTHERS_SMALL:, :] = block[FIRST_SMALL:, :]


def near_first_kernel(place, b0, b1, b2, b3, b4, out):
    for i, (s, k) in enumerate(SLOTS):
        block, mine_at, _ = first_block(s, k, (b0, b1, b2, b3, b4))
        out[i] = block[mine_at + HEADS_ROWS : mine_at + HEADS_ROWS + HALF_ROWS, :]


def first_block(s, k, blocks):
    if k:
        return blocks[4].at[s], OTHERS_MINE, OTHERS_SMALL
    return blocks[s], FIRST_MINE, FIRST_SMALL


def pack_heads_kernel(layer, place, w_qkv, keep, give):
    for s, k in SLOTS:
        for j in range(3):
            (keep, give)[k][s, :, j * LANES : (j + 1) * LANES] = heads_of(place, w_qkv, layer, s, k, j)


def pair_kernel(place, keep, came, *outs):
    for s, out in enumerate(outs):
        out[0], out[1] = keep[s], came[s]


def pack_units_kernel(layer, place, w_fc1, *outs):
    units = outs[0].shape[2]
    for s, k in SLOTS:
        outs[s][k] = w_fc1[layer, :, pl.ds(slot_start(place, s, k, units), units)]


def pack_units_grads_kernel(layer, place, w_fc1, grads, *outs):
    units = outs[0].shape[1]
    low = grads[...].astype(BF)
    for s in range(4):
        for k in range(2):
            lanes = pl.ds(slot_start(place, s, k, units), units)
            outs[s][k * HALF : (k + 1) * HALF, :] = w_fc1[layer, pl.ds(half_start(place, False), HALF), lanes]
            outs[s][(1 + k) * ROWS : (2 + k) * ROWS, :] = low[:, k * units : (k + 1) * units]


def near_units_kernel(place, b0, b1, b2, b3, out):
    for s, block in enumerate((b0, b1, b2, b3)):
        out[s] = block[:ROWS, :]


def others_units_grads_kernel(place, b0, b1, b2, b3, far, out):
    for s, block in enumerate((b0, b1, b2, b3)):
        out[s, :HALF, :] = block[HALF:ROWS, :]
        out[s, HALF:ROWS, :] = far[s, HALF:, :]
        out[s, ROWS:, :] = block[ROWS:, :]


def send_blocks(place, packed):
    return [packed[0]] + [swap(packed[s], 2 * s) for s in (1, 2, 3)]


def others_kernel(place, b0, b1, b2, b3, out):
    for s, block in enumerate((b0, b1, b2, b3)):
        out[s] = block[1]


def swap_others(place, blocks, after=()):
    (other,) = call(others_kernel, [((4,) + blocks[0].shape[1:], BF)], place, blocks, after=after)
    return [*blocks, swap(other, 1)]


def block_of(s, k, blocks):
    return blocks[4].at[s] if k else blocks[s].at[0]


def project_heads(normed, weight, cosine, sine, q_out, k_out, v_out, values_down):
    step = 256
    for start in range(0, normed.shape[0], step):
        rows = slice(start, start + step)
        mixed = dot(normed[rows, :], weight[...])
        q_out[rows, :] = turn(mixed[:, :LANES], cosine[rows, :], sine[rows, :], 1.0).astype(BF)
        k_out[rows, :] = turn(mixed[:, LANES : 2 * LANES], cosine[rows, :], sine[rows, :], 1.0).astype(BF)
        values = mixed[:, 2 * LANES :]
        v_out[rows, :] = values.astype(BF)
        values_down[:, rows] = values.T.astype(BF)


def own_head(head):
    down = lax.broadcasted_iota(jnp.int32, (LANES, 1), 0)
    return (down >= head * HEAD_DIM) & (down < (head + 1) * HEAD_DIM)


def softmax_block(keys, chosen, block):
    scores = mask_diagonal(dot_general(keys, chosen, (1, 1)), block)
    row_max = jnp.max(scores, axis=0, keepdims=True)
    exponent = jnp.exp(scores - row_max)
    row_total = jnp.sum(exponent, axis=0, keepdims=True)
    return exponent * (1.0 / row_total), row_max + jnp.log(row_total)


BLOCK = 256
HEADS_HERE = LANES // HEAD_DIM


def first_attend_kernel(place, b0, b1, b2, b3, b4, cosine, sine, normed, xhat_out, weight, params, q_out, k_out, v_out, att_out, log_out, values_down):
    for s, k in SLOTS:
        rows = slot_rows(place, s, k)
        block, mine_at, small_at = first_block(s, k, (b0, b1, b2, b3, b4))
        for j in range(3):
            weight[rows, j * LANES : (j + 1) * LANES] = block[mine_at + j * ROWS : mine_at + (j + 1) * ROWS, :]
        params[:, rows] = block[small_at:, :].astype(F32)
        for b in range(8):
            normed[rows, b * LANES : (b + 1) * LANES] = block[b * ROWS : (b + 1) * ROWS, :]
    gain, shift = params[0:1, :], params[2:3, :]

    def norm_rows(rows):
        xhat = standardize(normed[rows, :].astype(F32))[0]
        xhat_out[rows, :] = xhat.astype(BF)
        normed[rows, :] = (xhat * gain + shift).astype(BF)

    loop_rows(normed.shape[0], 4 * ROWS, norm_rows)
    project_heads(normed, weight, cosine, sine, q_out, k_out, v_out, values_down)
    for start in range(0, normed.shape[0], BLOCK):
        stop = start + BLOCK
        queries = q_out[start:stop, :] * SCORE_SCALE
        total = jnp.zeros((LANES, BLOCK), F32)
        for head in range(HEADS_HERE):
            chosen = jnp.where(head_mask(head), queries, 0.0).astype(BF)
            probabilities, log_total = softmax_block(k_out[:stop, :], chosen, BLOCK)
            log_out[head : head + 1, start:stop] = log_total
            found = dot(values_down[:, :stop], probabilities.astype(BF))
            total = total + jnp.where(own_head(head), found, 0.0)
        att_out[start:stop, :] = total.T.astype(BF)


GELU_A = 0.7978845608028654
GELU_B = 0.044715


def gelu(pre):
    return pre * (0.5 + 0.5 * jnp.tanh(GELU_A * pre * (1.0 + GELU_B * pre * pre)))


def gelu_slope(pre):
    square = pre * pre
    wave = jnp.tanh(GELU_A * pre * (1.0 + GELU_B * square))
    return 0.5 * (1.0 + wave) + 0.5 * pre * (1.0 - wave * wave) * (GELU_A * (1.0 + 3.0 * GELU_B * square))


def loop_rows(count, step, body):
    def one(i, carry):
        body(pl.ds(pl.multiple_of(i * step, step), step))
        return carry

    lax.fori_loop(0, count // step, one, 0)


def put_slots(place, rows_of_block, keep, give):
    for s in range(4):
        keep[s] = rows_of_block(slot_rows(place, s, 0))
        give[s] = rows_of_block(slot_rows(place, s, 1))


def put_pairs(place, rows_of_block, outs):
    for s, k in SLOTS:
        outs[s][k] = rows_of_block(slot_rows(place, s, k))


def first_units_kernel(place, normed, near, far, bias, w_fc2, w_dense, attended, weight, act, slope, whole):
    for s, k in SLOTS:
        for part, other_plane in ((near.at[SLOTS.index((s, k))], False), (far.at[SLOTS.index((s, k))], True)):
            start = slot_start(place, s, k, ROWS) + half_start(place, other_plane)
            for b in range(4):
                rows = pl.ds(pl.multiple_of(start, HALF), HALF)
                weight[rows, b * LANES : (b + 1) * LANES] = part[b * HALF : (b + 1) * HALF, :]
    shift = bias[0:1, :].astype(F32)

    def rows_done(rows):
        found = dot(normed[rows, :], weight[...]) + shift
        slope[rows, :] = gelu_slope(found)
        act[rows, :] = gelu(found).astype(BF)
        whole[rows, :] = (dot(act[rows, :], w_fc2[0]) + dot(attended[rows, :], w_dense[0])).astype(BF)

    loop_rows(normed.shape[0], 256, rows_done)


def split_kernel(place, whole, keep, give):
    put_slots(place, lambda rows: whole[rows, :], keep, give)


def split_sum_kernel(place, keep, came, for_x, for_y, corner):
    def rows_done(rows):
        for s, out in ((1, for_x), (2, for_y), (3, corner)):
            out[rows, :] = keep[s, rows, :] + came[s, rows, :]

    loop_rows(for_x.shape[0], 16, rows_done)


def begin_scatter(place, keep, give, after=()):
    came = swap(give, 1)
    shape = (keep.shape[1:], BF)
    for_x, for_y, corner = call(split_sum_kernel, [shape] * 3, place, [keep, came], after=after)
    from_corner, from_x, from_y = swap(corner, 6), swap(for_x, 2), swap(for_y, 4)
    return [keep, came, from_x, from_y, from_corner], for_x


def sum_terms(terms):
    total = terms[0][0].astype(F32) + terms[1][0].astype(F32)
    for term in terms[2:]:
        total = total + term[...].astype(F32)
    return total


def next_hidden_kernel(place, *refs):
    terms, (hidden, params, hidden_out, normed) = refs[:5], refs[5:]
    found = hidden[...].astype(F32) + sum_terms(terms) + params[4:5, :]
    hidden_out[...] = found
    normed[...] = (standardize(found)[0] * params[1:2, :] + params[3:4, :]).astype(BF)


def low_kernel(place, wide, low):
    low[...] = wide[...].astype(BF)


def assemble_kernel(place, *refs):
    for (s, k), piece in zip(SLOTS, refs[:8]):
        refs[8][slot_rows(place, s, k), :] = piece[...]


def last_hidden_kernel(place, act, attended, w_fc2, w_dense, keep, give, whole):
    def rows_done(rows):
        whole[rows, :] = (dot(act[rows, :], w_fc2[1]) + dot(attended[rows, :], w_dense[1])).astype(BF)

    loop_rows(act.shape[0], 256, rows_done)
    put_slots(place, lambda rows: whole[rows, :], keep, give)


def last_sum_kernel(place, *refs):
    terms, (hidden, params, out, token) = refs[:5], refs[5:]
    token[...] = jnp.zeros_like(token)
    out[...] = hidden[...] + sum_terms(terms) + params[5:6, :]


SMALL_ROWS = 16


def put_halves(out, value, start, rows):
    half = out.shape[1]
    for j in range(2):
        out[j * rows + start : j * rows + start + value.shape[0], :] = value[:, j * half : (j + 1) * half]


def second_ready_kernel(place, b0, b1, b2, b3, other, far, weight, grads):
    units = weight.shape[1]
    for s, k in SLOTS:
        block = other.at[s] if k else (b0, b1, b2, b3)[s]
        parts = (block[:HALF, :], block[HALF:ROWS, :] if k else far[s, :HALF, :])
        for part, other_plane in zip(parts, (False, True)):
            start = slot_start(place, s, k, ROWS) + half_start(place, other_plane)
            weight[pl.ds(pl.multiple_of(start, HALF), HALF), :] = part
        for j in range(2):
            grads[slot_rows(place, s, k), j * units : (j + 1) * units] = block[(1 + j) * ROWS : (2 + j) * ROWS, :]


def second_units_kernel(place, *refs):
    pieces, refs = refs[:8], refs[8:]
    bias, weight, grads, normed, act, pre, chunk = refs
    units = weight.shape[1]
    for (s, k), piece in zip(SLOTS, pieces):
        normed[slot_rows(place, s, k), :] = piece[...]
    shift = bias[1:2, :].astype(F32)

    def rows_done(rows):
        found = dot(normed[rows, :], weight[...]) + shift
        pre[rows, :] = found
        act[rows, :] = gelu(found).astype(BF)

    loop_rows(normed.shape[0], 256, rows_done)
    for start in range(0, units, 256):
        put_halves(chunk, outer_sum(act[:, start : start + 256], grads[...]).astype(BF), start, units)


def units_back(layer, place, grads, w_fc2, slope_of, normed, weight, chunk, sums, part_normed, grad_pre, grad_w):
    sums[...] = jnp.zeros_like(sums)
    width = grads.shape[1]
    units = weight.shape[1]

    def rows_done(rows):
        found = (times_transposed(grads[rows, :], w_fc2[layer]) * slope_of(rows)).astype(BF)
        grad_pre[rows, :] = found
        sums[0:1, :width] += jnp.sum(grads[rows, :].astype(F32), axis=0, keepdims=True)
        sums[1:2, :units] += jnp.sum(found.astype(F32), axis=0, keepdims=True)
        part_normed[rows, :] = times_transposed(found, weight[...])

    loop_rows(grads.shape[0], 256, rows_done)
    for start in range(0, width, 256):
        rows = slice(start, start + 256)
        grad_w[rows, :] = outer_sum(normed[:, rows], grad_pre[...]).astype(BF)
    for i, (s, k) in enumerate(SLOTS):
        chunk[i * ROWS : (i + 1) * ROWS, :] = grad_w[slot_rows(place, s, k), :]


def second_units_back_kernel(place, grads, w_fc2, w_dense, pre, normed, weight, chunk, sums, part_normed, grad_att, grad_pre, grad_w):
    def slope_of(rows):
        grad_att[rows, :] = times_transposed(grads[rows, :], w_dense[1]).astype(BF)
        return gelu_slope(pre[rows, :])

    units_back(1, place, grads, w_fc2, slope_of, normed, weight, chunk, sums, part_normed, grad_pre, grad_w)


def first_units_back_kernel(place, *refs):
    pieces, refs = refs[:8], refs[8:]
    act, w_fc2, slope, normed, weight, grads, chunk_rows, chunk, sums, part_normed, grad_pre, grad_w = refs
    for (s, k), piece in zip(SLOTS, pieces):
        grads[slot_rows(place, s, k), :] = piece[...]
    units_back(
        0, place, grads, w_fc2, lambda rows: slope[rows, :], normed, weight, chunk, sums, part_normed, grad_pre, grad_w
    )
    units = act.shape[1]
    for start in range(0, units, 256):
        put_halves(chunk_rows, outer_sum(act[:, start : start + 256], grads[...]).astype(BF), start, units)


def attend_back_block(start, q_ref, k_ref, v_ref, grad_att, keys_down, k_sum, v_sum, cosine, sine, mixed, found_p):
    stop = start + BLOCK
    queries = q_ref[start:stop, :] * SCORE_SCALE
    grad_queries = jnp.zeros((LANES, BLOCK), F32)
    for head in range(HEADS_HERE):
        chosen = jnp.where(head_mask(head), queries, 0.0).astype(BF)
        chosen_grads = jnp.where(head_mask(head), grad_att, 0.0).astype(BF)
        probabilities = found_p(head, chosen)
        grad_probs = dot_general(v_ref[:stop, :], chosen_grads, (1, 1))
        row_inner = jnp.sum(grad_probs * probabilities, axis=0, keepdims=True)
        grad_scores = (probabilities * (grad_probs - row_inner)).astype(BF)
        k_sum[:stop, :] += dot(grad_scores, chosen)
        v_sum[:stop, :] += dot(probabilities.astype(BF), chosen_grads)
        grad_queries = grad_queries + jnp.where(own_head(head), dot(keys_down[:, :stop], grad_scores), 0.0)
    rows = slice(start, stop)
    mixed[rows, :LANES] = turn(grad_queries.T, cosine[rows, :], sine[rows, :], -1.0).astype(BF)


def mixed_rest(cosine, sine, mixed, k_sum, v_sum):
    mixed[:, LANES : 2 * LANES] = turn(k_sum[...], cosine[...], sine[...], -1.0).astype(BF)
    mixed[:, 2 * LANES :] = v_sum[...].astype(BF)


def mixed_outer(normed, mixed, grad_w):
    for start in range(0, normed.shape[1], 256):
        rows = slice(start, start + 256)
        grad_w[rows, :] = outer_sum(normed[:, rows], mixed[...]).astype(BF)


def mixed_inner(normed, weight, mixed, part_normed, whole):
    def rows_done(rows):
        whole[rows, :] = (times_transposed(mixed[rows, :], weight[...]) + part_normed[rows, :]).astype(BF)

    loop_rows(normed.shape[0], 256, rows_done)


def mixed_back(place, normed, weight, cosine, sine, mixed, k_sum, v_sum, grad_w, part_normed, whole):
    mixed_rest(cosine, sine, mixed, k_sum, v_sum)
    mixed_outer(normed, mixed, grad_w)
    mixed_inner(normed, weight, mixed, part_normed, whole)


def put_heads_chunk(place, chunk, grad_w, grad_dense):
    heads = grad_w.shape[1]
    for i, (s, k) in enumerate(SLOTS):
        rows = slice(i * ROWS, (i + 1) * ROWS)
        chunk[rows, :heads] = grad_w[slot_rows(place, s, k), :]
        chunk[rows, heads:] = grad_dense[:, rows]


def second_attend_kernel(place, normed, b0, b1, b2, b3, cosine, sine, grad_att, part_normed, att_out, mixed, keep_n, give_n, weight, q_ref, k_ref, v_ref, values_down, keys_down, k_sum, v_sum):
    for s, k in SLOTS:
        weight[slot_rows(place, s, k), :] = (b0, b1, b2, b3)[s][k]
    project_heads(normed, weight, cosine, sine, q_ref, k_ref, v_ref, values_down)
    k_sum[...] = jnp.zeros_like(k_sum)
    v_sum[...] = jnp.zeros_like(v_sum)
    keys_down[...] = (k_ref[...].astype(F32) * SCORE_SCALE).T.astype(BF)
    for start in range(0, normed.shape[0], BLOCK):
        stop = start + BLOCK
        total = [jnp.zeros((LANES, BLOCK), F32)]

        def found_p(head, chosen):
            probabilities, _ = softmax_block(k_ref[:stop, :], chosen, BLOCK)
            found = dot(values_down[:, :stop], probabilities.astype(BF))
            total[0] = total[0] + jnp.where(own_head(head), found, 0.0)
            return probabilities

        attend_back_block(start, q_ref, k_ref, v_ref, grad_att[start:stop, :], keys_down, k_sum, v_sum, cosine, sine, mixed, found_p)
        att_out[start:stop, :] = total[0].T.astype(BF)
    mixed_rest(cosine, sine, mixed, k_sum, v_sum)
    for s in range(4):
        rows = pl.ds(pl.multiple_of((place[0] ^ s) * 2 * ROWS, 2 * ROWS), 2 * ROWS)
        found = (times_transposed(mixed[rows, :], weight[...]) + part_normed[rows, :]).astype(BF)
        odd = place[1] == 1
        keep_n[s] = jnp.where(odd, found[ROWS:, :], found[:ROWS, :])
        give_n[s] = jnp.where(odd, found[:ROWS, :], found[ROWS:, :])


def second_heads_kernel(place, normed, mixed, attended, grads, chunk, grad_w):
    mixed_outer(normed, mixed, grad_w)
    put_heads_chunk(place, chunk, grad_w, outer_sum(attended[...], grads[...]).astype(BF))


def norm_back(gain_row, grad_normed, hidden, params, grads):
    xhat, scale = standardize(hidden[...].astype(F32))
    inner = grad_normed * params[gain_row : gain_row + 1, :]
    mean_inner = jnp.mean(inner, axis=-1, keepdims=True)
    mean_along = jnp.mean(inner * xhat, axis=-1, keepdims=True)
    return grads[...] + (inner - mean_inner - xhat * mean_along) * scale, xhat


def second_norm_back_kernel(place, *refs):
    terms, (hidden, params, grads, grads_out, grads_low, sums) = refs[:5], refs[5:]
    grad_normed = sum_terms(terms)
    found, xhat = norm_back(1, grad_normed, hidden, params, grads)
    grads_out[...] = found
    grads_low[...] = found.astype(BF)
    sums[0:1, :] = jnp.sum(grad_normed * xhat, axis=0, keepdims=True)
    sums[1:2, :] = jnp.sum(grad_normed, axis=0, keepdims=True)


def first_norm_back_kernel(place, *refs):
    terms, (hidden, params, grads, sums0, sums1, grads_out, small) = refs[:5], refs[5:]
    total = sum_terms(terms)
    grads_out[...] = norm_back(0, total[:ROWS, :], hidden, params, grads)[0]
    small[0:8, :] = total[ROWS : ROWS + 8, :LANES]
    for layer, sums in ((0, sums0), (1, sums1)):
        small[4 + layer : 5 + layer, :] = sums[0:1, slot_rows(place, 0, 0)]
        for j in range(4):
            small[8 + 4 * layer + j : 9 + 4 * layer + j, :] = sums[1:2, j * LANES : (j + 1) * LANES]


def first_attend_back_kernel(place, grads, w_dense, attended, q_ref, k_ref, v_ref, log_in, cosine, sine, normed, xhat, weight, part_normed, ln_sums1, chunk, keep_n, give_n, keys_down, k_sum, v_sum, mixed, grad_w, whole, ln_sums):
    k_sum[...] = jnp.zeros_like(k_sum)
    v_sum[...] = jnp.zeros_like(v_sum)
    keys_down[...] = (k_ref[...].astype(F32) * SCORE_SCALE).T.astype(BF)
    for start in range(0, normed.shape[0], BLOCK):
        stop = start + BLOCK

        def found_p(head, chosen):
            scores = mask_diagonal(dot_general(k_ref[:stop, :], chosen, (1, 1)), BLOCK)
            return jnp.exp(scores - log_in[head : head + 1, start:stop])

        grad_att = times_transposed(grads[start:stop, :], w_dense[0]).astype(BF)
        attend_back_block(start, q_ref, k_ref, v_ref, grad_att, keys_down, k_sum, v_sum, cosine, sine, mixed, found_p)
    mixed_back(place, normed, weight, cosine, sine, mixed, k_sum, v_sum, grad_w, part_normed, whole)
    put_heads_chunk(place, chunk, grad_w, outer_sum(attended[...], grads[...]).astype(BF))
    ln_sums[...] = jnp.zeros_like(ln_sums)

    def rows_done(rows):
        part = whole[rows, :].astype(F32)
        ln_sums[0:1, :] += jnp.sum(part * xhat[rows, :].astype(F32), axis=0, keepdims=True)
        ln_sums[2:3, :] += jnp.sum(part, axis=0, keepdims=True)

    loop_rows(normed.shape[0], 256, rows_done)
    ln_sums[1:2, :] = ln_sums1[0:1, :]
    ln_sums[3:4, :] = ln_sums1[1:2, :]
    for s in range(4):
        for k, out in ((0, keep_n), (1, give_n)):
            rows = slot_rows(place, s, k)
            out[s, :ROWS, :] = whole[rows, :]
            out[s, ROWS:, :] = jnp.zeros((EXTRA, out.shape[2]), BF)
            out[s, ROWS : ROWS + 8, :LANES] = ln_sums[:, rows].astype(BF)


INWARD, ACROSS, OUTWARD = [(0, 1), (3, 2)], [(1, 2), (2, 1)], [(1, 0), (2, 3)]


def along(value, pairs):
    return lax.ppermute(value, "rep", pairs)


def low_sum(left, right):
    return left[...] + right[...]


def is_middle(place):
    return (place[2] == 1) | (place[2] == 2)


def tick_kernel(has, place, *refs):
    refs = list(refs)
    if has[0]:
        chunk, came = refs.pop(0), refs.pop(0)
    if has[1]:
        before, crossed = refs.pop(0), refs.pop(0)
    if has[2]:
        coming = refs.pop(0)
    half = refs.pop(0) if has[0] else None
    going = refs.pop(0) if has[1] else None

    def half_rows(rows):
        half[rows, :] = low_sum(chunk.at[rows, :], came.at[rows, :])

    def going_rows(rows):
        found = low_sum(before.at[rows, :], crossed.at[rows, :])
        going[rows, :] = jnp.where(is_middle(place), found, coming[rows, :]) if has[2] else found

    for body, out, rows in ((half_rows, half, has[0] and chunk.shape[0]), (going_rows, going, has[1] and before.shape[0])):
        if out is not None:
            loop_rows(rows, 208 if rows % 208 == 0 else 256, body)
            if out.shape[0] > rows:
                out[rows:, :] = coming[rows:, :]


def tick(place, step, last, coming, after=(), joint=False):
    if step is not None and last is not None and not joint:
        (half,) = tick(place, step, None, None, after)
        (going,) = tick(place, None, last, coming, (half,))
        return half, going
    ins, outs = [], []
    for pair in (step, last):
        if pair is not None:
            ins += pair
            outs.append((pair[0].shape if coming is None or pair is step else coming.shape, pair[0].dtype))
    if coming is not None:
        ins.append(coming)
    has = (step is not None, last is not None, coming is not None)
    return call(partial(tick_kernel, has), outs, place, ins, after=after)


def add_small_kernel(place, chunk, small, out):
    rows = chunk.shape[0]
    out[:rows, :] = chunk[...]
    out[rows:, :LANES] = small[...].astype(BF)
    out[rows:, LANES:] = jnp.zeros((SMALL_ROWS, chunk.shape[1] - LANES), BF)


def pick_kernel(place, total, came, o0, o1, o2, o3, *rest):
    heads = o0.shape[2]
    for i, (s, k) in enumerate(SLOTS):
        out = (o0, o1, o2, o3)[s]

        def rows_done(rows):
            here = pl.ds(pl.multiple_of(rows.start + i * ROWS, rows.size), rows.size)
            found = jnp.where(is_middle(place), total[here, :], came[here, :])
            out[k, rows, :] = found[:, :heads]
            if rest:
                rest[0][rows, i * ROWS : (i + 1) * ROWS] = found[:, heads:].astype(F32)

        loop_rows(ROWS, 32, rows_done)


def pick_both_kernel(place, total_f, came_f, total_q, came_q, o0, o1, o2, o3, dense):
    units = total_f.shape[1]
    heads = o0.shape[2] - units
    for i, (s, k) in enumerate(SLOTS):
        out = (o0, o1, o2, o3)[s]

        def rows_done(rows):
            here = pl.ds(pl.multiple_of(rows.start + i * ROWS, rows.size), rows.size)
            out[k, rows, :units] = jnp.where(is_middle(place), total_f[here, :], came_f[here, :])
            found = jnp.where(is_middle(place), total_q[here, :], came_q[here, :])
            out[k, rows, units:] = found[:, :heads]
            dense[rows, i * ROWS : (i + 1) * ROWS] = found[:, heads:].astype(F32)

        loop_rows(ROWS, 32, rows_done)


def pick_both(place, units_pair, heads_pair, heads, after=()):
    columns = units_pair[0].shape[1] + heads
    outs = [((2, ROWS, columns), BF)] * 4 + [((ROWS, 8 * LANES), F32)]
    return call(pick_both_kernel, outs, place, [*units_pair, *heads_pair], after=after)


def pick(place, total, came, heads, after=()):
    outs = [((2, ROWS, heads), BF)] * 4
    if heads < total.shape[1]:
        outs.append(((ROWS, 8 * LANES), F32))
    return call(pick_kernel, outs, place, [total, came], after=after)


def chosen_sum(place, total, outward):
    middle = (place[2] == 1) | (place[2] == 2)
    return jnp.where(middle, total, outward).astype(F32)


def final_call(body, place, ins, shape, layer, before=None, after=()):
    skip = len(after) + (before is not None)

    def run(place, *refs):
        *ins, out, token, found, sems = refs[skip:]
        body(place, ins, out.at[layer], found, sems)
        token[...] = jnp.zeros_like(token)

    return pl.pallas_call(
        run,
        name=body.__name__,
        out_shape=[jax.ShapeDtypeStruct((2,) + shape, F32), jax.ShapeDtypeStruct((8, LANES), F32)],
        in_specs=[pl.BlockSpec(memory_space=pltpu.SMEM)]
        + [pl.BlockSpec(memory_space=pltpu.HBM)] * (before is not None)
        + [pl.BlockSpec(memory_space=pl.ANY)] * len(after)
        + [pl.BlockSpec(memory_space=pltpu.VMEM)] * len(ins),
        out_specs=[pl.BlockSpec(memory_space=pltpu.HBM), pl.BlockSpec(memory_space=pltpu.VMEM)],
        scratch_shapes=[pltpu.VMEM(shape, F32), pltpu.SemaphoreType.DMA((8,))],
        input_output_aliases={} if before is None else {1: 0},
        compiler_params=pltpu.CompilerParams(vmem_limit_bytes=16 * 1024 * 1024),
        cost_estimate=SMALL,
    )(place, *([] if before is None else [before]), *after, *ins)


def final_rows_start(place, total, came, out, found, sems):
    half, rows = total.shape[1], out.shape[0]
    step = rows // 4

    def move(i):
        put = pl.ds(pl.multiple_of(i * step, step), step)
        return pltpu.make_async_copy(found.at[put, :], out.at[put, :], sems.at[i])

    def one(i, carry):
        put = pl.ds(pl.multiple_of(i * step, step), step)
        for j in range(2):
            part = pl.ds(pl.multiple_of(i * step + j * rows, step), step)
            found[put, j * half : (j + 1) * half] = jnp.where(is_middle(place), total[part, :], came[part, :]).astype(F32)
        move(i).start()
        return carry

    lax.fori_loop(0, 4, one, 0)
    return [move(i) for i in range(4)]


def final_rows_kernel(place, ins, out, found, sems):
    for move in final_rows_start(place, *ins, out, found, sems):
        move.wait()


def final_units_kernel(place, blocks, out, found, sems):
    units, moves = out.shape[1] // 8, []
    for i, (s, k) in enumerate(SLOTS):
        put = slice(i * units, (i + 1) * units)
        block = block_of(s, k, blocks)

        def rows_done(rows):
            found[rows, put] = block[rows, :units].astype(F32)

        loop_rows(ROWS, 32, rows_done)
        moves.append(pltpu.make_async_copy(found.at[:, put], out.at[:, slot_rows(place, s, k, units)], sems.at[i]))
        moves[-1].start()
    for move in moves:
        move.wait()


def final_heads_kernel(place, blocks, out, found, sems):
    third = out.shape[1] // 3
    for s, k in SLOTS:
        block = block_of(s, k, blocks)

        def rows_done(rows):
            part = block[rows, block.shape[1] - 3 * LANES :].astype(F32)
            for j in range(3):
                lanes = pl.ds(pl.multiple_of(j * third + slot_start(place, s, k, LANES), LANES), LANES)
                found[rows, lanes] = part[:, j * LANES : (j + 1) * LANES]

        loop_rows(ROWS, 32, rows_done)
    move = pltpu.make_async_copy(found, out, sems.at[0])
    move.start()
    move.wait()


def last_rows_kernel(place, before, total, came, out, gain, shift, bias_fc1, bias_fc2, found, sems):
    rows = slice(total.shape[0] - SMALL_ROWS, total.shape[0])
    small = jnp.where(is_middle(place), total[rows, :LANES], came[rows, :LANES]).astype(F32)
    moves = final_rows_start(place, total, came, out.at[0], found, sems)
    gain[...] = small[0:2, :]
    shift[...] = small[2:4, :]
    bias_fc2[...] = small[4:6, :]
    for layer in range(2):
        for j in range(4):
            bias_fc1[layer : layer + 1, j * LANES : (j + 1) * LANES] = small[8 + 4 * layer + j : 9 + 4 * layer + j, :]
    for move in moves:
        move.wait()


def local_plane(hidden_in, ln_gain, ln_bias, w_qkv, w_dense, w_fc1, b_fc1, w_fc2, b_fc2, output_grad):
    index = lax.axis_index("grp")
    place = jnp.stack([index // 2, index % 2, lax.axis_index("rep")]).astype(jnp.int32)
    span, width = hidden_in.shape[1:]
    seq = span * 8
    units = b_fc1.shape[1]
    own = 3 * LANES
    cosine, sine = rotary_tables(seq)
    hidden0 = hidden_in.reshape(span, width)
    grads1 = output_grad.reshape(span, width)

    wide, column, chunk_shape = ((seq, width), BF), ((seq, LANES), BF), ((seq, units), BF)
    blocks_n, blocks_n0 = ((4, ROWS, width), BF), ((4, ROWS + EXTRA, width), BF)
    blocks_f, blocks_q = ((2, ROWS, units), BF), ((2, ROWS, own), BF)
    mine, mine_low = ((span, width), F32), ((span, width), BF)
    sums_shape, part_shape = ((8, width), F32), ((seq, width), F32)
    head_scratch = [pltpu.VMEM((LANES, seq), BF), pltpu.VMEM((seq, LANES), F32), pltpu.VMEM((seq, LANES), F32)]
    back_scratch = [pltpu.VMEM((seq, own), BF), pltpu.VMEM((width, own), BF), pltpu.VMEM((seq, width), BF)]
    column_scratch = [pltpu.VMEM((seq, LANES), BF)] * 3
    units_scratch = [pltpu.VMEM((seq, units), BF), pltpu.VMEM((width, units), BF)]

    rows = [hidden0.shape, ln_gain.shape, ln_bias.shape, b_fc2.shape, w_qkv.shape[1:], (HALF, w_fc1.shape[2])]
    rows = [rows[0], *rows[4:], *rows[1:4]]
    packed = pl.pallas_call(
        pack_first_kernel,
        name="pack_first_kernel",
        out_shape=[jax.ShapeDtypeStruct((FIRST_ROWS, LANES), BF)] * 4,
        in_specs=[pl.BlockSpec(memory_space=pltpu.HBM)] * 6,
        out_specs=[pl.BlockSpec(memory_space=pltpu.VMEM)] * 4,
        scratch_shapes=[pltpu.VMEM(shape, BF) for shape in rows] + [pltpu.SemaphoreType.DMA((6,))],
        compiler_params=pltpu.CompilerParams(vmem_limit_bytes=60 * 1024 * 1024),
        cost_estimate=SMALL,
    )(hidden0, w_qkv, w_fc1, ln_gain, ln_bias, b_fc2)
    first = send_blocks(place, packed)
    packed = call(partial(pack_units_grads_kernel, 1), [((3 * ROWS, units), BF)] * 4, place, [w_fc1, grads1])
    keep, give = call(partial(pack_heads_kernel, 1), [((4, ROWS, own), BF)] * 2, place, [w_qkv], after=[packed[0]])
    pairs1 = call(pair_kernel, [blocks_q] * 4, place, [keep, swap(give, 1)])
    (others0,) = call(others_first_kernel, [((4, OTHERS_ROWS, LANES), BF)], place, first, after=[pairs1[0]])
    units1 = send_blocks(place, packed)
    first = [*first, swap(others0, 1)]
    (near0,) = call(near_first_kernel, [((8, HALF_ROWS, LANES), BF)], place, first)
    far0 = along(near0, INWARD + OUTWARD)

    normed0, xhat0, weight_q0, params, q0, k0, v0, att0, log0 = call(
        first_attend_kernel,
        [wide, wide, ((width, own), BF), ((EXTRA, width), F32), column, column, column, column, ((8, seq), F32)],
        place,
        [*first, cosine, sine],
        [pltpu.VMEM((LANES, seq), BF)],
        after=[near0],
    )
    weight_f0, act0, slope0, partial_sum = call(
        first_units_kernel,
        [((width, units), BF), ((seq, units), BF), ((seq, units), F32), wide],
        place,
        [normed0, near0, far0, b_fc1, w_fc2, w_dense, att0],
    )
    (near1,) = call(near_units_kernel, [((4, ROWS, units), BF)], place, units1, after=[partial_sum])
    far1 = along(near1, INWARD + OUTWARD)
    keep, give = call(split_kernel, [blocks_n, blocks_n], place, [partial_sum], after=[near1])
    terms, sent = begin_scatter(place, keep, give)
    (others1,) = call(others_units_grads_kernel, [((4, 3 * ROWS, units), BF)], place, [*units1, far1], after=terms[2:])
    hidden1, normed1_own = call(next_hidden_kernel, [mine, mine_low], place, [*terms, hidden0, params], after=[others1])
    pieces = gather_pieces(normed1_own)

    weight_f1, grad_branch1 = call(
        second_ready_kernel, [((width, units), BF), wide], place, [*units1, swap(others1, 1), far1]
    )
    normed1, act1, pre1, chunk1 = call(
        second_units_kernel,
        [wide, ((seq, units), BF), ((seq, units), F32), chunk_shape],
        place,
        [*pieces, b_fc1, weight_f1, grad_branch1],
    )
    came1 = along(chunk1, INWARD + OUTWARD)
    heads1 = send_blocks(place, pairs1)
    chunk2, sums1, part_normed, grad_att1 = call(
        second_units_back_kernel,
        [chunk_shape, sums_shape, part_shape, column],
        place,
        [grad_branch1, w_fc2, w_dense, pre1, normed1, weight_f1],
        units_scratch,
    )
    att1, mixed1, keep, give = call(
        second_attend_kernel,
        [column, ((seq, own), BF), blocks_n, blocks_n],
        place,
        [normed1, *heads1, cosine, sine, grad_att1, part_normed],
        [
            pltpu.VMEM((width, own), BF),
            *column_scratch,
            pltpu.VMEM((LANES, seq), BF),
            *head_scratch,
        ],
    )
    terms, sent = begin_scatter(place, keep, give)
    (half1,) = tick(place, (chunk1, came1), None, None, after=[give])
    (chunk3,) = call(
        second_heads_kernel,
        [chunk_shape],
        place,
        [normed1, mixed1, att1, grad_branch1],
        [pltpu.VMEM((width, own), BF)],
        after=[half1, sent],
    )
    cross1, came2 = along(half1, ACROSS), along(chunk2, INWARD + OUTWARD)
    grads0, grads0_low, ln_sums1 = call(
        second_norm_back_kernel, [mine, mine_low, sums_shape], place, [*terms, hidden1, params, grads1], after=[half1]
    )

    keep_h, give_h = call(
        last_hidden_kernel,
        [blocks_n, blocks_n],
        place,
        [act1, att1, w_fc2, w_dense],
        [pltpu.VMEM((seq, width), BF)],
        after=[chunk3],
    )
    pieces = gather_pieces(grads0_low)
    half2, total1 = tick(place, (chunk2, came2), (half1, cross1), chunk3, after=[pieces[2], give_h], joint=True)
    cross2, came3 = along(half2, ACROSS), along(total1, INWARD + OUTWARD)
    grad_branch0, chunk6, chunk4, sums0, part_normed = call(
        first_units_back_kernel,
        [wide, chunk_shape, chunk_shape, sums_shape, part_shape],
        place,
        [*pieces, act0, w_fc2, slope0, normed0, weight_f0],
        units_scratch,
        after=[half2],
    )
    chunk5, keep, give = call(
        first_attend_back_kernel,
        [chunk_shape, blocks_n0, blocks_n0],
        place,
        [grad_branch0, w_dense, att0, q0, k0, v0, log0, cosine, sine, normed0, xhat0, weight_q0, part_normed, ln_sums1],
        [*head_scratch, *back_scratch, pltpu.VMEM((8, width), F32)],
    )
    half3, total2 = tick(place, (chunk3, came3), (half2, cross2), chunk4, after=[chunk5], joint=True)
    cross3, came4 = along(half3, ACROSS), along(total2, INWARD + OUTWARD)
    token = ((8, LANES), F32)
    terms, sent = begin_scatter(place, keep, give, after=[half3])
    out_fc2, done = final_call(final_rows_kernel, place, [total1, came3], (units, width), 1, after=[sent])
    input_grad, small_sums = call(
        first_norm_back_kernel,
        [mine, ((SMALL_ROWS, LANES), F32)],
        place,
        [*terms, hidden0, params, grads0, sums0, sums1],
        after=[done],
    )
    half4, total3 = tick(place, (chunk4, came4), (half3, cross3), chunk5, after=[small_sums], joint=True)
    cross4, came5 = along(half4, ACROSS), along(total3, INWARD + OUTWARD)
    (chunk6,) = call(
        add_small_kernel, [((seq + SMALL_ROWS, units), BF)], place, [chunk6, small_sums], after=[half4]
    )
    terms, _ = begin_scatter(place, keep_h, give_h, after=[half4])
    hidden_out, done_h = call(last_sum_kernel, [mine, token], place, [*terms, hidden1, params], after=[chunk6])
    half5, total4 = tick(place, (chunk5, came5), (half4, cross4), chunk6, after=[done_h], joint=True)
    cross5, came6 = along(half5, ACROSS), along(total4, INWARD + OUTWARD)
    *picked1, dense1 = pick_both(place, (total2, came4), (total3, came5), own, after=[half5])
    blocks1 = swap_others(place, send_blocks(place, picked1))
    half6, total5 = tick(place, (chunk6, came6), (half5, cross5), None, after=[blocks1[1]], joint=True)
    cross6, came7 = along(half6, ACROSS), along(total5, INWARD + OUTWARD)
    picked4 = pick(place, total4, came6, units, after=[half6])
    out_fc1, done1 = final_call(final_units_kernel, place, blocks1, (ROWS, w_fc1.shape[2]), 1, after=[picked4[0]])
    out_qkv, done3 = final_call(final_heads_kernel, place, blocks1, (ROWS, w_qkv.shape[2]), 1, after=[done1])
    blocks4 = swap_others(place, send_blocks(place, picked4), after=[done3])
    (total6,) = tick(place, None, (half6, cross6), None, after=[blocks4[1]])
    came8 = along(total6, INWARD + OUTWARD)
    *picked5, dense0 = pick(place, total5, came7, own, after=[total6])
    out_fc1, done4 = final_call(final_units_kernel, place, blocks4, (ROWS, w_fc1.shape[2]), 0, out_fc1, after=[picked5[0]])
    blocks5 = swap_others(place, send_blocks(place, picked5), after=[done4])
    out_qkv, done5 = final_call(final_heads_kernel, place, blocks5, (ROWS, w_qkv.shape[2]), 0, out_qkv)
    vector = jax.ShapeDtypeStruct((2, LANES), F32)
    out_fc2, out_gain, out_shift, out_b_fc1, out_b_fc2 = pl.pallas_call(
        lambda place, before, token, *refs: last_rows_kernel(place, before, *refs),
        name="last_rows_kernel",
        out_shape=[jax.ShapeDtypeStruct((2, units, width), F32), vector, vector, jax.ShapeDtypeStruct((2, units), F32), vector],
        in_specs=[pl.BlockSpec(memory_space=pltpu.SMEM), pl.BlockSpec(memory_space=pltpu.HBM)]
        + [pl.BlockSpec(memory_space=pl.ANY)]
        + [pl.BlockSpec(memory_space=pltpu.VMEM)] * 2,
        out_specs=[pl.BlockSpec(memory_space=pltpu.HBM)] + [pl.BlockSpec(memory_space=pltpu.VMEM)] * 4,
        scratch_shapes=[pltpu.VMEM((units, width), F32), pltpu.SemaphoreType.DMA((4,))],
        input_output_aliases={1: 0},
        compiler_params=pltpu.CompilerParams(vmem_limit_bytes=16 * 1024 * 1024),
        cost_estimate=SMALL,
    )(place, out_fc2, done5, total6, came8)
    out_dense = jnp.stack([dense0, dense1])
    return (
        hidden_out[None],
        input_grad[None],
        out_gain,
        out_shift,
        out_qkv,
        out_dense,
        out_fc1,
        out_b_fc1,
        out_fc2,
        out_b_fc2,
    )


def local(hidden_in, ln_gain, ln_bias, w_qkv, w_dense, w_fc1, b_fc1, w_fc2, b_fc2, output_grad):
    arguments = (hidden_in, ln_gain, ln_bias, w_qkv, w_dense, w_fc1, b_fc1, w_fc2, b_fc2, output_grad)
    plane = lax.axis_size("grp") == 8 and lax.axis_size("rep") == 4
    plane = plane and hidden_in.shape[:2] == (1, ROWS) and w_qkv.shape == (2, LANES, 3 * 8 * LANES)
    return (local_plane if plane else local_any)(*arguments)


def solution(mesh):
    in_specs = (
        P("rep", "grp", None),
        P(None, "grp"),
        P(None, "grp"),
        P(None, "grp", None),
        P(None, "grp", None),
        P(None, "grp", None),
        P(None, "grp"),
        P(None, "grp", None),
        P(None, "grp"),
        P("rep", "grp", None),
    )
    out_specs = (
        P("rep", "grp", None),
        P("rep", "grp", None),
        P(None, "grp"),
        P(None, "grp"),
        P(None, "grp", None),
        P(None, "grp", None),
        P(None, "grp", None),
        P(None, "grp"),
        P(None, "grp", None),
        P(None, "grp"),
    )
    return jax.shard_map(local, mesh=mesh, in_specs=in_specs, out_specs=out_specs, check_vma=False)
```

```python
from functools import partial

import jax
import jax.numpy as jnp
import numpy as np
from jax import lax
from jax.experimental import pallas as pl
from jax.experimental.pallas import tpu as pltpu
from jax.sharding import PartitionSpec as P

HEAD_DIM = 64
ROT = 32
LANES = 128

EPSILON = 1e-05
SCORE_SCALE = 0.125
NEGATIVE = -1000000000.0
BF = jnp.bfloat16
F32 = jnp.float32


def dot(left, right):
    return jnp.dot(left, right, preferred_element_type=F32)


def dot_general(left, right, contract):
    return lax.dot_general(left, right, ((contract[:1], contract[1:]), ((), ())), preferred_element_type=F32)


def outer_sum(left, right):
    return dot_general(left, right, (0, 0))


def times_transposed(left, right):
    return dot_general(left, right, (1, 1))


def head_mask(head):
    lane = lax.broadcasted_iota(jnp.int32, (1, LANES), 1)
    return (lane >= head * HEAD_DIM) & (lane < (head + 1) * HEAD_DIM)


def turn(part, cosine, sine, sign):
    even = lax.broadcasted_iota(jnp.int32, part.shape, 1) % 2 == 0
    partner = jnp.where(even, pltpu.roll(part, LANES - 1, 1), pltpu.roll(part, 1, 1))
    return part * cosine + partner * (sine * sign)


def mask_diagonal(scores, block):
    keys, queries = scores.shape
    key_place = lax.broadcasted_iota(jnp.int32, (block, queries), 0)
    query_place = lax.broadcasted_iota(jnp.int32, (block, queries), 1)
    last = jnp.where(key_place <= query_place, scores[keys - block :], NEGATIVE)
    if keys == block:
        return last
    return jnp.concatenate([scores[: keys - block], last], axis=0)


def attend_kernel(heads, block, mix_q, mix_k, mix_v, cosine, sine, q_out, k_out, v_out, att_out, log_out):
    seq = mix_q.shape[0]
    q_out[...] = turn(mix_q[...], cosine[...], sine[...], 1.0).astype(BF)
    k_out[...] = turn(mix_k[...], cosine[...], sine[...], 1.0).astype(BF)
    v_out[...] = mix_v[...].astype(BF)
    values_down = mix_v[...].T.astype(BF)
    for start in range(0, seq, block):
        stop = start + block
        queries = q_out[start:stop, :] * SCORE_SCALE
        keys = k_out[:stop, :]
        total = jnp.zeros((LANES, block), F32)
        for head in range(heads):
            chosen = jnp.where(head_mask(head), queries, 0.0).astype(BF)
            scores = mask_diagonal(dot_general(keys, chosen, (1, 1)), block)
            row_max = jnp.max(scores, axis=0, keepdims=True)
            exponent = jnp.exp(scores - row_max)
            row_total = jnp.sum(exponent, axis=0, keepdims=True)
            probabilities = (exponent * (1.0 / row_total)).astype(BF)
            log_out[head : head + 1, start:stop] = row_max + jnp.log(row_total)
            found = dot(values_down[:, :stop], probabilities)
            down = lax.broadcasted_iota(jnp.int32, (LANES, 1), 0)
            own = (down >= head * HEAD_DIM) & (down < (head + 1) * HEAD_DIM)
            total = total + jnp.where(own, found, 0.0)
        att_out[start:stop, :] = total.T.astype(BF)


def attend_back_kernel(heads, block, q_in, k_in, v_in, grad_att, log_in, cosine, sine, q_out, k_out, v_out, k_sum, v_sum):
    seq = q_in.shape[0]
    k_sum[...] = jnp.zeros_like(k_sum)
    v_sum[...] = jnp.zeros_like(v_sum)
    keys_down = (k_in[...].astype(F32) * SCORE_SCALE).T.astype(BF)
    for start in range(0, seq, block):
        stop = start + block
        queries = q_in[start:stop, :] * SCORE_SCALE
        grads = grad_att[start:stop, :]
        grad_queries = jnp.zeros((LANES, block), F32)
        for head in range(heads):
            chosen = jnp.where(head_mask(head), queries, 0.0).astype(BF)
            chosen_grads = jnp.where(head_mask(head), grads, 0.0).astype(BF)
            scores = mask_diagonal(dot_general(k_in[:stop, :], chosen, (1, 1)), block)
            probabilities = jnp.exp(scores - log_in[head : head + 1, start:stop])
            grad_probs = dot_general(v_in[:stop, :], chosen_grads, (1, 1))
            row_inner = jnp.sum(grad_probs * probabilities, axis=0, keepdims=True)
            grad_scores = (probabilities * (grad_probs - row_inner)).astype(BF)
            k_sum[:stop, :] += dot(grad_scores, chosen)
            v_sum[:stop, :] += dot(probabilities.astype(BF), chosen_grads)
            down = lax.broadcasted_iota(jnp.int32, (LANES, 1), 0)
            own = (down >= head * HEAD_DIM) & (down < (head + 1) * HEAD_DIM)
            grad_queries = grad_queries + jnp.where(own, dot(keys_down[:, :stop], grad_scores), 0.0)
        q_out[start:stop, :] = turn(
            grad_queries.T, cosine[start:stop, :], sine[start:stop, :], -1.0
        ).astype(BF)
    k_out[...] = turn(k_sum[...], cosine[...], sine[...], -1.0).astype(BF)
    v_out[...] = v_sum[...].astype(BF)


VMEM_LIMIT = 48 * 1024 * 1024


def attend(mix_q, mix_k, mix_v, heads, cosine, sine):
    seq = mix_q.shape[0]
    out = jax.ShapeDtypeStruct((seq, LANES), BF)
    return pl.pallas_call(
        partial(attend_kernel, heads, min(256, seq)),
        out_shape=(out, out, out, out, jax.ShapeDtypeStruct((heads, seq), F32)),
        compiler_params=pltpu.CompilerParams(vmem_limit_bytes=VMEM_LIMIT),
    )(mix_q, mix_k, mix_v, cosine, sine)


def attend_back(queries, keys, values, grad_att, log_total, heads, cosine, sine):
    seq = queries.shape[0]
    out = jax.ShapeDtypeStruct((seq, LANES), BF)
    return pl.pallas_call(
        partial(attend_back_kernel, heads, min(256, seq)),
        out_shape=(out, out, out),
        scratch_shapes=[pltpu.VMEM((seq, LANES), F32), pltpu.VMEM((seq, LANES), F32)],
        compiler_params=pltpu.CompilerParams(vmem_limit_bytes=VMEM_LIMIT),
    )(queries, keys, values, grad_att, log_total, cosine, sine)


def rotary_tables(seq):
    frequency = (1.0 / 10000.0 ** (np.arange(ROT // 2, dtype=np.float32) * 2.0 / ROT)).astype(np.float32)
    angles = np.arange(seq, dtype=np.float32)[:, None] * frequency[None, :]
    cosine, sine = np.cos(angles.astype(np.float64)), np.sin(angles.astype(np.float64))
    cosine = np.repeat(cosine, 2, axis=1)
    sine = np.repeat(sine, 2, axis=1) * np.tile([-1.0, 1.0], ROT // 2)
    rest = HEAD_DIM - ROT
    cosine = np.concatenate([cosine, np.ones((seq, rest))], axis=1)
    sine = np.concatenate([sine, np.zeros((seq, rest))], axis=1)
    repeats = (1, LANES // HEAD_DIM)
    return np.tile(cosine, repeats).astype(np.float32), np.tile(sine, repeats).astype(np.float32)


def swap(value, bits):
    return lax.ppermute(value, "grp", [(i, i ^ bits) for i in range(8)])


def add_low(left, right):
    return (left.astype(F32) + right.astype(F32)).astype(BF)


def by_chip(parts, chip):
    x, y = chip % 2 == 1, chip // 2 == 1
    near = jnp.where(x, jnp.stack([parts[1], parts[0]]), jnp.stack([parts[0], parts[1]]))
    far = jnp.where(x, jnp.stack([parts[3], parts[2]]), jnp.stack([parts[2], parts[3]]))
    return jnp.where(y, jnp.concatenate([far, near]), jnp.concatenate([near, far]))


def gather_rows(part):
    size = lax.axis_size("grp")
    if size != 8:
        return lax.all_gather(part, "grp", axis=0, tiled=True)
    rows, width = part.shape
    half = rows // 2
    index = lax.axis_index("grp")
    along_x, along_y = swap(part, 2), swap(part, 4)
    corner = jnp.concatenate([swap(along_y[:half], 2), swap(along_x[half:], 4)])
    mine = by_chip([part, along_x, along_y, corner], index // 2)
    other = swap(mine, 1)
    odd = index % 2 == 1
    both = jnp.stack([jnp.where(odd, other, mine), jnp.where(odd, mine, other)], axis=1)
    return both.reshape(8 * rows, width)


def scatter_sum(whole):
    size = lax.axis_size("grp")
    if size != 8:
        return lax.psum_scatter(whole, "grp", scatter_dimension=0, tiled=True).astype(F32)
    rows, width = whole.shape[0] // 8, whole.shape[1]
    half = rows // 2
    index = lax.axis_index("grp")
    chip, core = index // 2, index % 2
    blocks = whole.reshape(4, 2, rows, width)
    keep = lax.dynamic_index_in_dim(blocks, core, 1, False)
    give = lax.dynamic_index_in_dim(blocks, 1 - core, 1, False)
    summed = add_low(keep, swap(give, 1))
    own, for_x, for_y, corner = [lax.dynamic_index_in_dim(summed, chip ^ s, 0, False) for s in range(4)]
    by_x, by_y = swap(corner[:half], 2), swap(corner[half:], 4)
    for_y = jnp.concatenate([add_low(for_y[:half], by_x), for_y[half:]])
    for_x = jnp.concatenate([for_x[:half], add_low(for_x[half:], by_y)])
    return own.astype(F32) + swap(for_y, 4).astype(F32) + swap(for_x, 2).astype(F32)


def exchange(blocks):
    size = lax.axis_size("grp")
    if size != 8:
        return lax.all_to_all(blocks, "grp", 0, 0)
    index = lax.axis_index("grp")
    chip, core = index // 2, index % 2
    pairs = blocks.reshape((4, 2) + blocks.shape[1:])
    keep = lax.dynamic_index_in_dim(pairs, core, 1, False)
    give = lax.dynamic_index_in_dim(pairs, 1 - core, 1, False)
    came = swap(give, 1)
    odd = core == 1
    both = jnp.stack([jnp.where(odd, came, keep), jnp.where(odd, keep, came)], axis=1)
    parts = [lax.dynamic_index_in_dim(both, chip ^ s, 0, False) for s in range(4)]
    parts = [parts[0]] + [swap(parts[s], 2 * s) for s in (1, 2, 3)]
    return by_chip(parts, chip).reshape(blocks.shape)


def rep_sum(part):
    if lax.axis_size("rep") != 4:
        return lax.psum(part, "rep").astype(F32)
    place = lax.axis_index("rep")
    inward = lax.ppermute(part, "rep", [(0, 1), (3, 2)])
    half_sum = add_low(part, inward)
    across = lax.ppermute(half_sum, "rep", [(1, 2), (2, 1)])
    total = add_low(half_sum, across)
    outward = lax.ppermute(total, "rep", [(1, 0), (2, 3)])
    return jnp.where((place == 1) | (place == 2), total, outward).astype(F32)


def columns_of(w_qkv, w_fc1, group):
    rows, qkv = w_qkv.shape
    heads = w_qkv.reshape(rows, 3, group, qkv // 3 // group).transpose(2, 0, 1, 3).reshape(group, rows, -1)
    units = w_fc1.reshape(rows, group, -1).transpose(1, 0, 2)
    found = exchange(jnp.concatenate([heads, units], axis=2))
    found = found.reshape(group * rows, -1)
    return found[:, : qkv // group], found[:, qkv // group :]


def rows_of(grad_qkv, grad_fc1, group):
    rows = grad_qkv.shape[0] // group
    both = jnp.concatenate([grad_qkv, grad_fc1], axis=1).reshape(group, rows, -1)
    found = exchange(both)
    qkv = grad_qkv.shape[1]
    heads = found[:, :, :qkv].reshape(group, rows, 3, qkv // 3).transpose(1, 2, 0, 3).reshape(rows, -1)
    units = found[:, :, qkv:].transpose(1, 0, 2).reshape(rows, -1)
    return heads, units


def standardize(hidden):
    centered = hidden - jnp.mean(hidden, axis=-1, keepdims=True)
    scale = lax.rsqrt(jnp.mean(centered * centered, axis=-1, keepdims=True) + EPSILON)
    return centered * scale, scale


def widen(part):
    return jnp.pad(part, ((0, 0), (0, LANES - part.shape[1])))


def forward_layer(normed, weights, heads, tables):
    qkv_cols, fc1_cols, b_fc1, w_dense, w_fc2 = weights
    mixed = dot(normed, qkv_cols)
    own = heads * HEAD_DIM
    queries, keys, values, attended, log_total = attend(
        *(widen(mixed[:, i * own : (i + 1) * own]) for i in range(3)), heads, *tables
    )
    pre_act = dot(normed, fc1_cols) + b_fc1.astype(F32)
    activation = jax.nn.gelu(pre_act, approximate=True).astype(BF)
    partial_sum = (dot(attended[:, :own], w_dense) + dot(activation, w_fc2)).astype(BF)
    stored = (normed, queries, keys, values, attended, log_total, pre_act, activation)
    return partial_sum, stored


def backward_layer(grad_branch, weights, stored, heads, tables):
    qkv_cols, fc1_cols, b_fc1, w_dense, w_fc2 = weights
    normed, queries, keys, values, attended, log_total, pre_act, activation = stored
    own = heads * HEAD_DIM
    grad_w_fc2 = outer_sum(activation, grad_branch).astype(BF)
    grad_w_dense = outer_sum(attended[:, :own], grad_branch).astype(BF)
    _, gelu_back = jax.vjp(partial(jax.nn.gelu, approximate=True), pre_act)
    grad_pre = gelu_back(times_transposed(grad_branch, w_fc2))[0].astype(BF)
    grad_attended = widen(times_transposed(grad_branch, w_dense).astype(BF))
    grad_mixed = attend_back(queries, keys, values, grad_attended, log_total, heads, *tables)
    grad_mixed = jnp.concatenate([part[:, :own] for part in grad_mixed], axis=1)
    grad_fc1 = outer_sum(normed, grad_pre).astype(BF)
    grad_b_fc1 = jnp.sum(grad_pre.astype(F32), axis=0)
    grad_qkv = outer_sum(normed, grad_mixed).astype(BF)
    grad_normed = (times_transposed(grad_pre, fc1_cols) + times_transposed(grad_mixed, qkv_cols)).astype(BF)
    return grad_normed, (grad_w_fc2, grad_w_dense, grad_fc1, grad_qkv, grad_b_fc1)


def local_any(hidden_in, ln_gain, ln_bias, w_qkv, w_dense, w_fc1, b_fc1, w_fc2, b_fc2, output_grad):
    group = lax.axis_size("grp")
    index = lax.axis_index("grp")
    layers = w_qkv.shape[0]
    span, width = hidden_in.shape[1:]
    seq = span * group
    heads = width // HEAD_DIM // group
    tables = rotary_tables(seq)
    small = jnp.concatenate([ln_gain, ln_bias, b_fc2])
    small = lax.all_gather(small, "grp", axis=1, tiled=True).astype(F32)
    gains, shifts, b_fc2_all = small[:layers], small[layers : 2 * layers], small[2 * layers :]
    hidden = hidden_in.reshape(span, width).astype(F32)
    hidden_all = gather_rows(hidden_in.reshape(span, width))
    weights = []
    for layer in range(layers):
        qkv_cols, fc1_cols = columns_of(w_qkv[layer], w_fc1[layer], group)
        weights.append((qkv_cols, fc1_cols, b_fc1[layer], w_dense[layer], w_fc2[layer]))

    inputs, stored_layers = [], []
    for layer in range(layers):
        inputs.append(hidden)
        if layer == 0:
            normed = (standardize(hidden_all.astype(F32))[0] * gains[0] + shifts[0]).astype(BF)
        else:
            normed = gather_rows((standardize(hidden)[0] * gains[layer] + shifts[layer]).astype(BF))
        partial_sum, stored = forward_layer(normed, weights[layer], heads, tables)
        stored_layers.append(stored)
        hidden = hidden + scatter_sum(partial_sum) + b_fc2_all[layer]

    grad_hidden = output_grad.reshape(span, width)
    small_grads, large_grads = [None] * layers, [None] * layers
    for layer in reversed(range(layers)):
        grad_low = grad_hidden.astype(BF)
        grad_branch = gather_rows(grad_low)
        grad_normed, found = backward_layer(grad_branch, weights[layer], stored_layers[layer], heads, tables)
        grad_w_fc2, grad_w_dense, grad_fc1, grad_qkv, grad_b_fc1 = found
        grad_qkv, grad_fc1 = rows_of(grad_qkv, grad_fc1, group)
        large_grads[layer] = tuple(rep_sum(part) for part in (grad_w_fc2, grad_w_dense, grad_fc1, grad_qkv))
        grad_normed = scatter_sum(grad_normed)
        xhat, scale = standardize(inputs[layer])
        inner = grad_normed * gains[layer]
        mean_inner = jnp.mean(inner, axis=-1, keepdims=True)
        mean_along = jnp.mean(inner * xhat, axis=-1, keepdims=True)
        small_grads[layer] = jnp.concatenate(
            [
                jnp.sum(grad_normed * xhat, axis=0),
                jnp.sum(grad_normed, axis=0),
                jnp.sum(grad_low.astype(F32), axis=0),
                lax.dynamic_update_slice(
                    jnp.zeros((group * grad_b_fc1.shape[0],), F32), grad_b_fc1, (index * grad_b_fc1.shape[0],)
                ),
            ]
        )
        grad_hidden = grad_hidden + (inner - mean_inner - xhat * mean_along) * scale

    summed = lax.psum(jnp.stack(small_grads), ("rep", "grp"))
    own = width // group
    units = b_fc1.shape[1]

    def pick(start, count):
        return lax.dynamic_slice_in_dim(summed, start + index * count, count, 1)

    stacked = [jnp.stack([large_grads[layer][member] for layer in range(layers)]) for member in range(4)]
    return (
        hidden[None],
        grad_hidden[None],
        pick(0, own),
        pick(width, own),
        stacked[3],
        stacked[1],
        stacked[2],
        pick(3 * width, units),
        stacked[0],
        pick(2 * width, own),
    )


SLOTS = [(s, k) for s in range(4) for k in range(2)]
ROWS = 128
EXTRA = 16


def slot_start(place, s, k, size):
    return pl.multiple_of(((place[0] ^ s) * 2 + (place[1] ^ k)) * size, size)


def slot_rows(place, s, k, size=ROWS):
    return pl.ds(slot_start(place, s, k, size), size)


SMALL = pl.CostEstimate(flops=0, bytes_accessed=0, transcendentals=0)


def call(body, outs, place, ins, scratch=(), after=(), hbm=0, mib=16, held=0):
    def run(place, *refs):
        body(place, *refs[len(after) :])

    return pl.pallas_call(
        run,
        name=getattr(body, "func", body).__name__,
        out_shape=[jax.ShapeDtypeStruct(*out) for out in outs],
        in_specs=[pl.BlockSpec(memory_space=pltpu.SMEM)]
        + [pl.BlockSpec(memory_space=pl.ANY)] * len(after)
        + [pl.BlockSpec(memory_space=pltpu.HBM)] * hbm
        + [pl.BlockSpec(memory_space=pltpu.VMEM)] * (len(ins) - hbm),
        out_specs=[pl.BlockSpec(memory_space=pltpu.VMEM)] * len(outs),
        scratch_shapes=list(scratch),
        input_output_aliases={1 + len(after) + len(ins) - held + i: i for i in range(held)},
        compiler_params=pltpu.CompilerParams(vmem_limit_bytes=mib * 1024 * 1024),
        cost_estimate=SMALL,
    )(place, *after, *ins)


def gather_pieces(part):
    mine = [part, swap(part, 2), swap(part, 4), swap(part, 6)]
    other = [swap(piece, 1) for piece in mine]
    return [piece for pair in zip(mine, other) for piece in pair]


def put_columns(out, start, value):
    rows = value.shape[0]
    for b in range(value.shape[1] // LANES):
        out[start + b * rows : start + (b + 1) * rows, :] = value[:, b * LANES : (b + 1) * LANES]


def heads_of(place, w_qkv, layer, s, k, j):
    start = j * (w_qkv.shape[2] // 3) + slot_start(place, s, k, LANES)
    return w_qkv[layer, :, pl.ds(pl.multiple_of(start, LANES), LANES)]


HALF = ROWS // 2
HEADS_ROWS, HALF_ROWS = 3 * ROWS, 4 * HALF
FIRST_MINE = 8 * ROWS
FIRST_OTHERS = FIRST_MINE + HEADS_ROWS + HALF_ROWS
FIRST_SMALL = FIRST_OTHERS + HEADS_ROWS + HALF_ROWS
FIRST_ROWS = FIRST_SMALL + EXTRA
OTHERS_MINE = 8 * ROWS
OTHERS_SMALL = OTHERS_MINE + HEADS_ROWS + HALF_ROWS
OTHERS_ROWS = OTHERS_SMALL + EXTRA


def half_start(place, other):
    parity = place[2] & 1
    return pl.multiple_of((1 - parity if other else parity) * HALF, HALF)


def pack_first_kernel(hidden_from, qkv_from, fc1_from, gain_from, shift_from, bias_from, o0, o1, o2, o3, hidden, w_qkv, w_fc1, gain, shift, bias, sems):
    index = lax.axis_index("grp")
    place = (index // 2, index % 2, lax.axis_index("rep"))
    outs = (o0, o1, o2, o3)
    pairs = (
        (hidden_from, hidden),
        (gain_from, gain),
        (shift_from, shift),
        (bias_from, bias),
        (qkv_from.at[0], w_qkv),
        (fc1_from.at[0, pl.ds(half_start(place, False), HALF), :], w_fc1),
    )
    moves = [pltpu.make_async_copy(*pair, sems.at[i]) for i, pair in enumerate(pairs)]
    for move in moves:
        move.start()
    for move in moves[:4]:
        move.wait()
    for out in outs:
        put_columns(out, 0, hidden[...])
        out[FIRST_SMALL:, :] = jnp.zeros((EXTRA, LANES), BF)
        for i, part in enumerate((gain, shift, bias)):
            out[FIRST_SMALL + 2 * i : FIRST_SMALL + 2 * i + 2, :] = part[...]
    moves[4].wait()
    third = w_qkv.shape[1] // 3
    for s, k in SLOTS:
        row = (FIRST_MINE, FIRST_OTHERS)[k]
        for j in range(3):
            lanes = pl.ds(pl.multiple_of(j * third + slot_start(place, s, k, LANES), LANES), LANES)
            outs[s][row + j * ROWS : row + (j + 1) * ROWS, :] = w_qkv[:, lanes]
    moves[5].wait()
    for s, k in SLOTS:
        row = (FIRST_MINE, FIRST_OTHERS)[k] + HEADS_ROWS
        put_columns(outs[s], row, w_fc1[:, pl.ds(slot_start(place, s, k, 4 * LANES), 4 * LANES)])


def others_first_kernel(place, b0, b1, b2, b3, out):
    for s, block in enumerate((b0, b1, b2, b3)):
        out[s, :OTHERS_MINE, :] = block[:FIRST_MINE, :]
        out[s, OTHERS_MINE:OTHERS_SMALL, :] = block[FIRST_OTHERS:FIRST_SMALL, :]
        out[s, OTHERS_SMALL:, :] = block[FIRST_SMALL:, :]


def near_first_kernel(place, b0, b1, b2, b3, b4, out):
    for i, (s, k) in enumerate(SLOTS):
        block, mine_at, _ = first_block(s, k, (b0, b1, b2, b3, b4))
        out[i] = block[mine_at + HEADS_ROWS : mine_at + HEADS_ROWS + HALF_ROWS, :]


def first_block(s, k, blocks):
    if k:
        return blocks[4].at[s], OTHERS_MINE, OTHERS_SMALL
    return blocks[s], FIRST_MINE, FIRST_SMALL


def pack_heads_kernel(layer, place, w_qkv, keep, give):
    for s, k in SLOTS:
        for j in range(3):
            (keep, give)[k][s, :, j * LANES : (j + 1) * LANES] = heads_of(place, w_qkv, layer, s, k, j)


def pair_kernel(place, keep, came, *outs):
    for s, out in enumerate(outs):
        out[0], out[1] = keep[s], came[s]


def pack_units_kernel(layer, place, w_fc1, *outs):
    units = outs[0].shape[2]
    for s, k in SLOTS:
        outs[s][k] = w_fc1[layer, :, pl.ds(slot_start(place, s, k, units), units)]


def pack_units_grads_kernel(layer, place, w_fc1, grads, *outs):
    units = outs[0].shape[1]
    low = grads[...].astype(BF)
    for s in range(4):
        for k in range(2):
            lanes = pl.ds(slot_start(place, s, k, units), units)
            outs[s][k * HALF : (k + 1) * HALF, :] = w_fc1[layer, pl.ds(half_start(place, False), HALF), lanes]
            outs[s][(1 + k) * ROWS : (2 + k) * ROWS, :] = low[:, k * units : (k + 1) * units]


def near_units_kernel(place, b0, b1, b2, b3, out):
    for s, block in enumerate((b0, b1, b2, b3)):
        out[s] = block[:ROWS, :]


def others_units_grads_kernel(place, b0, b1, b2, b3, far, out):
    for s, block in enumerate((b0, b1, b2, b3)):
        out[s, :HALF, :] = block[HALF:ROWS, :]
        out[s, HALF:ROWS, :] = far[s, HALF:, :]
        out[s, ROWS:, :] = block[ROWS:, :]


def send_blocks(place, packed):
    return [packed[0]] + [swap(packed[s], 2 * s) for s in (1, 2, 3)]


def others_kernel(place, b0, b1, b2, b3, out):
    for s, block in enumerate((b0, b1, b2, b3)):
        out[s] = block[1]


def swap_others(place, blocks, after=()):
    (other,) = call(others_kernel, [((4,) + blocks[0].shape[1:], BF)], place, blocks, after=after)
    return [*blocks, swap(other, 1)]


def block_of(s, k, blocks):
    return blocks[4].at[s] if k else blocks[s].at[0]


def project_heads(normed, weight, cosine, sine, q_out, k_out, v_out, values_down):
    step = 256
    for start in range(0, normed.shape[0], step):
        rows = slice(start, start + step)
        mixed = dot(normed[rows, :], weight[...])
        q_out[rows, :] = turn(mixed[:, :LANES], cosine[rows, :], sine[rows, :], 1.0).astype(BF)
        k_out[rows, :] = turn(mixed[:, LANES : 2 * LANES], cosine[rows, :], sine[rows, :], 1.0).astype(BF)
        values = mixed[:, 2 * LANES :]
        v_out[rows, :] = values.astype(BF)
        values_down[:, rows] = values.T.astype(BF)


def own_head(head):
    down = lax.broadcasted_iota(jnp.int32, (LANES, 1), 0)
    return (down >= head * HEAD_DIM) & (down < (head + 1) * HEAD_DIM)


def softmax_block(keys, chosen, block):
    scores = mask_diagonal(dot_general(keys, chosen, (1, 1)), block)
    row_max = jnp.max(scores, axis=0, keepdims=True)
    exponent = jnp.exp(scores - row_max)
    row_total = jnp.sum(exponent, axis=0, keepdims=True)
    return exponent * (1.0 / row_total), row_max + jnp.log(row_total)


BLOCK = 256
HEADS_HERE = LANES // HEAD_DIM


def first_attend_kernel(place, b0, b1, b2, b3, b4, cosine, sine, normed, xhat_out, weight, params, q_out, k_out, v_out, att_out, log_out, values_down):
    for s, k in SLOTS:
        rows = slot_rows(place, s, k)
        block, mine_at, small_at = first_block(s, k, (b0, b1, b2, b3, b4))
        for j in range(3):
            weight[rows, j * LANES : (j + 1) * LANES] = block[mine_at + j * ROWS : mine_at + (j + 1) * ROWS, :]
        params[:, rows] = block[small_at:, :].astype(F32)
        for b in range(8):
            normed[rows, b * LANES : (b + 1) * LANES] = block[b * ROWS : (b + 1) * ROWS, :]
    gain, shift = params[0:1, :], params[2:3, :]

    def norm_rows(rows):
        xhat = standardize(normed[rows, :].astype(F32))[0]
        xhat_out[rows, :] = xhat.astype(BF)
        normed[rows, :] = (xhat * gain + shift).astype(BF)

    loop_rows(normed.shape[0], 4 * ROWS, norm_rows)
    project_heads(normed, weight, cosine, sine, q_out, k_out, v_out, values_down)
    for start in range(0, normed.shape[0], BLOCK):
        stop = start + BLOCK
        queries = q_out[start:stop, :] * SCORE_SCALE
        total = jnp.zeros((LANES, BLOCK), F32)
        for head in range(HEADS_HERE):
            chosen = jnp.where(head_mask(head), queries, 0.0).astype(BF)
            probabilities, log_total = softmax_block(k_out[:stop, :], chosen, BLOCK)
            log_out[head : head + 1, start:stop] = log_total
            found = dot(values_down[:, :stop], probabilities.astype(BF))
            total = total + jnp.where(own_head(head), found, 0.0)
        att_out[start:stop, :] = total.T.astype(BF)


GELU_A = 0.7978845608028654
GELU_B = 0.044715


def gelu(pre):
    return pre * (0.5 + 0.5 * jnp.tanh(GELU_A * pre * (1.0 + GELU_B * pre * pre)))


def gelu_slope(pre):
    square = pre * pre
    wave = jnp.tanh(GELU_A * pre * (1.0 + GELU_B * square))
    return 0.5 * (1.0 + wave) + 0.5 * pre * (1.0 - wave * wave) * (GELU_A * (1.0 + 3.0 * GELU_B * square))


def loop_rows(count, step, body):
    def one(i, carry):
        body(pl.ds(pl.multiple_of(i * step, step), step))
        return carry

    lax.fori_loop(0, count // step, one, 0)


def put_slots(place, rows_of_block, keep, give):
    for s in range(4):
        keep[s] = rows_of_block(slot_rows(place, s, 0))
        give[s] = rows_of_block(slot_rows(place, s, 1))


def put_pairs(place, rows_of_block, outs):
    for s, k in SLOTS:
        outs[s][k] = rows_of_block(slot_rows(place, s, k))


def first_units_kernel(place, normed, near, far, bias, w_fc2, w_dense, attended, weight, act, slope, whole):
    for s, k in SLOTS:
        for part, other_plane in ((near.at[SLOTS.index((s, k))], False), (far.at[SLOTS.index((s, k))], True)):
            start = slot_start(place, s, k, ROWS) + half_start(place, other_plane)
            for b in range(4):
                rows = pl.ds(pl.multiple_of(start, HALF), HALF)
                weight[rows, b * LANES : (b + 1) * LANES] = part[b * HALF : (b + 1) * HALF, :]
    shift = bias[0:1, :].astype(F32)

    def rows_done(rows):
        found = dot(normed[rows, :], weight[...]) + shift
        slope[rows, :] = gelu_slope(found)
        act[rows, :] = gelu(found).astype(BF)
        whole[rows, :] = (dot(act[rows, :], w_fc2[0]) + dot(attended[rows, :], w_dense[0])).astype(BF)

    loop_rows(normed.shape[0], 256, rows_done)


def split_kernel(place, whole, keep, give):
    put_slots(place, lambda rows: whole[rows, :], keep, give)


def split_sum_kernel(place, keep, came, for_x, for_y, corner):
    def rows_done(rows):
        for s, out in ((1, for_x), (2, for_y), (3, corner)):
            out[rows, :] = keep[s, rows, :] + came[s, rows, :]

    loop_rows(for_x.shape[0], 16, rows_done)


def begin_scatter(place, keep, give, after=()):
    came = swap(give, 1)
    shape = (keep.shape[1:], BF)
    for_x, for_y, corner = call(split_sum_kernel, [shape] * 3, place, [keep, came], after=after)
    from_corner, from_x, from_y = swap(corner, 6), swap(for_x, 2), swap(for_y, 4)
    return [keep, came, from_x, from_y, from_corner], for_x


def sum_terms(terms):
    total = terms[0][0].astype(F32) + terms[1][0].astype(F32)
    for term in terms[2:]:
        total = total + term[...].astype(F32)
    return total


def next_hidden_kernel(place, *refs):
    terms, (hidden, params, hidden_out, normed) = refs[:5], refs[5:]
    found = hidden[...].astype(F32) + sum_terms(terms) + params[4:5, :]
    hidden_out[...] = found
    normed[...] = (standardize(found)[0] * params[1:2, :] + params[3:4, :]).astype(BF)


def low_kernel(place, wide, low):
    low[...] = wide[...].astype(BF)


def assemble_kernel(place, *refs):
    for (s, k), piece in zip(SLOTS, refs[:8]):
        refs[8][slot_rows(place, s, k), :] = piece[...]


def last_hidden_kernel(place, act, attended, w_fc2, w_dense, keep, give, whole):
    def rows_done(rows):
        whole[rows, :] = (dot(act[rows, :], w_fc2[1]) + dot(attended[rows, :], w_dense[1])).astype(BF)

    loop_rows(act.shape[0], 256, rows_done)
    put_slots(place, lambda rows: whole[rows, :], keep, give)


def last_hidden_of_core(core, place, *refs):
    @pl.when(place[1] == core)
    def work():
        last_hidden_kernel(place, *refs[:4], *refs[-3:])


def last_sum_kernel(place, *refs):
    terms, (hidden, params, out, token) = refs[:5], refs[5:]
    token[...] = jnp.zeros_like(token)
    out[...] = hidden[...] + sum_terms(terms) + params[5:6, :]


SMALL_ROWS = 16


def put_halves(out, value, start, rows):
    half = out.shape[1]
    for j in range(2):
        out[j * rows + start : j * rows + start + value.shape[0], :] = value[:, j * half : (j + 1) * half]


def second_ready_kernel(place, b0, b1, b2, b3, other, far, weight, grads):
    units = weight.shape[1]
    for s, k in SLOTS:
        block = other.at[s] if k else (b0, b1, b2, b3)[s]
        parts = (block[:HALF, :], block[HALF:ROWS, :] if k else far[s, :HALF, :])
        for part, other_plane in zip(parts, (False, True)):
            start = slot_start(place, s, k, ROWS) + half_start(place, other_plane)
            weight[pl.ds(pl.multiple_of(start, HALF), HALF), :] = part
        for j in range(2):
            grads[slot_rows(place, s, k), j * units : (j + 1) * units] = block[(1 + j) * ROWS : (2 + j) * ROWS, :]


def second_units_kernel(place, *refs):
    pieces, refs = refs[:8], refs[8:]
    bias, weight, grads, normed, act, pre, chunk = refs
    units = weight.shape[1]
    for (s, k), piece in zip(SLOTS, pieces):
        normed[slot_rows(place, s, k), :] = piece[...]
    shift = bias[1:2, :].astype(F32)

    def rows_done(rows):
        found = dot(normed[rows, :], weight[...]) + shift
        pre[rows, :] = found
        act[rows, :] = gelu(found).astype(BF)

    loop_rows(normed.shape[0], 256, rows_done)
    for start in range(0, units, 256):
        put_halves(chunk, outer_sum(act[:, start : start + 256], grads[...]).astype(BF), start, units)


def units_back(layer, place, grads, w_fc2, slope_of, normed, weight, chunk, sums, part_normed, grad_pre, grad_w):
    sums[...] = jnp.zeros_like(sums)
    width = grads.shape[1]
    units = weight.shape[1]

    def rows_done(rows):
        found = (times_transposed(grads[rows, :], w_fc2[layer]) * slope_of(rows)).astype(BF)
        grad_pre[rows, :] = found
        sums[0:1, :width] += jnp.sum(grads[rows, :].astype(F32), axis=0, keepdims=True)
        sums[1:2, :units] += jnp.sum(found.astype(F32), axis=0, keepdims=True)
        part_normed[rows, :] = times_transposed(found, weight[...])

    loop_rows(grads.shape[0], 256, rows_done)
    for start in range(0, width, 256):
        rows = slice(start, start + 256)
        grad_w[rows, :] = outer_sum(normed[:, rows], grad_pre[...]).astype(BF)
    for i, (s, k) in enumerate(SLOTS):
        chunk[i * ROWS : (i + 1) * ROWS, :] = grad_w[slot_rows(place, s, k), :]


def second_units_back_kernel(place, grads, w_fc2, w_dense, pre, normed, weight, chunk, sums, part_normed, grad_att, grad_pre, grad_w):
    def slope_of(rows):
        grad_att[rows, :] = times_transposed(grads[rows, :], w_dense[1]).astype(BF)
        return gelu_slope(pre[rows, :])

    units_back(1, place, grads, w_fc2, slope_of, normed, weight, chunk, sums, part_normed, grad_pre, grad_w)


def first_units_back_kernel(place, *refs):
    pieces, refs = refs[:8], refs[8:]
    act, w_fc2, slope, normed, weight, grads, chunk_rows, chunk, sums, part_normed, grad_pre, grad_w = refs
    for (s, k), piece in zip(SLOTS, pieces):
        grads[slot_rows(place, s, k), :] = piece[...]
    units_back(
        0, place, grads, w_fc2, lambda rows: slope[rows, :], normed, weight, chunk, sums, part_normed, grad_pre, grad_w
    )
    units = act.shape[1]
    for start in range(0, units, 256):
        put_halves(chunk_rows, outer_sum(act[:, start : start + 256], grads[...]).astype(BF), start, units)


def attend_back_block(start, q_ref, k_ref, v_ref, grad_att, keys_down, k_sum, v_sum, cosine, sine, mixed, found_p):
    stop = start + BLOCK
    queries = q_ref[start:stop, :] * SCORE_SCALE
    grad_queries = jnp.zeros((LANES, BLOCK), F32)
    for head in range(HEADS_HERE):
        chosen = jnp.where(head_mask(head), queries, 0.0).astype(BF)
        chosen_grads = jnp.where(head_mask(head), grad_att, 0.0).astype(BF)
        probabilities = found_p(head, chosen)
        grad_probs = dot_general(v_ref[:stop, :], chosen_grads, (1, 1))
        row_inner = jnp.sum(grad_probs * probabilities, axis=0, keepdims=True)
        grad_scores = (probabilities * (grad_probs - row_inner)).astype(BF)
        k_sum[:stop, :] += dot(grad_scores, chosen)
        v_sum[:stop, :] += dot(probabilities.astype(BF), chosen_grads)
        grad_queries = grad_queries + jnp.where(own_head(head), dot(keys_down[:, :stop], grad_scores), 0.0)
    rows = slice(start, stop)
    mixed[rows, :LANES] = turn(grad_queries.T, cosine[rows, :], sine[rows, :], -1.0).astype(BF)


def mixed_rest(cosine, sine, mixed, k_sum, v_sum):
    mixed[:, LANES : 2 * LANES] = turn(k_sum[...], cosine[...], sine[...], -1.0).astype(BF)
    mixed[:, 2 * LANES :] = v_sum[...].astype(BF)


def mixed_outer(normed, mixed, grad_w):
    for start in range(0, normed.shape[1], 256):
        rows = slice(start, start + 256)
        grad_w[rows, :] = outer_sum(normed[:, rows], mixed[...]).astype(BF)


def mixed_inner(normed, weight, mixed, part_normed, whole):
    def rows_done(rows):
        whole[rows, :] = (times_transposed(mixed[rows, :], weight[...]) + part_normed[rows, :]).astype(BF)

    loop_rows(normed.shape[0], 256, rows_done)


def mixed_back(place, normed, weight, cosine, sine, mixed, k_sum, v_sum, grad_w, part_normed, whole):
    mixed_rest(cosine, sine, mixed, k_sum, v_sum)
    mixed_outer(normed, mixed, grad_w)
    mixed_inner(normed, weight, mixed, part_normed, whole)


def put_heads_chunk(place, chunk, grad_w, grad_dense):
    heads = grad_w.shape[1]
    for i, (s, k) in enumerate(SLOTS):
        rows = slice(i * ROWS, (i + 1) * ROWS)
        chunk[rows, :heads] = grad_w[slot_rows(place, s, k), :]
        chunk[rows, heads:] = grad_dense[:, rows]


def second_attend_kernel(place, normed, b0, b1, b2, b3, cosine, sine, grad_att, part_normed, att_out, mixed, keep_n, give_n, weight, q_ref, k_ref, v_ref, values_down, keys_down, k_sum, v_sum):
    for s, k in SLOTS:
        weight[slot_rows(place, s, k), :] = (b0, b1, b2, b3)[s][k]
    project_heads(normed, weight, cosine, sine, q_ref, k_ref, v_ref, values_down)
    k_sum[...] = jnp.zeros_like(k_sum)
    v_sum[...] = jnp.zeros_like(v_sum)
    keys_down[...] = (k_ref[...].astype(F32) * SCORE_SCALE).T.astype(BF)
    for start in range(0, normed.shape[0], BLOCK):
        stop = start + BLOCK
        total = [jnp.zeros((LANES, BLOCK), F32)]

        def found_p(head, chosen):
            probabilities, _ = softmax_block(k_ref[:stop, :], chosen, BLOCK)
            found = dot(values_down[:, :stop], probabilities.astype(BF))
            total[0] = total[0] + jnp.where(own_head(head), found, 0.0)
            return probabilities

        attend_back_block(start, q_ref, k_ref, v_ref, grad_att[start:stop, :], keys_down, k_sum, v_sum, cosine, sine, mixed, found_p)
        att_out[start:stop, :] = total[0].T.astype(BF)
    mixed_rest(cosine, sine, mixed, k_sum, v_sum)
    for s in range(4):
        rows = pl.ds(pl.multiple_of((place[0] ^ s) * 2 * ROWS, 2 * ROWS), 2 * ROWS)
        found = (times_transposed(mixed[rows, :], weight[...]) + part_normed[rows, :]).astype(BF)
        odd = place[1] == 1
        keep_n[s] = jnp.where(odd, found[ROWS:, :], found[:ROWS, :])
        give_n[s] = jnp.where(odd, found[:ROWS, :], found[ROWS:, :])


def second_heads_kernel(place, normed, mixed, attended, grads, chunk, grad_w):
    mixed_outer(normed, mixed, grad_w)
    put_heads_chunk(place, chunk, grad_w, outer_sum(attended[...], grads[...]).astype(BF))


def norm_back(gain_row, grad_normed, hidden, params, grads):
    xhat, scale = standardize(hidden[...].astype(F32))
    inner = grad_normed * params[gain_row : gain_row + 1, :]
    mean_inner = jnp.mean(inner, axis=-1, keepdims=True)
    mean_along = jnp.mean(inner * xhat, axis=-1, keepdims=True)
    return grads[...] + (inner - mean_inner - xhat * mean_along) * scale, xhat


def second_norm_back_kernel(place, *refs):
    terms, (hidden, params, grads, grads_out, grads_low, sums) = refs[:5], refs[5:]
    grad_normed = sum_terms(terms)
    found, xhat = norm_back(1, grad_normed, hidden, params, grads)
    grads_out[...] = found
    grads_low[...] = found.astype(BF)
    sums[0:1, :] = jnp.sum(grad_normed * xhat, axis=0, keepdims=True)
    sums[1:2, :] = jnp.sum(grad_normed, axis=0, keepdims=True)


def first_norm_back_kernel(place, *refs):
    terms, (hidden, params, grads, sums0, sums1, grads_out, small) = refs[:5], refs[5:]
    total = sum_terms(terms)
    grads_out[...] = norm_back(0, total[:ROWS, :], hidden, params, grads)[0]
    small[0:8, :] = total[ROWS : ROWS + 8, :LANES]
    for layer, sums in ((0, sums0), (1, sums1)):
        small[4 + layer : 5 + layer, :] = sums[0:1, slot_rows(place, 0, 0)]
        for j in range(4):
            small[8 + 4 * layer + j : 9 + 4 * layer + j, :] = sums[1:2, j * LANES : (j + 1) * LANES]


def first_attend_back_kernel(place, grads, w_dense, q_ref, k_ref, v_ref, log_in, cosine, sine, normed, xhat, weight, part_normed, ln_sums1, mixed, keep_n, give_n, keys_down, k_sum, v_sum, whole, ln_sums):
    k_sum[...] = jnp.zeros_like(k_sum)
    v_sum[...] = jnp.zeros_like(v_sum)
    keys_down[...] = (k_ref[...].astype(F32) * SCORE_SCALE).T.astype(BF)
    for start in range(0, normed.shape[0], BLOCK):
        stop = start + BLOCK

        def found_p(head, chosen):
            scores = mask_diagonal(dot_general(k_ref[:stop, :], chosen, (1, 1)), BLOCK)
            return jnp.exp(scores - log_in[head : head + 1, start:stop])

        grad_att = times_transposed(grads[start:stop, :], w_dense[0]).astype(BF)
        attend_back_block(start, q_ref, k_ref, v_ref, grad_att, keys_down, k_sum, v_sum, cosine, sine, mixed, found_p)
    mixed_rest(cosine, sine, mixed, k_sum, v_sum)
    mixed_inner(normed, weight, mixed, part_normed, whole)
    ln_sums[...] = jnp.zeros_like(ln_sums)

    def rows_done(rows):
        part = whole[rows, :].astype(F32)
        ln_sums[0:1, :] += jnp.sum(part * xhat[rows, :].astype(F32), axis=0, keepdims=True)
        ln_sums[2:3, :] += jnp.sum(part, axis=0, keepdims=True)

    loop_rows(normed.shape[0], 256, rows_done)
    ln_sums[1:2, :] = ln_sums1[0:1, :]
    ln_sums[3:4, :] = ln_sums1[1:2, :]
    for s in range(4):
        for k, out in ((0, keep_n), (1, give_n)):
            rows = slot_rows(place, s, k)
            out[s, :ROWS, :] = whole[rows, :]
            out[s, ROWS:, :] = jnp.zeros((EXTRA, out.shape[2]), BF)
            out[s, ROWS : ROWS + 8, :LANES] = ln_sums[:, rows].astype(BF)


INWARD, ACROSS, OUTWARD = [(0, 1), (3, 2)], [(1, 2), (2, 1)], [(1, 0), (2, 3)]


def along(value, pairs):
    return lax.ppermute(value, "rep", pairs)


def low_sum(left, right):
    return left[...] + right[...]


def is_middle(place):
    return (place[2] == 1) | (place[2] == 2)


def tick_kernel(has, place, *refs):
    refs = list(refs)
    if has[0]:
        chunk, came = refs.pop(0), refs.pop(0)
    if has[1]:
        before, crossed = refs.pop(0), refs.pop(0)
    if has[2]:
        coming = refs.pop(0)
    half = refs.pop(0) if has[0] else None
    going = refs.pop(0) if has[1] else None

    def half_rows(rows):
        half[rows, :] = low_sum(chunk.at[rows, :], came.at[rows, :])

    def going_rows(rows):
        found = low_sum(before.at[rows, :], crossed.at[rows, :])
        going[rows, :] = jnp.where(is_middle(place), found, coming[rows, :]) if has[2] else found

    for body, out, rows in ((half_rows, half, has[0] and chunk.shape[0]), (going_rows, going, has[1] and before.shape[0])):
        if out is not None:
            loop_rows(rows, 208 if rows % 208 == 0 else 256, body)
            if out.shape[0] > rows:
                out[rows:, :] = coming[rows:, :]


def tick(place, step, last, coming, after=(), joint=False):
    if step is not None and last is not None and not joint:
        (half,) = tick(place, step, None, None, after)
        (going,) = tick(place, None, last, coming, (half,))
        return half, going
    ins, outs = [], []
    for pair in (step, last):
        if pair is not None:
            ins += pair
            outs.append((pair[0].shape if coming is None or pair is step else coming.shape, pair[0].dtype))
    if coming is not None:
        ins.append(coming)
    has = (step is not None, last is not None, coming is not None)
    return call(partial(tick_kernel, has), outs, place, ins, after=after)


def add_small_kernel(place, chunk, small, out):
    rows = chunk.shape[0]
    out[:rows, :] = chunk[...]
    out[rows:, :LANES] = small[...].astype(BF)
    out[rows:, LANES:] = jnp.zeros((SMALL_ROWS, chunk.shape[1] - LANES), BF)


def pick_kernel(place, total, came, o0, o1, o2, o3, *rest):
    heads = o0.shape[2]
    for i, (s, k) in enumerate(SLOTS):
        out = (o0, o1, o2, o3)[s]

        def rows_done(rows):
            here = pl.ds(pl.multiple_of(rows.start + i * ROWS, rows.size), rows.size)
            found = jnp.where(is_middle(place), total[here, :], came[here, :])
            out[k, rows, :] = found[:, :heads]
            if rest:
                rest[0][rows, i * ROWS : (i + 1) * ROWS] = found[:, heads:].astype(F32)

        loop_rows(ROWS, 32, rows_done)


def pick_both_kernel(place, total_f, came_f, total_q, came_q, o0, o1, o2, o3, dense):
    units = total_f.shape[1]
    heads = o0.shape[2] - units
    for i, (s, k) in enumerate(SLOTS):
        out = (o0, o1, o2, o3)[s]

        def rows_done(rows):
            here = pl.ds(pl.multiple_of(rows.start + i * ROWS, rows.size), rows.size)
            out[k, rows, :units] = jnp.where(is_middle(place), total_f[here, :], came_f[here, :])
            found = jnp.where(is_middle(place), total_q[here, :], came_q[here, :])
            out[k, rows, units:] = found[:, :heads]
            dense[rows, i * ROWS : (i + 1) * ROWS] = found[:, heads:].astype(F32)

        loop_rows(ROWS, 32, rows_done)


def pick_both(place, units_pair, heads_pair, heads, after=()):
    columns = units_pair[0].shape[1] + heads
    outs = [((2, ROWS, columns), BF)] * 4 + [((ROWS, 8 * LANES), F32)]
    return call(pick_both_kernel, outs, place, [*units_pair, *heads_pair], after=after)


def pick(place, total, came, heads, after=()):
    outs = [((2, ROWS, heads), BF)] * 4
    if heads < total.shape[1]:
        outs.append(((ROWS, 8 * LANES), F32))
    return call(pick_kernel, outs, place, [total, came], after=after)


def chosen_sum(place, total, outward):
    middle = (place[2] == 1) | (place[2] == 2)
    return jnp.where(middle, total, outward).astype(F32)


def final_call(body, place, ins, shape, layer, before=None, after=()):
    skip = len(after) + (before is not None)

    def run(place, *refs):
        *ins, out, token, found, sems = refs[skip:]
        body(place, ins, out.at[layer], found, sems)
        token[...] = jnp.zeros_like(token)

    return pl.pallas_call(
        run,
        name=body.__name__,
        out_shape=[jax.ShapeDtypeStruct((2,) + shape, F32), jax.ShapeDtypeStruct((8, LANES), F32)],
        in_specs=[pl.BlockSpec(memory_space=pltpu.SMEM)]
        + [pl.BlockSpec(memory_space=pltpu.HBM)] * (before is not None)
        + [pl.BlockSpec(memory_space=pl.ANY)] * len(after)
        + [pl.BlockSpec(memory_space=pltpu.VMEM)] * len(ins),
        out_specs=[pl.BlockSpec(memory_space=pltpu.HBM), pl.BlockSpec(memory_space=pltpu.VMEM)],
        scratch_shapes=[pltpu.VMEM(shape, F32), pltpu.SemaphoreType.DMA((8,))],
        input_output_aliases={} if before is None else {1: 0},
        compiler_params=pltpu.CompilerParams(vmem_limit_bytes=16 * 1024 * 1024),
        cost_estimate=SMALL,
    )(place, *([] if before is None else [before]), *after, *ins)


def final_rows_start(place, total, came, out, found, sems):
    half, rows = total.shape[1], out.shape[0]
    step = rows // 4

    def move(i):
        put = pl.ds(pl.multiple_of(i * step, step), step)
        return pltpu.make_async_copy(found.at[put, :], out.at[put, :], sems.at[i])

    def one(i, carry):
        put = pl.ds(pl.multiple_of(i * step, step), step)
        for j in range(2):
            part = pl.ds(pl.multiple_of(i * step + j * rows, step), step)
            found[put, j * half : (j + 1) * half] = jnp.where(is_middle(place), total[part, :], came[part, :]).astype(F32)
        move(i).start()
        return carry

    lax.fori_loop(0, 4, one, 0)
    return [move(i) for i in range(4)]


def final_rows_kernel(place, ins, out, found, sems):
    for move in final_rows_start(place, *ins, out, found, sems):
        move.wait()


def final_units_kernel(place, blocks, out, found, sems):
    units, moves = out.shape[1] // 8, []
    for i, (s, k) in enumerate(SLOTS):
        put = slice(i * units, (i + 1) * units)
        block = block_of(s, k, blocks)

        def rows_done(rows):
            found[rows, put] = block[rows, :units].astype(F32)

        loop_rows(ROWS, 32, rows_done)
        moves.append(pltpu.make_async_copy(found.at[:, put], out.at[:, slot_rows(place, s, k, units)], sems.at[i]))
        moves[-1].start()
    for move in moves:
        move.wait()


def final_heads_kernel(place, blocks, out, found, sems):
    third = out.shape[1] // 3
    for s, k in SLOTS:
        block = block_of(s, k, blocks)

        def rows_done(rows):
            part = block[rows, block.shape[1] - 3 * LANES :].astype(F32)
            for j in range(3):
                lanes = pl.ds(pl.multiple_of(j * third + slot_start(place, s, k, LANES), LANES), LANES)
                found[rows, lanes] = part[:, j * LANES : (j + 1) * LANES]

        loop_rows(ROWS, 32, rows_done)
    move = pltpu.make_async_copy(found, out, sems.at[0])
    move.start()
    move.wait()


def last_rows_kernel(place, before, total, came, out, gain, shift, bias_fc1, bias_fc2, found, sems):
    rows = slice(total.shape[0] - SMALL_ROWS, total.shape[0])
    small = jnp.where(is_middle(place), total[rows, :LANES], came[rows, :LANES]).astype(F32)
    moves = final_rows_start(place, total, came, out.at[0], found, sems)
    gain[...] = small[0:2, :]
    shift[...] = small[2:4, :]
    bias_fc2[...] = small[4:6, :]
    for layer in range(2):
        for j in range(4):
            bias_fc1[layer : layer + 1, j * LANES : (j + 1) * LANES] = small[8 + 4 * layer + j : 9 + 4 * layer + j, :]
    for move in moves:
        move.wait()


def local_plane(hidden_in, ln_gain, ln_bias, w_qkv, w_dense, w_fc1, b_fc1, w_fc2, b_fc2, output_grad):
    index = lax.axis_index("grp")
    place = jnp.stack([index // 2, index % 2, lax.axis_index("rep")]).astype(jnp.int32)
    span, width = hidden_in.shape[1:]
    seq = span * 8
    units = b_fc1.shape[1]
    own = 3 * LANES
    cosine, sine = rotary_tables(seq)
    hidden0 = hidden_in.reshape(span, width)
    grads1 = output_grad.reshape(span, width)

    wide, column, chunk_shape = ((seq, width), BF), ((seq, LANES), BF), ((seq, units), BF)
    blocks_n, blocks_n0 = ((4, ROWS, width), BF), ((4, ROWS + EXTRA, width), BF)
    blocks_f, blocks_q = ((2, ROWS, units), BF), ((2, ROWS, own), BF)
    mine, mine_low = ((span, width), F32), ((span, width), BF)
    sums_shape, part_shape = ((8, width), F32), ((seq, width), F32)
    head_scratch = [pltpu.VMEM((LANES, seq), BF), pltpu.VMEM((seq, LANES), F32), pltpu.VMEM((seq, LANES), F32)]
    back_scratch = [pltpu.VMEM((seq, own), BF), pltpu.VMEM((width, own), BF), pltpu.VMEM((seq, width), BF)]
    column_scratch = [pltpu.VMEM((seq, LANES), BF)] * 3
    units_scratch = [pltpu.VMEM((seq, units), BF), pltpu.VMEM((width, units), BF)]

    rows = [hidden0.shape, ln_gain.shape, ln_bias.shape, b_fc2.shape, w_qkv.shape[1:], (HALF, w_fc1.shape[2])]
    rows = [rows[0], *rows[4:], *rows[1:4]]
    packed = pl.pallas_call(
        pack_first_kernel,
        name="pack_first_kernel",
        out_shape=[jax.ShapeDtypeStruct((FIRST_ROWS, LANES), BF)] * 4,
        in_specs=[pl.BlockSpec(memory_space=pltpu.HBM)] * 6,
        out_specs=[pl.BlockSpec(memory_space=pltpu.VMEM)] * 4,
        scratch_shapes=[pltpu.VMEM(shape, BF) for shape in rows] + [pltpu.SemaphoreType.DMA((6,))],
        compiler_params=pltpu.CompilerParams(vmem_limit_bytes=60 * 1024 * 1024),
        cost_estimate=SMALL,
    )(hidden0, w_qkv, w_fc1, ln_gain, ln_bias, b_fc2)
    first = send_blocks(place, packed)
    packed = call(partial(pack_units_grads_kernel, 1), [((3 * ROWS, units), BF)] * 4, place, [w_fc1, grads1])
    keep, give = call(partial(pack_heads_kernel, 1), [((4, ROWS, own), BF)] * 2, place, [w_qkv], after=[packed[0]])
    pairs1 = call(pair_kernel, [blocks_q] * 4, place, [keep, swap(give, 1)])
    (others0,) = call(others_first_kernel, [((4, OTHERS_ROWS, LANES), BF)], place, first, after=[pairs1[0]])
    units1 = send_blocks(place, packed)
    first = [*first, swap(others0, 1)]
    (near0,) = call(near_first_kernel, [((8, HALF_ROWS, LANES), BF)], place, first)
    far0 = along(near0, INWARD + OUTWARD)

    normed0, xhat0, weight_q0, params, q0, k0, v0, att0, log0 = call(
        first_attend_kernel,
        [wide, wide, ((width, own), BF), ((EXTRA, width), F32), column, column, column, column, ((8, seq), F32)],
        place,
        [*first, cosine, sine],
        [pltpu.VMEM((LANES, seq), BF)],
        after=[near0],
    )
    weight_f0, act0, slope0, partial_sum = call(
        first_units_kernel,
        [((width, units), BF), ((seq, units), BF), ((seq, units), F32), wide],
        place,
        [normed0, near0, far0, b_fc1, w_fc2, w_dense, att0],
    )
    (near1,) = call(near_units_kernel, [((4, ROWS, units), BF)], place, units1, after=[partial_sum])
    far1 = along(near1, INWARD + OUTWARD)
    keep, give = call(split_kernel, [blocks_n, blocks_n], place, [partial_sum], after=[near1])
    terms, sent = begin_scatter(place, keep, give)
    (others1,) = call(others_units_grads_kernel, [((4, 3 * ROWS, units), BF)], place, [*units1, far1], after=terms[2:])
    hidden1, normed1_own = call(next_hidden_kernel, [mine, mine_low], place, [*terms, hidden0, params], after=[others1])
    pieces = gather_pieces(normed1_own)

    weight_f1, grad_branch1 = call(
        second_ready_kernel, [((width, units), BF), wide], place, [*units1, swap(others1, 1), far1]
    )
    normed1, act1, pre1, chunk1 = call(
        second_units_kernel,
        [wide, ((seq, units), BF), ((seq, units), F32), chunk_shape],
        place,
        [*pieces, b_fc1, weight_f1, grad_branch1],
    )
    came1 = along(chunk1, INWARD + OUTWARD)
    heads1 = send_blocks(place, pairs1)
    chunk2, sums1, part_normed, grad_att1 = call(
        second_units_back_kernel,
        [chunk_shape, sums_shape, part_shape, column],
        place,
        [grad_branch1, w_fc2, w_dense, pre1, normed1, weight_f1],
        units_scratch,
    )
    att1, mixed1, keep, give = call(
        second_attend_kernel,
        [column, ((seq, own), BF), blocks_n, blocks_n],
        place,
        [normed1, *heads1, cosine, sine, grad_att1, part_normed],
        [
            pltpu.VMEM((width, own), BF),
            *column_scratch,
            pltpu.VMEM((LANES, seq), BF),
            *head_scratch,
        ],
    )
    terms, sent = begin_scatter(place, keep, give)
    (half1,) = tick(place, (chunk1, came1), None, None, after=[give])
    (chunk3,) = call(
        second_heads_kernel,
        [chunk_shape],
        place,
        [normed1, mixed1, att1, grad_branch1],
        [pltpu.VMEM((width, own), BF)],
        after=[half1, sent],
    )
    cross1, came2 = along(half1, ACROSS), along(chunk2, INWARD + OUTWARD)
    grads0, grads0_low, ln_sums1 = call(
        second_norm_back_kernel, [mine, mine_low, sums_shape], place, [*terms, hidden1, params, grads1], after=[half1]
    )

    pieces = gather_pieces(grads0_low)
    half2, total1 = tick(place, (chunk2, came2), (half1, cross1), chunk3, after=[pieces[1]], joint=True)
    cross2, came3 = along(half2, ACROSS), along(total1, INWARD + OUTWARD)
    grad_branch0, chunk6, chunk4, sums0, part_normed = call(
        first_units_back_kernel,
        [wide, chunk_shape, chunk_shape, sums_shape, part_shape],
        place,
        [*pieces, act0, w_fc2, slope0, normed0, weight_f0],
        units_scratch,
        after=[half2],
    )
    mixed0, keep, give = call(
        first_attend_back_kernel,
        [((seq, own), BF), blocks_n0, blocks_n0],
        place,
        [grad_branch0, w_dense, q0, k0, v0, log0, cosine, sine, normed0, xhat0, weight_q0, part_normed, ln_sums1],
        [*head_scratch, pltpu.VMEM((seq, width), BF), pltpu.VMEM((8, width), F32)],
    )
    last_ins, whole_scratch = [act1, att1, w_fc2, w_dense], [pltpu.VMEM((seq, width), BF)]
    blocks_h = call(partial(last_hidden_of_core, 0), [blocks_n, blocks_n], place, last_ins, whole_scratch, after=[mixed0])
    half3, total2 = tick(place, (chunk3, came3), (half2, cross2), chunk4, after=[blocks_h[0]], joint=True)
    keep_h, give_h = call(
        partial(last_hidden_of_core, 1), [blocks_n, blocks_n], place, [*last_ins, *blocks_h], whole_scratch, after=[half3], held=2
    )
    cross3, came4 = along(half3, ACROSS), along(total2, INWARD + OUTWARD)
    (chunk5,) = call(
        second_heads_kernel,
        [chunk_shape],
        place,
        [normed0, mixed0, att0, grad_branch0],
        [pltpu.VMEM((width, own), BF)],
        after=[half3],
    )
    token = ((8, LANES), F32)
    terms, sent = begin_scatter(place, keep, give, after=[half3])
    out_fc2, done = final_call(final_rows_kernel, place, [total1, came3], (units, width), 1, after=[sent])
    input_grad, small_sums = call(
        first_norm_back_kernel,
        [mine, ((SMALL_ROWS, LANES), F32)],
        place,
        [*terms, hidden0, params, grads0, sums0, sums1],
        after=[done],
    )
    half4, total3 = tick(place, (chunk4, came4), (half3, cross3), chunk5, after=[small_sums], joint=True)
    cross4, came5 = along(half4, ACROSS), along(total3, INWARD + OUTWARD)
    (chunk6,) = call(
        add_small_kernel, [((seq + SMALL_ROWS, units), BF)], place, [chunk6, small_sums], after=[half4]
    )
    terms, _ = begin_scatter(place, keep_h, give_h, after=[half4])
    hidden_out, done_h = call(last_sum_kernel, [mine, token], place, [*terms, hidden1, params], after=[chunk6])
    half5, total4 = tick(place, (chunk5, came5), (half4, cross4), chunk6, after=[done_h], joint=True)
    cross5, came6 = along(half5, ACROSS), along(total4, INWARD + OUTWARD)
    *picked1, dense1 = pick_both(place, (total2, came4), (total3, came5), own, after=[half5])
    blocks1 = swap_others(place, send_blocks(place, picked1))
    half6, total5 = tick(place, (chunk6, came6), (half5, cross5), None, after=[blocks1[1]], joint=True)
    cross6, came7 = along(half6, ACROSS), along(total5, INWARD + OUTWARD)
    picked4 = pick(place, total4, came6, units, after=[half6])
    out_fc1, done1 = final_call(final_units_kernel, place, blocks1, (ROWS, w_fc1.shape[2]), 1, after=[picked4[0]])
    out_qkv, done3 = final_call(final_heads_kernel, place, blocks1, (ROWS, w_qkv.shape[2]), 1, after=[done1])
    blocks4 = swap_others(place, send_blocks(place, picked4), after=[done3])
    (total6,) = tick(place, None, (half6, cross6), None, after=[blocks4[1]])
    came8 = along(total6, INWARD + OUTWARD)
    *picked5, dense0 = pick(place, total5, came7, own, after=[total6])
    out_fc1, done4 = final_call(final_units_kernel, place, blocks4, (ROWS, w_fc1.shape[2]), 0, out_fc1, after=[picked5[0]])
    blocks5 = swap_others(place, send_blocks(place, picked5), after=[done4])
    out_qkv, done5 = final_call(final_heads_kernel, place, blocks5, (ROWS, w_qkv.shape[2]), 0, out_qkv)
    vector = jax.ShapeDtypeStruct((2, LANES), F32)
    out_fc2, out_gain, out_shift, out_b_fc1, out_b_fc2 = pl.pallas_call(
        lambda place, before, token, *refs: last_rows_kernel(place, before, *refs),
        name="last_rows_kernel",
        out_shape=[jax.ShapeDtypeStruct((2, units, width), F32), vector, vector, jax.ShapeDtypeStruct((2, units), F32), vector],
        in_specs=[pl.BlockSpec(memory_space=pltpu.SMEM), pl.BlockSpec(memory_space=pltpu.HBM)]
        + [pl.BlockSpec(memory_space=pl.ANY)]
        + [pl.BlockSpec(memory_space=pltpu.VMEM)] * 2,
        out_specs=[pl.BlockSpec(memory_space=pltpu.HBM)] + [pl.BlockSpec(memory_space=pltpu.VMEM)] * 4,
        scratch_shapes=[pltpu.VMEM((units, width), F32), pltpu.SemaphoreType.DMA((4,))],
        input_output_aliases={1: 0},
        compiler_params=pltpu.CompilerParams(vmem_limit_bytes=16 * 1024 * 1024),
        cost_estimate=SMALL,
    )(place, out_fc2, done5, total6, came8)
    out_dense = jnp.stack([dense0, dense1])
    return (
        hidden_out[None],
        input_grad[None],
        out_gain,
        out_shift,
        out_qkv,
        out_dense,
        out_fc1,
        out_b_fc1,
        out_fc2,
        out_b_fc2,
    )


def local(hidden_in, ln_gain, ln_bias, w_qkv, w_dense, w_fc1, b_fc1, w_fc2, b_fc2, output_grad):
    arguments = (hidden_in, ln_gain, ln_bias, w_qkv, w_dense, w_fc1, b_fc1, w_fc2, b_fc2, output_grad)
    plane = lax.axis_size("grp") == 8 and lax.axis_size("rep") == 4
    plane = plane and hidden_in.shape[:2] == (1, ROWS) and w_qkv.shape == (2, LANES, 3 * 8 * LANES)
    return (local_plane if plane else local_any)(*arguments)


def solution(mesh):
    in_specs = (
        P("rep", "grp", None),
        P(None, "grp"),
        P(None, "grp"),
        P(None, "grp", None),
        P(None, "grp", None),
        P(None, "grp", None),
        P(None, "grp"),
        P(None, "grp", None),
        P(None, "grp"),
        P("rep", "grp", None),
    )
    out_specs = (
        P("rep", "grp", None),
        P("rep", "grp", None),
        P(None, "grp"),
        P(None, "grp"),
        P(None, "grp", None),
        P(None, "grp", None),
        P(None, "grp", None),
        P(None, "grp"),
        P(None, "grp", None),
        P(None, "grp"),
    )
    return jax.shard_map(local, mesh=mesh, in_specs=in_specs, out_specs=out_specs, check_vma=False)
```

```python
from functools import partial

import jax
import jax.numpy as jnp
import numpy as np
from jax import lax
from jax.experimental import pallas as pl
from jax.experimental.pallas import tpu as pltpu
from jax.sharding import PartitionSpec as P

HEAD_DIM = 64
ROT = 32
LANES = 128

EPSILON = 1e-05
SCORE_SCALE = 0.125
NEGATIVE = -1000000000.0
BF = jnp.bfloat16
F32 = jnp.float32


def dot(left, right):
    return jnp.dot(left, right, preferred_element_type=F32)


def dot_general(left, right, contract):
    return lax.dot_general(left, right, ((contract[:1], contract[1:]), ((), ())), preferred_element_type=F32)


def outer_sum(left, right):
    return dot_general(left, right, (0, 0))


def times_transposed(left, right):
    return dot_general(left, right, (1, 1))


def head_mask(head):
    lane = lax.broadcasted_iota(jnp.int32, (1, LANES), 1)
    return (lane >= head * HEAD_DIM) & (lane < (head + 1) * HEAD_DIM)


def turn(part, cosine, sine, sign):
    even = lax.broadcasted_iota(jnp.int32, part.shape, 1) % 2 == 0
    partner = jnp.where(even, pltpu.roll(part, LANES - 1, 1), pltpu.roll(part, 1, 1))
    return part * cosine + partner * (sine * sign)


def mask_diagonal(scores, block):
    keys, queries = scores.shape
    key_place = lax.broadcasted_iota(jnp.int32, (block, queries), 0)
    query_place = lax.broadcasted_iota(jnp.int32, (block, queries), 1)
    last = jnp.where(key_place <= query_place, scores[keys - block :], NEGATIVE)
    if keys == block:
        return last
    return jnp.concatenate([scores[: keys - block], last], axis=0)


def attend_kernel(heads, block, mix_q, mix_k, mix_v, cosine, sine, q_out, k_out, v_out, att_out, log_out):
    seq = mix_q.shape[0]
    q_out[...] = turn(mix_q[...], cosine[...], sine[...], 1.0).astype(BF)
    k_out[...] = turn(mix_k[...], cosine[...], sine[...], 1.0).astype(BF)
    v_out[...] = mix_v[...].astype(BF)
    values_down = mix_v[...].T.astype(BF)
    for start in range(0, seq, block):
        stop = start + block
        queries = q_out[start:stop, :] * SCORE_SCALE
        keys = k_out[:stop, :]
        total = jnp.zeros((LANES, block), F32)
        for head in range(heads):
            chosen = jnp.where(head_mask(head), queries, 0.0).astype(BF)
            scores = mask_diagonal(dot_general(keys, chosen, (1, 1)), block)
            row_max = jnp.max(scores, axis=0, keepdims=True)
            exponent = jnp.exp(scores - row_max)
            row_total = jnp.sum(exponent, axis=0, keepdims=True)
            probabilities = (exponent * (1.0 / row_total)).astype(BF)
            log_out[head : head + 1, start:stop] = row_max + jnp.log(row_total)
            found = dot(values_down[:, :stop], probabilities)
            down = lax.broadcasted_iota(jnp.int32, (LANES, 1), 0)
            own = (down >= head * HEAD_DIM) & (down < (head + 1) * HEAD_DIM)
            total = total + jnp.where(own, found, 0.0)
        att_out[start:stop, :] = total.T.astype(BF)


def attend_back_kernel(heads, block, q_in, k_in, v_in, grad_att, log_in, cosine, sine, q_out, k_out, v_out, k_sum, v_sum):
    seq = q_in.shape[0]
    k_sum[...] = jnp.zeros_like(k_sum)
    v_sum[...] = jnp.zeros_like(v_sum)
    keys_down = (k_in[...].astype(F32) * SCORE_SCALE).T.astype(BF)
    for start in range(0, seq, block):
        stop = start + block
        queries = q_in[start:stop, :] * SCORE_SCALE
        grads = grad_att[start:stop, :]
        grad_queries = jnp.zeros((LANES, block), F32)
        for head in range(heads):
            chosen = jnp.where(head_mask(head), queries, 0.0).astype(BF)
            chosen_grads = jnp.where(head_mask(head), grads, 0.0).astype(BF)
            scores = mask_diagonal(dot_general(k_in[:stop, :], chosen, (1, 1)), block)
            probabilities = jnp.exp(scores - log_in[head : head + 1, start:stop])
            grad_probs = dot_general(v_in[:stop, :], chosen_grads, (1, 1))
            row_inner = jnp.sum(grad_probs * probabilities, axis=0, keepdims=True)
            grad_scores = (probabilities * (grad_probs - row_inner)).astype(BF)
            k_sum[:stop, :] += dot(grad_scores, chosen)
            v_sum[:stop, :] += dot(probabilities.astype(BF), chosen_grads)
            down = lax.broadcasted_iota(jnp.int32, (LANES, 1), 0)
            own = (down >= head * HEAD_DIM) & (down < (head + 1) * HEAD_DIM)
            grad_queries = grad_queries + jnp.where(own, dot(keys_down[:, :stop], grad_scores), 0.0)
        q_out[start:stop, :] = turn(
            grad_queries.T, cosine[start:stop, :], sine[start:stop, :], -1.0
        ).astype(BF)
    k_out[...] = turn(k_sum[...], cosine[...], sine[...], -1.0).astype(BF)
    v_out[...] = v_sum[...].astype(BF)


VMEM_LIMIT = 48 * 1024 * 1024


def attend(mix_q, mix_k, mix_v, heads, cosine, sine):
    seq = mix_q.shape[0]
    out = jax.ShapeDtypeStruct((seq, LANES), BF)
    return pl.pallas_call(
        partial(attend_kernel, heads, min(256, seq)),
        out_shape=(out, out, out, out, jax.ShapeDtypeStruct((heads, seq), F32)),
        compiler_params=pltpu.CompilerParams(vmem_limit_bytes=VMEM_LIMIT),
    )(mix_q, mix_k, mix_v, cosine, sine)


def attend_back(queries, keys, values, grad_att, log_total, heads, cosine, sine):
    seq = queries.shape[0]
    out = jax.ShapeDtypeStruct((seq, LANES), BF)
    return pl.pallas_call(
        partial(attend_back_kernel, heads, min(256, seq)),
        out_shape=(out, out, out),
        scratch_shapes=[pltpu.VMEM((seq, LANES), F32), pltpu.VMEM((seq, LANES), F32)],
        compiler_params=pltpu.CompilerParams(vmem_limit_bytes=VMEM_LIMIT),
    )(queries, keys, values, grad_att, log_total, cosine, sine)


def rotary_tables(seq):
    frequency = (1.0 / 10000.0 ** (np.arange(ROT // 2, dtype=np.float32) * 2.0 / ROT)).astype(np.float32)
    angles = np.arange(seq, dtype=np.float32)[:, None] * frequency[None, :]
    cosine, sine = np.cos(angles.astype(np.float64)), np.sin(angles.astype(np.float64))
    cosine = np.repeat(cosine, 2, axis=1)
    sine = np.repeat(sine, 2, axis=1) * np.tile([-1.0, 1.0], ROT // 2)
    rest = HEAD_DIM - ROT
    cosine = np.concatenate([cosine, np.ones((seq, rest))], axis=1)
    sine = np.concatenate([sine, np.zeros((seq, rest))], axis=1)
    repeats = (1, LANES // HEAD_DIM)
    return np.tile(cosine, repeats).astype(np.float32), np.tile(sine, repeats).astype(np.float32)


def swap(value, bits):
    return lax.ppermute(value, "grp", [(i, i ^ bits) for i in range(8)])


def add_low(left, right):
    return (left.astype(F32) + right.astype(F32)).astype(BF)


def by_chip(parts, chip):
    x, y = chip % 2 == 1, chip // 2 == 1
    near = jnp.where(x, jnp.stack([parts[1], parts[0]]), jnp.stack([parts[0], parts[1]]))
    far = jnp.where(x, jnp.stack([parts[3], parts[2]]), jnp.stack([parts[2], parts[3]]))
    return jnp.where(y, jnp.concatenate([far, near]), jnp.concatenate([near, far]))


def gather_rows(part):
    size = lax.axis_size("grp")
    if size != 8:
        return lax.all_gather(part, "grp", axis=0, tiled=True)
    rows, width = part.shape
    half = rows // 2
    index = lax.axis_index("grp")
    along_x, along_y = swap(part, 2), swap(part, 4)
    corner = jnp.concatenate([swap(along_y[:half], 2), swap(along_x[half:], 4)])
    mine = by_chip([part, along_x, along_y, corner], index // 2)
    other = swap(mine, 1)
    odd = index % 2 == 1
    both = jnp.stack([jnp.where(odd, other, mine), jnp.where(odd, mine, other)], axis=1)
    return both.reshape(8 * rows, width)


def scatter_sum(whole):
    size = lax.axis_size("grp")
    if size != 8:
        return lax.psum_scatter(whole, "grp", scatter_dimension=0, tiled=True).astype(F32)
    rows, width = whole.shape[0] // 8, whole.shape[1]
    half = rows // 2
    index = lax.axis_index("grp")
    chip, core = index // 2, index % 2
    blocks = whole.reshape(4, 2, rows, width)
    keep = lax.dynamic_index_in_dim(blocks, core, 1, False)
    give = lax.dynamic_index_in_dim(blocks, 1 - core, 1, False)
    summed = add_low(keep, swap(give, 1))
    own, for_x, for_y, corner = [lax.dynamic_index_in_dim(summed, chip ^ s, 0, False) for s in range(4)]
    by_x, by_y = swap(corner[:half], 2), swap(corner[half:], 4)
    for_y = jnp.concatenate([add_low(for_y[:half], by_x), for_y[half:]])
    for_x = jnp.concatenate([for_x[:half], add_low(for_x[half:], by_y)])
    return own.astype(F32) + swap(for_y, 4).astype(F32) + swap(for_x, 2).astype(F32)


def exchange(blocks):
    size = lax.axis_size("grp")
    if size != 8:
        return lax.all_to_all(blocks, "grp", 0, 0)
    index = lax.axis_index("grp")
    chip, core = index // 2, index % 2
    pairs = blocks.reshape((4, 2) + blocks.shape[1:])
    keep = lax.dynamic_index_in_dim(pairs, core, 1, False)
    give = lax.dynamic_index_in_dim(pairs, 1 - core, 1, False)
    came = swap(give, 1)
    odd = core == 1
    both = jnp.stack([jnp.where(odd, came, keep), jnp.where(odd, keep, came)], axis=1)
    parts = [lax.dynamic_index_in_dim(both, chip ^ s, 0, False) for s in range(4)]
    parts = [parts[0]] + [swap(parts[s], 2 * s) for s in (1, 2, 3)]
    return by_chip(parts, chip).reshape(blocks.shape)


def rep_sum(part):
    if lax.axis_size("rep") != 4:
        return lax.psum(part, "rep").astype(F32)
    place = lax.axis_index("rep")
    inward = lax.ppermute(part, "rep", [(0, 1), (3, 2)])
    half_sum = add_low(part, inward)
    across = lax.ppermute(half_sum, "rep", [(1, 2), (2, 1)])
    total = add_low(half_sum, across)
    outward = lax.ppermute(total, "rep", [(1, 0), (2, 3)])
    return jnp.where((place == 1) | (place == 2), total, outward).astype(F32)


def columns_of(w_qkv, w_fc1, group):
    rows, qkv = w_qkv.shape
    heads = w_qkv.reshape(rows, 3, group, qkv // 3 // group).transpose(2, 0, 1, 3).reshape(group, rows, -1)
    units = w_fc1.reshape(rows, group, -1).transpose(1, 0, 2)
    found = exchange(jnp.concatenate([heads, units], axis=2))
    found = found.reshape(group * rows, -1)
    return found[:, : qkv // group], found[:, qkv // group :]


def rows_of(grad_qkv, grad_fc1, group):
    rows = grad_qkv.shape[0] // group
    both = jnp.concatenate([grad_qkv, grad_fc1], axis=1).reshape(group, rows, -1)
    found = exchange(both)
    qkv = grad_qkv.shape[1]
    heads = found[:, :, :qkv].reshape(group, rows, 3, qkv // 3).transpose(1, 2, 0, 3).reshape(rows, -1)
    units = found[:, :, qkv:].transpose(1, 0, 2).reshape(rows, -1)
    return heads, units


def standardize(hidden):
    centered = hidden - jnp.mean(hidden, axis=-1, keepdims=True)
    scale = lax.rsqrt(jnp.mean(centered * centered, axis=-1, keepdims=True) + EPSILON)
    return centered * scale, scale


def widen(part):
    return jnp.pad(part, ((0, 0), (0, LANES - part.shape[1])))


def forward_layer(normed, weights, heads, tables):
    qkv_cols, fc1_cols, b_fc1, w_dense, w_fc2 = weights
    mixed = dot(normed, qkv_cols)
    own = heads * HEAD_DIM
    queries, keys, values, attended, log_total = attend(
        *(widen(mixed[:, i * own : (i + 1) * own]) for i in range(3)), heads, *tables
    )
    pre_act = dot(normed, fc1_cols) + b_fc1.astype(F32)
    activation = jax.nn.gelu(pre_act, approximate=True).astype(BF)
    partial_sum = (dot(attended[:, :own], w_dense) + dot(activation, w_fc2)).astype(BF)
    stored = (normed, queries, keys, values, attended, log_total, pre_act, activation)
    return partial_sum, stored


def backward_layer(grad_branch, weights, stored, heads, tables):
    qkv_cols, fc1_cols, b_fc1, w_dense, w_fc2 = weights
    normed, queries, keys, values, attended, log_total, pre_act, activation = stored
    own = heads * HEAD_DIM
    grad_w_fc2 = outer_sum(activation, grad_branch).astype(BF)
    grad_w_dense = outer_sum(attended[:, :own], grad_branch).astype(BF)
    _, gelu_back = jax.vjp(partial(jax.nn.gelu, approximate=True), pre_act)
    grad_pre = gelu_back(times_transposed(grad_branch, w_fc2))[0].astype(BF)
    grad_attended = widen(times_transposed(grad_branch, w_dense).astype(BF))
    grad_mixed = attend_back(queries, keys, values, grad_attended, log_total, heads, *tables)
    grad_mixed = jnp.concatenate([part[:, :own] for part in grad_mixed], axis=1)
    grad_fc1 = outer_sum(normed, grad_pre).astype(BF)
    grad_b_fc1 = jnp.sum(grad_pre.astype(F32), axis=0)
    grad_qkv = outer_sum(normed, grad_mixed).astype(BF)
    grad_normed = (times_transposed(grad_pre, fc1_cols) + times_transposed(grad_mixed, qkv_cols)).astype(BF)
    return grad_normed, (grad_w_fc2, grad_w_dense, grad_fc1, grad_qkv, grad_b_fc1)


def local_any(hidden_in, ln_gain, ln_bias, w_qkv, w_dense, w_fc1, b_fc1, w_fc2, b_fc2, output_grad):
    group = lax.axis_size("grp")
    index = lax.axis_index("grp")
    layers = w_qkv.shape[0]
    span, width = hidden_in.shape[1:]
    seq = span * group
    heads = width // HEAD_DIM // group
    tables = rotary_tables(seq)
    small = jnp.concatenate([ln_gain, ln_bias, b_fc2])
    small = lax.all_gather(small, "grp", axis=1, tiled=True).astype(F32)
    gains, shifts, b_fc2_all = small[:layers], small[layers : 2 * layers], small[2 * layers :]
    hidden = hidden_in.reshape(span, width).astype(F32)
    hidden_all = gather_rows(hidden_in.reshape(span, width))
    weights = []
    for layer in range(layers):
        qkv_cols, fc1_cols = columns_of(w_qkv[layer], w_fc1[layer], group)
        weights.append((qkv_cols, fc1_cols, b_fc1[layer], w_dense[layer], w_fc2[layer]))

    inputs, stored_layers = [], []
    for layer in range(layers):
        inputs.append(hidden)
        if layer == 0:
            normed = (standardize(hidden_all.astype(F32))[0] * gains[0] + shifts[0]).astype(BF)
        else:
            normed = gather_rows((standardize(hidden)[0] * gains[layer] + shifts[layer]).astype(BF))
        partial_sum, stored = forward_layer(normed, weights[layer], heads, tables)
        stored_layers.append(stored)
        hidden = hidden + scatter_sum(partial_sum) + b_fc2_all[layer]

    grad_hidden = output_grad.reshape(span, width)
    small_grads, large_grads = [None] * layers, [None] * layers
    for layer in reversed(range(layers)):
        grad_low = grad_hidden.astype(BF)
        grad_branch = gather_rows(grad_low)
        grad_normed, found = backward_layer(grad_branch, weights[layer], stored_layers[layer], heads, tables)
        grad_w_fc2, grad_w_dense, grad_fc1, grad_qkv, grad_b_fc1 = found
        grad_qkv, grad_fc1 = rows_of(grad_qkv, grad_fc1, group)
        large_grads[layer] = tuple(rep_sum(part) for part in (grad_w_fc2, grad_w_dense, grad_fc1, grad_qkv))
        grad_normed = scatter_sum(grad_normed)
        xhat, scale = standardize(inputs[layer])
        inner = grad_normed * gains[layer]
        mean_inner = jnp.mean(inner, axis=-1, keepdims=True)
        mean_along = jnp.mean(inner * xhat, axis=-1, keepdims=True)
        small_grads[layer] = jnp.concatenate(
            [
                jnp.sum(grad_normed * xhat, axis=0),
                jnp.sum(grad_normed, axis=0),
                jnp.sum(grad_low.astype(F32), axis=0),
                lax.dynamic_update_slice(
                    jnp.zeros((group * grad_b_fc1.shape[0],), F32), grad_b_fc1, (index * grad_b_fc1.shape[0],)
                ),
            ]
        )
        grad_hidden = grad_hidden + (inner - mean_inner - xhat * mean_along) * scale

    summed = lax.psum(jnp.stack(small_grads), ("rep", "grp"))
    own = width // group
    units = b_fc1.shape[1]

    def pick(start, count):
        return lax.dynamic_slice_in_dim(summed, start + index * count, count, 1)

    stacked = [jnp.stack([large_grads[layer][member] for layer in range(layers)]) for member in range(4)]
    return (
        hidden[None],
        grad_hidden[None],
        pick(0, own),
        pick(width, own),
        stacked[3],
        stacked[1],
        stacked[2],
        pick(3 * width, units),
        stacked[0],
        pick(2 * width, own),
    )


SLOTS = [(s, k) for s in range(4) for k in range(2)]
ROWS = 128
EXTRA = 16


def slot_start(place, s, k, size):
    return pl.multiple_of(((place[0] ^ s) * 2 + (place[1] ^ k)) * size, size)


def slot_rows(place, s, k, size=ROWS):
    return pl.ds(slot_start(place, s, k, size), size)


SMALL = pl.CostEstimate(flops=0, bytes_accessed=0, transcendentals=0)


def call(body, outs, place, ins, scratch=(), after=(), hbm=0, mib=16, held=0):
    def run(place, *refs):
        body(place, *refs[len(after) :])

    return pl.pallas_call(
        run,
        name=getattr(body, "func", body).__name__,
        out_shape=[jax.ShapeDtypeStruct(*out) for out in outs],
        in_specs=[pl.BlockSpec(memory_space=pltpu.SMEM)]
        + [pl.BlockSpec(memory_space=pl.ANY)] * len(after)
        + [pl.BlockSpec(memory_space=pltpu.HBM)] * hbm
        + [pl.BlockSpec(memory_space=pltpu.VMEM)] * (len(ins) - hbm),
        out_specs=[pl.BlockSpec(memory_space=pltpu.VMEM)] * len(outs),
        scratch_shapes=list(scratch),
        input_output_aliases={1 + len(after) + len(ins) - held + i: i for i in range(held)},
        compiler_params=pltpu.CompilerParams(vmem_limit_bytes=mib * 1024 * 1024),
        cost_estimate=SMALL,
    )(place, *after, *ins)


def gather_pieces(part):
    mine = [part, swap(part, 2), swap(part, 4), swap(part, 6)]
    other = [swap(piece, 1) for piece in mine]
    return [piece for pair in zip(mine, other) for piece in pair]


def put_columns(out, start, value):
    rows = value.shape[0]
    for b in range(value.shape[1] // LANES):
        out[start + b * rows : start + (b + 1) * rows, :] = value[:, b * LANES : (b + 1) * LANES]


def heads_of(place, w_qkv, layer, s, k, j):
    start = j * (w_qkv.shape[2] // 3) + slot_start(place, s, k, LANES)
    return w_qkv[layer, :, pl.ds(pl.multiple_of(start, LANES), LANES)]


HALF = ROWS // 2
HEADS_ROWS, HALF_ROWS = 3 * ROWS, 4 * HALF
FIRST_MINE = 8 * ROWS
FIRST_OTHERS = FIRST_MINE + HEADS_ROWS + HALF_ROWS
FIRST_SMALL = FIRST_OTHERS + HEADS_ROWS + HALF_ROWS
FIRST_ROWS = FIRST_SMALL + EXTRA
OTHERS_MINE = 8 * ROWS
OTHERS_SMALL = OTHERS_MINE + HEADS_ROWS + HALF_ROWS
OTHERS_ROWS = OTHERS_SMALL + EXTRA


def half_start(place, other):
    parity = place[2] & 1
    return pl.multiple_of((1 - parity if other else parity) * HALF, HALF)


def pack_first_kernel(hidden_from, qkv_from, fc1_from, gain_from, shift_from, bias_from, o0, o1, o2, o3, hidden, w_qkv, w_fc1, gain, shift, bias, sems):
    index = lax.axis_index("grp")
    place = (index // 2, index % 2, lax.axis_index("rep"))
    outs = (o0, o1, o2, o3)
    pairs = (
        (hidden_from, hidden),
        (gain_from, gain),
        (shift_from, shift),
        (bias_from, bias),
        (qkv_from.at[0], w_qkv),
        (fc1_from.at[0, pl.ds(half_start(place, False), HALF), :], w_fc1),
    )
    moves = [pltpu.make_async_copy(*pair, sems.at[i]) for i, pair in enumerate(pairs)]
    for move in moves:
        move.start()
    for move in moves[:4]:
        move.wait()
    for out in outs:
        put_columns(out, 0, hidden[...])
        out[FIRST_SMALL:, :] = jnp.zeros((EXTRA, LANES), BF)
        for i, part in enumerate((gain, shift, bias)):
            out[FIRST_SMALL + 2 * i : FIRST_SMALL + 2 * i + 2, :] = part[...]
    moves[4].wait()
    third = w_qkv.shape[1] // 3
    for s, k in SLOTS:
        row = (FIRST_MINE, FIRST_OTHERS)[k]
        for j in range(3):
            lanes = pl.ds(pl.multiple_of(j * third + slot_start(place, s, k, LANES), LANES), LANES)
            outs[s][row + j * ROWS : row + (j + 1) * ROWS, :] = w_qkv[:, lanes]
    moves[5].wait()
    for s, k in SLOTS:
        row = (FIRST_MINE, FIRST_OTHERS)[k] + HEADS_ROWS
        put_columns(outs[s], row, w_fc1[:, pl.ds(slot_start(place, s, k, 4 * LANES), 4 * LANES)])


def others_first_kernel(place, b0, b1, b2, b3, out):
    for s, block in enumerate((b0, b1, b2, b3)):
        out[s, :OTHERS_MINE, :] = block[:FIRST_MINE, :]
        out[s, OTHERS_MINE:OTHERS_SMALL, :] = block[FIRST_OTHERS:FIRST_SMALL, :]
        out[s, OTHERS_SMALL:, :] = block[FIRST_SMALL:, :]


def near_first_kernel(place, b0, b1, b2, b3, b4, out):
    for i, (s, k) in enumerate(SLOTS):
        block, mine_at, _ = first_block(s, k, (b0, b1, b2, b3, b4))
        out[i] = block[mine_at + HEADS_ROWS : mine_at + HEADS_ROWS + HALF_ROWS, :]


def first_block(s, k, blocks):
    if k:
        return blocks[4].at[s], OTHERS_MINE, OTHERS_SMALL
    return blocks[s], FIRST_MINE, FIRST_SMALL


def pack_heads_kernel(layer, place, w_qkv, keep, give):
    for s, k in SLOTS:
        for j in range(3):
            (keep, give)[k][s, :, j * LANES : (j + 1) * LANES] = heads_of(place, w_qkv, layer, s, k, j)


def pair_kernel(place, keep, came, *outs):
    for s, out in enumerate(outs):
        out[0], out[1] = keep[s], came[s]


def pack_units_kernel(layer, place, w_fc1, *outs):
    units = outs[0].shape[2]
    for s, k in SLOTS:
        outs[s][k] = w_fc1[layer, :, pl.ds(slot_start(place, s, k, units), units)]


def pack_units_grads_kernel(layer, place, w_fc1, grads, *outs):
    units = outs[0].shape[1]
    low = grads[...].astype(BF)
    for s in range(4):
        for k in range(2):
            lanes = pl.ds(slot_start(place, s, k, units), units)
            outs[s][k * HALF : (k + 1) * HALF, :] = w_fc1[layer, pl.ds(half_start(place, False), HALF), lanes]
            outs[s][(1 + k) * ROWS : (2 + k) * ROWS, :] = low[:, k * units : (k + 1) * units]


def near_units_kernel(place, b0, b1, b2, b3, out):
    for s, block in enumerate((b0, b1, b2, b3)):
        out[s] = block[:ROWS, :]


def others_units_grads_kernel(place, b0, b1, b2, b3, far, out):
    for s, block in enumerate((b0, b1, b2, b3)):
        out[s, :HALF, :] = block[HALF:ROWS, :]
        out[s, HALF:ROWS, :] = far[s, HALF:, :]
        out[s, ROWS:, :] = block[ROWS:, :]


def send_blocks(place, packed):
    return [packed[0]] + [swap(packed[s], 2 * s) for s in (1, 2, 3)]


def others_kernel(place, b0, b1, b2, b3, out):
    for s, block in enumerate((b0, b1, b2, b3)):
        out[s] = block[1]


def swap_others(place, blocks, after=()):
    (other,) = call(others_kernel, [((4,) + blocks[0].shape[1:], BF)], place, blocks, after=after)
    return [*blocks, swap(other, 1)]


def block_of(s, k, blocks):
    return blocks[4].at[s] if k else blocks[s].at[0]


def project_heads(normed, weight, cosine, sine, q_out, k_out, v_out, values_down):
    step = 256
    for start in range(0, normed.shape[0], step):
        rows = slice(start, start + step)
        mixed = dot(normed[rows, :], weight[...])
        q_out[rows, :] = turn(mixed[:, :LANES], cosine[rows, :], sine[rows, :], 1.0).astype(BF)
        k_out[rows, :] = turn(mixed[:, LANES : 2 * LANES], cosine[rows, :], sine[rows, :], 1.0).astype(BF)
        values = mixed[:, 2 * LANES :]
        v_out[rows, :] = values.astype(BF)
        values_down[:, rows] = values.T.astype(BF)


def own_head(head):
    down = lax.broadcasted_iota(jnp.int32, (LANES, 1), 0)
    return (down >= head * HEAD_DIM) & (down < (head + 1) * HEAD_DIM)


def softmax_block(keys, chosen, block):
    scores = mask_diagonal(dot_general(keys, chosen, (1, 1)), block)
    row_max = jnp.max(scores, axis=0, keepdims=True)
    exponent = jnp.exp(scores - row_max)
    row_total = jnp.sum(exponent, axis=0, keepdims=True)
    return exponent * (1.0 / row_total), row_max + jnp.log(row_total)


BLOCK = 256
HEADS_HERE = LANES // HEAD_DIM


def first_attend_kernel(place, b0, b1, b2, b3, b4, cosine, sine, normed, xhat_out, weight, params, q_out, k_out, v_out, att_out, log_out, values_down):
    for s, k in SLOTS:
        rows = slot_rows(place, s, k)
        block, mine_at, small_at = first_block(s, k, (b0, b1, b2, b3, b4))
        for j in range(3):
            weight[rows, j * LANES : (j + 1) * LANES] = block[mine_at + j * ROWS : mine_at + (j + 1) * ROWS, :]
        params[:, rows] = block[small_at:, :].astype(F32)
        for b in range(8):
            normed[rows, b * LANES : (b + 1) * LANES] = block[b * ROWS : (b + 1) * ROWS, :]
    gain, shift = params[0:1, :], params[2:3, :]

    def norm_rows(rows):
        xhat = standardize(normed[rows, :].astype(F32))[0]
        xhat_out[rows, :] = xhat.astype(BF)
        normed[rows, :] = (xhat * gain + shift).astype(BF)

    loop_rows(normed.shape[0], 4 * ROWS, norm_rows)
    project_heads(normed, weight, cosine, sine, q_out, k_out, v_out, values_down)
    for start in range(0, normed.shape[0], BLOCK):
        stop = start + BLOCK
        queries = q_out[start:stop, :] * SCORE_SCALE
        total = jnp.zeros((LANES, BLOCK), F32)
        for head in range(HEADS_HERE):
            chosen = jnp.where(head_mask(head), queries, 0.0).astype(BF)
            probabilities, log_total = softmax_block(k_out[:stop, :], chosen, BLOCK)
            log_out[head : head + 1, start:stop] = log_total
            found = dot(values_down[:, :stop], probabilities.astype(BF))
            total = total + jnp.where(own_head(head), found, 0.0)
        att_out[start:stop, :] = total.T.astype(BF)


GELU_A = 0.7978845608028654
GELU_B = 0.044715


def gelu(pre):
    return pre * (0.5 + 0.5 * jnp.tanh(GELU_A * pre * (1.0 + GELU_B * pre * pre)))


def gelu_slope(pre):
    square = pre * pre
    wave = jnp.tanh(GELU_A * pre * (1.0 + GELU_B * square))
    return 0.5 * (1.0 + wave) + 0.5 * pre * (1.0 - wave * wave) * (GELU_A * (1.0 + 3.0 * GELU_B * square))


def loop_rows(count, step, body):
    def one(i, carry):
        body(pl.ds(pl.multiple_of(i * step, step), step))
        return carry

    lax.fori_loop(0, count // step, one, 0)


def put_slots(place, rows_of_block, keep, give):
    for s in range(4):
        keep[s] = rows_of_block(slot_rows(place, s, 0))
        give[s] = rows_of_block(slot_rows(place, s, 1))


def put_pairs(place, rows_of_block, outs):
    for s, k in SLOTS:
        outs[s][k] = rows_of_block(slot_rows(place, s, k))


def first_units_kernel(place, normed, near, far, bias, w_fc2, w_dense, attended, weight, act, slope, whole):
    for s, k in SLOTS:
        for part, other_plane in ((near.at[SLOTS.index((s, k))], False), (far.at[SLOTS.index((s, k))], True)):
            start = slot_start(place, s, k, ROWS) + half_start(place, other_plane)
            for b in range(4):
                rows = pl.ds(pl.multiple_of(start, HALF), HALF)
                weight[rows, b * LANES : (b + 1) * LANES] = part[b * HALF : (b + 1) * HALF, :]
    shift = bias[0:1, :].astype(F32)

    def rows_done(rows):
        found = dot(normed[rows, :], weight[...]) + shift
        slope[rows, :] = gelu_slope(found)
        act[rows, :] = gelu(found).astype(BF)
        whole[rows, :] = (dot(act[rows, :], w_fc2[0]) + dot(attended[rows, :], w_dense[0])).astype(BF)

    loop_rows(normed.shape[0], 256, rows_done)


def split_kernel(place, whole, keep, give):
    put_slots(place, lambda rows: whole[rows, :], keep, give)


def split_sum_kernel(place, keep, came, for_x, for_y, corner):
    def rows_done(rows):
        for s, out in ((1, for_x), (2, for_y), (3, corner)):
            out[rows, :] = keep[s, rows, :] + came[s, rows, :]

    loop_rows(for_x.shape[0], 16, rows_done)


def begin_scatter(place, keep, give, after=()):
    came = swap(give, 1)
    shape = (keep.shape[1:], BF)
    for_x, for_y, corner = call(split_sum_kernel, [shape] * 3, place, [keep, came], after=after)
    from_corner, from_x, from_y = swap(corner, 6), swap(for_x, 2), swap(for_y, 4)
    return [keep, came, from_x, from_y, from_corner], for_x


def sum_terms(terms):
    total = terms[0][0].astype(F32) + terms[1][0].astype(F32)
    for term in terms[2:]:
        total = total + term[...].astype(F32)
    return total


def next_hidden_kernel(place, *refs):
    terms, (hidden, params, hidden_out, normed) = refs[:5], refs[5:]
    found = hidden[...].astype(F32) + sum_terms(terms) + params[4:5, :]
    hidden_out[...] = found
    normed[...] = (standardize(found)[0] * params[1:2, :] + params[3:4, :]).astype(BF)


def low_kernel(place, wide, low):
    low[...] = wide[...].astype(BF)


def assemble_kernel(place, *refs):
    for (s, k), piece in zip(SLOTS, refs[:8]):
        refs[8][slot_rows(place, s, k), :] = piece[...]


def last_hidden_kernel(place, act, attended, w_fc2, w_dense, keep, give, whole):
    def rows_done(rows):
        whole[rows, :] = (dot(act[rows, :], w_fc2[1]) + dot(attended[rows, :], w_dense[1])).astype(BF)

    loop_rows(act.shape[0], 256, rows_done)
    put_slots(place, lambda rows: whole[rows, :], keep, give)


def last_hidden_of_core(core, place, *refs):
    @pl.when(place[1] == core)
    def work():
        last_hidden_kernel(place, *refs[:4], *refs[-3:])


def last_sum_kernel(place, *refs):
    terms, (hidden, params, out, token) = refs[:5], refs[5:]
    token[...] = jnp.zeros_like(token)
    out[...] = hidden[...] + sum_terms(terms) + params[5:6, :]


SMALL_ROWS = 16


def put_halves(out, value, start, rows):
    half = out.shape[1]
    for j in range(2):
        out[j * rows + start : j * rows + start + value.shape[0], :] = value[:, j * half : (j + 1) * half]


def second_ready_kernel(place, b0, b1, b2, b3, other, far, weight, grads):
    units = weight.shape[1]
    for s, k in SLOTS:
        block = other.at[s] if k else (b0, b1, b2, b3)[s]
        parts = (block[:HALF, :], block[HALF:ROWS, :] if k else far[s, :HALF, :])
        for part, other_plane in zip(parts, (False, True)):
            start = slot_start(place, s, k, ROWS) + half_start(place, other_plane)
            weight[pl.ds(pl.multiple_of(start, HALF), HALF), :] = part
        for j in range(2):
            grads[slot_rows(place, s, k), j * units : (j + 1) * units] = block[(1 + j) * ROWS : (2 + j) * ROWS, :]


def second_units_kernel(place, *refs):
    pieces, refs = refs[:8], refs[8:]
    bias, weight, grads, normed, act, pre, chunk = refs
    units = weight.shape[1]
    for (s, k), piece in zip(SLOTS, pieces):
        normed[slot_rows(place, s, k), :] = piece[...]
    shift = bias[1:2, :].astype(F32)

    def rows_done(rows):
        found = dot(normed[rows, :], weight[...]) + shift
        pre[rows, :] = found
        act[rows, :] = gelu(found).astype(BF)

    loop_rows(normed.shape[0], 256, rows_done)
    for start in range(0, units, 256):
        put_halves(chunk, outer_sum(act[:, start : start + 256], grads[...]).astype(BF), start, units)


def units_back(layer, place, grads, w_fc2, slope_of, normed, weight, chunk, sums, part_normed, grad_pre, grad_w):
    sums[...] = jnp.zeros_like(sums)
    width = grads.shape[1]
    units = weight.shape[1]

    def rows_done(rows):
        found = (times_transposed(grads[rows, :], w_fc2[layer]) * slope_of(rows)).astype(BF)
        grad_pre[rows, :] = found
        sums[0:1, :width] += jnp.sum(grads[rows, :].astype(F32), axis=0, keepdims=True)
        sums[1:2, :units] += jnp.sum(found.astype(F32), axis=0, keepdims=True)
        part_normed[rows, :] = times_transposed(found, weight[...])

    loop_rows(grads.shape[0], 256, rows_done)
    for start in range(0, width, 256):
        rows = slice(start, start + 256)
        grad_w[rows, :] = outer_sum(normed[:, rows], grad_pre[...]).astype(BF)
    for i, (s, k) in enumerate(SLOTS):
        chunk[i * ROWS : (i + 1) * ROWS, :] = grad_w[slot_rows(place, s, k), :]


def second_units_back_kernel(place, grads, w_fc2, w_dense, pre, normed, weight, chunk, sums, part_normed, grad_att, grad_pre, grad_w):
    def slope_of(rows):
        grad_att[rows, :] = times_transposed(grads[rows, :], w_dense[1]).astype(BF)
        return gelu_slope(pre[rows, :])

    units_back(1, place, grads, w_fc2, slope_of, normed, weight, chunk, sums, part_normed, grad_pre, grad_w)


def first_units_back_kernel(place, *refs):
    pieces, refs = refs[:8], refs[8:]
    act, w_fc2, slope, normed, weight, grads, chunk_rows, chunk, sums, part_normed, grad_pre, grad_w = refs
    for (s, k), piece in zip(SLOTS, pieces):
        grads[slot_rows(place, s, k), :] = piece[...]
    units_back(
        0, place, grads, w_fc2, lambda rows: slope[rows, :], normed, weight, chunk, sums, part_normed, grad_pre, grad_w
    )
    units = act.shape[1]
    for start in range(0, units, 256):
        put_halves(chunk_rows, outer_sum(act[:, start : start + 256], grads[...]).astype(BF), start, units)


def attend_back_block(start, q_ref, k_ref, v_ref, grad_att, keys_down, k_sum, v_sum, cosine, sine, mixed, found_p):
    stop = start + BLOCK
    queries = q_ref[start:stop, :] * SCORE_SCALE
    grad_queries = jnp.zeros((LANES, BLOCK), F32)
    for head in range(HEADS_HERE):
        chosen = jnp.where(head_mask(head), queries, 0.0).astype(BF)
        chosen_grads = jnp.where(head_mask(head), grad_att, 0.0).astype(BF)
        probabilities = found_p(head, chosen)
        grad_probs = dot_general(v_ref[:stop, :], chosen_grads, (1, 1))
        row_inner = jnp.sum(grad_probs * probabilities, axis=0, keepdims=True)
        grad_scores = (probabilities * (grad_probs - row_inner)).astype(BF)
        k_sum[:stop, :] += dot(grad_scores, chosen)
        v_sum[:stop, :] += dot(probabilities.astype(BF), chosen_grads)
        grad_queries = grad_queries + jnp.where(own_head(head), dot(keys_down[:, :stop], grad_scores), 0.0)
    rows = slice(start, stop)
    mixed[rows, :LANES] = turn(grad_queries.T, cosine[rows, :], sine[rows, :], -1.0).astype(BF)


def mixed_rest(cosine, sine, mixed, k_sum, v_sum):
    mixed[:, LANES : 2 * LANES] = turn(k_sum[...], cosine[...], sine[...], -1.0).astype(BF)
    mixed[:, 2 * LANES :] = v_sum[...].astype(BF)


def mixed_outer(normed, mixed, grad_w):
    for start in range(0, normed.shape[1], 256):
        rows = slice(start, start + 256)
        grad_w[rows, :] = outer_sum(normed[:, rows], mixed[...]).astype(BF)


def mixed_inner(normed, weight, mixed, part_normed, whole):
    def rows_done(rows):
        whole[rows, :] = (times_transposed(mixed[rows, :], weight[...]) + part_normed[rows, :]).astype(BF)

    loop_rows(normed.shape[0], 256, rows_done)


def mixed_back(place, normed, weight, cosine, sine, mixed, k_sum, v_sum, grad_w, part_normed, whole):
    mixed_rest(cosine, sine, mixed, k_sum, v_sum)
    mixed_outer(normed, mixed, grad_w)
    mixed_inner(normed, weight, mixed, part_normed, whole)


def put_heads_chunk(place, chunk, grad_w, grad_dense):
    heads = grad_w.shape[1]
    for i, (s, k) in enumerate(SLOTS):
        rows = slice(i * ROWS, (i + 1) * ROWS)
        chunk[rows, :heads] = grad_w[slot_rows(place, s, k), :]
        chunk[rows, heads:] = grad_dense[:, rows]


def second_attend_kernel(place, normed, b0, b1, b2, b3, cosine, sine, grad_att, part_normed, att_out, mixed, keep_n, give_n, weight, q_ref, k_ref, v_ref, values_down, keys_down, k_sum, v_sum):
    for s, k in SLOTS:
        weight[slot_rows(place, s, k), :] = (b0, b1, b2, b3)[s][k]
    project_heads(normed, weight, cosine, sine, q_ref, k_ref, v_ref, values_down)
    k_sum[...] = jnp.zeros_like(k_sum)
    v_sum[...] = jnp.zeros_like(v_sum)
    keys_down[...] = (k_ref[...].astype(F32) * SCORE_SCALE).T.astype(BF)
    for start in range(0, normed.shape[0], BLOCK):
        stop = start + BLOCK
        total = [jnp.zeros((LANES, BLOCK), F32)]

        def found_p(head, chosen):
            probabilities, _ = softmax_block(k_ref[:stop, :], chosen, BLOCK)
            found = dot(values_down[:, :stop], probabilities.astype(BF))
            total[0] = total[0] + jnp.where(own_head(head), found, 0.0)
            return probabilities

        attend_back_block(start, q_ref, k_ref, v_ref, grad_att[start:stop, :], keys_down, k_sum, v_sum, cosine, sine, mixed, found_p)
        att_out[start:stop, :] = total[0].T.astype(BF)
    mixed_rest(cosine, sine, mixed, k_sum, v_sum)
    for s in range(4):
        rows = pl.ds(pl.multiple_of((place[0] ^ s) * 2 * ROWS, 2 * ROWS), 2 * ROWS)
        found = (times_transposed(mixed[rows, :], weight[...]) + part_normed[rows, :]).astype(BF)
        odd = place[1] == 1
        keep_n[s] = jnp.where(odd, found[ROWS:, :], found[:ROWS, :])
        give_n[s] = jnp.where(odd, found[:ROWS, :], found[ROWS:, :])


def second_heads_kernel(place, normed, mixed, attended, grads, chunk, grad_w):
    mixed_outer(normed, mixed, grad_w)
    put_heads_chunk(place, chunk, grad_w, outer_sum(attended[...], grads[...]).astype(BF))


def norm_back(gain_row, grad_normed, hidden, params, grads):
    xhat, scale = standardize(hidden[...].astype(F32))
    inner = grad_normed * params[gain_row : gain_row + 1, :]
    mean_inner = jnp.mean(inner, axis=-1, keepdims=True)
    mean_along = jnp.mean(inner * xhat, axis=-1, keepdims=True)
    return grads[...] + (inner - mean_inner - xhat * mean_along) * scale, xhat


def second_norm_back_kernel(place, *refs):
    terms, (hidden, params, grads, grads_out, grads_low, sums) = refs[:5], refs[5:]
    grad_normed = sum_terms(terms)
    found, xhat = norm_back(1, grad_normed, hidden, params, grads)
    grads_out[...] = found
    grads_low[...] = found.astype(BF)
    sums[0:1, :] = jnp.sum(grad_normed * xhat, axis=0, keepdims=True)
    sums[1:2, :] = jnp.sum(grad_normed, axis=0, keepdims=True)


def first_norm_back_kernel(place, *refs):
    terms, (hidden, params, grads, sums0, sums1, grads_out, small) = refs[:5], refs[5:]
    total = sum_terms(terms)
    grads_out[...] = norm_back(0, total[:ROWS, :], hidden, params, grads)[0]
    small[0:8, :] = total[ROWS : ROWS + 8, :LANES]
    for layer, sums in ((0, sums0), (1, sums1)):
        small[4 + layer : 5 + layer, :] = sums[0:1, slot_rows(place, 0, 0)]
        for j in range(4):
            small[8 + 4 * layer + j : 9 + 4 * layer + j, :] = sums[1:2, j * LANES : (j + 1) * LANES]


def first_attend_back_kernel(place, grads, w_dense, q_ref, k_ref, v_ref, log_in, cosine, sine, normed, xhat, weight, part_normed, ln_sums1, mixed, keep_n, give_n, keys_down, k_sum, v_sum, whole, ln_sums):
    k_sum[...] = jnp.zeros_like(k_sum)
    v_sum[...] = jnp.zeros_like(v_sum)
    keys_down[...] = (k_ref[...].astype(F32) * SCORE_SCALE).T.astype(BF)
    for start in range(0, normed.shape[0], BLOCK):
        stop = start + BLOCK

        def found_p(head, chosen):
            scores = mask_diagonal(dot_general(k_ref[:stop, :], chosen, (1, 1)), BLOCK)
            return jnp.exp(scores - log_in[head : head + 1, start:stop])

        grad_att = times_transposed(grads[start:stop, :], w_dense[0]).astype(BF)
        attend_back_block(start, q_ref, k_ref, v_ref, grad_att, keys_down, k_sum, v_sum, cosine, sine, mixed, found_p)
    mixed_rest(cosine, sine, mixed, k_sum, v_sum)
    mixed_inner(normed, weight, mixed, part_normed, whole)
    ln_sums[...] = jnp.zeros_like(ln_sums)

    def rows_done(rows):
        part = whole[rows, :].astype(F32)
        ln_sums[0:1, :] += jnp.sum(part * xhat[rows, :].astype(F32), axis=0, keepdims=True)
        ln_sums[2:3, :] += jnp.sum(part, axis=0, keepdims=True)

    loop_rows(normed.shape[0], 256, rows_done)
    ln_sums[1:2, :] = ln_sums1[0:1, :]
    ln_sums[3:4, :] = ln_sums1[1:2, :]
    for s in range(4):
        for k, out in ((0, keep_n), (1, give_n)):
            rows = slot_rows(place, s, k)
            out[s, :ROWS, :] = whole[rows, :]
            out[s, ROWS:, :] = jnp.zeros((EXTRA, out.shape[2]), BF)
            out[s, ROWS : ROWS + 8, :LANES] = ln_sums[:, rows].astype(BF)


INWARD, ACROSS, OUTWARD = [(0, 1), (3, 2)], [(1, 2), (2, 1)], [(1, 0), (2, 3)]


def along(value, pairs):
    return lax.ppermute(value, "rep", pairs)


def low_sum(left, right):
    return left[...] + right[...]


def is_middle(place):
    return (place[2] == 1) | (place[2] == 2)


def tick_kernel(has, place, *refs):
    refs = list(refs)
    if has[0]:
        chunk, came = refs.pop(0), refs.pop(0)
    if has[1]:
        before, crossed = refs.pop(0), refs.pop(0)
    if has[2]:
        coming = refs.pop(0)
    half = refs.pop(0) if has[0] else None
    going = refs.pop(0) if has[1] else None

    def half_rows(rows):
        half[rows, :] = low_sum(chunk.at[rows, :], came.at[rows, :])

    def going_rows(rows):
        found = low_sum(before.at[rows, :], crossed.at[rows, :])
        going[rows, :] = jnp.where(is_middle(place), found, coming[rows, :]) if has[2] else found

    for body, out, rows in ((half_rows, half, has[0] and chunk.shape[0]), (going_rows, going, has[1] and before.shape[0])):
        if out is not None:
            loop_rows(rows, 208 if rows % 208 == 0 else 256, body)
            if out.shape[0] > rows:
                out[rows:, :] = coming[rows:, :]


def tick(place, step, last, coming, after=(), joint=False):
    if step is not None and last is not None and not joint:
        (half,) = tick(place, step, None, None, after)
        (going,) = tick(place, None, last, coming, (half,))
        return half, going
    ins, outs = [], []
    for pair in (step, last):
        if pair is not None:
            ins += pair
            outs.append((pair[0].shape if coming is None or pair is step else coming.shape, pair[0].dtype))
    if coming is not None:
        ins.append(coming)
    has = (step is not None, last is not None, coming is not None)
    return call(partial(tick_kernel, has), outs, place, ins, after=after)


def add_small_kernel(place, chunk, small, out):
    rows = chunk.shape[0]
    out[:rows, :] = chunk[...]
    out[rows:, :LANES] = small[...].astype(BF)
    out[rows:, LANES:] = jnp.zeros((SMALL_ROWS, chunk.shape[1] - LANES), BF)


def pick_kernel(place, total, came, o0, o1, o2, o3, *rest):
    heads = o0.shape[2]
    for i, (s, k) in enumerate(SLOTS):
        out = (o0, o1, o2, o3)[s]

        def rows_done(rows):
            here = pl.ds(pl.multiple_of(rows.start + i * ROWS, rows.size), rows.size)
            found = jnp.where(is_middle(place), total[here, :], came[here, :])
            out[k, rows, :] = found[:, :heads]
            if rest:
                rest[0][rows, i * ROWS : (i + 1) * ROWS] = found[:, heads:].astype(F32)

        loop_rows(ROWS, 32, rows_done)


def pick_both_kernel(place, total_f, came_f, total_q, came_q, o0, o1, o2, o3, dense):
    units = total_f.shape[1]
    heads = o0.shape[2] - units
    for i, (s, k) in enumerate(SLOTS):
        out = (o0, o1, o2, o3)[s]

        def rows_done(rows):
            here = pl.ds(pl.multiple_of(rows.start + i * ROWS, rows.size), rows.size)
            out[k, rows, :units] = jnp.where(is_middle(place), total_f[here, :], came_f[here, :])
            found = jnp.where(is_middle(place), total_q[here, :], came_q[here, :])
            out[k, rows, units:] = found[:, :heads]
            dense[rows, i * ROWS : (i + 1) * ROWS] = found[:, heads:].astype(F32)

        loop_rows(ROWS, 32, rows_done)


def pick_both(place, units_pair, heads_pair, heads, after=()):
    columns = units_pair[0].shape[1] + heads
    outs = [((2, ROWS, columns), BF)] * 4 + [((ROWS, 8 * LANES), F32)]
    return call(pick_both_kernel, outs, place, [*units_pair, *heads_pair], after=after)


def pick(place, total, came, heads, after=()):
    outs = [((2, ROWS, heads), BF)] * 4
    if heads < total.shape[1]:
        outs.append(((ROWS, 8 * LANES), F32))
    return call(pick_kernel, outs, place, [total, came], after=after)


def chosen_sum(place, total, outward):
    middle = (place[2] == 1) | (place[2] == 2)
    return jnp.where(middle, total, outward).astype(F32)


def final_call(body, place, ins, shape, layer, before=None, after=()):
    skip = len(after) + (before is not None)

    def run(place, *refs):
        *ins, out, token, found, sems = refs[skip:]
        body(place, ins, out.at[layer], found, sems)
        token[...] = jnp.zeros_like(token)

    return pl.pallas_call(
        run,
        name=body.__name__,
        out_shape=[jax.ShapeDtypeStruct((2,) + shape, F32), jax.ShapeDtypeStruct((8, LANES), F32)],
        in_specs=[pl.BlockSpec(memory_space=pltpu.SMEM)]
        + [pl.BlockSpec(memory_space=pltpu.HBM)] * (before is not None)
        + [pl.BlockSpec(memory_space=pl.ANY)] * len(after)
        + [pl.BlockSpec(memory_space=pltpu.VMEM)] * len(ins),
        out_specs=[pl.BlockSpec(memory_space=pltpu.HBM), pl.BlockSpec(memory_space=pltpu.VMEM)],
        scratch_shapes=[pltpu.VMEM(shape, F32), pltpu.SemaphoreType.DMA((8,))],
        input_output_aliases={} if before is None else {1: 0},
        compiler_params=pltpu.CompilerParams(vmem_limit_bytes=16 * 1024 * 1024),
        cost_estimate=SMALL,
    )(place, *([] if before is None else [before]), *after, *ins)


def final_rows_start(place, total, came, out, found, sems):
    half, rows = total.shape[1], out.shape[0]
    step = rows // 4

    def move(i):
        put = pl.ds(pl.multiple_of(i * step, step), step)
        return pltpu.make_async_copy(found.at[put, :], out.at[put, :], sems.at[i])

    def one(i, carry):
        put = pl.ds(pl.multiple_of(i * step, step), step)
        for j in range(2):
            part = pl.ds(pl.multiple_of(i * step + j * rows, step), step)
            found[put, j * half : (j + 1) * half] = jnp.where(is_middle(place), total[part, :], came[part, :]).astype(F32)
        move(i).start()
        return carry

    lax.fori_loop(0, 4, one, 0)
    return [move(i) for i in range(4)]


def final_rows_kernel(place, ins, out, found, sems):
    for move in final_rows_start(place, *ins, out, found, sems):
        move.wait()


def final_units_kernel(place, blocks, out, found, sems):
    units, moves = out.shape[1] // 8, []
    for i, (s, k) in enumerate(SLOTS):
        put = slice(i * units, (i + 1) * units)
        block = block_of(s, k, blocks)

        def rows_done(rows):
            found[rows, put] = block[rows, :units].astype(F32)

        loop_rows(ROWS, 32, rows_done)
        moves.append(pltpu.make_async_copy(found.at[:, put], out.at[:, slot_rows(place, s, k, units)], sems.at[i]))
        moves[-1].start()
    for move in moves:
        move.wait()


def final_heads_kernel(place, blocks, out, found, sems):
    third = out.shape[1] // 3
    for s, k in SLOTS:
        block = block_of(s, k, blocks)

        def rows_done(rows):
            part = block[rows, block.shape[1] - 3 * LANES :].astype(F32)
            for j in range(3):
                lanes = pl.ds(pl.multiple_of(j * third + slot_start(place, s, k, LANES), LANES), LANES)
                found[rows, lanes] = part[:, j * LANES : (j + 1) * LANES]

        loop_rows(ROWS, 32, rows_done)
    move = pltpu.make_async_copy(found, out, sems.at[0])
    move.start()
    move.wait()


def last_rows_kernel(place, before, total, came, out, gain, shift, bias_fc1, bias_fc2, found, sems):
    rows = slice(total.shape[0] - SMALL_ROWS, total.shape[0])
    small = jnp.where(is_middle(place), total[rows, :LANES], came[rows, :LANES]).astype(F32)
    moves = final_rows_start(place, total, came, out.at[0], found, sems)
    gain[...] = small[0:2, :]
    shift[...] = small[2:4, :]
    bias_fc2[...] = small[4:6, :]
    for layer in range(2):
        for j in range(4):
            bias_fc1[layer : layer + 1, j * LANES : (j + 1) * LANES] = small[8 + 4 * layer + j : 9 + 4 * layer + j, :]
    for move in moves:
        move.wait()


def local_plane(hidden_in, ln_gain, ln_bias, w_qkv, w_dense, w_fc1, b_fc1, w_fc2, b_fc2, output_grad):
    index = lax.axis_index("grp")
    place = jnp.stack([index // 2, index % 2, lax.axis_index("rep")]).astype(jnp.int32)
    span, width = hidden_in.shape[1:]
    seq = span * 8
    units = b_fc1.shape[1]
    own = 3 * LANES
    cosine, sine = rotary_tables(seq)
    hidden0 = hidden_in.reshape(span, width)
    grads1 = output_grad.reshape(span, width)

    wide, column, chunk_shape = ((seq, width), BF), ((seq, LANES), BF), ((seq, units), BF)
    blocks_n, blocks_n0 = ((4, ROWS, width), BF), ((4, ROWS + EXTRA, width), BF)
    blocks_f, blocks_q = ((2, ROWS, units), BF), ((2, ROWS, own), BF)
    mine, mine_low = ((span, width), F32), ((span, width), BF)
    sums_shape, part_shape = ((8, width), F32), ((seq, width), F32)
    head_scratch = [pltpu.VMEM((LANES, seq), BF), pltpu.VMEM((seq, LANES), F32), pltpu.VMEM((seq, LANES), F32)]
    back_scratch = [pltpu.VMEM((seq, own), BF), pltpu.VMEM((width, own), BF), pltpu.VMEM((seq, width), BF)]
    column_scratch = [pltpu.VMEM((seq, LANES), BF)] * 3
    units_scratch = [pltpu.VMEM((seq, units), BF), pltpu.VMEM((width, units), BF)]

    rows = [hidden0.shape, ln_gain.shape, ln_bias.shape, b_fc2.shape, w_qkv.shape[1:], (HALF, w_fc1.shape[2])]
    rows = [rows[0], *rows[4:], *rows[1:4]]
    packed = pl.pallas_call(
        pack_first_kernel,
        name="pack_first_kernel",
        out_shape=[jax.ShapeDtypeStruct((FIRST_ROWS, LANES), BF)] * 4,
        in_specs=[pl.BlockSpec(memory_space=pltpu.HBM)] * 6,
        out_specs=[pl.BlockSpec(memory_space=pltpu.VMEM)] * 4,
        scratch_shapes=[pltpu.VMEM(shape, BF) for shape in rows] + [pltpu.SemaphoreType.DMA((6,))],
        compiler_params=pltpu.CompilerParams(vmem_limit_bytes=60 * 1024 * 1024),
        cost_estimate=SMALL,
    )(hidden0, w_qkv, w_fc1, ln_gain, ln_bias, b_fc2)
    first = send_blocks(place, packed)
    packed = call(partial(pack_units_grads_kernel, 1), [((3 * ROWS, units), BF)] * 4, place, [w_fc1, grads1])
    keep, give = call(partial(pack_heads_kernel, 1), [((4, ROWS, own), BF)] * 2, place, [w_qkv], after=[packed[0]])
    pairs1 = call(pair_kernel, [blocks_q] * 4, place, [keep, swap(give, 1)])
    (others0,) = call(others_first_kernel, [((4, OTHERS_ROWS, LANES), BF)], place, first, after=[pairs1[0]])
    units1 = send_blocks(place, packed)
    first = [*first, swap(others0, 1)]
    (near0,) = call(near_first_kernel, [((8, HALF_ROWS, LANES), BF)], place, first)
    far0 = along(near0, INWARD + OUTWARD)

    normed0, xhat0, weight_q0, params, q0, k0, v0, att0, log0 = call(
        first_attend_kernel,
        [wide, wide, ((width, own), BF), ((EXTRA, width), F32), column, column, column, column, ((8, seq), F32)],
        place,
        [*first, cosine, sine],
        [pltpu.VMEM((LANES, seq), BF)],
        after=[near0],
    )
    weight_f0, act0, slope0, partial_sum = call(
        first_units_kernel,
        [((width, units), BF), ((seq, units), BF), ((seq, units), F32), wide],
        place,
        [normed0, near0, far0, b_fc1, w_fc2, w_dense, att0],
    )
    (near1,) = call(near_units_kernel, [((4, ROWS, units), BF)], place, units1, after=[partial_sum])
    far1 = along(near1, INWARD + OUTWARD)
    keep, give = call(split_kernel, [blocks_n, blocks_n], place, [partial_sum], after=[near1])
    terms, sent = begin_scatter(place, keep, give)
    (others1,) = call(others_units_grads_kernel, [((4, 3 * ROWS, units), BF)], place, [*units1, far1], after=terms[2:])
    hidden1, normed1_own = call(next_hidden_kernel, [mine, mine_low], place, [*terms, hidden0, params], after=[others1])
    pieces = gather_pieces(normed1_own)

    weight_f1, grad_branch1 = call(
        second_ready_kernel, [((width, units), BF), wide], place, [*units1, swap(others1, 1), far1]
    )
    normed1, act1, pre1, chunk1 = call(
        second_units_kernel,
        [wide, ((seq, units), BF), ((seq, units), F32), chunk_shape],
        place,
        [*pieces, b_fc1, weight_f1, grad_branch1],
    )
    came1 = along(chunk1, INWARD + OUTWARD)
    heads1 = send_blocks(place, pairs1)
    chunk2, sums1, part_normed, grad_att1 = call(
        second_units_back_kernel,
        [chunk_shape, sums_shape, part_shape, column],
        place,
        [grad_branch1, w_fc2, w_dense, pre1, normed1, weight_f1],
        units_scratch,
    )
    att1, mixed1, keep, give = call(
        second_attend_kernel,
        [column, ((seq, own), BF), blocks_n, blocks_n],
        place,
        [normed1, *heads1, cosine, sine, grad_att1, part_normed],
        [
            pltpu.VMEM((width, own), BF),
            *column_scratch,
            pltpu.VMEM((LANES, seq), BF),
            *head_scratch,
        ],
    )
    terms, sent = begin_scatter(place, keep, give)
    (half1,) = tick(place, (chunk1, came1), None, None, after=[give])
    (chunk3,) = call(
        second_heads_kernel,
        [chunk_shape],
        place,
        [normed1, mixed1, att1, grad_branch1],
        [pltpu.VMEM((width, own), BF)],
        after=[half1, sent],
    )
    cross1, came2 = along(half1, ACROSS), along(chunk2, INWARD + OUTWARD)
    grads0, grads0_low, ln_sums1 = call(
        second_norm_back_kernel, [mine, mine_low, sums_shape], place, [*terms, hidden1, params, grads1], after=[half1, chunk3]
    )

    pieces = gather_pieces(grads0_low)
    half2, total1 = tick(place, (chunk2, came2), (half1, cross1), chunk3, after=[pieces[1]])
    cross2, came3 = along(half2, ACROSS), along(total1, INWARD + OUTWARD)
    grad_branch0, chunk6, chunk4, sums0, part_normed = call(
        first_units_back_kernel,
        [wide, chunk_shape, chunk_shape, sums_shape, part_shape],
        place,
        [*pieces, act0, w_fc2, slope0, normed0, weight_f0],
        units_scratch,
        after=[half2],
    )
    mixed0, keep, give = call(
        first_attend_back_kernel,
        [((seq, own), BF), blocks_n0, blocks_n0],
        place,
        [grad_branch0, w_dense, q0, k0, v0, log0, cosine, sine, normed0, xhat0, weight_q0, part_normed, ln_sums1],
        [*head_scratch, pltpu.VMEM((seq, width), BF), pltpu.VMEM((8, width), F32)],
    )
    last_ins, whole_scratch = [act1, att1, w_fc2, w_dense], [pltpu.VMEM((seq, width), BF)]
    blocks_h = call(partial(last_hidden_of_core, 0), [blocks_n, blocks_n], place, last_ins, whole_scratch, after=[mixed0])
    half3, total2 = tick(place, (chunk3, came3), (half2, cross2), chunk4, after=[blocks_h[0]], joint=True)
    keep_h, give_h = call(
        partial(last_hidden_of_core, 1), [blocks_n, blocks_n], place, [*last_ins, *blocks_h], whole_scratch, after=[half3], held=2
    )
    cross3, came4 = along(half3, ACROSS), along(total2, INWARD + OUTWARD)
    (chunk5,) = call(
        second_heads_kernel,
        [chunk_shape],
        place,
        [normed0, mixed0, att0, grad_branch0],
        [pltpu.VMEM((width, own), BF)],
        after=[half3],
    )
    token = ((8, LANES), F32)
    terms, sent = begin_scatter(place, keep, give, after=[half3])
    out_fc2, done = final_call(final_rows_kernel, place, [total1, came3], (units, width), 1, after=[sent])
    input_grad, small_sums = call(
        first_norm_back_kernel,
        [mine, ((SMALL_ROWS, LANES), F32)],
        place,
        [*terms, hidden0, params, grads0, sums0, sums1],
        after=[done],
    )
    half4, total3 = tick(place, (chunk4, came4), (half3, cross3), chunk5, after=[small_sums], joint=True)
    cross4, came5 = along(half4, ACROSS), along(total3, INWARD + OUTWARD)
    (chunk6,) = call(
        add_small_kernel, [((seq + SMALL_ROWS, units), BF)], place, [chunk6, small_sums], after=[half4]
    )
    terms, _ = begin_scatter(place, keep_h, give_h, after=[half4])
    hidden_out, done_h = call(last_sum_kernel, [mine, token], place, [*terms, hidden1, params], after=[chunk6])
    half5, total4 = tick(place, (chunk5, came5), (half4, cross4), chunk6, after=[done_h], joint=True)
    cross5, came6 = along(half5, ACROSS), along(total4, INWARD + OUTWARD)
    *picked1, dense1 = pick_both(place, (total2, came4), (total3, came5), own, after=[half5])
    blocks1 = swap_others(place, send_blocks(place, picked1))
    half6, total5 = tick(place, (chunk6, came6), (half5, cross5), None, after=[blocks1[1]], joint=True)
    cross6, came7 = along(half6, ACROSS), along(total5, INWARD + OUTWARD)
    picked4 = pick(place, total4, came6, units, after=[half6])
    out_fc1, done1 = final_call(final_units_kernel, place, blocks1, (ROWS, w_fc1.shape[2]), 1, after=[picked4[0]])
    out_qkv, done3 = final_call(final_heads_kernel, place, blocks1, (ROWS, w_qkv.shape[2]), 1, after=[done1])
    blocks4 = swap_others(place, send_blocks(place, picked4), after=[done3])
    (total6,) = tick(place, None, (half6, cross6), None, after=[blocks4[1]])
    came8 = along(total6, INWARD + OUTWARD)
    *picked5, dense0 = pick(place, total5, came7, own, after=[total6])
    out_fc1, done4 = final_call(final_units_kernel, place, blocks4, (ROWS, w_fc1.shape[2]), 0, out_fc1, after=[picked5[0]])
    blocks5 = swap_others(place, send_blocks(place, picked5), after=[done4])
    out_qkv, done5 = final_call(final_heads_kernel, place, blocks5, (ROWS, w_qkv.shape[2]), 0, out_qkv)
    vector = jax.ShapeDtypeStruct((2, LANES), F32)
    out_fc2, out_gain, out_shift, out_b_fc1, out_b_fc2 = pl.pallas_call(
        lambda place, before, token, *refs: last_rows_kernel(place, before, *refs),
        name="last_rows_kernel",
        out_shape=[jax.ShapeDtypeStruct((2, units, width), F32), vector, vector, jax.ShapeDtypeStruct((2, units), F32), vector],
        in_specs=[pl.BlockSpec(memory_space=pltpu.SMEM), pl.BlockSpec(memory_space=pltpu.HBM)]
        + [pl.BlockSpec(memory_space=pl.ANY)]
        + [pl.BlockSpec(memory_space=pltpu.VMEM)] * 2,
        out_specs=[pl.BlockSpec(memory_space=pltpu.HBM)] + [pl.BlockSpec(memory_space=pltpu.VMEM)] * 4,
        scratch_shapes=[pltpu.VMEM((units, width), F32), pltpu.SemaphoreType.DMA((4,))],
        input_output_aliases={1: 0},
        compiler_params=pltpu.CompilerParams(vmem_limit_bytes=16 * 1024 * 1024),
        cost_estimate=SMALL,
    )(place, out_fc2, done5, total6, came8)
    out_dense = jnp.stack([dense0, dense1])
    return (
        hidden_out[None],
        input_grad[None],
        out_gain,
        out_shift,
        out_qkv,
        out_dense,
        out_fc1,
        out_b_fc1,
        out_fc2,
        out_b_fc2,
    )


def local(hidden_in, ln_gain, ln_bias, w_qkv, w_dense, w_fc1, b_fc1, w_fc2, b_fc2, output_grad):
    arguments = (hidden_in, ln_gain, ln_bias, w_qkv, w_dense, w_fc1, b_fc1, w_fc2, b_fc2, output_grad)
    plane = lax.axis_size("grp") == 8 and lax.axis_size("rep") == 4
    plane = plane and hidden_in.shape[:2] == (1, ROWS) and w_qkv.shape == (2, LANES, 3 * 8 * LANES)
    return (local_plane if plane else local_any)(*arguments)


def solution(mesh):
    in_specs = (
        P("rep", "grp", None),
        P(None, "grp"),
        P(None, "grp"),
        P(None, "grp", None),
        P(None, "grp", None),
        P(None, "grp", None),
        P(None, "grp"),
        P(None, "grp", None),
        P(None, "grp"),
        P("rep", "grp", None),
    )
    out_specs = (
        P("rep", "grp", None),
        P("rep", "grp", None),
        P(None, "grp"),
        P(None, "grp"),
        P(None, "grp", None),
        P(None, "grp", None),
        P(None, "grp", None),
        P(None, "grp"),
        P(None, "grp", None),
        P(None, "grp"),
    )
    return jax.shard_map(local, mesh=mesh, in_specs=in_specs, out_specs=out_specs, check_vma=False)
```

```python
from functools import partial

import jax
import jax.numpy as jnp
import numpy as np
from jax import lax
from jax.experimental import pallas as pl
from jax.experimental.pallas import tpu as pltpu
from jax.sharding import PartitionSpec as P

HEAD_DIM = 64
ROT = 32
LANES = 128

EPSILON = 1e-05
SCORE_SCALE = 0.125
NEGATIVE = -1000000000.0
BF = jnp.bfloat16
F32 = jnp.float32


def dot(left, right):
    return jnp.dot(left, right, preferred_element_type=F32)


def dot_general(left, right, contract):
    return lax.dot_general(left, right, ((contract[:1], contract[1:]), ((), ())), preferred_element_type=F32)


def outer_sum(left, right):
    return dot_general(left, right, (0, 0))


def times_transposed(left, right):
    return dot_general(left, right, (1, 1))


def head_mask(head):
    lane = lax.broadcasted_iota(jnp.int32, (1, LANES), 1)
    return (lane >= head * HEAD_DIM) & (lane < (head + 1) * HEAD_DIM)


def turn(part, cosine, sine, sign):
    even = lax.broadcasted_iota(jnp.int32, part.shape, 1) % 2 == 0
    partner = jnp.where(even, pltpu.roll(part, LANES - 1, 1), pltpu.roll(part, 1, 1))
    return part * cosine + partner * (sine * sign)


def mask_diagonal(scores, block):
    keys, queries = scores.shape
    key_place = lax.broadcasted_iota(jnp.int32, (block, queries), 0)
    query_place = lax.broadcasted_iota(jnp.int32, (block, queries), 1)
    last = jnp.where(key_place <= query_place, scores[keys - block :], NEGATIVE)
    if keys == block:
        return last
    return jnp.concatenate([scores[: keys - block], last], axis=0)


def attend_kernel(heads, block, mix_q, mix_k, mix_v, cosine, sine, q_out, k_out, v_out, att_out, log_out):
    seq = mix_q.shape[0]
    q_out[...] = turn(mix_q[...], cosine[...], sine[...], 1.0).astype(BF)
    k_out[...] = turn(mix_k[...], cosine[...], sine[...], 1.0).astype(BF)
    v_out[...] = mix_v[...].astype(BF)
    values_down = mix_v[...].T.astype(BF)
    for start in range(0, seq, block):
        stop = start + block
        queries = q_out[start:stop, :] * SCORE_SCALE
        keys = k_out[:stop, :]
        total = jnp.zeros((LANES, block), F32)
        for head in range(heads):
            chosen = jnp.where(head_mask(head), queries, 0.0).astype(BF)
            scores = mask_diagonal(dot_general(keys, chosen, (1, 1)), block)
            row_max = jnp.max(scores, axis=0, keepdims=True)
            exponent = jnp.exp(scores - row_max)
            row_total = jnp.sum(exponent, axis=0, keepdims=True)
            probabilities = (exponent * (1.0 / row_total)).astype(BF)
            log_out[head : head + 1, start:stop] = row_max + jnp.log(row_total)
            found = dot(values_down[:, :stop], probabilities)
            down = lax.broadcasted_iota(jnp.int32, (LANES, 1), 0)
            own = (down >= head * HEAD_DIM) & (down < (head + 1) * HEAD_DIM)
            total = total + jnp.where(own, found, 0.0)
        att_out[start:stop, :] = total.T.astype(BF)


def attend_back_kernel(heads, block, q_in, k_in, v_in, grad_att, log_in, cosine, sine, q_out, k_out, v_out, k_sum, v_sum):
    seq = q_in.shape[0]
    k_sum[...] = jnp.zeros_like(k_sum)
    v_sum[...] = jnp.zeros_like(v_sum)
    keys_down = (k_in[...].astype(F32) * SCORE_SCALE).T.astype(BF)
    for start in range(0, seq, block):
        stop = start + block
        queries = q_in[start:stop, :] * SCORE_SCALE
        grads = grad_att[start:stop, :]
        grad_queries = jnp.zeros((LANES, block), F32)
        for head in range(heads):
            chosen = jnp.where(head_mask(head), queries, 0.0).astype(BF)
            chosen_grads = jnp.where(head_mask(head), grads, 0.0).astype(BF)
            scores = mask_diagonal(dot_general(k_in[:stop, :], chosen, (1, 1)), block)
            probabilities = jnp.exp(scores - log_in[head : head + 1, start:stop])
            grad_probs = dot_general(v_in[:stop, :], chosen_grads, (1, 1))
            row_inner = jnp.sum(grad_probs * probabilities, axis=0, keepdims=True)
            grad_scores = (probabilities * (grad_probs - row_inner)).astype(BF)
            k_sum[:stop, :] += dot(grad_scores, chosen)
            v_sum[:stop, :] += dot(probabilities.astype(BF), chosen_grads)
            down = lax.broadcasted_iota(jnp.int32, (LANES, 1), 0)
            own = (down >= head * HEAD_DIM) & (down < (head + 1) * HEAD_DIM)
            grad_queries = grad_queries + jnp.where(own, dot(keys_down[:, :stop], grad_scores), 0.0)
        q_out[start:stop, :] = turn(
            grad_queries.T, cosine[start:stop, :], sine[start:stop, :], -1.0
        ).astype(BF)
    k_out[...] = turn(k_sum[...], cosine[...], sine[...], -1.0).astype(BF)
    v_out[...] = v_sum[...].astype(BF)


VMEM_LIMIT = 48 * 1024 * 1024


def attend(mix_q, mix_k, mix_v, heads, cosine, sine):
    seq = mix_q.shape[0]
    out = jax.ShapeDtypeStruct((seq, LANES), BF)
    return pl.pallas_call(
        partial(attend_kernel, heads, min(256, seq)),
        out_shape=(out, out, out, out, jax.ShapeDtypeStruct((heads, seq), F32)),
        compiler_params=pltpu.CompilerParams(vmem_limit_bytes=VMEM_LIMIT),
    )(mix_q, mix_k, mix_v, cosine, sine)


def attend_back(queries, keys, values, grad_att, log_total, heads, cosine, sine):
    seq = queries.shape[0]
    out = jax.ShapeDtypeStruct((seq, LANES), BF)
    return pl.pallas_call(
        partial(attend_back_kernel, heads, min(256, seq)),
        out_shape=(out, out, out),
        scratch_shapes=[pltpu.VMEM((seq, LANES), F32), pltpu.VMEM((seq, LANES), F32)],
        compiler_params=pltpu.CompilerParams(vmem_limit_bytes=VMEM_LIMIT),
    )(queries, keys, values, grad_att, log_total, cosine, sine)


def rotary_tables(seq):
    frequency = (1.0 / 10000.0 ** (np.arange(ROT // 2, dtype=np.float32) * 2.0 / ROT)).astype(np.float32)
    angles = np.arange(seq, dtype=np.float32)[:, None] * frequency[None, :]
    cosine, sine = np.cos(angles.astype(np.float64)), np.sin(angles.astype(np.float64))
    cosine = np.repeat(cosine, 2, axis=1)
    sine = np.repeat(sine, 2, axis=1) * np.tile([-1.0, 1.0], ROT // 2)
    rest = HEAD_DIM - ROT
    cosine = np.concatenate([cosine, np.ones((seq, rest))], axis=1)
    sine = np.concatenate([sine, np.zeros((seq, rest))], axis=1)
    repeats = (1, LANES // HEAD_DIM)
    return np.tile(cosine, repeats).astype(np.float32), np.tile(sine, repeats).astype(np.float32)


def swap(value, bits):
    return lax.ppermute(value, "grp", [(i, i ^ bits) for i in range(8)])


def add_low(left, right):
    return (left.astype(F32) + right.astype(F32)).astype(BF)


def by_chip(parts, chip):
    x, y = chip % 2 == 1, chip // 2 == 1
    near = jnp.where(x, jnp.stack([parts[1], parts[0]]), jnp.stack([parts[0], parts[1]]))
    far = jnp.where(x, jnp.stack([parts[3], parts[2]]), jnp.stack([parts[2], parts[3]]))
    return jnp.where(y, jnp.concatenate([far, near]), jnp.concatenate([near, far]))


def gather_rows(part):
    size = lax.axis_size("grp")
    if size != 8:
        return lax.all_gather(part, "grp", axis=0, tiled=True)
    rows, width = part.shape
    half = rows // 2
    index = lax.axis_index("grp")
    along_x, along_y = swap(part, 2), swap(part, 4)
    corner = jnp.concatenate([swap(along_y[:half], 2), swap(along_x[half:], 4)])
    mine = by_chip([part, along_x, along_y, corner], index // 2)
    other = swap(mine, 1)
    odd = index % 2 == 1
    both = jnp.stack([jnp.where(odd, other, mine), jnp.where(odd, mine, other)], axis=1)
    return both.reshape(8 * rows, width)


def scatter_sum(whole):
    size = lax.axis_size("grp")
    if size != 8:
        return lax.psum_scatter(whole, "grp", scatter_dimension=0, tiled=True).astype(F32)
    rows, width = whole.shape[0] // 8, whole.shape[1]
    half = rows // 2
    index = lax.axis_index("grp")
    chip, core = index // 2, index % 2
    blocks = whole.reshape(4, 2, rows, width)
    keep = lax.dynamic_index_in_dim(blocks, core, 1, False)
    give = lax.dynamic_index_in_dim(blocks, 1 - core, 1, False)
    summed = add_low(keep, swap(give, 1))
    own, for_x, for_y, corner = [lax.dynamic_index_in_dim(summed, chip ^ s, 0, False) for s in range(4)]
    by_x, by_y = swap(corner[:half], 2), swap(corner[half:], 4)
    for_y = jnp.concatenate([add_low(for_y[:half], by_x), for_y[half:]])
    for_x = jnp.concatenate([for_x[:half], add_low(for_x[half:], by_y)])
    return own.astype(F32) + swap(for_y, 4).astype(F32) + swap(for_x, 2).astype(F32)


def exchange(blocks):
    size = lax.axis_size("grp")
    if size != 8:
        return lax.all_to_all(blocks, "grp", 0, 0)
    index = lax.axis_index("grp")
    chip, core = index // 2, index % 2
    pairs = blocks.reshape((4, 2) + blocks.shape[1:])
    keep = lax.dynamic_index_in_dim(pairs, core, 1, False)
    give = lax.dynamic_index_in_dim(pairs, 1 - core, 1, False)
    came = swap(give, 1)
    odd = core == 1
    both = jnp.stack([jnp.where(odd, came, keep), jnp.where(odd, keep, came)], axis=1)
    parts = [lax.dynamic_index_in_dim(both, chip ^ s, 0, False) for s in range(4)]
    parts = [parts[0]] + [swap(parts[s], 2 * s) for s in (1, 2, 3)]
    return by_chip(parts, chip).reshape(blocks.shape)


def rep_sum(part):
    if lax.axis_size("rep") != 4:
        return lax.psum(part, "rep").astype(F32)
    place = lax.axis_index("rep")
    inward = lax.ppermute(part, "rep", [(0, 1), (3, 2)])
    half_sum = add_low(part, inward)
    across = lax.ppermute(half_sum, "rep", [(1, 2), (2, 1)])
    total = add_low(half_sum, across)
    outward = lax.ppermute(total, "rep", [(1, 0), (2, 3)])
    return jnp.where((place == 1) | (place == 2), total, outward).astype(F32)


def columns_of(w_qkv, w_fc1, group):
    rows, qkv = w_qkv.shape
    heads = w_qkv.reshape(rows, 3, group, qkv // 3 // group).transpose(2, 0, 1, 3).reshape(group, rows, -1)
    units = w_fc1.reshape(rows, group, -1).transpose(1, 0, 2)
    found = exchange(jnp.concatenate([heads, units], axis=2))
    found = found.reshape(group * rows, -1)
    return found[:, : qkv // group], found[:, qkv // group :]


def rows_of(grad_qkv, grad_fc1, group):
    rows = grad_qkv.shape[0] // group
    both = jnp.concatenate([grad_qkv, grad_fc1], axis=1).reshape(group, rows, -1)
    found = exchange(both)
    qkv = grad_qkv.shape[1]
    heads = found[:, :, :qkv].reshape(group, rows, 3, qkv // 3).transpose(1, 2, 0, 3).reshape(rows, -1)
    units = found[:, :, qkv:].transpose(1, 0, 2).reshape(rows, -1)
    return heads, units


def standardize(hidden):
    centered = hidden - jnp.mean(hidden, axis=-1, keepdims=True)
    scale = lax.rsqrt(jnp.mean(centered * centered, axis=-1, keepdims=True) + EPSILON)
    return centered * scale, scale


def widen(part):
    return jnp.pad(part, ((0, 0), (0, LANES - part.shape[1])))


def forward_layer(normed, weights, heads, tables):
    qkv_cols, fc1_cols, b_fc1, w_dense, w_fc2 = weights
    mixed = dot(normed, qkv_cols)
    own = heads * HEAD_DIM
    queries, keys, values, attended, log_total = attend(
        *(widen(mixed[:, i * own : (i + 1) * own]) for i in range(3)), heads, *tables
    )
    pre_act = dot(normed, fc1_cols) + b_fc1.astype(F32)
    activation = jax.nn.gelu(pre_act, approximate=True).astype(BF)
    partial_sum = (dot(attended[:, :own], w_dense) + dot(activation, w_fc2)).astype(BF)
    stored = (normed, queries, keys, values, attended, log_total, pre_act, activation)
    return partial_sum, stored


def backward_layer(grad_branch, weights, stored, heads, tables):
    qkv_cols, fc1_cols, b_fc1, w_dense, w_fc2 = weights
    normed, queries, keys, values, attended, log_total, pre_act, activation = stored
    own = heads * HEAD_DIM
    grad_w_fc2 = outer_sum(activation, grad_branch).astype(BF)
    grad_w_dense = outer_sum(attended[:, :own], grad_branch).astype(BF)
    _, gelu_back = jax.vjp(partial(jax.nn.gelu, approximate=True), pre_act)
    grad_pre = gelu_back(times_transposed(grad_branch, w_fc2))[0].astype(BF)
    grad_attended = widen(times_transposed(grad_branch, w_dense).astype(BF))
    grad_mixed = attend_back(queries, keys, values, grad_attended, log_total, heads, *tables)
    grad_mixed = jnp.concatenate([part[:, :own] for part in grad_mixed], axis=1)
    grad_fc1 = outer_sum(normed, grad_pre).astype(BF)
    grad_b_fc1 = jnp.sum(grad_pre.astype(F32), axis=0)
    grad_qkv = outer_sum(normed, grad_mixed).astype(BF)
    grad_normed = (times_transposed(grad_pre, fc1_cols) + times_transposed(grad_mixed, qkv_cols)).astype(BF)
    return grad_normed, (grad_w_fc2, grad_w_dense, grad_fc1, grad_qkv, grad_b_fc1)


def local_any(hidden_in, ln_gain, ln_bias, w_qkv, w_dense, w_fc1, b_fc1, w_fc2, b_fc2, output_grad):
    group = lax.axis_size("grp")
    index = lax.axis_index("grp")
    layers = w_qkv.shape[0]
    span, width = hidden_in.shape[1:]
    seq = span * group
    heads = width // HEAD_DIM // group
    tables = rotary_tables(seq)
    small = jnp.concatenate([ln_gain, ln_bias, b_fc2])
    small = lax.all_gather(small, "grp", axis=1, tiled=True).astype(F32)
    gains, shifts, b_fc2_all = small[:layers], small[layers : 2 * layers], small[2 * layers :]
    hidden = hidden_in.reshape(span, width).astype(F32)
    hidden_all = gather_rows(hidden_in.reshape(span, width))
    weights = []
    for layer in range(layers):
        qkv_cols, fc1_cols = columns_of(w_qkv[layer], w_fc1[layer], group)
        weights.append((qkv_cols, fc1_cols, b_fc1[layer], w_dense[layer], w_fc2[layer]))

    inputs, stored_layers = [], []
    for layer in range(layers):
        inputs.append(hidden)
        if layer == 0:
            normed = (standardize(hidden_all.astype(F32))[0] * gains[0] + shifts[0]).astype(BF)
        else:
            normed = gather_rows((standardize(hidden)[0] * gains[layer] + shifts[layer]).astype(BF))
        partial_sum, stored = forward_layer(normed, weights[layer], heads, tables)
        stored_layers.append(stored)
        hidden = hidden + scatter_sum(partial_sum) + b_fc2_all[layer]

    grad_hidden = output_grad.reshape(span, width)
    small_grads, large_grads = [None] * layers, [None] * layers
    for layer in reversed(range(layers)):
        grad_low = grad_hidden.astype(BF)
        grad_branch = gather_rows(grad_low)
        grad_normed, found = backward_layer(grad_branch, weights[layer], stored_layers[layer], heads, tables)
        grad_w_fc2, grad_w_dense, grad_fc1, grad_qkv, grad_b_fc1 = found
        grad_qkv, grad_fc1 = rows_of(grad_qkv, grad_fc1, group)
        large_grads[layer] = tuple(rep_sum(part) for part in (grad_w_fc2, grad_w_dense, grad_fc1, grad_qkv))
        grad_normed = scatter_sum(grad_normed)
        xhat, scale = standardize(inputs[layer])
        inner = grad_normed * gains[layer]
        mean_inner = jnp.mean(inner, axis=-1, keepdims=True)
        mean_along = jnp.mean(inner * xhat, axis=-1, keepdims=True)
        small_grads[layer] = jnp.concatenate(
            [
                jnp.sum(grad_normed * xhat, axis=0),
                jnp.sum(grad_normed, axis=0),
                jnp.sum(grad_low.astype(F32), axis=0),
                lax.dynamic_update_slice(
                    jnp.zeros((group * grad_b_fc1.shape[0],), F32), grad_b_fc1, (index * grad_b_fc1.shape[0],)
                ),
            ]
        )
        grad_hidden = grad_hidden + (inner - mean_inner - xhat * mean_along) * scale

    summed = lax.psum(jnp.stack(small_grads), ("rep", "grp"))
    own = width // group
    units = b_fc1.shape[1]

    def pick(start, count):
        return lax.dynamic_slice_in_dim(summed, start + index * count, count, 1)

    stacked = [jnp.stack([large_grads[layer][member] for layer in range(layers)]) for member in range(4)]
    return (
        hidden[None],
        grad_hidden[None],
        pick(0, own),
        pick(width, own),
        stacked[3],
        stacked[1],
        stacked[2],
        pick(3 * width, units),
        stacked[0],
        pick(2 * width, own),
    )


SLOTS = [(s, k) for s in range(4) for k in range(2)]
ROWS = 128
EXTRA = 16


def slot_start(place, s, k, size):
    return pl.multiple_of(((place[0] ^ s) * 2 + (place[1] ^ k)) * size, size)


def slot_rows(place, s, k, size=ROWS):
    return pl.ds(slot_start(place, s, k, size), size)


SMALL = pl.CostEstimate(flops=0, bytes_accessed=0, transcendentals=0)


def call(body, outs, place, ins, scratch=(), after=(), hbm=0, mib=16, held=0):
    def run(place, *refs):
        body(place, *refs[len(after) :])

    return pl.pallas_call(
        run,
        name=getattr(body, "func", body).__name__,
        out_shape=[jax.ShapeDtypeStruct(*out) for out in outs],
        in_specs=[pl.BlockSpec(memory_space=pltpu.SMEM)]
        + [pl.BlockSpec(memory_space=pl.ANY)] * len(after)
        + [pl.BlockSpec(memory_space=pltpu.HBM)] * hbm
        + [pl.BlockSpec(memory_space=pltpu.VMEM)] * (len(ins) - hbm),
        out_specs=[pl.BlockSpec(memory_space=pltpu.VMEM)] * len(outs),
        scratch_shapes=list(scratch),
        input_output_aliases={1 + len(after) + len(ins) - held + i: i for i in range(held)},
        compiler_params=pltpu.CompilerParams(vmem_limit_bytes=mib * 1024 * 1024),
        cost_estimate=SMALL,
    )(place, *after, *ins)


def gather_pieces(part):
    mine = [part, swap(part, 2), swap(part, 4), swap(part, 6)]
    other = [swap(piece, 1) for piece in mine]
    return [piece for pair in zip(mine, other) for piece in pair]


def put_columns(out, start, value):
    rows = value.shape[0]
    for b in range(value.shape[1] // LANES):
        out[start + b * rows : start + (b + 1) * rows, :] = value[:, b * LANES : (b + 1) * LANES]


def heads_of(place, w_qkv, layer, s, k, j):
    start = j * (w_qkv.shape[2] // 3) + slot_start(place, s, k, LANES)
    return w_qkv[layer, :, pl.ds(pl.multiple_of(start, LANES), LANES)]


HALF = ROWS // 2
HEADS_ROWS, HALF_ROWS = 3 * ROWS, 4 * HALF
FIRST_MINE = 8 * ROWS
FIRST_OTHERS = FIRST_MINE + HEADS_ROWS + HALF_ROWS
FIRST_SMALL = FIRST_OTHERS + HEADS_ROWS + HALF_ROWS
FIRST_ROWS = FIRST_SMALL + EXTRA
OTHERS_MINE = 8 * ROWS
OTHERS_SMALL = OTHERS_MINE + HEADS_ROWS + HALF_ROWS
OTHERS_ROWS = OTHERS_SMALL + EXTRA


def half_start(place, other):
    parity = place[2] & 1
    return pl.multiple_of((1 - parity if other else parity) * HALF, HALF)


def pack_first_kernel(hidden_from, qkv_from, fc1_from, gain_from, shift_from, bias_from, o0, o1, o2, o3, hidden, w_qkv, w_fc1, gain, shift, bias, sems):
    index = lax.axis_index("grp")
    place = (index // 2, index % 2, lax.axis_index("rep"))
    outs = (o0, o1, o2, o3)
    pairs = (
        (hidden_from, hidden),
        (gain_from, gain),
        (shift_from, shift),
        (bias_from, bias),
        (qkv_from.at[0], w_qkv),
        (fc1_from.at[0, pl.ds(half_start(place, False), HALF), :], w_fc1),
    )
    moves = [pltpu.make_async_copy(*pair, sems.at[i]) for i, pair in enumerate(pairs)]
    for move in moves:
        move.start()
    for move in moves[:4]:
        move.wait()
    for out in outs:
        put_columns(out, 0, hidden[...])
        out[FIRST_SMALL:, :] = jnp.zeros((EXTRA, LANES), BF)
        for i, part in enumerate((gain, shift, bias)):
            out[FIRST_SMALL + 2 * i : FIRST_SMALL + 2 * i + 2, :] = part[...]
    moves[4].wait()
    third = w_qkv.shape[1] // 3
    for s, k in SLOTS:
        row = (FIRST_MINE, FIRST_OTHERS)[k]
        for j in range(3):
            lanes = pl.ds(pl.multiple_of(j * third + slot_start(place, s, k, LANES), LANES), LANES)
            outs[s][row + j * ROWS : row + (j + 1) * ROWS, :] = w_qkv[:, lanes]
    moves[5].wait()
    for s, k in SLOTS:
        row = (FIRST_MINE, FIRST_OTHERS)[k] + HEADS_ROWS
        put_columns(outs[s], row, w_fc1[:, pl.ds(slot_start(place, s, k, 4 * LANES), 4 * LANES)])


def others_first_kernel(place, b0, b1, b2, b3, out):
    for s, block in enumerate((b0, b1, b2, b3)):
        out[s, :OTHERS_MINE, :] = block[:FIRST_MINE, :]
        out[s, OTHERS_MINE:OTHERS_SMALL, :] = block[FIRST_OTHERS:FIRST_SMALL, :]
        out[s, OTHERS_SMALL:, :] = block[FIRST_SMALL:, :]


def near_first_kernel(place, b0, b1, b2, b3, b4, out):
    for i, (s, k) in enumerate(SLOTS):
        block, mine_at, _ = first_block(s, k, (b0, b1, b2, b3, b4))
        out[i] = block[mine_at + HEADS_ROWS : mine_at + HEADS_ROWS + HALF_ROWS, :]


def first_block(s, k, blocks):
    if k:
        return blocks[4].at[s], OTHERS_MINE, OTHERS_SMALL
    return blocks[s], FIRST_MINE, FIRST_SMALL


def pack_heads_kernel(layer, place, w_qkv, keep, give):
    for s, k in SLOTS:
        for j in range(3):
            (keep, give)[k][s, :, j * LANES : (j + 1) * LANES] = heads_of(place, w_qkv, layer, s, k, j)


def pair_kernel(place, keep, came, *outs):
    for s, out in enumerate(outs):
        out[0], out[1] = keep[s], came[s]


def pack_units_kernel(layer, place, w_fc1, *outs):
    units = outs[0].shape[2]
    for s, k in SLOTS:
        outs[s][k] = w_fc1[layer, :, pl.ds(slot_start(place, s, k, units), units)]


def pack_units_grads_kernel(layer, place, w_fc1, grads, *outs):
    units = outs[0].shape[1]
    low = grads[...].astype(BF)
    for s in range(4):
        for k in range(2):
            lanes = pl.ds(slot_start(place, s, k, units), units)
            outs[s][k * HALF : (k + 1) * HALF, :] = w_fc1[layer, pl.ds(half_start(place, False), HALF), lanes]
            outs[s][(1 + k) * ROWS : (2 + k) * ROWS, :] = low[:, k * units : (k + 1) * units]


def near_units_kernel(place, b0, b1, b2, b3, out):
    for s, block in enumerate((b0, b1, b2, b3)):
        out[s] = block[:ROWS, :]


def others_units_grads_kernel(place, b0, b1, b2, b3, far, out):
    for s, block in enumerate((b0, b1, b2, b3)):
        out[s, :HALF, :] = block[HALF:ROWS, :]
        out[s, HALF:ROWS, :] = far[s, HALF:, :]
        out[s, ROWS:, :] = block[ROWS:, :]


def send_blocks(place, packed):
    return [packed[0]] + [swap(packed[s], 2 * s) for s in (1, 2, 3)]


def others_kernel(place, b0, b1, b2, b3, out):
    for s, block in enumerate((b0, b1, b2, b3)):
        out[s] = block[1]


def swap_others(place, blocks, after=()):
    (other,) = call(others_kernel, [((4,) + blocks[0].shape[1:], BF)], place, blocks, after=after)
    return [*blocks, swap(other, 1)]


def block_of(s, k, blocks):
    return blocks[4].at[s] if k else blocks[s].at[0]


def project_heads(normed, weight, cosine, sine, q_out, k_out, v_out, values_down):
    step = 256
    for start in range(0, normed.shape[0], step):
        rows = slice(start, start + step)
        mixed = dot(normed[rows, :], weight[...])
        q_out[rows, :] = turn(mixed[:, :LANES], cosine[rows, :], sine[rows, :], 1.0).astype(BF)
        k_out[rows, :] = turn(mixed[:, LANES : 2 * LANES], cosine[rows, :], sine[rows, :], 1.0).astype(BF)
        values = mixed[:, 2 * LANES :]
        v_out[rows, :] = values.astype(BF)
        values_down[:, rows] = values.T.astype(BF)


def own_head(head):
    down = lax.broadcasted_iota(jnp.int32, (LANES, 1), 0)
    return (down >= head * HEAD_DIM) & (down < (head + 1) * HEAD_DIM)


def softmax_block(keys, chosen, block):
    scores = mask_diagonal(dot_general(keys, chosen, (1, 1)), block)
    row_max = jnp.max(scores, axis=0, keepdims=True)
    exponent = jnp.exp(scores - row_max)
    row_total = jnp.sum(exponent, axis=0, keepdims=True)
    return exponent * (1.0 / row_total), row_max + jnp.log(row_total)


BLOCK = 256
HEADS_HERE = LANES // HEAD_DIM


def first_attend_kernel(place, b0, b1, b2, b3, b4, cosine, sine, normed, xhat_out, weight, params, q_out, k_out, v_out, att_out, log_out, values_down):
    for s, k in SLOTS:
        rows = slot_rows(place, s, k)
        block, mine_at, small_at = first_block(s, k, (b0, b1, b2, b3, b4))
        for j in range(3):
            weight[rows, j * LANES : (j + 1) * LANES] = block[mine_at + j * ROWS : mine_at + (j + 1) * ROWS, :]
        params[:, rows] = block[small_at:, :].astype(F32)
        for b in range(8):
            normed[rows, b * LANES : (b + 1) * LANES] = block[b * ROWS : (b + 1) * ROWS, :]
    gain, shift = params[0:1, :], params[2:3, :]

    def norm_rows(rows):
        xhat = standardize(normed[rows, :].astype(F32))[0]
        xhat_out[rows, :] = xhat.astype(BF)
        normed[rows, :] = (xhat * gain + shift).astype(BF)

    loop_rows(normed.shape[0], 4 * ROWS, norm_rows)
    project_heads(normed, weight, cosine, sine, q_out, k_out, v_out, values_down)
    for start in range(0, normed.shape[0], BLOCK):
        stop = start + BLOCK
        queries = q_out[start:stop, :] * SCORE_SCALE
        total = jnp.zeros((LANES, BLOCK), F32)
        for head in range(HEADS_HERE):
            chosen = jnp.where(head_mask(head), queries, 0.0).astype(BF)
            probabilities, log_total = softmax_block(k_out[:stop, :], chosen, BLOCK)
            log_out[head : head + 1, start:stop] = log_total
            found = dot(values_down[:, :stop], probabilities.astype(BF))
            total = total + jnp.where(own_head(head), found, 0.0)
        att_out[start:stop, :] = total.T.astype(BF)


GELU_A = 0.7978845608028654
GELU_B = 0.044715


def gelu(pre):
    return pre * (0.5 + 0.5 * jnp.tanh(GELU_A * pre * (1.0 + GELU_B * pre * pre)))


def gelu_slope(pre):
    square = pre * pre
    wave = jnp.tanh(GELU_A * pre * (1.0 + GELU_B * square))
    return 0.5 * (1.0 + wave) + 0.5 * pre * (1.0 - wave * wave) * (GELU_A * (1.0 + 3.0 * GELU_B * square))


def loop_rows(count, step, body):
    def one(i, carry):
        body(pl.ds(pl.multiple_of(i * step, step), step))
        return carry

    lax.fori_loop(0, count // step, one, 0)


def put_slots(place, rows_of_block, keep, give):
    for s in range(4):
        keep[s] = rows_of_block(slot_rows(place, s, 0))
        give[s] = rows_of_block(slot_rows(place, s, 1))


def put_pairs(place, rows_of_block, outs):
    for s, k in SLOTS:
        outs[s][k] = rows_of_block(slot_rows(place, s, k))


def first_units_kernel(place, normed, near, far, bias, w_fc2, w_dense, attended, weight, act, slope, whole):
    for s, k in SLOTS:
        for part, other_plane in ((near.at[SLOTS.index((s, k))], False), (far.at[SLOTS.index((s, k))], True)):
            start = slot_start(place, s, k, ROWS) + half_start(place, other_plane)
            for b in range(4):
                rows = pl.ds(pl.multiple_of(start, HALF), HALF)
                weight[rows, b * LANES : (b + 1) * LANES] = part[b * HALF : (b + 1) * HALF, :]
    shift = bias[0:1, :].astype(F32)

    def rows_done(rows):
        found = dot(normed[rows, :], weight[...]) + shift
        slope[rows, :] = gelu_slope(found)
        act[rows, :] = gelu(found).astype(BF)
        whole[rows, :] = (dot(act[rows, :], w_fc2[0]) + dot(attended[rows, :], w_dense[0])).astype(BF)

    loop_rows(normed.shape[0], 256, rows_done)


def split_kernel(place, whole, keep, give):
    put_slots(place, lambda rows: whole[rows, :], keep, give)


def split_sum_kernel(place, keep, came, for_x, for_y, corner):
    def rows_done(rows):
        for s, out in ((1, for_x), (2, for_y), (3, corner)):
            out[rows, :] = keep[s, rows, :] + came[s, rows, :]

    loop_rows(for_x.shape[0], 16, rows_done)


def begin_scatter(place, keep, give, after=()):
    came = swap(give, 1)
    shape = (keep.shape[1:], BF)
    for_x, for_y, corner = call(split_sum_kernel, [shape] * 3, place, [keep, came], after=after)
    from_corner, from_x, from_y = swap(corner, 6), swap(for_x, 2), swap(for_y, 4)
    return [keep, came, from_x, from_y, from_corner], for_x


def sum_terms(terms):
    total = terms[0][0].astype(F32) + terms[1][0].astype(F32)
    for term in terms[2:]:
        total = total + term[...].astype(F32)
    return total


def next_hidden_kernel(place, *refs):
    terms, (hidden, params, hidden_out, normed) = refs[:5], refs[5:]
    found = hidden[...].astype(F32) + sum_terms(terms) + params[4:5, :]
    hidden_out[...] = found
    normed[...] = (standardize(found)[0] * params[1:2, :] + params[3:4, :]).astype(BF)


def low_kernel(place, wide, low):
    low[...] = wide[...].astype(BF)


def assemble_kernel(place, *refs):
    for (s, k), piece in zip(SLOTS, refs[:8]):
        refs[8][slot_rows(place, s, k), :] = piece[...]


def last_hidden_kernel(place, act, attended, w_fc2, w_dense, keep, give, whole):
    def rows_done(rows):
        whole[rows, :] = (dot(act[rows, :], w_fc2[1]) + dot(attended[rows, :], w_dense[1])).astype(BF)

    loop_rows(act.shape[0], 256, rows_done)
    put_slots(place, lambda rows: whole[rows, :], keep, give)


def last_hidden_of_core(core, place, *refs):
    @pl.when(place[1] == core)
    def work():
        last_hidden_kernel(place, *refs[:4], *refs[-3:])


def last_sum_kernel(place, *refs):
    terms, (hidden, params, out, token) = refs[:5], refs[5:]
    token[...] = jnp.zeros_like(token)
    out[...] = hidden[...] + sum_terms(terms) + params[5:6, :]


SMALL_ROWS = 16


def put_halves(out, value, start, rows):
    half = out.shape[1]
    for j in range(2):
        out[j * rows + start : j * rows + start + value.shape[0], :] = value[:, j * half : (j + 1) * half]


def second_ready_kernel(place, b0, b1, b2, b3, other, far, weight, grads):
    units = weight.shape[1]
    for s, k in SLOTS:
        block = other.at[s] if k else (b0, b1, b2, b3)[s]
        parts = (block[:HALF, :], block[HALF:ROWS, :] if k else far[s, :HALF, :])
        for part, other_plane in zip(parts, (False, True)):
            start = slot_start(place, s, k, ROWS) + half_start(place, other_plane)
            weight[pl.ds(pl.multiple_of(start, HALF), HALF), :] = part
        for j in range(2):
            grads[slot_rows(place, s, k), j * units : (j + 1) * units] = block[(1 + j) * ROWS : (2 + j) * ROWS, :]


def second_units_kernel(place, *refs):
    pieces, refs = refs[:8], refs[8:]
    bias, weight, grads, normed, act, pre, chunk = refs
    units = weight.shape[1]
    for (s, k), piece in zip(SLOTS, pieces):
        normed[slot_rows(place, s, k), :] = piece[...]
    shift = bias[1:2, :].astype(F32)

    def rows_done(rows):
        found = dot(normed[rows, :], weight[...]) + shift
        pre[rows, :] = found
        act[rows, :] = gelu(found).astype(BF)

    loop_rows(normed.shape[0], 256, rows_done)
    for start in range(0, units, 256):
        put_halves(chunk, outer_sum(act[:, start : start + 256], grads[...]).astype(BF), start, units)


def units_back(layer, place, grads, w_fc2, slope_of, normed, weight, chunk, sums, part_normed, grad_pre, grad_w):
    sums[...] = jnp.zeros_like(sums)
    width = grads.shape[1]
    units = weight.shape[1]

    def rows_done(rows):
        found = (times_transposed(grads[rows, :], w_fc2[layer]) * slope_of(rows)).astype(BF)
        grad_pre[rows, :] = found
        sums[0:1, :width] += jnp.sum(grads[rows, :].astype(F32), axis=0, keepdims=True)
        sums[1:2, :units] += jnp.sum(found.astype(F32), axis=0, keepdims=True)
        part_normed[rows, :] = times_transposed(found, weight[...])

    loop_rows(grads.shape[0], 256, rows_done)
    for start in range(0, width, 256):
        rows = slice(start, start + 256)
        grad_w[rows, :] = outer_sum(normed[:, rows], grad_pre[...]).astype(BF)
    for i, (s, k) in enumerate(SLOTS):
        chunk[i * ROWS : (i + 1) * ROWS, :] = grad_w[slot_rows(place, s, k), :]


def second_units_back_kernel(place, grads, w_fc2, w_dense, pre, normed, weight, chunk, sums, part_normed, grad_att, grad_pre, grad_w):
    def slope_of(rows):
        grad_att[rows, :] = times_transposed(grads[rows, :], w_dense[1]).astype(BF)
        return gelu_slope(pre[rows, :])

    units_back(1, place, grads, w_fc2, slope_of, normed, weight, chunk, sums, part_normed, grad_pre, grad_w)


def first_units_back_kernel(place, *refs):
    pieces, refs = refs[:8], refs[8:]
    act, w_fc2, slope, normed, weight, grads, chunk_rows, chunk, sums, part_normed, grad_pre, grad_w = refs
    for (s, k), piece in zip(SLOTS, pieces):
        grads[slot_rows(place, s, k), :] = piece[...]
    units_back(
        0, place, grads, w_fc2, lambda rows: slope[rows, :], normed, weight, chunk, sums, part_normed, grad_pre, grad_w
    )
    units = act.shape[1]
    for start in range(0, units, 256):
        put_halves(chunk_rows, outer_sum(act[:, start : start + 256], grads[...]).astype(BF), start, units)


def attend_back_block(start, q_ref, k_ref, v_ref, grad_att, keys_down, k_sum, v_sum, cosine, sine, mixed, found_p):
    stop = start + BLOCK
    queries = q_ref[start:stop, :] * SCORE_SCALE
    grad_queries = jnp.zeros((LANES, BLOCK), F32)
    for head in range(HEADS_HERE):
        chosen = jnp.where(head_mask(head), queries, 0.0).astype(BF)
        chosen_grads = jnp.where(head_mask(head), grad_att, 0.0).astype(BF)
        probabilities = found_p(head, chosen)
        grad_probs = dot_general(v_ref[:stop, :], chosen_grads, (1, 1))
        row_inner = jnp.sum(grad_probs * probabilities, axis=0, keepdims=True)
        grad_scores = (probabilities * (grad_probs - row_inner)).astype(BF)
        k_sum[:stop, :] += dot(grad_scores, chosen)
        v_sum[:stop, :] += dot(probabilities.astype(BF), chosen_grads)
        grad_queries = grad_queries + jnp.where(own_head(head), dot(keys_down[:, :stop], grad_scores), 0.0)
    rows = slice(start, stop)
    mixed[rows, :LANES] = turn(grad_queries.T, cosine[rows, :], sine[rows, :], -1.0).astype(BF)


def mixed_rest(cosine, sine, mixed, k_sum, v_sum):
    mixed[:, LANES : 2 * LANES] = turn(k_sum[...], cosine[...], sine[...], -1.0).astype(BF)
    mixed[:, 2 * LANES :] = v_sum[...].astype(BF)


def mixed_outer(normed, mixed, grad_w):
    for start in range(0, normed.shape[1], 256):
        rows = slice(start, start + 256)
        grad_w[rows, :] = outer_sum(normed[:, rows], mixed[...]).astype(BF)


def mixed_inner(normed, weight, mixed, part_normed, whole):
    def rows_done(rows):
        whole[rows, :] = (times_transposed(mixed[rows, :], weight[...]) + part_normed[rows, :]).astype(BF)

    loop_rows(normed.shape[0], 256, rows_done)


def mixed_back(place, normed, weight, cosine, sine, mixed, k_sum, v_sum, grad_w, part_normed, whole):
    mixed_rest(cosine, sine, mixed, k_sum, v_sum)
    mixed_outer(normed, mixed, grad_w)
    mixed_inner(normed, weight, mixed, part_normed, whole)


def put_heads_chunk(place, chunk, grad_w, grad_dense):
    heads = grad_w.shape[1]
    for i, (s, k) in enumerate(SLOTS):
        rows = slice(i * ROWS, (i + 1) * ROWS)
        chunk[rows, :heads] = grad_w[slot_rows(place, s, k), :]
        chunk[rows, heads:] = grad_dense[:, rows]


def second_attend_kernel(place, normed, b0, b1, b2, b3, cosine, sine, grad_att, part_normed, att_out, mixed, keep_n, give_n, weight, q_ref, k_ref, v_ref, values_down, keys_down, k_sum, v_sum):
    for s, k in SLOTS:
        weight[slot_rows(place, s, k), :] = (b0, b1, b2, b3)[s][k]
    project_heads(normed, weight, cosine, sine, q_ref, k_ref, v_ref, values_down)
    k_sum[...] = jnp.zeros_like(k_sum)
    v_sum[...] = jnp.zeros_like(v_sum)
    keys_down[...] = (k_ref[...].astype(F32) * SCORE_SCALE).T.astype(BF)
    for start in range(0, normed.shape[0], BLOCK):
        stop = start + BLOCK
        total = [jnp.zeros((LANES, BLOCK), F32)]

        def found_p(head, chosen):
            probabilities, _ = softmax_block(k_ref[:stop, :], chosen, BLOCK)
            found = dot(values_down[:, :stop], probabilities.astype(BF))
            total[0] = total[0] + jnp.where(own_head(head), found, 0.0)
            return probabilities

        attend_back_block(start, q_ref, k_ref, v_ref, grad_att[start:stop, :], keys_down, k_sum, v_sum, cosine, sine, mixed, found_p)
        att_out[start:stop, :] = total[0].T.astype(BF)
    mixed_rest(cosine, sine, mixed, k_sum, v_sum)
    for s in range(4):
        rows = pl.ds(pl.multiple_of((place[0] ^ s) * 2 * ROWS, 2 * ROWS), 2 * ROWS)
        found = (times_transposed(mixed[rows, :], weight[...]) + part_normed[rows, :]).astype(BF)
        odd = place[1] == 1
        keep_n[s] = jnp.where(odd, found[ROWS:, :], found[:ROWS, :])
        give_n[s] = jnp.where(odd, found[:ROWS, :], found[ROWS:, :])


def second_heads_kernel(place, normed, mixed, attended, grads, chunk, grad_w):
    mixed_outer(normed, mixed, grad_w)
    put_heads_chunk(place, chunk, grad_w, outer_sum(attended[...], grads[...]).astype(BF))


def norm_back(gain_row, grad_normed, hidden, params, grads):
    xhat, scale = standardize(hidden[...].astype(F32))
    inner = grad_normed * params[gain_row : gain_row + 1, :]
    mean_inner = jnp.mean(inner, axis=-1, keepdims=True)
    mean_along = jnp.mean(inner * xhat, axis=-1, keepdims=True)
    return grads[...] + (inner - mean_inner - xhat * mean_along) * scale, xhat


def second_norm_back_kernel(place, *refs):
    terms, (hidden, params, grads, grads_out, grads_low, sums) = refs[:5], refs[5:]
    grad_normed = sum_terms(terms)
    found, xhat = norm_back(1, grad_normed, hidden, params, grads)
    grads_out[...] = found
    grads_low[...] = found.astype(BF)
    sums[0:1, :] = jnp.sum(grad_normed * xhat, axis=0, keepdims=True)
    sums[1:2, :] = jnp.sum(grad_normed, axis=0, keepdims=True)


def first_norm_back_kernel(place, *refs):
    terms, (hidden, params, grads, sums0, sums1, grads_out, small) = refs[:5], refs[5:]
    total = sum_terms(terms)
    grads_out[...] = norm_back(0, total[:ROWS, :], hidden, params, grads)[0]
    small[0:8, :] = total[ROWS : ROWS + 8, :LANES]
    for layer, sums in ((0, sums0), (1, sums1)):
        small[4 + layer : 5 + layer, :] = sums[0:1, slot_rows(place, 0, 0)]
        for j in range(4):
            small[8 + 4 * layer + j : 9 + 4 * layer + j, :] = sums[1:2, j * LANES : (j + 1) * LANES]


def first_attend_back_kernel(place, grads, w_dense, q_ref, k_ref, v_ref, log_in, cosine, sine, normed, xhat, weight, part_normed, ln_sums1, mixed, keep_n, give_n, keys_down, k_sum, v_sum, whole, ln_sums):
    k_sum[...] = jnp.zeros_like(k_sum)
    v_sum[...] = jnp.zeros_like(v_sum)
    keys_down[...] = (k_ref[...].astype(F32) * SCORE_SCALE).T.astype(BF)
    for start in range(0, normed.shape[0], BLOCK):
        stop = start + BLOCK

        def found_p(head, chosen):
            scores = mask_diagonal(dot_general(k_ref[:stop, :], chosen, (1, 1)), BLOCK)
            return jnp.exp(scores - log_in[head : head + 1, start:stop])

        grad_att = times_transposed(grads[start:stop, :], w_dense[0]).astype(BF)
        attend_back_block(start, q_ref, k_ref, v_ref, grad_att, keys_down, k_sum, v_sum, cosine, sine, mixed, found_p)
    mixed_rest(cosine, sine, mixed, k_sum, v_sum)
    mixed_inner(normed, weight, mixed, part_normed, whole)
    ln_sums[...] = jnp.zeros_like(ln_sums)

    def rows_done(rows):
        part = whole[rows, :].astype(F32)
        ln_sums[0:1, :] += jnp.sum(part * xhat[rows, :].astype(F32), axis=0, keepdims=True)
        ln_sums[2:3, :] += jnp.sum(part, axis=0, keepdims=True)

    loop_rows(normed.shape[0], 256, rows_done)
    ln_sums[1:2, :] = ln_sums1[0:1, :]
    ln_sums[3:4, :] = ln_sums1[1:2, :]
    for s in range(4):
        for k, out in ((0, keep_n), (1, give_n)):
            rows = slot_rows(place, s, k)
            out[s, :ROWS, :] = whole[rows, :]
            out[s, ROWS:, :] = jnp.zeros((EXTRA, out.shape[2]), BF)
            out[s, ROWS : ROWS + 8, :LANES] = ln_sums[:, rows].astype(BF)


INWARD, ACROSS, OUTWARD = [(0, 1), (3, 2)], [(1, 2), (2, 1)], [(1, 0), (2, 3)]


def along(value, pairs):
    return lax.ppermute(value, "rep", pairs)


def low_sum(left, right):
    return left[...] + right[...]


def is_middle(place):
    return (place[2] == 1) | (place[2] == 2)


def tick_kernel(has, place, *refs):
    refs = list(refs)
    if has[0]:
        chunk, came = refs.pop(0), refs.pop(0)
    if has[1]:
        before, crossed = refs.pop(0), refs.pop(0)
    if has[2]:
        coming = refs.pop(0)
    half = refs.pop(0) if has[0] else None
    going = refs.pop(0) if has[1] else None

    def half_rows(rows):
        half[rows, :] = low_sum(chunk.at[rows, :], came.at[rows, :])

    def going_rows(rows):
        found = low_sum(before.at[rows, :], crossed.at[rows, :])
        going[rows, :] = jnp.where(is_middle(place), found, coming[rows, :]) if has[2] else found

    for body, out, rows in ((half_rows, half, has[0] and chunk.shape[0]), (going_rows, going, has[1] and before.shape[0])):
        if out is not None:
            loop_rows(rows, 208 if rows % 208 == 0 else 256, body)
            if out.shape[0] > rows:
                out[rows:, :] = coming[rows:, :]


def tick(place, step, last, coming, after=(), joint=False):
    if step is not None and last is not None and not joint:
        (half,) = tick(place, step, None, None, after)
        (going,) = tick(place, None, last, coming, (half,))
        return half, going
    ins, outs = [], []
    for pair in (step, last):
        if pair is not None:
            ins += pair
            outs.append((pair[0].shape if coming is None or pair is step else coming.shape, pair[0].dtype))
    if coming is not None:
        ins.append(coming)
    has = (step is not None, last is not None, coming is not None)
    return call(partial(tick_kernel, has), outs, place, ins, after=after)


def add_small_kernel(place, chunk, small, out):
    rows = chunk.shape[0]
    out[:rows, :] = chunk[...]
    out[rows:, :LANES] = small[...].astype(BF)
    out[rows:, LANES:] = jnp.zeros((SMALL_ROWS, chunk.shape[1] - LANES), BF)


def pick_kernel(place, total, came, o0, o1, o2, o3, *rest):
    heads = o0.shape[2]
    for i, (s, k) in enumerate(SLOTS):
        out = (o0, o1, o2, o3)[s]

        def rows_done(rows):
            here = pl.ds(pl.multiple_of(rows.start + i * ROWS, rows.size), rows.size)
            found = jnp.where(is_middle(place), total[here, :], came[here, :])
            out[k, rows, :] = found[:, :heads]
            if rest:
                rest[0][rows, i * ROWS : (i + 1) * ROWS] = found[:, heads:].astype(F32)

        loop_rows(ROWS, 32, rows_done)


def pick_both_kernel(place, total_f, came_f, total_q, came_q, o0, o1, o2, o3, dense):
    units = total_f.shape[1]
    heads = o0.shape[2] - units
    for i, (s, k) in enumerate(SLOTS):
        out = (o0, o1, o2, o3)[s]

        def rows_done(rows):
            here = pl.ds(pl.multiple_of(rows.start + i * ROWS, rows.size), rows.size)
            out[k, rows, :units] = jnp.where(is_middle(place), total_f[here, :], came_f[here, :])
            found = jnp.where(is_middle(place), total_q[here, :], came_q[here, :])
            out[k, rows, units:] = found[:, :heads]
            dense[rows, i * ROWS : (i + 1) * ROWS] = found[:, heads:].astype(F32)

        loop_rows(ROWS, 32, rows_done)


def pick_both(place, units_pair, heads_pair, heads, after=()):
    columns = units_pair[0].shape[1] + heads
    outs = [((2, ROWS, columns), BF)] * 4 + [((ROWS, 8 * LANES), F32)]
    return call(pick_both_kernel, outs, place, [*units_pair, *heads_pair], after=after)


def pick(place, total, came, heads, after=()):
    outs = [((2, ROWS, heads), BF)] * 4
    if heads < total.shape[1]:
        outs.append(((ROWS, 8 * LANES), F32))
    return call(pick_kernel, outs, place, [total, came], after=after)


def chosen_sum(place, total, outward):
    middle = (place[2] == 1) | (place[2] == 2)
    return jnp.where(middle, total, outward).astype(F32)


def final_call(body, place, ins, shape, layer, before=None, after=()):
    skip = len(after) + (before is not None)

    def run(place, *refs):
        *ins, out, token, found, sems = refs[skip:]
        body(place, ins, out.at[layer], found, sems)
        token[...] = jnp.zeros_like(token)

    return pl.pallas_call(
        run,
        name=body.__name__,
        out_shape=[jax.ShapeDtypeStruct((2,) + shape, F32), jax.ShapeDtypeStruct((8, LANES), F32)],
        in_specs=[pl.BlockSpec(memory_space=pltpu.SMEM)]
        + [pl.BlockSpec(memory_space=pltpu.HBM)] * (before is not None)
        + [pl.BlockSpec(memory_space=pl.ANY)] * len(after)
        + [pl.BlockSpec(memory_space=pltpu.VMEM)] * len(ins),
        out_specs=[pl.BlockSpec(memory_space=pltpu.HBM), pl.BlockSpec(memory_space=pltpu.VMEM)],
        scratch_shapes=[pltpu.VMEM(shape, F32), pltpu.SemaphoreType.DMA((8,))],
        input_output_aliases={} if before is None else {1: 0},
        compiler_params=pltpu.CompilerParams(vmem_limit_bytes=16 * 1024 * 1024),
        cost_estimate=SMALL,
    )(place, *([] if before is None else [before]), *after, *ins)


def final_rows_start(place, total, came, out, found, sems):
    half, rows = total.shape[1], out.shape[0]
    step = rows // 4

    def move(i):
        put = pl.ds(pl.multiple_of(i * step, step), step)
        return pltpu.make_async_copy(found.at[put, :], out.at[put, :], sems.at[i])

    def one(i, carry):
        put = pl.ds(pl.multiple_of(i * step, step), step)
        for j in range(2):
            part = pl.ds(pl.multiple_of(i * step + j * rows, step), step)
            found[put, j * half : (j + 1) * half] = jnp.where(is_middle(place), total[part, :], came[part, :]).astype(F32)
        move(i).start()
        return carry

    lax.fori_loop(0, 4, one, 0)
    return [move(i) for i in range(4)]


def final_rows_kernel(place, ins, out, found, sems):
    for move in final_rows_start(place, *ins, out, found, sems):
        move.wait()


def final_units_kernel(place, blocks, out, found, sems):
    units, moves = out.shape[1] // 8, []
    for i, (s, k) in enumerate(SLOTS):
        put = slice(i * units, (i + 1) * units)
        block = block_of(s, k, blocks)

        def rows_done(rows):
            found[rows, put] = block[rows, :units].astype(F32)

        loop_rows(ROWS, 32, rows_done)
        moves.append(pltpu.make_async_copy(found.at[:, put], out.at[:, slot_rows(place, s, k, units)], sems.at[i]))
        moves[-1].start()
    for move in moves:
        move.wait()


def final_heads_kernel(place, blocks, out, found, sems):
    third = out.shape[1] // 3
    for s, k in SLOTS:
        block = block_of(s, k, blocks)

        def rows_done(rows):
            part = block[rows, block.shape[1] - 3 * LANES :].astype(F32)
            for j in range(3):
                lanes = pl.ds(pl.multiple_of(j * third + slot_start(place, s, k, LANES), LANES), LANES)
                found[rows, lanes] = part[:, j * LANES : (j + 1) * LANES]

        loop_rows(ROWS, 32, rows_done)
    move = pltpu.make_async_copy(found, out, sems.at[0])
    move.start()
    move.wait()


def last_rows_kernel(place, before, total, came, out, gain, shift, bias_fc1, bias_fc2, found, sems):
    rows = slice(total.shape[0] - SMALL_ROWS, total.shape[0])
    small = jnp.where(is_middle(place), total[rows, :LANES], came[rows, :LANES]).astype(F32)
    moves = final_rows_start(place, total, came, out.at[0], found, sems)
    gain[...] = small[0:2, :]
    shift[...] = small[2:4, :]
    bias_fc2[...] = small[4:6, :]
    for layer in range(2):
        for j in range(4):
            bias_fc1[layer : layer + 1, j * LANES : (j + 1) * LANES] = small[8 + 4 * layer + j : 9 + 4 * layer + j, :]
    for move in moves:
        move.wait()


def local_plane(hidden_in, ln_gain, ln_bias, w_qkv, w_dense, w_fc1, b_fc1, w_fc2, b_fc2, output_grad):
    index = lax.axis_index("grp")
    place = jnp.stack([index // 2, index % 2, lax.axis_index("rep")]).astype(jnp.int32)
    span, width = hidden_in.shape[1:]
    seq = span * 8
    units = b_fc1.shape[1]
    own = 3 * LANES
    cosine, sine = rotary_tables(seq)
    hidden0 = hidden_in.reshape(span, width)
    grads1 = output_grad.reshape(span, width)

    wide, column, chunk_shape = ((seq, width), BF), ((seq, LANES), BF), ((seq, units), BF)
    blocks_n, blocks_n0 = ((4, ROWS, width), BF), ((4, ROWS + EXTRA, width), BF)
    blocks_f, blocks_q = ((2, ROWS, units), BF), ((2, ROWS, own), BF)
    mine, mine_low = ((span, width), F32), ((span, width), BF)
    sums_shape, part_shape = ((8, width), F32), ((seq, width), F32)
    head_scratch = [pltpu.VMEM((LANES, seq), BF), pltpu.VMEM((seq, LANES), F32), pltpu.VMEM((seq, LANES), F32)]
    back_scratch = [pltpu.VMEM((seq, own), BF), pltpu.VMEM((width, own), BF), pltpu.VMEM((seq, width), BF)]
    column_scratch = [pltpu.VMEM((seq, LANES), BF)] * 3
    units_scratch = [pltpu.VMEM((seq, units), BF), pltpu.VMEM((width, units), BF)]

    rows = [hidden0.shape, ln_gain.shape, ln_bias.shape, b_fc2.shape, w_qkv.shape[1:], (HALF, w_fc1.shape[2])]
    rows = [rows[0], *rows[4:], *rows[1:4]]
    packed = pl.pallas_call(
        pack_first_kernel,
        name="pack_first_kernel",
        out_shape=[jax.ShapeDtypeStruct((FIRST_ROWS, LANES), BF)] * 4,
        in_specs=[pl.BlockSpec(memory_space=pltpu.HBM)] * 6,
        out_specs=[pl.BlockSpec(memory_space=pltpu.VMEM)] * 4,
        scratch_shapes=[pltpu.VMEM(shape, BF) for shape in rows] + [pltpu.SemaphoreType.DMA((6,))],
        compiler_params=pltpu.CompilerParams(vmem_limit_bytes=60 * 1024 * 1024),
        cost_estimate=SMALL,
    )(hidden0, w_qkv, w_fc1, ln_gain, ln_bias, b_fc2)
    first = send_blocks(place, packed)
    packed = call(partial(pack_units_grads_kernel, 1), [((3 * ROWS, units), BF)] * 4, place, [w_fc1, grads1])
    keep, give = call(partial(pack_heads_kernel, 1), [((4, ROWS, own), BF)] * 2, place, [w_qkv], after=[packed[0]])
    pairs1 = call(pair_kernel, [blocks_q] * 4, place, [keep, swap(give, 1)])
    (others0,) = call(others_first_kernel, [((4, OTHERS_ROWS, LANES), BF)], place, first, after=[pairs1[0]])
    units1 = send_blocks(place, packed)
    first = [*first, swap(others0, 1)]
    (near0,) = call(near_first_kernel, [((8, HALF_ROWS, LANES), BF)], place, first)
    far0 = along(near0, INWARD + OUTWARD)

    normed0, xhat0, weight_q0, params, q0, k0, v0, att0, log0 = call(
        first_attend_kernel,
        [wide, wide, ((width, own), BF), ((EXTRA, width), F32), column, column, column, column, ((8, seq), F32)],
        place,
        [*first, cosine, sine],
        [pltpu.VMEM((LANES, seq), BF)],
        after=[near0],
    )
    weight_f0, act0, slope0, partial_sum = call(
        first_units_kernel,
        [((width, units), BF), ((seq, units), BF), ((seq, units), F32), wide],
        place,
        [normed0, near0, far0, b_fc1, w_fc2, w_dense, att0],
    )
    (near1,) = call(near_units_kernel, [((4, ROWS, units), BF)], place, units1, after=[partial_sum])
    far1 = along(near1, INWARD + OUTWARD)
    keep, give = call(split_kernel, [blocks_n, blocks_n], place, [partial_sum], after=[near1])
    terms, sent = begin_scatter(place, keep, give)
    hidden1, normed1_own = call(next_hidden_kernel, [mine, mine_low], place, [*terms, hidden0, params], after=[far1])
    (others1,) = call(others_units_grads_kernel, [((4, 3 * ROWS, units), BF)], place, [*units1, far1], after=[normed1_own])
    pieces = gather_pieces(normed1_own)

    weight_f1, grad_branch1 = call(
        second_ready_kernel, [((width, units), BF), wide], place, [*units1, swap(others1, 1), far1]
    )
    normed1, act1, pre1, chunk1 = call(
        second_units_kernel,
        [wide, ((seq, units), BF), ((seq, units), F32), chunk_shape],
        place,
        [*pieces, b_fc1, weight_f1, grad_branch1],
    )
    came1 = along(chunk1, INWARD + OUTWARD)
    heads1 = send_blocks(place, pairs1)
    chunk2, sums1, part_normed, grad_att1 = call(
        second_units_back_kernel,
        [chunk_shape, sums_shape, part_shape, column],
        place,
        [grad_branch1, w_fc2, w_dense, pre1, normed1, weight_f1],
        units_scratch,
    )
    att1, mixed1, keep, give = call(
        second_attend_kernel,
        [column, ((seq, own), BF), blocks_n, blocks_n],
        place,
        [normed1, *heads1, cosine, sine, grad_att1, part_normed],
        [
            pltpu.VMEM((width, own), BF),
            *column_scratch,
            pltpu.VMEM((LANES, seq), BF),
            *head_scratch,
        ],
    )
    terms, sent = begin_scatter(place, keep, give)
    (half1,) = tick(place, (chunk1, came1), None, None, after=[give])
    (chunk3,) = call(
        second_heads_kernel,
        [chunk_shape],
        place,
        [normed1, mixed1, att1, grad_branch1],
        [pltpu.VMEM((width, own), BF)],
        after=[half1, sent],
    )
    cross1, came2 = along(half1, ACROSS), along(chunk2, INWARD + OUTWARD)
    grads0, grads0_low, ln_sums1 = call(
        second_norm_back_kernel, [mine, mine_low, sums_shape], place, [*terms, hidden1, params, grads1], after=[half1]
    )

    pieces = gather_pieces(grads0_low)
    half2, total1 = tick(place, (chunk2, came2), (half1, cross1), chunk3, after=[pieces[1]], joint=True)
    cross2, came3 = along(half2, ACROSS), along(total1, INWARD + OUTWARD)
    grad_branch0, chunk6, chunk4, sums0, part_normed = call(
        first_units_back_kernel,
        [wide, chunk_shape, chunk_shape, sums_shape, part_shape],
        place,
        [*pieces, act0, w_fc2, slope0, normed0, weight_f0],
        units_scratch,
        after=[half2],
    )
    mixed0, keep, give = call(
        first_attend_back_kernel,
        [((seq, own), BF), blocks_n0, blocks_n0],
        place,
        [grad_branch0, w_dense, q0, k0, v0, log0, cosine, sine, normed0, xhat0, weight_q0, part_normed, ln_sums1],
        [*head_scratch, pltpu.VMEM((seq, width), BF), pltpu.VMEM((8, width), F32)],
    )
    last_ins, whole_scratch = [act1, att1, w_fc2, w_dense], [pltpu.VMEM((seq, width), BF)]
    blocks_h = call(partial(last_hidden_of_core, 0), [blocks_n, blocks_n], place, last_ins, whole_scratch, after=[mixed0])
    half3, total2 = tick(place, (chunk3, came3), (half2, cross2), chunk4, after=[blocks_h[0]], joint=True)
    keep_h, give_h = call(
        partial(last_hidden_of_core, 1), [blocks_n, blocks_n], place, [*last_ins, *blocks_h], whole_scratch, after=[half3], held=2
    )
    cross3, came4 = along(half3, ACROSS), along(total2, INWARD + OUTWARD)
    (chunk5,) = call(
        second_heads_kernel,
        [chunk_shape],
        place,
        [normed0, mixed0, att0, grad_branch0],
        [pltpu.VMEM((width, own), BF)],
        after=[half3],
    )
    token = ((8, LANES), F32)
    terms, sent = begin_scatter(place, keep, give, after=[half3])
    out_fc2, done = final_call(final_rows_kernel, place, [total1, came3], (units, width), 1, after=[sent])
    input_grad, small_sums = call(
        first_norm_back_kernel,
        [mine, ((SMALL_ROWS, LANES), F32)],
        place,
        [*terms, hidden0, params, grads0, sums0, sums1],
        after=[done],
    )
    half4, total3 = tick(place, (chunk4, came4), (half3, cross3), chunk5, after=[small_sums], joint=True)
    cross4, came5 = along(half4, ACROSS), along(total3, INWARD + OUTWARD)
    (chunk6,) = call(
        add_small_kernel, [((seq + SMALL_ROWS, units), BF)], place, [chunk6, small_sums], after=[half4]
    )
    terms, _ = begin_scatter(place, keep_h, give_h, after=[half4])
    hidden_out, done_h = call(last_sum_kernel, [mine, token], place, [*terms, hidden1, params], after=[chunk6])
    half5, total4 = tick(place, (chunk5, came5), (half4, cross4), chunk6, after=[done_h], joint=True)
    cross5, came6 = along(half5, ACROSS), along(total4, INWARD + OUTWARD)
    *picked1, dense1 = pick_both(place, (total2, came4), (total3, came5), own, after=[half5])
    blocks1 = swap_others(place, send_blocks(place, picked1))
    half6, total5 = tick(place, (chunk6, came6), (half5, cross5), None, after=[blocks1[1]], joint=True)
    cross6, came7 = along(half6, ACROSS), along(total5, INWARD + OUTWARD)
    picked4 = pick(place, total4, came6, units, after=[half6])
    out_fc1, done1 = final_call(final_units_kernel, place, blocks1, (ROWS, w_fc1.shape[2]), 1, after=[picked4[0]])
    out_qkv, done3 = final_call(final_heads_kernel, place, blocks1, (ROWS, w_qkv.shape[2]), 1, after=[done1])
    blocks4 = swap_others(place, send_blocks(place, picked4), after=[done3])
    (total6,) = tick(place, None, (half6, cross6), None, after=[blocks4[1]])
    came8 = along(total6, INWARD + OUTWARD)
    *picked5, dense0 = pick(place, total5, came7, own, after=[total6])
    out_fc1, done4 = final_call(final_units_kernel, place, blocks4, (ROWS, w_fc1.shape[2]), 0, out_fc1, after=[picked5[0]])
    blocks5 = swap_others(place, send_blocks(place, picked5), after=[done4])
    out_qkv, done5 = final_call(final_heads_kernel, place, blocks5, (ROWS, w_qkv.shape[2]), 0, out_qkv)
    vector = jax.ShapeDtypeStruct((2, LANES), F32)
    out_fc2, out_gain, out_shift, out_b_fc1, out_b_fc2 = pl.pallas_call(
        lambda place, before, token, *refs: last_rows_kernel(place, before, *refs),
        name="last_rows_kernel",
        out_shape=[jax.ShapeDtypeStruct((2, units, width), F32), vector, vector, jax.ShapeDtypeStruct((2, units), F32), vector],
        in_specs=[pl.BlockSpec(memory_space=pltpu.SMEM), pl.BlockSpec(memory_space=pltpu.HBM)]
        + [pl.BlockSpec(memory_space=pl.ANY)]
        + [pl.BlockSpec(memory_space=pltpu.VMEM)] * 2,
        out_specs=[pl.BlockSpec(memory_space=pltpu.HBM)] + [pl.BlockSpec(memory_space=pltpu.VMEM)] * 4,
        scratch_shapes=[pltpu.VMEM((units, width), F32), pltpu.SemaphoreType.DMA((4,))],
        input_output_aliases={1: 0},
        compiler_params=pltpu.CompilerParams(vmem_limit_bytes=16 * 1024 * 1024),
        cost_estimate=SMALL,
    )(place, out_fc2, done5, total6, came8)
    out_dense = jnp.stack([dense0, dense1])
    return (
        hidden_out[None],
        input_grad[None],
        out_gain,
        out_shift,
        out_qkv,
        out_dense,
        out_fc1,
        out_b_fc1,
        out_fc2,
        out_b_fc2,
    )


def local(hidden_in, ln_gain, ln_bias, w_qkv, w_dense, w_fc1, b_fc1, w_fc2, b_fc2, output_grad):
    arguments = (hidden_in, ln_gain, ln_bias, w_qkv, w_dense, w_fc1, b_fc1, w_fc2, b_fc2, output_grad)
    plane = lax.axis_size("grp") == 8 and lax.axis_size("rep") == 4
    plane = plane and hidden_in.shape[:2] == (1, ROWS) and w_qkv.shape == (2, LANES, 3 * 8 * LANES)
    return (local_plane if plane else local_any)(*arguments)


def solution(mesh):
    in_specs = (
        P("rep", "grp", None),
        P(None, "grp"),
        P(None, "grp"),
        P(None, "grp", None),
        P(None, "grp", None),
        P(None, "grp", None),
        P(None, "grp"),
        P(None, "grp", None),
        P(None, "grp"),
        P("rep", "grp", None),
    )
    out_specs = (
        P("rep", "grp", None),
        P("rep", "grp", None),
        P(None, "grp"),
        P(None, "grp"),
        P(None, "grp", None),
        P(None, "grp", None),
        P(None, "grp", None),
        P(None, "grp"),
        P(None, "grp", None),
        P(None, "grp"),
    )
    return jax.shard_map(local, mesh=mesh, in_specs=in_specs, out_specs=out_specs, check_vma=False)
```
